256 devices in a mesh: dp: 16 (over z_hi, y, core), ctx: 16 (over z_lo, x).
Axes of the slice: x: 4, y: 4, z: 8 (z_hi: 2, z_lo: 4; z = z_hi * 4 + z_lo), core: 2. Of those that a mesh axis runs over, the one named last changes fastest.
Arguments:
- q_self: bfloat16 [16, 2048, 2048], P('dp', 'ctx'), may hold values from -128 to 128
- k_self: bfloat16 [16, 2048, 2048], P('dp', 'ctx'), may hold values from -10 to 10
- v_self: bfloat16 [16, 2048, 2048], P('dp', 'ctx'), may hold values from -6 to 6
- q_cross: bfloat16 [16, 2048, 2048], P('dp', 'ctx'), may hold values from -128 to 128
- db_keys: bfloat16 [32, 128, 2048], P('dp'), may hold values from -10 to 10
- db_values: bfloat16 [32, 128, 2048], P('dp'), may hold values from -6 to 6
- nb_shard: int32 [16, 32, 2], P('dp', 'ctx'), may hold values from 0 to 15, as said below
- nb_row: int32 [16, 32, 2], P('dp', 'ctx'), may hold values from 0 to 1
Outputs:
- mixed: bfloat16 [16, 2048, 2048], P('dp', 'ctx')
The draws below stay inside these ranges and needn't reach their ends.
Inputs may be any that keep to these rules, and one draw needn't show every extreme that they name: `nb_shard`: at most 1 of the neighbours of the groups of one device lie on one shard, and some shard holds exactly 1 of them.
All inputs are finite; a program needn't handle non-finite values.
Results may differ from the reference program's by a relative error of at most 0.0045.
Values may be sent and summed in bfloat16 or wider, within the bound.
A program may use at most 128 MiB of HBM per device.

```python
import jax
import jax.numpy as jnp
from jax import lax

HEADS = 16
HD = 128
GROUP = 64
NEIGH = 2
NLEN = 128
DB_DEV = 2
GROUP_DEV = 2
SEQ = 2048
GROUPS = 32
DOCS = 16
DB_ROWS = 32
CAP = 1
N_DP = 16
N_CTX = 16


def self_base(key):
    first = jax.random.fold_in(key, 101)
    second = jax.random.fold_in(key, 102)
    queries = jnp.clip(jax.random.normal(first, (DOCS, SEQ, HEADS * HD), jnp.float32), -6.0, 6.0)
    keyset = jnp.clip(jax.random.normal(second, (DOCS, SEQ, HEADS * HD), jnp.float32), -6.0, 6.0)
    return (queries, 1.4 * keyset)


def neighbour_lists(key):
    first = jax.random.fold_in(key, 201)
    second = jax.random.fold_in(key, 202)
    per_block = GROUP_DEV * NEIGH
    pool = jnp.arange(CAP * N_DP, dtype=jnp.int32) % N_DP
    block_keys = jax.random.split(first, DOCS * N_CTX)
    shuffled = jax.vmap(lambda one: jax.random.permutation(one, pool))(block_keys)[:, :per_block]
    shards = shuffled.reshape(DOCS, GROUPS, NEIGH).astype(jnp.int32)
    rowids = jax.random.randint(second, (DOCS, GROUPS, NEIGH), 0, DB_DEV, dtype=jnp.int32)
    rowids = rowids.at[0, 0, 0].set(DB_DEV - 1).at[0, 0, 1].set(0)
    return (shards, rowids)


def database_base(key):
    first = jax.random.fold_in(key, 301)
    return 1.4 * jnp.clip(jax.random.normal(first, (DB_ROWS, NLEN, HEADS * HD), jnp.float32), -6.0, 6.0)


def draw_q_self(key, part):
    queries, keyset = self_base(key)
    return (1.4 * queries).astype(jnp.bfloat16)


def draw_k_self(key, part):
    queries, keyset = self_base(key)
    return keyset.astype(jnp.bfloat16)


def draw_q_cross(key, part):
    key = jax.random.fold_in(key, 3)
    normal_part = jnp.clip(jax.random.normal(key, (DOCS, SEQ, HEADS * HD), jnp.float32), -6.0, 6.0)
    return (1.4 * normal_part).astype(jnp.bfloat16)


def draw_db_keys(key, part):
    dbase = database_base(key)
    return dbase.astype(jnp.bfloat16)


def draw_nb_shard(key, part):
    shards, rowids = neighbour_lists(key)
    return shards


def draw_nb_row(key, part):
    shards, rowids = neighbour_lists(key)
    return rowids


def levels(own_key, shape, cuts, least, largest):
    factor_of, own = 1.0, jax.random.fold_in(own_key, 6)
    for dim, parts in cuts:
        steps = jnp.exp(jax.random.uniform(jax.random.fold_in(own, dim), (parts,), jnp.float32, least / len(cuts), largest / len(cuts)))
        factor_of = factor_of * jnp.repeat(steps, shape[dim] // parts).reshape([-1 if axis == dim else 1 for axis in range(len(shape))])
    return factor_of


def centred(key, shape, scale, limit, cuts=(), held_as=jnp.bfloat16):
    array = jax.random.normal(key, shape, jnp.float32) * scale
    if len(cuts) > 0:
        array = levels(key, shape, cuts, -0.22, 0.18) * array
    return jnp.clip(array, min=-limit, max=limit).astype(held_as)


def setup_inputs(seed: int = 0) -> dict:
    key_of = jax.random.split(jax.random.key(seed), 9)
    q_self = draw_q_self(jax.random.fold_in(key_of[8], 71), 0)
    k_self = draw_k_self(jax.random.fold_in(key_of[8], 71), 0)
    v_self = centred(key_of[2], (DOCS, SEQ, HEADS * HD), 1.0, 6.0, ((0, 16), (1, 16)))
    q_cross = draw_q_cross(jax.random.fold_in(key_of[8], 71), 0)
    db_keys = draw_db_keys(jax.random.fold_in(key_of[8], 71), 0)
    db_values = centred(key_of[5], (DB_ROWS, NLEN, HEADS * HD), 1.0, 6.0, ((0, 16),))
    nb_shard = draw_nb_shard(jax.random.fold_in(key_of[8], 71), 0)
    nb_row = draw_nb_row(jax.random.fold_in(key_of[8], 71), 0)
    return {"q_self": q_self, "k_self": k_self, "v_self": v_self, "q_cross": q_cross, "db_keys": db_keys, "db_values": db_values, "nb_shard": nb_shard, "nb_row": nb_row}


def self_document(packed):
    q_doc, k_doc, v_doc = packed
    score_scale = HD ** -0.5
    q_heads = q_doc.astype(jnp.float32).reshape(SEQ, HEADS, HD)
    k_heads = k_doc.astype(jnp.float32).reshape(SEQ, HEADS, HD)
    v_heads = v_doc.astype(jnp.float32).reshape(SEQ, HEADS, HD)
    block_len = min(512, SEQ)
    results = []
    for begin in range(0, SEQ, block_len):
        finish = begin + block_len
        scores = jnp.einsum("qhd,khd->hqk", q_heads[begin:finish], k_heads[:finish]) * score_scale
        allowed = jnp.arange(finish)[None, :] <= (begin + jnp.arange(block_len))[:, None]
        scores = jnp.where(allowed[None], scores, -1e30)
        row_top = jnp.max(scores, axis=-1, keepdims=True)
        weights = jnp.where(allowed[None], jnp.exp(scores - row_top), 0.0)
        totals = jnp.sum(weights, axis=-1)
        rounded = lax.optimization_barrier(weights.astype(jnp.bfloat16)).astype(jnp.float32)
        block_out = jnp.einsum("hqk,khd->qhd", rounded, v_heads[:finish])
        block_out = block_out / jnp.transpose(totals)[:, :, None]
        results.append(block_out.reshape(block_len, HEADS * HD))
    return jnp.concatenate(results, axis=0).astype(jnp.bfloat16)


def cross_document(packed, db_keys, db_values):
    q_doc, shard_doc, row_doc = packed
    score_scale = HD ** -0.5
    blocks = shard_doc * DB_DEV + row_doc
    keys_all = db_keys[blocks].astype(jnp.float32).reshape(GROUPS, NEIGH, NLEN, HEADS, HD)
    values_all = db_values[blocks].astype(jnp.float32).reshape(GROUPS, NEIGH, NLEN, HEADS, HD)
    q_heads = q_doc.astype(jnp.float32).reshape(GROUPS, GROUP, HEADS, HD)
    scores = jnp.einsum("cqhd,cnkhd->cnhqk", q_heads, keys_all) * score_scale
    row_top = jnp.max(scores, axis=-1)
    weights = jnp.exp(scores - row_top[..., None])
    totals = jnp.sum(weights, axis=-1)
    rounded = lax.optimization_barrier(weights.astype(jnp.bfloat16)).astype(jnp.float32)
    partial_value = jnp.einsum("cnhqk,cnkhd->cnqhd", rounded, values_all)
    partial_value = partial_value / jnp.transpose(totals, (0, 1, 3, 2))[..., None]
    spread = row_top + jnp.log(totals)
    peak = jnp.max(spread, axis=1, keepdims=True)
    shares = jnp.exp(spread - peak)
    denom = jnp.sum(shares, axis=1)
    shares_t = jnp.transpose(shares, (0, 1, 3, 2))[..., None]
    cross_out = jnp.sum(shares_t * partial_value, axis=1) / jnp.transpose(denom, (0, 2, 1))[..., None]
    return cross_out.reshape(SEQ, HEADS * HD)


def reference(q_self, k_self, v_self, q_cross, db_keys, db_values, nb_shard, nb_row):
    self_out = lax.map(self_document, (q_self, k_self, v_self))
    cross_out = lax.map(lambda packed: cross_document(packed, db_keys, db_values), (q_cross, nb_shard, nb_row))
    return (self_out.astype(jnp.float32) + cross_out).astype(jnp.bfloat16)
```

```python
import functools

import jax
import jax.numpy as jnp
from jax import lax
from jax.experimental import pallas as pl
from jax.experimental.pallas import tpu as pltpu
from jax.sharding import PartitionSpec as P

HEADS = 16
HD = 128
GROUP = 64
NEIGH = 2
NLEN = 128
TOK = 128
DB_DEV = 2
N_CTX = 16
N_DP = 16
HALF = 8
ROWS = 256
BLOCKS = N_CTX * TOK // ROWS
EXPO = HD**-0.5 * 1.4426950408889634
MESH = pl.DeviceIdType.MESH
NT = (((1,), (1,)), ((), ()))
NN = (((1,), (0,)), ((), ()))
IDX, QC, KS, VS, QS, OUT = range(6)


def cols(head):
    return pl.ds(pl.multiple_of(head * HD, HD), HD)


def kernel(
    qs_ref, ks_ref, vs_ref, qc_ref, kd_ref, vd_ref, shard_ref, row_ref, out_ref,
    qs, ks, vs, qc, kd, vd, idx, idx_s, cross, scores, mixed,
    send_sem, recv_sem, db_send, db_recv, far_send, far_recv, own_sem,
):
    dp = lax.axis_index("dp")
    me = lax.axis_index("ctx")
    near = lax.rem(dp, HALF)
    side = dp - near
    far_dp = (HALF - side) + near
    far_ctx = (3 - me // 4) * 4 + lax.rem(me, 4)

    def ctx_peer(k):
        return lax.rem(me + k, N_CTX)

    def dp_peer(k):
        return side + lax.rem(near + k, HALF)

    barrier = pltpu.get_barrier_semaphore()

    def greet_ctx(k, carry):
        pl.semaphore_signal(barrier, inc=1, device_id={"dp": dp, "ctx": ctx_peer(k)}, device_id_type=MESH)
        return carry

    def greet_dp(k, carry):
        pl.semaphore_signal(barrier, inc=1, device_id={"dp": dp_peer(k), "ctx": me}, device_id_type=MESH)
        return carry

    lax.fori_loop(1, N_CTX, greet_ctx, 0)
    lax.fori_loop(1, HALF, greet_dp, 0)
    pl.semaphore_signal(barrier, inc=1, device_id={"dp": far_dp, "ctx": far_ctx}, device_id_type=MESH)

    lane = lax.broadcasted_iota(jnp.int32, (8, 128), 1)
    tile = jnp.zeros((8, 128), jnp.int32)
    for g in range(TOK // GROUP):
        for n in range(NEIGH):
            block = shard_ref[0, g, n] * DB_DEV + row_ref[0, g, n]
            tile = jnp.where(lane == g * NEIGH + n, block, tile)
    idx[me] = tile

    own = []
    for slot, (src, dst) in enumerate(
        [
            (qc_ref.at[:, cols(me)], qc.at[me]),
            (ks_ref.at[:, cols(me)], ks.at[me]),
            (vs_ref.at[:, cols(me)], vs.at[me]),
            (qs_ref.at[:, cols(me)], qs.at[me]),
            (kd_ref.at[:, :, cols(me)], kd.at[pl.ds(dp * DB_DEV, DB_DEV)]),
            (vd_ref.at[:, :, cols(me)], vd.at[pl.ds(dp * DB_DEV, DB_DEV)]),
        ]
    ):
        copy = pltpu.make_async_copy(src, dst, own_sem.at[slot])
        copy.start()
        own.append(copy)

    pl.semaphore_wait(barrier, N_CTX - 1 + HALF - 1 + 1)

    def far_copy(kind):
        src, dst = ((kd_ref, kd), (vd_ref, vd))[kind]
        return pltpu.make_async_remote_copy(
            src.at[:, :, cols(far_ctx)], dst.at[pl.ds(dp * DB_DEV, DB_DEV)],
            far_send.at[kind], far_recv.at[kind],
            device_id={"dp": far_dp, "ctx": far_ctx}, device_id_type=MESH,
        )

    def near_copy(kind, k):
        src, dst = ((kd_ref, kd), (vd_ref, vd))[kind]
        return pltpu.make_async_remote_copy(
            src.at[:, :, cols(me)], dst.at[pl.ds(dp * DB_DEV, DB_DEV)],
            db_send.at[kind, 0, k], db_recv.at[kind, dp],
            device_id={"dp": dp_peer(k), "ctx": me}, device_id_type=MESH,
        )

    def pass_copy(kind, k):
        buf = (kd, vd)[kind]
        part = buf.at[pl.ds(far_dp * DB_DEV, DB_DEV)]
        return pltpu.make_async_remote_copy(
            part, part, db_send.at[kind, 1, k], db_recv.at[kind, far_dp],
            device_id={"dp": dp_peer(k), "ctx": me}, device_id_type=MESH,
        )

    def ctx_copy(kind, k):
        peer = ctx_peer(k)
        if kind == IDX:
            src = idx.at[me]
            dst = idx.at[me]
        else:
            arg, buf = {QC: (qc_ref, qc), KS: (ks_ref, ks), VS: (vs_ref, vs), QS: (qs_ref, qs)}[kind]
            src, dst = arg.at[:, cols(peer)], buf.at[me]
        return pltpu.make_async_remote_copy(
            src, dst, send_sem.at[kind, peer], recv_sem.at[kind, me],
            device_id={"dp": dp, "ctx": peer}, device_id_type=MESH,
        )

    def arrived(kind, source):
        buf = {IDX: idx, QC: qc, KS: ks, VS: vs, QS: qs}[kind].at[source]
        pltpu.make_async_remote_copy(
            buf, buf, send_sem.at[kind, source], recv_sem.at[kind, source],
            device_id={"dp": dp, "ctx": source}, device_id_type=MESH,
        ).wait_recv()

    far = [far_copy(kind) for kind in range(2)]
    for copy in far:
        copy.start()

    def start_first(k, carry):
        ctx_copy(IDX, k).start()
        ctx_copy(QC, k).start()
        return carry

    def start_near(k, carry):
        near_copy(0, k).start()
        near_copy(1, k).start()
        return carry

    def start_self(k, carry):
        ctx_copy(KS, k).start()
        ctx_copy(QS, k).start()
        ctx_copy(VS, k).start()
        return carry

    lax.fori_loop(1, HALF, start_near, 0)
    lax.fori_loop(1, N_CTX, start_first, 0)
    lax.fori_loop(1, N_CTX, start_self, 0)

    for copy in far:
        copy.wait_recv()

    def start_pass(k, carry):
        pass_copy(0, k).start()
        pass_copy(1, k).start()
        return carry

    lax.fori_loop(1, HALF, start_pass, 0)

    def wait_first(k, carry):
        arrived(IDX, ctx_peer(k))
        arrived(QC, ctx_peer(k))
        return carry

    def wait_blocks(k, carry):
        for home in (side, HALF - side):
            shard = home + lax.rem(near + k, HALF)
            for kind, buf in enumerate((kd, vd)):
                part = buf.at[pl.ds(shard * DB_DEV, DB_DEV)]
                pltpu.make_async_remote_copy(
                    part, part, db_send.at[kind, 0, k], db_recv.at[kind, shard],
                    device_id={"dp": dp_peer(k), "ctx": me}, device_id_type=MESH,
                ).wait_recv()
        return carry

    for copy in own:
        copy.wait()
    lax.fori_loop(1, N_CTX, wait_first, 0)
    numbers = pltpu.make_async_copy(idx, idx_s, own_sem.at[0])
    numbers.start()
    numbers.wait()
    lax.fori_loop(1, HALF, wait_blocks, 0)

    def cross_step(step, carry):
        for part in range(2):
            t = step * 2 + part
            for g in range(TOK // GROUP):
                first = idx_s[t, 0, g * NEIGH]
                second = idx_s[t, 0, g * NEIGH + 1]
                keys = jnp.concatenate([kd[first], kd[second]], axis=0)
                values = jnp.concatenate([vd[first], vd[second]], axis=0)
                rows = pl.ds(g * GROUP, GROUP)
                s = lax.dot_general(qc[t, rows, :], keys, NT, preferred_element_type=jnp.float32)
                top = jnp.max(s, axis=1, keepdims=True)
                w = jnp.exp2((s - top) * EXPO)
                total = jnp.sum(w, axis=1, keepdims=True)
                o = lax.dot_general(w.astype(jnp.bfloat16), values, NN, preferred_element_type=jnp.float32)
                cross[t, rows, :] = o / total
        return carry

    lax.fori_loop(0, N_CTX // 2, cross_step, 0)

    def out_copy(peer):
        return pltpu.make_async_remote_copy(
            mixed.at[peer], out_ref.at[:, cols(me)],
            send_sem.at[OUT, peer], recv_sem.at[OUT, me],
            device_id={"dp": dp, "ctx": peer}, device_id_type=MESH,
        )

    def own_out():
        return pltpu.make_async_copy(mixed.at[me], out_ref.at[:, cols(me)], own_sem.at[1])

    per = ROWS // TOK
    place = lax.broadcasted_iota(jnp.int32, (ROWS, ROWS), 0) - lax.broadcasted_iota(jnp.int32, (ROWS, ROWS), 1)
    for i in range(BLOCKS):
        for source in range(i * per, (i + 1) * per):

            @pl.when(me != source)
            def _():
                for kind in (KS, QS, VS):
                    arrived(kind, source)

        q = qs[pl.ds(i * per, per)].reshape(ROWS, HD)
        peak = None
        for j in range(i + 1):
            k = ks[pl.ds(j * per, per)].reshape(ROWS, HD)
            s = lax.dot_general(q, k, NT, preferred_element_type=jnp.float32)
            if j == i:
                s = jnp.where(place >= 0, s, -1e30)
            scores[i % 2, j] = s
            folded = jnp.maximum(s[:, :HD], s[:, HD:])
            peak = folded if peak is None else jnp.maximum(peak, folded)
        top = jnp.max(peak, axis=1, keepdims=True)
        total = jnp.zeros((ROWS, HD), jnp.float32)
        acc = jnp.zeros((ROWS, HD), jnp.float32)
        for j in range(i + 1):
            w = jnp.exp2((scores[i % 2, j] - top) * EXPO)
            total = total + (w[:, :HD] + w[:, HD:])
            v = vs[pl.ds(j * per, per)].reshape(ROWS, HD)
            acc = acc + lax.dot_general(w.astype(jnp.bfloat16), v, NN, preferred_element_type=jnp.float32)
        self_out = (acc / jnp.sum(total, axis=1, keepdims=True)).astype(jnp.bfloat16)
        both = self_out.astype(jnp.float32) + cross[pl.ds(i * per, per)].reshape(ROWS, HD)
        mixed[pl.ds(i * per, per)] = both.astype(jnp.bfloat16).reshape(per, TOK, HD)
        for source in range(i * per, (i + 1) * per):

            @pl.when(me != source)
            def _():
                out_copy(source).start()

            @pl.when(me == source)
            def _():
                own_out().start()

    def finish_ctx(k, carry):
        peer = ctx_peer(k)
        pltpu.make_async_remote_copy(
            mixed.at[peer], out_ref.at[:, cols(peer)],
            send_sem.at[OUT, peer], recv_sem.at[OUT, peer],
            device_id={"dp": dp, "ctx": peer}, device_id_type=MESH,
        ).wait_recv()
        for kind in (IDX, QC, KS, VS, QS):
            ctx_copy(kind, k).wait_send()
        out_copy(peer).wait_send()
        return carry

    def finish_dp(k, carry):
        for kind in range(2):
            near_copy(kind, k).wait_send()
            pass_copy(kind, k).wait_send()
        return carry

    for copy in far:
        copy.wait_send()
    lax.fori_loop(1, HALF, finish_dp, 0)
    own_out().wait()
    lax.fori_loop(1, N_CTX, finish_ctx, 0)


def shards(q_self, k_self, v_self, q_cross, db_keys, db_values, nb_shard, nb_row):
    anywhere = pl.BlockSpec(memory_space=pl.ANY)
    scalars = pl.BlockSpec(memory_space=pltpu.SMEM)
    head = pltpu.VMEM((N_CTX, TOK, HD), jnp.bfloat16)
    blocks = pltpu.VMEM((N_DP * DB_DEV, NLEN, HD), jnp.bfloat16)
    dma = pltpu.SemaphoreType.DMA
    out = pl.pallas_call(
        kernel,
        out_shape=jax.ShapeDtypeStruct((TOK, HEADS * HD), jnp.bfloat16),
        in_specs=[anywhere] * 6 + [scalars] * 2,
        out_specs=anywhere,
        scratch_shapes=[
            head, head, head, head, blocks, blocks,
            pltpu.VMEM((N_CTX, 8, 128), jnp.int32),
            pltpu.SMEM((N_CTX, 8, 128), jnp.int32),
            pltpu.VMEM((N_CTX, TOK, HD), jnp.float32),
            pltpu.VMEM((2, BLOCKS, ROWS, ROWS), jnp.float32),
            head,
            dma((6, N_CTX)), dma((6, N_CTX)),
            dma((2, 2, HALF)), dma((2, N_DP)),
            dma((2,)), dma((2,)), dma((6,)),
        ],
        compiler_params=pltpu.CompilerParams(
            collective_id=0, has_side_effects=True, vmem_limit_bytes=40 * 1024 * 1024
        ),
    )(q_self[0], k_self[0], v_self[0], q_cross[0], db_keys, db_values, nb_shard, nb_row)
    return out[None]


def solution(mesh):
    return jax.shard_map(
        shards,
        mesh=mesh,
        in_specs=(
            P("dp", "ctx", None),
            P("dp", "ctx", None),
            P("dp", "ctx", None),
            P("dp", "ctx", None),
            P("dp", None, None),
            P("dp", None, None),
            P("dp", "ctx", None),
            P("dp", "ctx", None),
        ),
        out_specs=P("dp", "ctx", None),
        check_vma=False,
    )
```

```python
import functools

import jax
import jax.numpy as jnp
from jax import lax
from jax.experimental import pallas as pl
from jax.experimental.pallas import tpu as pltpu
from jax.sharding import PartitionSpec as P

HEADS = 16
HD = 128
GROUP = 64
NEIGH = 2
NLEN = 128
TOK = 128
DB_DEV = 2
N_CTX = 16
N_DP = 16
HALF = 8
ROWS = 256
BLOCKS = N_CTX * TOK // ROWS
EXPO = HD**-0.5 * 1.4426950408889634
MESH = pl.DeviceIdType.MESH
NT = (((1,), (1,)), ((), ()))
NN = (((1,), (0,)), ((), ()))
IDX, QC, KS, VS, QS, OUT = range(6)


def cols(head):
    return pl.ds(pl.multiple_of(head * HD, HD), HD)


def kernel(
    qs_ref, ks_ref, vs_ref, qc_ref, kd_ref, vd_ref, shard_ref, row_ref, out_ref,
    qs, ks, vs, qc, kd, vd, idx, idx_s, cross, scores, mixed,
    send_sem, recv_sem, db_send, db_recv, far_send, far_recv, own_sem,
):
    dp = lax.axis_index("dp")
    me = lax.axis_index("ctx")
    near = lax.rem(dp, HALF)
    side = dp - near
    far_dp = (HALF - side) + near
    far_ctx = (3 - me // 4) * 4 + lax.rem(me, 4)

    def ctx_peer(k):
        return lax.rem(me + k, N_CTX)

    def dp_peer(k):
        return side + lax.rem(near + k, HALF)

    barrier = pltpu.get_barrier_semaphore()

    def greet_ctx(k, carry):
        pl.semaphore_signal(barrier, inc=1, device_id={"dp": dp, "ctx": ctx_peer(k)}, device_id_type=MESH)
        return carry

    def greet_dp(k, carry):
        pl.semaphore_signal(barrier, inc=1, device_id={"dp": dp_peer(k), "ctx": me}, device_id_type=MESH)
        return carry

    lax.fori_loop(1, N_CTX, greet_ctx, 0)
    lax.fori_loop(1, HALF, greet_dp, 0)
    pl.semaphore_signal(barrier, inc=1, device_id={"dp": far_dp, "ctx": far_ctx}, device_id_type=MESH)

    lane = lax.broadcasted_iota(jnp.int32, (8, 128), 1)
    tile = jnp.zeros((8, 128), jnp.int32)
    for g in range(TOK // GROUP):
        for n in range(NEIGH):
            block = shard_ref[0, g, n] * DB_DEV + row_ref[0, g, n]
            tile = jnp.where(lane == g * NEIGH + n, block, tile)
    idx[me] = tile

    own = []
    for slot, (src, dst) in enumerate(
        [
            (qc_ref.at[:, cols(me)], qc.at[me]),
            (ks_ref.at[:, cols(me)], ks.at[me]),
            (vs_ref.at[:, cols(me)], vs.at[me]),
            (qs_ref.at[:, cols(me)], qs.at[me]),
            (kd_ref.at[:, :, cols(me)], kd.at[pl.ds(dp * DB_DEV, DB_DEV)]),
            (vd_ref.at[:, :, cols(me)], vd.at[pl.ds(dp * DB_DEV, DB_DEV)]),
        ]
    ):
        copy = pltpu.make_async_copy(src, dst, own_sem.at[slot])
        copy.start()
        own.append(copy)

    pl.semaphore_wait(barrier, N_CTX - 1 + HALF - 1 + 1)

    def far_copy(kind):
        src, dst = ((kd_ref, kd), (vd_ref, vd))[kind]
        return pltpu.make_async_remote_copy(
            src.at[:, :, cols(far_ctx)], dst.at[pl.ds(dp * DB_DEV, DB_DEV)],
            far_send.at[kind], far_recv.at[kind],
            device_id={"dp": far_dp, "ctx": far_ctx}, device_id_type=MESH,
        )

    def near_copy(kind, k):
        src, dst = ((kd_ref, kd), (vd_ref, vd))[kind]
        return pltpu.make_async_remote_copy(
            src.at[:, :, cols(me)], dst.at[pl.ds(dp * DB_DEV, DB_DEV)],
            db_send.at[kind, 0, k], db_recv.at[kind, dp],
            device_id={"dp": dp_peer(k), "ctx": me}, device_id_type=MESH,
        )

    def pass_copy(kind, k):
        buf = (kd, vd)[kind]
        part = buf.at[pl.ds(far_dp * DB_DEV, DB_DEV)]
        return pltpu.make_async_remote_copy(
            part, part, db_send.at[kind, 1, k], db_recv.at[kind, far_dp],
            device_id={"dp": dp_peer(k), "ctx": me}, device_id_type=MESH,
        )

    def ctx_copy(kind, k):
        peer = ctx_peer(k)
        if kind == IDX:
            src = idx.at[me]
            dst = idx.at[me]
        else:
            arg, buf = {QC: (qc_ref, qc), KS: (ks_ref, ks), VS: (vs_ref, vs), QS: (qs_ref, qs)}[kind]
            src, dst = arg.at[:, cols(peer)], buf.at[me]
        return pltpu.make_async_remote_copy(
            src, dst, send_sem.at[kind, peer], recv_sem.at[kind, me],
            device_id={"dp": dp, "ctx": peer}, device_id_type=MESH,
        )

    def arrived(kind, source):
        buf = {IDX: idx, QC: qc, KS: ks, VS: vs, QS: qs}[kind].at[source]
        pltpu.make_async_remote_copy(
            buf, buf, send_sem.at[kind, source], recv_sem.at[kind, source],
            device_id={"dp": dp, "ctx": source}, device_id_type=MESH,
        ).wait_recv()

    far = [far_copy(kind) for kind in range(2)]
    for copy in far:
        copy.start()

    def start_first(k, carry):
        ctx_copy(IDX, k).start()
        ctx_copy(QC, k).start()
        return carry

    def start_near(k, carry):
        near_copy(0, k).start()
        near_copy(1, k).start()
        return carry

    def start_self(k, carry):
        ctx_copy(KS, k).start()
        ctx_copy(QS, k).start()
        ctx_copy(VS, k).start()
        return carry

    lax.fori_loop(1, HALF, start_near, 0)
    lax.fori_loop(1, N_CTX, start_first, 0)
    lax.fori_loop(1, N_CTX, start_self, 0)

    for copy in far:
        copy.wait_recv()

    def start_pass(k, carry):
        pass_copy(0, k).start()
        pass_copy(1, k).start()
        return carry

    lax.fori_loop(1, HALF, start_pass, 0)

    def wait_first(k, carry):
        arrived(IDX, ctx_peer(k))
        arrived(QC, ctx_peer(k))
        return carry

    def wait_blocks(k, carry):
        for home in (side, HALF - side):
            shard = home + lax.rem(near + k, HALF)
            for kind, buf in enumerate((kd, vd)):
                part = buf.at[pl.ds(shard * DB_DEV, DB_DEV)]
                pltpu.make_async_remote_copy(
                    part, part, db_send.at[kind, 0, k], db_recv.at[kind, shard],
                    device_id={"dp": dp_peer(k), "ctx": me}, device_id_type=MESH,
                ).wait_recv()
        return carry

    for copy in own:
        copy.wait()
    lax.fori_loop(1, N_CTX, wait_first, 0)
    numbers = pltpu.make_async_copy(idx, idx_s, own_sem.at[0])
    numbers.start()
    numbers.wait()
    lax.fori_loop(1, HALF, wait_blocks, 0)

    def cross_step(step, carry):
        for part in range(2):
            t = step * 2 + part
            for g in range(TOK // GROUP):
                first = idx_s[t, 0, g * NEIGH]
                second = idx_s[t, 0, g * NEIGH + 1]
                keys = jnp.concatenate([kd[first], kd[second]], axis=0)
                values = jnp.concatenate([vd[first], vd[second]], axis=0)
                rows = pl.ds(g * GROUP, GROUP)
                s = lax.dot_general(qc[t, rows, :], keys, NT, preferred_element_type=jnp.float32)
                top = jnp.max(s, axis=1, keepdims=True)
                w = jnp.exp2((s - top) * EXPO)
                total = jnp.sum(w, axis=1, keepdims=True)
                o = lax.dot_general(w.astype(jnp.bfloat16), values, NN, preferred_element_type=jnp.float32)
                cross[t, rows, :] = o / total
        return carry

    lax.fori_loop(0, N_CTX // 2, cross_step, 0)

    def out_copy(peer):
        return pltpu.make_async_remote_copy(
            mixed.at[peer], out_ref.at[:, cols(me)],
            send_sem.at[OUT, peer], recv_sem.at[OUT, me],
            device_id={"dp": dp, "ctx": peer}, device_id_type=MESH,
        )

    def own_out():
        return pltpu.make_async_copy(mixed.at[me], out_ref.at[:, cols(me)], own_sem.at[1])

    per = ROWS // TOK
    place = lax.broadcasted_iota(jnp.int32, (ROWS, ROWS), 0) - lax.broadcasted_iota(jnp.int32, (ROWS, ROWS), 1)
    for i in range(BLOCKS):
        for source in range(i * per, (i + 1) * per):

            @pl.when(me != source)
            def _():
                for kind in (KS, QS, VS):
                    arrived(kind, source)

        q = qs[pl.ds(i * per, per)].reshape(ROWS, HD)
        peak = None
        for j in range(i + 1):
            k = ks[pl.ds(j * per, per)].reshape(ROWS, HD)
            s = lax.dot_general(q, k, NT, preferred_element_type=jnp.float32)
            if j == i:
                s = jnp.where(place >= 0, s, -1e30)
            scores[i % 2, j] = s
            folded = jnp.maximum(s[:, :HD], s[:, HD:])
            peak = folded if peak is None else jnp.maximum(peak, folded)
        top = jnp.max(peak, axis=1, keepdims=True)
        total = jnp.zeros((ROWS, HD), jnp.float32)
        acc = jnp.zeros((ROWS, HD), jnp.float32)
        for j in range(i + 1):
            w = jnp.exp2((scores[i % 2, j] - top) * EXPO)
            total = total + (w[:, :HD] + w[:, HD:])
            v = vs[pl.ds(j * per, per)].reshape(ROWS, HD)
            acc = acc + lax.dot_general(w.astype(jnp.bfloat16), v, NN, preferred_element_type=jnp.float32)
        self_out = (acc / jnp.sum(total, axis=1, keepdims=True)).astype(jnp.bfloat16)
        both = self_out.astype(jnp.float32) + cross[pl.ds(i * per, per)].reshape(ROWS, HD)
        mixed[pl.ds(i * per, per)] = both.astype(jnp.bfloat16).reshape(per, TOK, HD)
        for source in range(i * per, (i + 1) * per):

            @pl.when(me != source)
            def _():
                out_copy(source).start()

            @pl.when(me == source)
            def _():
                own_out().start()

    def finish_ctx(k, carry):
        peer = ctx_peer(k)
        pltpu.make_async_remote_copy(
            mixed.at[peer], out_ref.at[:, cols(peer)],
            send_sem.at[OUT, peer], recv_sem.at[OUT, peer],
            device_id={"dp": dp, "ctx": peer}, device_id_type=MESH,
        ).wait_recv()
        for kind in (IDX, QC, KS, VS, QS):
            ctx_copy(kind, k).wait_send()
        out_copy(peer).wait_send()
        return carry

    def finish_dp(k, carry):
        for kind in range(2):
            near_copy(kind, k).wait_send()
            pass_copy(kind, k).wait_send()
        return carry

    for copy in far:
        copy.wait_send()
    lax.fori_loop(1, HALF, finish_dp, 0)
    own_out().wait()
    lax.fori_loop(1, N_CTX, finish_ctx, 0)


def shards(q_self, k_self, v_self, q_cross, db_keys, db_values, nb_shard, nb_row):
    anywhere = pl.BlockSpec(memory_space=pl.ANY)
    scalars = pl.BlockSpec(memory_space=pltpu.SMEM)
    head = pltpu.VMEM((N_CTX, TOK, HD), jnp.bfloat16)
    blocks = pltpu.VMEM((N_DP * DB_DEV, NLEN, HD), jnp.bfloat16)
    dma = pltpu.SemaphoreType.DMA
    out = pl.pallas_call(
        kernel,
        out_shape=jax.ShapeDtypeStruct((TOK, HEADS * HD), jnp.bfloat16),
        in_specs=[anywhere] * 6 + [scalars] * 2,
        out_specs=anywhere,
        scratch_shapes=[
            head, head, head, head, blocks, blocks,
            pltpu.VMEM((N_CTX, 8, 128), jnp.int32),
            pltpu.SMEM((N_CTX, 8, 128), jnp.int32),
            pltpu.VMEM((N_CTX, TOK, HD), jnp.float32),
            pltpu.VMEM((2, BLOCKS, ROWS, ROWS), jnp.float32),
            head,
            dma((6, N_CTX)), dma((6, N_CTX)),
            dma((2, 2, HALF)), dma((2, N_DP)),
            dma((2,)), dma((2,)), dma((6,)),
        ],
        compiler_params=pltpu.CompilerParams(
            collective_id=0, has_side_effects=True, vmem_limit_bytes=60 * 1024 * 1024
        ),
    )(q_self[0], k_self[0], v_self[0], q_cross[0], db_keys, db_values, nb_shard, nb_row)
    return out[None]


def solution(mesh):
    return jax.shard_map(
        shards,
        mesh=mesh,
        in_specs=(
            P("dp", "ctx", None),
            P("dp", "ctx", None),
            P("dp", "ctx", None),
            P("dp", "ctx", None),
            P("dp", None, None),
            P("dp", None, None),
            P("dp", "ctx", None),
            P("dp", "ctx", None),
        ),
        out_specs=P("dp", "ctx", None),
        check_vma=False,
    )
```

```python
import functools

import jax
import jax.numpy as jnp
from jax import lax
from jax.experimental import pallas as pl
from jax.experimental.pallas import tpu as pltpu
from jax.sharding import PartitionSpec as P

HEADS = 16
HD = 128
GROUP = 64
NEIGH = 2
NLEN = 128
TOK = 128
DB_DEV = 2
N_CTX = 16
N_DP = 16
HALF = 8
ROWS = 256
PER = ROWS // TOK
BLOCKS = N_CTX // PER
HALF_BLOCKS = HALF // PER
EXPO = HD**-0.5 * 1.4426950408889634
MESH = pl.DeviceIdType.MESH
NT = (((1,), (1,)), ((), ()))
NN = (((1,), (0,)), ((), ()))
IDX, QC, KS, VS, QS, OUT = range(6)


def cols(head):
    return pl.ds(pl.multiple_of(head * HD, HD), HD)


def kernel(
    qs_ref, ks_ref, vs_ref, qc_ref, kd_ref, vd_ref, shard_ref, row_ref, out_ref,
    qs, ks, vs, qc, kd, vd, idx, idx_s, cross, scores, tops, totals, accs, mixed,
    send_sem, recv_sem, db_send, pass_send, db_recv, own_sem,
):
    dp = lax.axis_index("dp")
    me = lax.axis_index("ctx")
    near = lax.rem(dp, HALF)
    side = dp - near
    core = lax.rem(near, 2)
    far_dp = (HALF - side) + near
    far_ctx = (3 - me // 4) * 4 + lax.rem(me, 4)
    other_core = dp + 1 - 2 * core
    lower = me < HALF
    upper = me >= HALF
    place = lax.rem(me, HALF)
    mine = me - place
    theirs = HALF - mine

    def ctx_peer(k):
        return lax.rem(me + k, N_CTX)

    def near_peer(k):
        return mine + lax.rem(place + k, HALF)

    def cross_peer(k):
        return theirs + lax.rem(place + k, HALF)

    def y_peer(k):
        return side + lax.rem(near + 2 * k, HALF)

    def loop(first, last, body):
        def step(k, carry):
            body(k)
            return carry

        lax.fori_loop(first, last, step, 0)

    barrier = pltpu.get_barrier_semaphore()

    def greet(dp_of, ctx_of):
        pl.semaphore_signal(barrier, inc=1, device_id={"dp": dp_of, "ctx": ctx_of}, device_id_type=MESH)

    loop(1, N_CTX, lambda k: greet(dp, ctx_peer(k)))
    loop(1, 4, lambda k: greet(y_peer(k), me))
    greet(other_core, me)
    greet(far_dp, far_ctx)

    lane = lax.broadcasted_iota(jnp.int32, (8, 128), 1)
    tile = jnp.zeros((8, 128), jnp.int32)
    for g in range(TOK // GROUP):
        for n in range(NEIGH):
            block = shard_ref[0, g, n] * DB_DEV + row_ref[0, g, n]
            tile = jnp.where(lane == g * NEIGH + n, block, tile)
    idx[me] = tile

    own = []
    for slot, (src, dst) in enumerate(
        [
            (qc_ref.at[:, cols(me)], qc.at[me]),
            (ks_ref.at[:, cols(me)], ks.at[me]),
            (vs_ref.at[:, cols(me)], vs.at[me]),
            (qs_ref.at[:, cols(me)], qs.at[me]),
            (kd_ref.at[:, :, cols(me)], kd.at[pl.ds(dp * DB_DEV, DB_DEV)]),
            (vd_ref.at[:, :, cols(me)], vd.at[pl.ds(dp * DB_DEV, DB_DEV)]),
        ]
    ):
        copy = pltpu.make_async_copy(src, dst, own_sem.at[slot])
        copy.start()
        own.append(copy)

    pl.semaphore_wait(barrier, N_CTX - 1 + 3 + 1 + 1)

    def shard_copy(kind, shard, send, target, target_ctx, head=None):
        arg, buf = ((kd_ref, kd), (vd_ref, vd))[kind]
        part = buf.at[pl.ds(shard * DB_DEV, DB_DEV)]
        src = part if head is None else arg.at[:, :, cols(head)]
        return pltpu.make_async_remote_copy(
            src, part, send, db_recv.at[kind, shard],
            device_id={"dp": target, "ctx": target_ctx}, device_id_type=MESH,
        )

    def far_copy(kind):
        return shard_copy(kind, dp, db_send.at[kind, 0, 0], far_dp, far_ctx, far_ctx)

    def y_copy(kind, k):
        return shard_copy(kind, dp, db_send.at[kind, 0, k], y_peer(k), me, me)

    def y_pass(kind, k):
        return shard_copy(kind, far_dp, db_send.at[kind, 1, k], y_peer(k), me)

    def core_pass(kind, home, k):
        shard = (side if home == 0 else HALF - side) + lax.rem(near + 2 * k, HALF)
        return shard_copy(kind, shard, pass_send.at[kind, home, k], other_core, me)

    def core_own(kind):
        return shard_copy(kind, dp, pass_send.at[kind, 0, 0], other_core, me, me)

    def ctx_copy(kind, peer):
        if kind == IDX:
            src, dst = idx.at[me], idx.at[me]
        else:
            arg, buf = {QC: (qc_ref, qc), KS: (ks_ref, ks), VS: (vs_ref, vs), QS: (qs_ref, qs)}[kind]
            src, dst = arg.at[:, cols(peer)], buf.at[me]
        return pltpu.make_async_remote_copy(
            src, dst, send_sem.at[kind, peer], recv_sem.at[kind, me],
            device_id={"dp": dp, "ctx": peer}, device_id_type=MESH,
        )

    def arrived(kind, source):
        buf = {IDX: idx, QC: qc, KS: ks, VS: vs, QS: qs}[kind].at[source]
        pltpu.make_async_remote_copy(
            buf, buf, send_sem.at[kind, source], recv_sem.at[kind, source],
            device_id={"dp": dp, "ctx": source}, device_id_type=MESH,
        ).wait_recv()

    def start(kinds, peer):
        for kind in kinds:
            ctx_copy(kind, peer).start()

    for kind in range(2):
        far_copy(kind).start()
    loop(1, N_CTX, lambda k: start((IDX,), ctx_peer(k)))

    def start_y(k):
        for kind in range(2):
            y_copy(kind, k).start()

    loop(1, 4, start_y)
    for kind in range(2):
        core_own(kind).start()

    def first_round(k):
        @pl.when(lower)
        def _():
            start((KS, VS), cross_peer(k))

        @pl.when(upper)
        def _():
            start((QS, QC), cross_peer(k))

        @pl.when(k >= 1)
        def _():
            start((QC, KS, QS, VS), near_peer(k))

    def second_round(k):
        @pl.when(lower)
        def _():
            start((QC, QS), cross_peer(k))

        @pl.when(upper)
        def _():
            start((KS, VS), cross_peer(k))

    loop(0, HALF, first_round)
    loop(0, HALF, second_round)

    tops[...] = jnp.full(tops.shape, -1e30, jnp.float32)
    totals[...] = jnp.zeros(totals.shape, jnp.float32)
    accs[...] = jnp.zeros(accs.shape, jnp.float32)

    def wait_shard(kind, shard):
        shard_copy(kind, shard, db_send.at[kind, 0, 0], other_core, me).wait_recv()

    for copy in own:
        copy.wait()
    for kind in range(2):
        wait_shard(kind, far_dp)

    def start_y_pass(k):
        for kind in range(2):
            y_pass(kind, k).start()

    loop(1, 4, start_y_pass)
    for kind in range(2):
        core_pass(kind, 1, 0).start()

    def pass_own(k):
        for kind in range(2):
            wait_shard(kind, side + lax.rem(near + 2 * k, HALF))
            core_pass(kind, 0, k).start()

    def pass_far(k):
        for kind in range(2):
            wait_shard(kind, HALF - side + lax.rem(near + 2 * k, HALF))
            core_pass(kind, 1, k).start()

    loop(1, 4, pass_own)
    loop(1, 4, pass_far)

    loop(1, N_CTX, lambda k: arrived(IDX, ctx_peer(k)))
    numbers = pltpu.make_async_copy(idx, idx_s, own_sem.at[0])
    numbers.start()
    numbers.wait()

    def wait_other_core(k):
        for kind in range(2):
            wait_shard(kind, 2 * k + 1 - core)

    loop(0, HALF, wait_other_core)

    def cross_rows(base):
        def step(k):
            for part in range(2):
                t = base + k * 2 + part
                for g in range(TOK // GROUP):
                    first = idx_s[t, 0, g * NEIGH]
                    second = idx_s[t, 0, g * NEIGH + 1]
                    keys = jnp.concatenate([kd[first], kd[second]], axis=0)
                    values = jnp.concatenate([vd[first], vd[second]], axis=0)
                    rows = pl.ds(g * GROUP, GROUP)
                    s = lax.dot_general(qc[t, rows, :], keys, NT, preferred_element_type=jnp.float32)
                    top = jnp.max(s, axis=1, keepdims=True)
                    w = jnp.exp2((s - top) * EXPO)
                    total = jnp.sum(w, axis=1, keepdims=True)
                    o = lax.dot_general(w.astype(jnp.bfloat16), values, NN, preferred_element_type=jnp.float32)
                    cross[t, rows, :] = o / total

        loop(0, HALF // 2, step)

    diagonal = lax.broadcasted_iota(jnp.int32, (ROWS, ROWS), 0) >= lax.broadcasted_iota(jnp.int32, (ROWS, ROWS), 1)

    def segment(i, begin, count, causal, slot):
        q = qs[pl.ds(i * PER, PER)].reshape(ROWS, HD)
        peak = None
        for j in range(count):
            k = ks[pl.ds((begin + j) * PER, PER)].reshape(ROWS, HD)
            s = lax.dot_general(q, k, NT, preferred_element_type=jnp.float32)
            if causal and j == count - 1:
                s = jnp.where(diagonal, s, -1e30)
            scores[slot, j] = s
            folded = jnp.maximum(s[:, :HD], s[:, HD:])
            peak = folded if peak is None else jnp.maximum(peak, folded)
        before = tops[i][:, :1]
        top = jnp.maximum(jnp.max(peak, axis=1, keepdims=True), before)
        keep = jnp.exp2((before - top) * EXPO)
        total = totals[i] * keep
        acc = accs[i] * keep
        for j in range(count):
            w = jnp.exp2((scores[slot, j] - top) * EXPO)
            total = total + (w[:, :HD] + w[:, HD:])
            v = vs[pl.ds((begin + j) * PER, PER)].reshape(ROWS, HD)
            acc = acc + lax.dot_general(w.astype(jnp.bfloat16), v, NN, preferred_element_type=jnp.float32)
        tops[i] = jnp.broadcast_to(top, (ROWS, HD))
        totals[i] = total
        accs[i] = acc

    def causal_rows(base):
        for i in range(HALF_BLOCKS):
            segment(base + i, base, i + 1, True, i % 2)

    def out_copy(peer):
        return pltpu.make_async_remote_copy(
            mixed.at[peer], out_ref.at[:, cols(me)],
            send_sem.at[OUT, peer], recv_sem.at[OUT, me],
            device_id={"dp": dp, "ctx": peer}, device_id_type=MESH,
        )

    def own_out():
        return pltpu.make_async_copy(mixed.at[me], out_ref.at[:, cols(me)], own_sem.at[1])

    def finish_rows(base):
        def step(n):
            i = base + n
            total = jnp.sum(totals[i], axis=1, keepdims=True)
            self_out = (accs[i] / total).astype(jnp.bfloat16)
            both = self_out.astype(jnp.float32) + cross[pl.ds(i * PER, PER)].reshape(ROWS, HD)
            mixed[pl.ds(i * PER, PER)] = both.astype(jnp.bfloat16).reshape(PER, TOK, HD)
            for part in range(PER):
                home = i * PER + part

                @pl.when(me != home)
                def _():
                    out_copy(home).start()

                @pl.when(me == home)
                def _():
                    own_out().start()

        loop(0, HALF_BLOCKS, step)

    def wait_near(k):
        for kind in (QC, KS, QS, VS):
            arrived(kind, near_peer(k))

    def wait_cross(kinds):
        def step(k):
            for kind in kinds:
                arrived(kind, cross_peer(k))

        loop(0, HALF, step)

    own_base = mine // PER
    other_base = theirs // PER

    loop(1, HALF, wait_near)
    cross_rows(mine)
    causal_rows(own_base)

    @pl.when(lower)
    def _():
        finish_rows(0)
        wait_cross((QS,))

    @pl.when(upper)
    def _():
        wait_cross((KS, VS))

    for i in range(HALF_BLOCKS):
        segment(HALF_BLOCKS + i, 0, HALF_BLOCKS, False, i % 2)

    @pl.when(upper)
    def _():
        finish_rows(HALF_BLOCKS)

    wait_cross((QC,))
    cross_rows(theirs)

    @pl.when(lower)
    def _():
        wait_cross((KS, VS))

    @pl.when(upper)
    def _():
        wait_cross((QS,))

    causal_rows(other_base)
    finish_rows(other_base)

    def finish_ctx(k):
        peer = ctx_peer(k)
        pltpu.make_async_remote_copy(
            mixed.at[peer], out_ref.at[:, cols(peer)],
            send_sem.at[OUT, peer], recv_sem.at[OUT, peer],
            device_id={"dp": dp, "ctx": peer}, device_id_type=MESH,
        ).wait_recv()
        for kind in (IDX, QC, KS, VS, QS):
            ctx_copy(kind, peer).wait_send()
        out_copy(peer).wait_send()

    def finish_y(k):
        for kind in range(2):
            y_copy(kind, k).wait_send()
            y_pass(kind, k).wait_send()
            core_pass(kind, 0, k).wait_send()
            core_pass(kind, 1, k).wait_send()

    for kind in range(2):
        far_copy(kind).wait_send()
        core_own(kind).wait_send()
        core_pass(kind, 1, 0).wait_send()
    loop(1, 4, finish_y)
    own_out().wait()
    loop(1, N_CTX, finish_ctx)


def shards(q_self, k_self, v_self, q_cross, db_keys, db_values, nb_shard, nb_row):
    anywhere = pl.BlockSpec(memory_space=pl.ANY)
    scalars = pl.BlockSpec(memory_space=pltpu.SMEM)
    head = pltpu.VMEM((N_CTX, TOK, HD), jnp.bfloat16)
    blocks = pltpu.VMEM((N_DP * DB_DEV, NLEN, HD), jnp.bfloat16)
    state = pltpu.VMEM((BLOCKS, ROWS, HD), jnp.float32)
    dma = pltpu.SemaphoreType.DMA
    out = pl.pallas_call(
        kernel,
        out_shape=jax.ShapeDtypeStruct((TOK, HEADS * HD), jnp.bfloat16),
        in_specs=[anywhere] * 6 + [scalars] * 2,
        out_specs=anywhere,
        scratch_shapes=[
            head, head, head, head, blocks, blocks,
            pltpu.VMEM((N_CTX, 8, 128), jnp.int32),
            pltpu.SMEM((N_CTX, 8, 128), jnp.int32),
            pltpu.VMEM((N_CTX, TOK, HD), jnp.float32),
            pltpu.VMEM((2, HALF_BLOCKS, ROWS, ROWS), jnp.float32),
            state, state, state,
            head,
            dma((6, N_CTX)), dma((6, N_CTX)),
            dma((2, 2, 4)), dma((2, 2, 4)), dma((2, N_DP)), dma((6,)),
        ],
        compiler_params=pltpu.CompilerParams(
            collective_id=0, has_side_effects=True, vmem_limit_bytes=60 * 1024 * 1024
        ),
    )(q_self[0], k_self[0], v_self[0], q_cross[0], db_keys, db_values, nb_shard, nb_row)
    return out[None]


def solution(mesh):
    return jax.shard_map(
        shards,
        mesh=mesh,
        in_specs=(
            P("dp", "ctx", None),
            P("dp", "ctx", None),
            P("dp", "ctx", None),
            P("dp", "ctx", None),
            P("dp", None, None),
            P("dp", None, None),
            P("dp", "ctx", None),
            P("dp", "ctx", None),
        ),
        out_specs=P("dp", "ctx", None),
        check_vma=False,
    )
```

```python
import jax
import jax.numpy as jnp
from jax import lax
from jax.experimental import pallas as pl
from jax.experimental.pallas import tpu as pltpu
from jax.sharding import PartitionSpec as P

HEADS = 16
HD = 128
GROUP = 64
NEIGH = 2
NLEN = 128
TOK = 128
DB_DEV = 2
N_DP = 16
HALF = 8
XS = 4
LOCAL = HEADS // XS
WIDE = LOCAL * HD
ROWS = 256
PER = ROWS // TOK
QB = XS // PER
EXPO = HD**-0.5 * 1.4426950408889634
MESH = pl.DeviceIdType.MESH
NT = (((1,), (1,)), ((), ()))
NN = (((1,), (0,)), ((), ()))
QC, KS, VS, QS, OUT = range(5)
ZK, ZV, ZQ2, ZQ3, ZQ3B, ZO2, ZS2, ZO3, ZS3, ZO3B, ZS3B = range(11)


def cols(head):
    return pl.ds(pl.multiple_of(head * HD, HD), HD)


def kernel(
    qs_ref, ks_ref, vs_ref, qc_ref, kd_ref, vd_ref, shard_ref, row_ref, out_ref,
    qs, ks, vs, qc, k0, v0, q2, q3, kd, vd, idx, idx_s, cross, scores, tops, totals, accs,
    part_out, stat_out, part_in, stat_in, mixed,
    x_send, x_recv, idx_send, idx_recv, z_send, z_recv,
    far_send, y_send, y_pass_send, core_send, db_recv, own_sem, db_own, number_sem,
):
    dp = lax.axis_index("dp")
    me = lax.axis_index("ctx")
    row = me // XS
    x = lax.rem(me, XS)
    near = lax.rem(dp, HALF)
    side = dp - near
    away = HALF - side
    core = lax.rem(near, 2)
    other_core = dp + 1 - 2 * core
    far_dp = away + near
    far_ctx = (3 - row) * XS + x

    def x_at(k):
        return lax.rem(x + k, XS)

    def y_at(home, k):
        return home + lax.rem(near + 2 * k, HALF)

    def loop(first, last, body):
        def step(k, carry):
            body(k)
            return carry

        lax.fori_loop(first, last, step, 0)

    barrier = pltpu.get_barrier_semaphore()

    def greet(dp_of, ctx_of):
        pl.semaphore_signal(barrier, inc=1, device_id={"dp": dp_of, "ctx": ctx_of}, device_id_type=MESH)

    for k in range(1, 4):
        greet(dp, row * XS + x_at(k))
        greet(dp, lax.rem(row + k, 4) * XS + x)
    greet(y_at(side, 1), me)
    greet(y_at(side, 3), me)
    greet(other_core, me)
    greet(far_dp, far_ctx)

    lane = lax.broadcasted_iota(jnp.int32, (8, 128), 1)
    tile = jnp.zeros((8, 128), jnp.int32)
    for g in range(TOK // GROUP):
        for n in range(NEIGH):
            block = shard_ref[0, g, n] * DB_DEV + row_ref[0, g, n]
            tile = jnp.where(lane == g * NEIGH + n, block, tile)
    idx[x] = tile

    arrays = {QC: (qc_ref, qc), KS: (ks_ref, ks), VS: (vs_ref, vs), QS: (qs_ref, qs)}
    blocks = ((kd_ref, kd), (vd_ref, vd))
    wide = pl.ds(pl.multiple_of(x * WIDE, WIDE), WIDE)

    def own_copy(kind, h):
        arg, buf = arrays[kind]
        return pltpu.make_async_copy(arg.at[:, cols(x * LOCAL + h)], buf.at[h, x], own_sem.at[kind, h])

    def own_db(kind):
        arg, buf = blocks[kind]
        return pltpu.make_async_copy(arg.at[:, :, wide], buf.at[pl.ds(dp * DB_DEV, DB_DEV)], db_own.at[kind])

    def start_own(h):
        for kind in (KS, VS, QS, QC):
            own_copy(kind, h).start()

    loop(0, LOCAL, start_own)
    for kind in range(2):
        own_db(kind).start()

    pl.semaphore_wait(barrier, 10)

    def shard_copy(kind, shard, send, target, target_ctx, whole):
        arg, buf = blocks[kind]
        part = buf.at[pl.ds(shard * DB_DEV, DB_DEV)]
        return pltpu.make_async_remote_copy(
            arg.at[:, :, wide] if whole else part, part, send, db_recv.at[kind, shard],
            device_id={"dp": target, "ctx": target_ctx}, device_id_type=MESH,
        )

    def far_copy(kind):
        return shard_copy(kind, dp, far_send.at[kind], far_dp, far_ctx, True)

    def y_own(kind, k):
        return shard_copy(kind, dp, y_send.at[kind, 0, k // 2], y_at(side, k), me, True)

    def y_far(kind, k):
        return shard_copy(kind, far_dp, y_send.at[kind, 1, k // 2], y_at(side, k), me, False)

    def y_pass(kind, home):
        k = 3 if kind == 0 else 1
        return shard_copy(kind, y_at(home, k), y_pass_send.at[kind, 0 if home is side else 1], y_at(side, 4 - k), me, False)

    def core_pass(kind, home, k):
        return shard_copy(
            kind, y_at(home, k), core_send.at[kind, 0 if home is side else 1, k], other_core, me, home is side and k == 0
        )

    def wait_shard(kind, shard):
        shard_copy(kind, shard, far_send.at[kind], other_core, me, False).wait_recv()

    def x_copy(kind, h, to):
        arg, buf = arrays[kind]
        return pltpu.make_async_remote_copy(
            arg.at[:, cols(to * LOCAL + h)], buf.at[h, x], x_send.at[kind, h, to], x_recv.at[kind, h, x],
            device_id={"dp": dp, "ctx": row * XS + to}, device_id_type=MESH,
        )

    def arrived(kind, h):
        own_copy(kind, h).wait()
        for k in range(1, XS):
            source = x_at(k)
            buf = arrays[kind][1].at[h, source]
            pltpu.make_async_remote_copy(
                buf, buf, x_send.at[kind, h, source], x_recv.at[kind, h, source],
                device_id={"dp": dp, "ctx": row * XS + source}, device_id_type=MESH,
            ).wait_recv()

    def idx_copy(to, slot):
        return pltpu.make_async_remote_copy(
            idx.at[slot], idx.at[slot], idx_send.at[to], idx_recv.at[slot],
            device_id={"dp": dp, "ctx": row * XS + to}, device_id_type=MESH,
        )

    def start_x(kinds):
        def step(h):
            for k in (1, 3, 2):
                for kind in kinds:
                    x_copy(kind, h, x_at(k)).start()

        loop(0, LOCAL, step)

    for kind in range(2):
        far_copy(kind).start()
    for k in range(1, XS):
        idx_copy(x_at(k), x).start()
    for kind in range(2):
        for k in (1, 3):
            y_own(kind, k).start()
        core_pass(kind, side, 0).start()

    @pl.when(row < 2)
    def _():
        start_x((KS, VS))
        start_x((QS,))

    @pl.when(row >= 2)
    def _():
        start_x((QS,))
        start_x((KS, VS))

    start_x((QC,))

    def z_copy(kind, h):
        src, dst, to = {
            ZK: (ks.at[h], k0.at[h], 1),
            ZV: (vs.at[h], v0.at[h], 1),
            ZQ2: (qs.at[h], q2.at[h], 1),
            ZQ3: (qs.at[h], q3.at[h], 1),
            ZQ3B: (qs.at[h], q3.at[h], 2),
            ZO2: (part_out.at[0, h], part_in.at[0, h], 2),
            ZS2: (stat_out.at[0, h], stat_in.at[0, h], 2),
            ZO3: (part_out.at[1, h], part_in.at[0, h], 3),
            ZS3: (stat_out.at[1, h], stat_in.at[0, h], 3),
            ZO3B: (part_out.at[1, h], part_in.at[1, h], 3),
            ZS3B: (stat_out.at[1, h], stat_in.at[1, h], 3),
        }[kind]
        return pltpu.make_async_remote_copy(
            src, dst, z_send.at[kind, h], z_recv.at[kind, h],
            device_id={"dp": dp, "ctx": to * XS + x}, device_id_type=MESH,
        )

    def relay(h):
        @pl.when(row == 0)
        def _():
            arrived(KS, h)
            z_copy(ZK, h).start()
            arrived(VS, h)
            z_copy(ZV, h).start()

        @pl.when(row == 2)
        def _():
            arrived(QS, h)
            z_copy(ZQ2, h).start()

        @pl.when(row == 3)
        def _():
            arrived(QS, h)
            z_copy(ZQ3, h).start()
            z_copy(ZQ3B, h).start()

    def far_stage():
        for kind in range(2):
            wait_shard(kind, far_dp)
            for k in (1, 3):
                y_far(kind, k).start()
            core_pass(kind, away, 0).start()

    def pass_stage(home):
        for kind in range(2):
            for k in (1, 3):
                wait_shard(kind, y_at(home, k))
                if (k == 3) == (kind == 0):
                    y_pass(kind, home).start()
                core_pass(kind, home, k).start()

    def last_stage():
        for home in (side, away):
            for kind in range(2):
                wait_shard(kind, y_at(home, 2))
                core_pass(kind, home, 2).start()

    diagonal = lax.broadcasted_iota(jnp.int32, (ROWS, ROWS), 0) >= lax.broadcasted_iota(jnp.int32, (ROWS, ROWS), 1)
    eye = lax.broadcasted_iota(jnp.int32, (TOK, TOK), 0) == lax.broadcasted_iota(jnp.int32, (TOK, TOK), 1)

    def attend(queries, h, b, chunks, slot):
        q = queries[h, pl.ds(b * PER, PER)].reshape(ROWS, HD)
        peak = None
        for j, (keys, values, c, masked) in enumerate(chunks):
            k = keys[h, pl.ds(c * PER, PER)].reshape(ROWS, HD)
            s = lax.dot_general(q, k, NT, preferred_element_type=jnp.float32)
            if masked:
                s = jnp.where(diagonal, s, -1e30)
            scores[slot, j] = s
            folded = jnp.maximum(s[:, :HD], s[:, HD:])
            peak = folded if peak is None else jnp.maximum(peak, folded)
        top = jnp.max(peak, axis=1, keepdims=True)
        total = jnp.zeros((ROWS, HD), jnp.float32)
        acc = jnp.zeros((ROWS, HD), jnp.float32)
        for j, (keys, values, c, masked) in enumerate(chunks):
            w = jnp.exp2((scores[slot, j] - top) * EXPO)
            total = total + (w[:, :HD] + w[:, HD:])
            v = values[h, pl.ds(c * PER, PER)].reshape(ROWS, HD)
            acc = acc + lax.dot_general(w.astype(jnp.bfloat16), v, NN, preferred_element_type=jnp.float32)
        return top, jnp.sum(total, axis=1, keepdims=True), acc

    def partial(queries, h, chunks, place):
        for b in range(QB):
            top, total, acc = attend(queries, h, b, chunks, b)
            part_out[place, h, pl.ds(b * PER, PER)] = (acc / total).astype(jnp.bfloat16).reshape(PER, TOK, HD)
            for p in range(PER):
                rows = slice(p * TOK, (p + 1) * TOK)
                at = b * PER + p
                stat_out[place, h, at : at + 1] = jnp.sum(jnp.where(eye, top[rows], 0.0), axis=0, keepdims=True)
                stat_out[place, h, XS + at : XS + at + 1] = jnp.sum(jnp.where(eye, total[rows], 0.0), axis=0, keepdims=True)

    def own_rows(h, extra, final):
        for b in range(QB):
            chunks = extra + [(ks, vs, c, c == b) for c in range(b + 1)]
            top, total, acc = attend(qs, h, b, chunks, b)
            at = h * QB + b
            if final:
                accs[at] = acc / total
            else:
                accs[at] = acc
                tops[at] = jnp.broadcast_to(top, (ROWS, HD))
                totals[at] = jnp.broadcast_to(total, (ROWS, HD))

    whole_own = [(ks, vs, c, False) for c in range(QB)]
    whole_first = [(k0, v0, c, False) for c in range(QB)]

    def between(h):
        @pl.when(row == 1)
        def _():
            arrived(KS, h)
            arrived(VS, h)
            z_copy(ZK, h).wait_recv()
            z_copy(ZV, h).wait_recv()
            z_copy(ZQ2, h).wait_recv()
            partial(q2, h, whole_first + whole_own, 0)
            z_copy(ZO2, h).start()
            z_copy(ZS2, h).start()
            z_copy(ZQ3, h).wait_recv()
            partial(q3, h, whole_first + whole_own, 1)
            z_copy(ZO3, h).start()
            z_copy(ZS3, h).start()

        @pl.when(row == 2)
        def _():
            arrived(KS, h)
            arrived(VS, h)
            z_copy(ZQ3B, h).wait_recv()
            partial(q3, h, whole_own, 1)
            z_copy(ZO3B, h).start()
            z_copy(ZS3B, h).start()

    def own_others(h):
        @pl.when(row == 0)
        def _():
            arrived(QS, h)
            own_rows(h, [], True)

        @pl.when(row == 2)
        def _():
            own_rows(h, [], False)

        @pl.when(row == 3)
        def _():
            arrived(KS, h)
            arrived(VS, h)
            own_rows(h, [], False)

    def own_second(h):
        @pl.when(row == 1)
        def _():
            arrived(QS, h)
            own_rows(h, whole_first, True)

    relay(0)
    for kind in range(2):
        own_db(kind).wait()
    far_stage()
    relay(1)
    pass_stage(side)
    loop(2, 4, relay)
    loop(0, 2, between)
    pass_stage(away)
    loop(2, 4, between)
    loop(0, LOCAL, own_others)
    last_stage()
    loop(0, LOCAL, own_second)

    for k in range(1, XS):
        idx_copy(x_at(k), x_at(k)).wait_recv()
    numbers = pltpu.make_async_copy(idx, idx_s, number_sem)
    numbers.start()
    numbers.wait()
    loop(0, LOCAL, lambda h: arrived(QC, h))

    def wait_other_core(k):
        for kind in range(2):
            wait_shard(kind, 2 * k + 1 - core)

    loop(0, HALF, wait_other_core)

    def cross_step(t):
        for g in range(TOK // GROUP):
            first = idx_s[t, 0, g * NEIGH]
            second = idx_s[t, 0, g * NEIGH + 1]
            rows = pl.ds(g * GROUP, GROUP)
            for h in range(LOCAL):
                at = pl.ds(h * HD, HD)
                keys = jnp.concatenate([kd[first, :, at], kd[second, :, at]], axis=0)
                values = jnp.concatenate([vd[first, :, at], vd[second, :, at]], axis=0)
                s = lax.dot_general(qc[h, t, rows, :], keys, NT, preferred_element_type=jnp.float32)
                top = jnp.max(s, axis=1, keepdims=True)
                w = jnp.exp2((s - top) * EXPO)
                total = jnp.sum(w, axis=1, keepdims=True)
                o = lax.dot_general(w.astype(jnp.bfloat16), values, NN, preferred_element_type=jnp.float32)
                cross[h, t, rows, :] = o / total

    loop(0, XS, cross_step)

    def merge(h, parts):
        for b in range(QB):
            at = h * QB + b
            for p in range(PER):
                rows = slice(p * TOK, (p + 1) * TOK)
                sub = b * PER + p
                top = tops[at, rows, :1]
                others = []
                for place in range(parts):
                    column = [
                        jnp.sum(jnp.where(eye, stat_in[place, h, n : n + 1], 0.0), axis=1, keepdims=True)
                        for n in (sub, XS + sub)
                    ]
                    others.append(column)
                peak = top
                for other_top, _ in others:
                    peak = jnp.maximum(peak, other_top)
                keep = jnp.exp2((top - peak) * EXPO)
                total = totals[at, rows, :1] * keep
                acc = accs[at, rows, :] * keep
                for place, (other_top, other_total) in enumerate(others):
                    w = jnp.exp2((other_top - peak) * EXPO) * other_total
                    total = total + w
                    acc = acc + part_in[place, h, sub].astype(jnp.float32) * w
                accs[at, rows, :] = acc / total

    def out_copy(h, t):
        return pltpu.make_async_remote_copy(
            mixed.at[h, t], out_ref.at[:, cols(x * LOCAL + h)], x_send.at[OUT, h, t], x_recv.at[OUT, h, x],
            device_id={"dp": dp, "ctx": row * XS + t}, device_id_type=MESH,
        )

    def own_out(h):
        return pltpu.make_async_copy(mixed.at[h, x], out_ref.at[:, cols(x * LOCAL + h)], own_sem.at[OUT, h])

    def emit(h):
        @pl.when(row == 2)
        def _():
            z_copy(ZO2, h).wait_recv()
            z_copy(ZS2, h).wait_recv()
            merge(h, 1)

        @pl.when(row == 3)
        def _():
            z_copy(ZO3, h).wait_recv()
            z_copy(ZS3, h).wait_recv()
            z_copy(ZO3B, h).wait_recv()
            z_copy(ZS3B, h).wait_recv()
            merge(h, 2)

        self_out = accs[pl.ds(h * QB, QB)].astype(jnp.bfloat16).astype(jnp.float32).reshape(XS, TOK, HD)
        mixed[h] = (self_out + cross[h]).astype(jnp.bfloat16)
        for k in (1, 3, 2):
            out_copy(h, x_at(k)).start()
        own_out(h).start()

    loop(0, LOCAL, emit)

    def finish(h):
        own_out(h).wait()
        for k in range(1, XS):
            peer = x_at(k)
            pltpu.make_async_remote_copy(
                mixed.at[h, peer], out_ref.at[:, cols(peer * LOCAL + h)], x_send.at[OUT, h, peer], x_recv.at[OUT, h, peer],
                device_id={"dp": dp, "ctx": row * XS + peer}, device_id_type=MESH,
            ).wait_recv()
            for kind in (QC, KS, VS, QS):
                x_copy(kind, h, peer).wait_send()
            out_copy(h, peer).wait_send()
        for at, kinds in enumerate(((ZK, ZV), (ZO2, ZS2, ZO3, ZS3), (ZQ2, ZO3B, ZS3B), (ZQ3, ZQ3B))):

            @pl.when(row == at)
            def _():
                for kind in kinds:
                    z_copy(kind, h).wait_send()

    for kind in range(2):
        far_copy(kind).wait_send()
        for k in (1, 3):
            y_own(kind, k).wait_send()
            y_far(kind, k).wait_send()
        for home in (side, away):
            y_pass(kind, home).wait_send()
            for k in range(4):
                core_pass(kind, home, k).wait_send()
    for k in range(1, XS):
        idx_copy(x_at(k), x).wait_send()
    loop(0, LOCAL, finish)


def shards(q_self, k_self, v_self, q_cross, db_keys, db_values, nb_shard, nb_row):
    anywhere = pl.BlockSpec(memory_space=pl.ANY)
    scalars = pl.BlockSpec(memory_space=pltpu.SMEM)
    heads = pltpu.VMEM((LOCAL, XS, TOK, HD), jnp.bfloat16)
    database = pltpu.VMEM((N_DP * DB_DEV, NLEN, WIDE), jnp.bfloat16)
    state = pltpu.VMEM((LOCAL * QB, ROWS, HD), jnp.float32)
    parts = pltpu.VMEM((2, LOCAL, XS, TOK, HD), jnp.bfloat16)
    stats = pltpu.VMEM((2, LOCAL, 8, 128), jnp.float32)
    dma = pltpu.SemaphoreType.DMA
    out = pl.pallas_call(
        kernel,
        out_shape=jax.ShapeDtypeStruct((TOK, HEADS * HD), jnp.bfloat16),
        in_specs=[anywhere] * 6 + [scalars] * 2,
        out_specs=anywhere,
        scratch_shapes=[
            heads, heads, heads, heads, heads, heads, heads, heads, database, database,
            pltpu.VMEM((XS, 8, 128), jnp.int32),
            pltpu.SMEM((XS, 8, 128), jnp.int32),
            pltpu.VMEM((LOCAL, XS, TOK, HD), jnp.float32),
            pltpu.VMEM((2, 2 * QB, ROWS, ROWS), jnp.float32),
            state, state, state,
            parts, stats, parts, stats, heads,
            dma((5, LOCAL, XS)), dma((5, LOCAL, XS)), dma((XS,)), dma((XS,)), dma((11, LOCAL)), dma((11, LOCAL)),
            dma((2,)), dma((2, 2, 2)), dma((2, 2)), dma((2, 2, 4)), dma((2, N_DP)), dma((5, LOCAL)), dma((2,)), dma,
        ],
        compiler_params=pltpu.CompilerParams(
            collective_id=0, has_side_effects=True, vmem_limit_bytes=60 * 1024 * 1024
        ),
    )(q_self[0], k_self[0], v_self[0], q_cross[0], db_keys, db_values, nb_shard, nb_row)
    return out[None]


def solution(mesh):
    return jax.shard_map(
        shards,
        mesh=mesh,
        in_specs=(
            P("dp", "ctx", None),
            P("dp", "ctx", None),
            P("dp", "ctx", None),
            P("dp", "ctx", None),
            P("dp", None, None),
            P("dp", None, None),
            P("dp", "ctx", None),
            P("dp", "ctx", None),
        ),
        out_specs=P("dp", "ctx", None),
        check_vma=False,
    )
```

```python
import jax
import jax.numpy as jnp
from jax import lax
from jax.experimental import pallas as pl
from jax.experimental.pallas import tpu as pltpu
from jax.sharding import PartitionSpec as P

HEADS = 16
HD = 128
GROUP = 64
NEIGH = 2
NLEN = 128
TOK = 128
DB_DEV = 2
N_DP = 16
HALF = 8
XS = 4
LOCAL = HEADS // XS
WIDE = LOCAL * HD
ROWS = 256
PER = ROWS // TOK
QB = XS // PER
EXPO = HD**-0.5 * 1.4426950408889634
MESH = pl.DeviceIdType.MESH
NT = (((1,), (1,)), ((), ()))
NN = (((1,), (0,)), ((), ()))
QC, KS, VS, QS, OUT = range(5)
ZK, ZV, ZQ2, ZQ3, ZQ3B, ZO2, ZS2, ZO3, ZS3, ZO3B, ZS3B = range(11)


def cols(head):
    return pl.ds(pl.multiple_of(head * HD, HD), HD)


def kernel(
    qs_ref, ks_ref, vs_ref, qc_ref, kd_ref, vd_ref, shard_ref, row_ref, out_ref,
    qs, ks, vs, qc, k0, v0, q2, q3, kd, vd, idx, idx_s, cross, scores, tops, totals, accs,
    part_out, stat_out, part_in, stat_in, mixed,
    x_send, x_recv, idx_send, idx_recv, z_send, z_recv,
    far_send, y_send, y_pass_send, core_send, db_recv, own_sem, db_own, number_sem, ready,
):
    dp = lax.axis_index("dp")
    me = lax.axis_index("ctx")
    row = me // XS
    x = lax.rem(me, XS)
    near = lax.rem(dp, HALF)
    side = dp - near
    away = HALF - side
    core = lax.rem(near, 2)
    other_core = dp + 1 - 2 * core
    far_dp = away + near
    far_ctx = (3 - row) * XS + x
    edge = (row == 0) | (row == 3)
    first_side = dp < HALF
    inner_ctx = (row // 2 + 1) * XS + x

    def x_at(k):
        return lax.rem(x + k, XS)

    def y_at(home, k):
        return home + lax.rem(near + 2 * k, HALF)

    def loop(first, last, body):
        def step(k, carry):
            body(k)
            return carry

        lax.fori_loop(first, last, step, 0)

    barrier = pltpu.get_barrier_semaphore()

    def greet(dp_of, ctx_of):
        pl.semaphore_signal(barrier, inc=1, device_id={"dp": dp_of, "ctx": ctx_of}, device_id_type=MESH)

    for k in range(1, 4):
        greet(dp, row * XS + x_at(k))
        greet(dp, lax.rem(row + k, 4) * XS + x)
    greet(y_at(side, 1), me)
    greet(y_at(side, 3), me)
    greet(other_core, me)

    @pl.when(edge & first_side)
    def _():
        greet(far_dp, far_ctx)

    lane = lax.broadcasted_iota(jnp.int32, (8, 128), 1)
    tile = jnp.zeros((8, 128), jnp.int32)
    for g in range(TOK // GROUP):
        for n in range(NEIGH):
            block = shard_ref[0, g, n] * DB_DEV + row_ref[0, g, n]
            tile = jnp.where(lane == g * NEIGH + n, block, tile)
    idx[x] = tile

    arrays = {QC: (qc_ref, qc), KS: (ks_ref, ks), VS: (vs_ref, vs), QS: (qs_ref, qs)}
    blocks = ((kd_ref, kd), (vd_ref, vd))
    wide = pl.ds(pl.multiple_of(x * WIDE, WIDE), WIDE)

    def own_copy(kind, h):
        arg, buf = arrays[kind]
        return pltpu.make_async_copy(arg.at[:, cols(x * LOCAL + h)], buf.at[h, x], own_sem.at[kind, h])

    def own_db(kind):
        arg, buf = blocks[kind]
        return pltpu.make_async_copy(arg.at[:, :, wide], buf.at[pl.ds(dp * DB_DEV, DB_DEV)], db_own.at[kind])

    def start_own(h):
        for kind in (KS, VS, QS, QC):
            own_copy(kind, h).start()

    loop(0, LOCAL, start_own)
    for kind in range(2):
        own_db(kind).start()

    pl.semaphore_wait(barrier, 9 + jnp.where(edge & (dp >= HALF), 1, 0))

    @pl.when(edge & (dp >= HALF))
    def _():
        pl.semaphore_signal(ready, inc=1, device_id={"dp": far_dp, "ctx": far_ctx}, device_id_type=MESH)

    def shard_copy(kind, shard, send, target, target_ctx, whole):
        arg, buf = blocks[kind]
        part = buf.at[pl.ds(shard * DB_DEV, DB_DEV)]
        return pltpu.make_async_remote_copy(
            arg.at[:, :, wide] if whole else part, part, send, db_recv.at[kind, shard],
            device_id={"dp": target, "ctx": target_ctx}, device_id_type=MESH,
        )

    def far_copy(kind):
        return shard_copy(kind, dp, far_send.at[kind], far_dp, far_ctx, True)

    def inner_copy(kind):
        return shard_copy(kind, far_dp, far_send.at[2 + kind], dp, inner_ctx, False)

    def y_own(kind, k):
        return shard_copy(kind, dp, y_send.at[kind, 0, k // 2], y_at(side, k), me, True)

    def y_far(kind, k):
        return shard_copy(kind, far_dp, y_send.at[kind, 1, k // 2], y_at(side, k), me, False)

    def y_pass(kind, home):
        k = 3 if kind == 0 else 1
        return shard_copy(kind, y_at(home, k), y_pass_send.at[kind, 0 if home is side else 1], y_at(side, 4 - k), me, False)

    def core_pass(kind, home, k):
        return shard_copy(
            kind, y_at(home, k), core_send.at[kind, 0 if home is side else 1, k], other_core, me, home is side and k == 0
        )

    def wait_shard(kind, shard):
        shard_copy(kind, shard, far_send.at[kind], other_core, me, False).wait_recv()

    def x_copy(kind, h, to):
        arg, buf = arrays[kind]
        return pltpu.make_async_remote_copy(
            arg.at[:, cols(to * LOCAL + h)], buf.at[h, x], x_send.at[kind, h, to], x_recv.at[kind, h, x],
            device_id={"dp": dp, "ctx": row * XS + to}, device_id_type=MESH,
        )

    def arrived(kind, h):
        own_copy(kind, h).wait()
        for k in range(1, XS):
            source = x_at(k)
            buf = arrays[kind][1].at[h, source]
            pltpu.make_async_remote_copy(
                buf, buf, x_send.at[kind, h, source], x_recv.at[kind, h, source],
                device_id={"dp": dp, "ctx": row * XS + source}, device_id_type=MESH,
            ).wait_recv()

    def idx_copy(to, slot):
        return pltpu.make_async_remote_copy(
            idx.at[slot], idx.at[slot], idx_send.at[to], idx_recv.at[slot],
            device_id={"dp": dp, "ctx": row * XS + to}, device_id_type=MESH,
        )

    def start_x(kinds):
        def step(h):
            for k in (1, 3, 2):
                for kind in kinds:
                    x_copy(kind, h, x_at(k)).start()

        loop(0, LOCAL, step)

    for kind in range(2):
        for k in (1, 3):
            y_own(kind, k).start()

    @pl.when(edge & (dp >= HALF))
    def _():
        for kind in range(2):
            far_copy(kind).start()

    @pl.when(row < 2)
    def _():
        start_x((KS, VS))
        start_x((QS,))

    @pl.when(row >= 2)
    def _():
        start_x((QS,))
        start_x((KS, VS))

    start_x((QC,))
    for k in range(1, XS):
        idx_copy(x_at(k), x).start()
    for kind in range(2):
        core_pass(kind, side, 0).start()

    @pl.when(edge & first_side)
    def _():
        pl.semaphore_wait(ready, 1)
        for kind in range(2):
            far_copy(kind).start()

    def z_copy(kind, h):
        src, dst, to = {
            ZK: (ks.at[h], k0.at[h], 1),
            ZV: (vs.at[h], v0.at[h], 1),
            ZQ2: (qs.at[h], q2.at[h], 1),
            ZQ3: (qs.at[h], q3.at[h], 1),
            ZQ3B: (qs.at[h], q3.at[h], 2),
            ZO2: (part_out.at[0, h], part_in.at[0, h], 2),
            ZS2: (stat_out.at[0, h], stat_in.at[0, h], 2),
            ZO3: (part_out.at[1, h], part_in.at[0, h], 3),
            ZS3: (stat_out.at[1, h], stat_in.at[0, h], 3),
            ZO3B: (part_out.at[1, h], part_in.at[1, h], 3),
            ZS3B: (stat_out.at[1, h], stat_in.at[1, h], 3),
        }[kind]
        return pltpu.make_async_remote_copy(
            src, dst, z_send.at[kind, h], z_recv.at[kind, h],
            device_id={"dp": dp, "ctx": to * XS + x}, device_id_type=MESH,
        )

    def relay(h):
        @pl.when(row == 0)
        def _():
            arrived(KS, h)
            z_copy(ZK, h).start()
            arrived(VS, h)
            z_copy(ZV, h).start()

        @pl.when(row == 2)
        def _():
            arrived(QS, h)
            z_copy(ZQ2, h).start()

        @pl.when(row == 3)
        def _():
            arrived(QS, h)
            z_copy(ZQ3, h).start()

    def far_stage():
        for kind in range(2):
            wait_shard(kind, far_dp)

            @pl.when(edge)
            def _():
                inner_copy(kind).start()

            for k in (1, 3):
                y_far(kind, k).start()
            core_pass(kind, away, 0).start()

    def pass_stage(home):
        for kind in range(2):
            for k in (1, 3):
                wait_shard(kind, y_at(home, k))
                if (k == 3) == (kind == 0):
                    y_pass(kind, home).start()
                core_pass(kind, home, k).start()

    def last_stage():
        for home in (side, away):
            for kind in range(2):
                wait_shard(kind, y_at(home, 2))
                core_pass(kind, home, 2).start()

    diagonal = lax.broadcasted_iota(jnp.int32, (ROWS, ROWS), 0) >= lax.broadcasted_iota(jnp.int32, (ROWS, ROWS), 1)
    eye = lax.broadcasted_iota(jnp.int32, (TOK, TOK), 0) == lax.broadcasted_iota(jnp.int32, (TOK, TOK), 1)

    def attend(queries, h, b, chunks, slot):
        q = queries[h, pl.ds(b * PER, PER)].reshape(ROWS, HD)
        peak = None
        for j, (keys, values, c, masked) in enumerate(chunks):
            k = keys[h, pl.ds(c * PER, PER)].reshape(ROWS, HD)
            s = lax.dot_general(q, k, NT, preferred_element_type=jnp.float32)
            if masked:
                s = jnp.where(diagonal, s, -1e30)
            scores[slot, j] = s
            folded = jnp.maximum(s[:, :HD], s[:, HD:])
            peak = folded if peak is None else jnp.maximum(peak, folded)
        top = jnp.max(peak, axis=1, keepdims=True)
        total = jnp.zeros((ROWS, HD), jnp.float32)
        acc = jnp.zeros((ROWS, HD), jnp.float32)
        for j, (keys, values, c, masked) in enumerate(chunks):
            w = jnp.exp2((scores[slot, j] - top) * EXPO)
            total = total + (w[:, :HD] + w[:, HD:])
            v = values[h, pl.ds(c * PER, PER)].reshape(ROWS, HD)
            acc = acc + lax.dot_general(w.astype(jnp.bfloat16), v, NN, preferred_element_type=jnp.float32)
        return top, jnp.sum(total, axis=1, keepdims=True), acc

    def partial(queries, h, chunks, place):
        for b in range(QB):
            top, total, acc = attend(queries, h, b, chunks, b)
            part_out[place, h, pl.ds(b * PER, PER)] = (acc / total).astype(jnp.bfloat16).reshape(PER, TOK, HD)
            for p in range(PER):
                rows = slice(p * TOK, (p + 1) * TOK)
                at = b * PER + p
                stat_out[place, h, at : at + 1] = jnp.sum(jnp.where(eye, top[rows], 0.0), axis=0, keepdims=True)
                stat_out[place, h, XS + at : XS + at + 1] = jnp.sum(jnp.where(eye, total[rows], 0.0), axis=0, keepdims=True)

    def own_rows(h, extra, final):
        for b in range(QB):
            chunks = extra + [(ks, vs, c, c == b) for c in range(b + 1)]
            top, total, acc = attend(qs, h, b, chunks, b)
            at = h * QB + b
            if final:
                accs[at] = acc / total
            else:
                accs[at] = acc
                tops[at] = jnp.broadcast_to(top, (ROWS, HD))
                totals[at] = jnp.broadcast_to(total, (ROWS, HD))

    whole_own = [(ks, vs, c, False) for c in range(QB)]
    whole_first = [(k0, v0, c, False) for c in range(QB)]

    def between(h):
        @pl.when(row == 1)
        def _():
            arrived(KS, h)
            arrived(VS, h)
            z_copy(ZK, h).wait_recv()
            z_copy(ZV, h).wait_recv()
            z_copy(ZQ2, h).wait_recv()
            partial(q2, h, whole_first + whole_own, 0)
            z_copy(ZO2, h).start()
            z_copy(ZS2, h).start()
            z_copy(ZQ3, h).wait_recv()
            partial(q3, h, whole_first + whole_own, 1)
            z_copy(ZO3, h).start()
            z_copy(ZS3, h).start()
            arrived(QS, h)
            own_rows(h, whole_first, True)

        @pl.when(row == 2)
        def _():
            arrived(KS, h)
            arrived(VS, h)
            z_copy(ZQ3B, h).wait_recv()
            partial(q3, h, whole_own, 1)
            z_copy(ZO3B, h).start()
            z_copy(ZS3B, h).start()

    def own_others(h):
        @pl.when(row == 0)
        def _():
            arrived(QS, h)
            own_rows(h, [], True)

        @pl.when(row == 2)
        def _():
            own_rows(h, [], False)

        @pl.when(row == 3)
        def _():
            arrived(KS, h)
            arrived(VS, h)
            own_rows(h, [], False)

    for kind in range(2):
        own_db(kind).wait()

    @pl.when(row == 0)
    def _():
        relay(0)
        relay(1)
        far_stage()
        relay(2)
        pass_stage(side)
        relay(3)

    @pl.when(row == 1)
    def _():
        pass_stage(side)
        far_stage()

    @pl.when(row >= 2)
    def _():
        loop(0, LOCAL, relay)
        far_stage()

        @pl.when(row == 3)
        def _():
            loop(0, LOCAL, lambda h: z_copy(ZQ3B, h).start())

        pass_stage(side)

    loop(0, 2, between)
    pass_stage(away)
    loop(2, 4, between)
    loop(0, LOCAL, own_others)
    last_stage()

    for k in range(1, XS):
        idx_copy(x_at(k), x_at(k)).wait_recv()
    numbers = pltpu.make_async_copy(idx, idx_s, number_sem)
    numbers.start()
    numbers.wait()
    loop(0, LOCAL, lambda h: arrived(QC, h))

    def wait_other_core(k):
        for kind in range(2):
            wait_shard(kind, 2 * k + 1 - core)

    loop(0, HALF, wait_other_core)

    def cross_head(h):
        def step(t):
            for g in range(TOK // GROUP):
                first = idx_s[t, 0, g * NEIGH]
                second = idx_s[t, 0, g * NEIGH + 1]
                rows = pl.ds(g * GROUP, GROUP)
                at = cols(h)
                keys = jnp.concatenate([kd[first, :, at], kd[second, :, at]], axis=0)
                values = jnp.concatenate([vd[first, :, at], vd[second, :, at]], axis=0)
                s = lax.dot_general(qc[h, t, rows, :], keys, NT, preferred_element_type=jnp.float32)
                top = jnp.max(s, axis=1, keepdims=True)
                w = jnp.exp2((s - top) * EXPO)
                total = jnp.sum(w, axis=1, keepdims=True)
                o = lax.dot_general(w.astype(jnp.bfloat16), values, NN, preferred_element_type=jnp.float32)
                cross[h, t, rows, :] = o / total

        for t in range(XS):
            step(t)

    def merge(h, parts):
        for b in range(QB):
            at = h * QB + b
            for p in range(PER):
                rows = slice(p * TOK, (p + 1) * TOK)
                sub = b * PER + p
                top = tops[at, rows, :1]
                others = []
                for place in range(parts):
                    column = [
                        jnp.sum(jnp.where(eye, stat_in[place, h, n : n + 1], 0.0), axis=1, keepdims=True)
                        for n in (sub, XS + sub)
                    ]
                    others.append(column)
                peak = top
                for other_top, _ in others:
                    peak = jnp.maximum(peak, other_top)
                keep = jnp.exp2((top - peak) * EXPO)
                total = totals[at, rows, :1] * keep
                acc = accs[at, rows, :] * keep
                for place, (other_top, other_total) in enumerate(others):
                    w = jnp.exp2((other_top - peak) * EXPO) * other_total
                    total = total + w
                    acc = acc + part_in[place, h, sub].astype(jnp.float32) * w
                accs[at, rows, :] = acc / total

    def out_copy(h, t):
        return pltpu.make_async_remote_copy(
            mixed.at[h, t], out_ref.at[:, cols(x * LOCAL + h)], x_send.at[OUT, h, t], x_recv.at[OUT, h, x],
            device_id={"dp": dp, "ctx": row * XS + t}, device_id_type=MESH,
        )

    def own_out(h):
        return pltpu.make_async_copy(mixed.at[h, x], out_ref.at[:, cols(x * LOCAL + h)], own_sem.at[OUT, h])

    def emit(h):
        @pl.when(row == 2)
        def _():
            z_copy(ZO2, h).wait_recv()
            z_copy(ZS2, h).wait_recv()
            merge(h, 1)

        @pl.when(row == 3)
        def _():
            z_copy(ZO3, h).wait_recv()
            z_copy(ZS3, h).wait_recv()
            z_copy(ZO3B, h).wait_recv()
            z_copy(ZS3B, h).wait_recv()
            merge(h, 2)

        self_out = accs[pl.ds(h * QB, QB)].astype(jnp.bfloat16).astype(jnp.float32).reshape(XS, TOK, HD)
        mixed[h] = (self_out + cross[h]).astype(jnp.bfloat16)
        for k in (1, 3, 2):
            out_copy(h, x_at(k)).start()
        own_out(h).start()

    def head_out(h):
        cross_head(h)
        emit(h)

    loop(0, LOCAL, head_out)

    def finish(h):
        own_out(h).wait()
        for k in range(1, XS):
            peer = x_at(k)
            pltpu.make_async_remote_copy(
                mixed.at[h, peer], out_ref.at[:, cols(peer * LOCAL + h)], x_send.at[OUT, h, peer], x_recv.at[OUT, h, peer],
                device_id={"dp": dp, "ctx": row * XS + peer}, device_id_type=MESH,
            ).wait_recv()
            for kind in (QC, KS, VS, QS):
                x_copy(kind, h, peer).wait_send()
            out_copy(h, peer).wait_send()
        for at, kinds in enumerate(((ZK, ZV), (ZO2, ZS2, ZO3, ZS3), (ZQ2, ZO3B, ZS3B), (ZQ3, ZQ3B))):

            @pl.when(row == at)
            def _():
                for kind in kinds:
                    z_copy(kind, h).wait_send()

    @pl.when(edge)
    def _():
        for kind in range(2):
            far_copy(kind).wait_send()
            inner_copy(kind).wait_send()

    for kind in range(2):
        for k in (1, 3):
            y_own(kind, k).wait_send()
            y_far(kind, k).wait_send()
        for home in (side, away):
            y_pass(kind, home).wait_send()
            for k in range(4):
                core_pass(kind, home, k).wait_send()
    for k in range(1, XS):
        idx_copy(x_at(k), x).wait_send()
    loop(0, LOCAL, finish)


def shards(q_self, k_self, v_self, q_cross, db_keys, db_values, nb_shard, nb_row):
    anywhere = pl.BlockSpec(memory_space=pl.ANY)
    scalars = pl.BlockSpec(memory_space=pltpu.SMEM)
    heads = pltpu.VMEM((LOCAL, XS, TOK, HD), jnp.bfloat16)
    database = pltpu.VMEM((N_DP * DB_DEV, NLEN, WIDE), jnp.bfloat16)
    state = pltpu.VMEM((LOCAL * QB, ROWS, HD), jnp.float32)
    parts = pltpu.VMEM((2, LOCAL, XS, TOK, HD), jnp.bfloat16)
    stats = pltpu.VMEM((2, LOCAL, 8, 128), jnp.float32)
    dma = pltpu.SemaphoreType.DMA
    out = pl.pallas_call(
        kernel,
        out_shape=jax.ShapeDtypeStruct((TOK, HEADS * HD), jnp.bfloat16),
        in_specs=[anywhere] * 6 + [scalars] * 2,
        out_specs=anywhere,
        scratch_shapes=[
            heads, heads, heads, heads, heads, heads, heads, heads, database, database,
            pltpu.VMEM((XS, 8, 128), jnp.int32),
            pltpu.SMEM((XS, 8, 128), jnp.int32),
            pltpu.VMEM((LOCAL, XS, TOK, HD), jnp.float32),
            pltpu.VMEM((2, 2 * QB, ROWS, ROWS), jnp.float32),
            state, state, state,
            parts, stats, parts, stats, heads,
            dma((5, LOCAL, XS)), dma((5, LOCAL, XS)), dma((XS,)), dma((XS,)), dma((11, LOCAL)), dma((11, LOCAL)),
            dma((4,)), dma((2, 2, 2)), dma((2, 2)), dma((2, 2, 4)), dma((2, N_DP)), dma((5, LOCAL)), dma((2,)), dma,
            pltpu.SemaphoreType.REGULAR,
        ],
        compiler_params=pltpu.CompilerParams(
            collective_id=0, has_side_effects=True, vmem_limit_bytes=60 * 1024 * 1024
        ),
    )(q_self[0], k_self[0], v_self[0], q_cross[0], db_keys, db_values, nb_shard, nb_row)
    return out[None]


def solution(mesh):
    return jax.shard_map(
        shards,
        mesh=mesh,
        in_specs=(
            P("dp", "ctx", None),
            P("dp", "ctx", None),
            P("dp", "ctx", None),
            P("dp", "ctx", None),
            P("dp", None, None),
            P("dp", None, None),
            P("dp", "ctx", None),
            P("dp", "ctx", None),
        ),
        out_specs=P("dp", "ctx", None),
        check_vma=False,
    )
```

```python
import jax
import jax.numpy as jnp
from jax import lax
from jax.experimental import pallas as pl
from jax.experimental.pallas import tpu as pltpu
from jax.sharding import PartitionSpec as P

HEADS = 16
HD = 128
GROUP = 64
NEIGH = 2
NLEN = 128
TOK = 128
DB_DEV = 2
N_DP = 16
HALF = 8
XS = 4
LOCAL = HEADS // XS
WIDE = LOCAL * HD
ROWS = 256
PER = ROWS // TOK
QB = XS // PER
EXPO = HD**-0.5 * 1.4426950408889634
MESH = pl.DeviceIdType.MESH
NT = (((1,), (1,)), ((), ()))
NN = (((1,), (0,)), ((), ()))
QC, KS, VS, QS, OUT = range(5)
ZK, ZV, ZQ2, ZQ3, ZQ3B, ZO2, ZS2, ZO3, ZS3, ZO3B, ZS3B, ZOC = range(12)


def cols(head):
    return pl.ds(pl.multiple_of(head * HD, HD), HD)


def kernel(
    qs_ref, ks_ref, vs_ref, qc_ref, kd_ref, vd_ref, shard_ref, row_ref, out_ref,
    qs, ks, vs, qc, k0, v0, q2, q3, kd, vd, idx, idx_s, cross, scores, tops, totals, accs,
    part_out, stat_out, part_in, stat_in, mixed, cross_out,
    x_send, x_recv, qc_recv, idx_send, idx_recv, z_send, z_recv,
    far_send, side_send, y_send, y_pass_send, core_send, db_recv, own_sem, db_own, number_sem, ready,
):
    dp = lax.axis_index("dp")
    me = lax.axis_index("ctx")
    row = me // XS
    x = lax.rem(me, XS)
    near = lax.rem(dp, HALF)
    side = dp - near
    away = HALF - side
    core = lax.rem(near, 2)
    other_core = dp + 1 - 2 * core
    far_dp = away + near
    far_ctx = (3 - row) * XS + x
    edge = (row == 0) | (row == 3)
    first_side = dp < HALF
    inner = (row == 1) | (row == 2)
    pair = row + 1 - 2 * lax.rem(row, 2)

    def x_at(k):
        return lax.rem(x + k, XS)

    def y_at(home, k):
        return home + lax.rem(near + 2 * k, HALF)

    def loop(first, last, body):
        def step(k, carry):
            body(k)
            return carry

        lax.fori_loop(first, last, step, 0)

    barrier = pltpu.get_barrier_semaphore()

    def greet(dp_of, ctx_of):
        pl.semaphore_signal(barrier, inc=1, device_id={"dp": dp_of, "ctx": ctx_of}, device_id_type=MESH)

    for k in range(1, 4):
        greet(dp, row * XS + x_at(k))
        greet(dp, lax.rem(row + k, 4) * XS + x)
        greet(dp, pair * XS + x_at(k))
        greet(y_at(side, k), me)
    greet(other_core, me)

    @pl.when(edge & first_side)
    def _():
        greet(far_dp, far_ctx)

    lane = lax.broadcasted_iota(jnp.int32, (8, 128), 1)
    tile = jnp.zeros((8, 128), jnp.int32)
    for g in range(TOK // GROUP):
        for n in range(NEIGH):
            block = shard_ref[0, g, n] * DB_DEV + row_ref[0, g, n]
            tile = jnp.where(lane == g * NEIGH + n, block, tile)
    idx[me] = tile

    arrays = {QC: (qc_ref, qc), KS: (ks_ref, ks), VS: (vs_ref, vs), QS: (qs_ref, qs)}
    blocks = ((kd_ref, kd), (vd_ref, vd))
    wide = pl.ds(pl.multiple_of(x * WIDE, WIDE), WIDE)

    def own_copy(kind, h):
        arg, buf = arrays[kind]
        if kind == QC:
            buf = buf.at[0]
        return pltpu.make_async_copy(arg.at[:, cols(x * LOCAL + h)], buf.at[h, x], own_sem.at[kind, h])

    def own_db(kind):
        arg, buf = blocks[kind]
        return pltpu.make_async_copy(arg.at[:, :, wide], buf.at[pl.ds(dp * DB_DEV, DB_DEV)], db_own.at[kind])

    def start_own(h):
        for kind in (KS, VS, QS):
            own_copy(kind, h).start()

        @pl.when(edge)
        def _():
            own_copy(QC, h).start()

    loop(0, LOCAL, start_own)

    @pl.when(edge)
    def _():
        for kind in range(2):
            own_db(kind).start()

    pl.semaphore_wait(barrier, 13 + jnp.where(edge & (dp >= HALF), 1, 0))

    @pl.when(edge & (dp >= HALF))
    def _():
        pl.semaphore_signal(ready, inc=1, device_id={"dp": far_dp, "ctx": far_ctx}, device_id_type=MESH)

    def shard_copy(kind, shard, send, target, target_ctx, whole):
        arg, buf = blocks[kind]
        part = buf.at[pl.ds(shard * DB_DEV, DB_DEV)]
        return pltpu.make_async_remote_copy(
            arg.at[:, :, wide] if whole else part, part, send, db_recv.at[kind, shard],
            device_id={"dp": target, "ctx": target_ctx}, device_id_type=MESH,
        )

    def far_copy(kind):
        return shard_copy(kind, dp, far_send.at[kind], far_dp, far_ctx, True)

    def side_copy(k):
        return shard_copy(1, dp, side_send.at[0, k], y_at(side, k), me, True)

    def side_pass(k):
        return shard_copy(1, y_at(side, k), side_send.at[1, k], dp, pair * XS + x, False)

    def y_own(kind, k):
        return shard_copy(kind, dp, y_send.at[kind, 0, k // 2], y_at(side, k), me, True)

    def y_far(kind, k):
        return shard_copy(kind, far_dp, y_send.at[kind, 1, k // 2], y_at(side, k), me, False)

    def y_pass(kind, home):
        k = 3 if kind == 0 else 1
        return shard_copy(kind, y_at(home, k), y_pass_send.at[kind, 0 if home is side else 1], y_at(side, 4 - k), me, False)

    def core_pass(kind, home, k):
        return shard_copy(
            kind, y_at(home, k), core_send.at[kind, 0 if home is side else 1, k], other_core, me, home is side and k == 0
        )

    def wait_shard(kind, shard):
        shard_copy(kind, shard, far_send.at[kind], other_core, me, False).wait_recv()

    def x_copy(kind, h, to):
        arg, buf = arrays[kind]
        return pltpu.make_async_remote_copy(
            arg.at[:, cols(to * LOCAL + h)], buf.at[h, x], x_send.at[kind, h, to], x_recv.at[kind, h, x],
            device_id={"dp": dp, "ctx": row * XS + to}, device_id_type=MESH,
        )

    def qc_copy(part, h, to):
        return pltpu.make_async_remote_copy(
            qc_ref.at[:, cols(to * LOCAL + h)], qc.at[part, h, x], x_send.at[QC, h, to], qc_recv.at[part, h, x],
            device_id={"dp": dp, "ctx": (row if part == 0 else pair) * XS + to}, device_id_type=MESH,
        )

    def qc_arrived(part, h):
        for k in range(part ^ 1, XS):
            source = x_at(k)
            buf = qc.at[part, h, source]
            pltpu.make_async_remote_copy(
                buf, buf, x_send.at[QC, h, source], qc_recv.at[part, h, source],
                device_id={"dp": dp, "ctx": (row if part == 0 else pair) * XS + source}, device_id_type=MESH,
            ).wait_recv()

    def arrived(kind, h):
        own_copy(kind, h).wait()
        for k in range(1, XS):
            source = x_at(k)
            buf = arrays[kind][1].at[h, source]
            pltpu.make_async_remote_copy(
                buf, buf, x_send.at[kind, h, source], x_recv.at[kind, h, source],
                device_id={"dp": dp, "ctx": row * XS + source}, device_id_type=MESH,
            ).wait_recv()

    def idx_copy(to_row, to, slot):
        return pltpu.make_async_remote_copy(
            idx.at[slot], idx.at[slot], idx_send.at[to], idx_recv.at[slot],
            device_id={"dp": dp, "ctx": to_row * XS + to}, device_id_type=MESH,
        )

    def start_x(kinds):
        def step(h):
            for k in (1, 3, 2):
                for kind in kinds:
                    x_copy(kind, h, x_at(k)).start()

        loop(0, LOCAL, step)

    @pl.when(edge)
    def _():
        for k in (1, 3):
            y_own(0, k).start()

    @pl.when(inner)
    def _():
        for k in (1, 3, 2):
            side_copy(k).start()

    @pl.when(edge & (dp >= HALF))
    def _():
        for kind in range(2):
            far_copy(kind).start()

    @pl.when(row < 2)
    def _():
        start_x((KS, VS))
        start_x((QS,))

    @pl.when(row >= 2)
    def _():
        start_x((QS,))
        start_x((KS, VS))

    def start_qc(part):
        def step(h):
            for k in (1, 3, 2, 0)[: 3 + part]:
                qc_copy(part, h, x_at(k)).start()

        loop(0, LOCAL, step)
        for k in (1, 3, 2, 0)[: 3 + part]:
            idx_copy(row if part == 0 else pair, x_at(k), me).start()

    @pl.when(edge)
    def _():
        for kind in range(2):
            core_pass(kind, side, 0).start()
        start_qc(0)

    @pl.when(inner)
    def _():
        start_qc(1)

    @pl.when(edge & first_side)
    def _():
        pl.semaphore_wait(ready, 1)
        for kind in range(2):
            far_copy(kind).start()

    def z_copy(kind, h):
        src, dst, to = {
            ZK: (ks.at[h], k0.at[h], 1),
            ZV: (vs.at[h], v0.at[h], 1),
            ZQ2: (qs.at[h], q2.at[h], 1),
            ZQ3: (qs.at[h], q3.at[h], 1),
            ZQ3B: (qs.at[h], q3.at[h], 2),
            ZO2: (part_out.at[0, h], part_in.at[0, h], 2),
            ZS2: (stat_out.at[0, h], stat_in.at[0, h], 2),
            ZO3: (part_out.at[1, h], part_in.at[0, h], 3),
            ZS3: (stat_out.at[1, h], stat_in.at[0, h], 3),
            ZO3B: (part_out.at[1, h], part_in.at[1, h], 3),
            ZS3B: (stat_out.at[1, h], stat_in.at[1, h], 3),
            ZOC: (cross_out.at[h], cross_out.at[h], pair),
        }[kind]
        return pltpu.make_async_remote_copy(
            src, dst, z_send.at[kind, h], z_recv.at[kind, h],
            device_id={"dp": dp, "ctx": to * XS + x}, device_id_type=MESH,
        )

    def relay(h):
        @pl.when(row == 0)
        def _():
            arrived(KS, h)
            z_copy(ZK, h).start()
            arrived(VS, h)
            z_copy(ZV, h).start()

        @pl.when(row == 2)
        def _():
            arrived(QS, h)
            z_copy(ZQ2, h).start()

        @pl.when(row == 3)
        def _():
            arrived(QS, h)
            z_copy(ZQ3, h).start()

    def far_stage():
        for kind in range(2):
            wait_shard(kind, far_dp)
            for k in (1, 3):
                y_far(kind, k).start()
            core_pass(kind, away, 0).start()

    def pass_stage(home):
        for kind in range(1 if home is side else 2):
            for k in (1, 3):
                wait_shard(kind, y_at(home, k))
                if (k == 3) == (kind == 0):
                    y_pass(kind, home).start()
                core_pass(kind, home, k).start()

    def values_stage():
        for k in (1, 3, 2):
            wait_shard(1, y_at(side, k))
            core_pass(1, side, k).start()

    def side_stage():
        for k in (1, 3, 2):
            wait_shard(1, y_at(side, k))
            side_pass(k).start()

    def last_stage():
        for home, kind in ((side, 0), (away, 0), (away, 1)):
            wait_shard(kind, y_at(home, 2))
            core_pass(kind, home, 2).start()

    diagonal = lax.broadcasted_iota(jnp.int32, (ROWS, ROWS), 0) >= lax.broadcasted_iota(jnp.int32, (ROWS, ROWS), 1)
    eye = lax.broadcasted_iota(jnp.int32, (TOK, TOK), 0) == lax.broadcasted_iota(jnp.int32, (TOK, TOK), 1)

    def attend(queries, h, b, chunks, slot):
        q = queries[h, pl.ds(b * PER, PER)].reshape(ROWS, HD)
        peak = None
        for j, (keys, values, c, masked) in enumerate(chunks):
            k = keys[h, pl.ds(c * PER, PER)].reshape(ROWS, HD)
            s = lax.dot_general(q, k, NT, preferred_element_type=jnp.float32)
            if masked:
                s = jnp.where(diagonal, s, -1e30)
            scores[slot, j] = s
            folded = jnp.maximum(s[:, :HD], s[:, HD:])
            peak = folded if peak is None else jnp.maximum(peak, folded)
        top = jnp.max(peak, axis=1, keepdims=True)
        total = jnp.zeros((ROWS, HD), jnp.float32)
        acc = jnp.zeros((ROWS, HD), jnp.float32)
        for j, (keys, values, c, masked) in enumerate(chunks):
            w = jnp.exp2((scores[slot, j] - top) * EXPO)
            total = total + (w[:, :HD] + w[:, HD:])
            v = values[h, pl.ds(c * PER, PER)].reshape(ROWS, HD)
            acc = acc + lax.dot_general(w.astype(jnp.bfloat16), v, NN, preferred_element_type=jnp.float32)
        return top, jnp.sum(total, axis=1, keepdims=True), acc

    def partial(queries, h, chunks, place):
        for b in range(QB):
            top, total, acc = attend(queries, h, b, chunks, b)
            part_out[place, h, pl.ds(b * PER, PER)] = (acc / total).astype(jnp.bfloat16).reshape(PER, TOK, HD)
            for p in range(PER):
                rows = slice(p * TOK, (p + 1) * TOK)
                at = b * PER + p
                stat_out[place, h, at : at + 1] = jnp.sum(jnp.where(eye, top[rows], 0.0), axis=0, keepdims=True)
                stat_out[place, h, XS + at : XS + at + 1] = jnp.sum(jnp.where(eye, total[rows], 0.0), axis=0, keepdims=True)

    def own_rows(h, extra, final):
        for b in range(QB):
            chunks = extra + [(ks, vs, c, c == b) for c in range(b + 1)]
            top, total, acc = attend(qs, h, b, chunks, b)
            at = h * QB + b
            if final:
                accs[at] = acc / total
            else:
                accs[at] = acc
                tops[at] = jnp.broadcast_to(top, (ROWS, HD))
                totals[at] = jnp.broadcast_to(total, (ROWS, HD))

    whole_own = [(ks, vs, c, False) for c in range(QB)]
    whole_first = [(k0, v0, c, False) for c in range(QB)]

    def between(h):
        @pl.when(row == 1)
        def _():
            arrived(KS, h)
            arrived(VS, h)
            z_copy(ZK, h).wait_recv()
            z_copy(ZV, h).wait_recv()
            z_copy(ZQ2, h).wait_recv()
            partial(q2, h, whole_first + whole_own, 0)
            z_copy(ZO2, h).start()
            z_copy(ZS2, h).start()
            z_copy(ZQ3, h).wait_recv()
            partial(q3, h, whole_first + whole_own, 1)
            z_copy(ZO3, h).start()
            z_copy(ZS3, h).start()
            arrived(QS, h)
            own_rows(h, whole_first, True)

        @pl.when(row == 2)
        def _():
            arrived(KS, h)
            arrived(VS, h)
            z_copy(ZQ3B, h).wait_recv()
            partial(q3, h, whole_own, 1)
            z_copy(ZO3B, h).start()
            z_copy(ZS3B, h).start()

    def own_others(h):
        @pl.when(row == 0)
        def _():
            arrived(QS, h)
            own_rows(h, [], True)

        @pl.when(row == 2)
        def _():
            own_rows(h, [], False)

        @pl.when(row == 3)
        def _():
            arrived(KS, h)
            arrived(VS, h)
            own_rows(h, [], False)

    @pl.when(row == 0)
    def _():
        relay(0)
        relay(1)
        far_stage()
        relay(2)
        pass_stage(side)
        relay(3)

    @pl.when(row == 3)
    def _():
        loop(0, LOCAL, relay)
        loop(0, LOCAL, lambda h: z_copy(ZQ3B, h).start())
        far_stage()
        pass_stage(side)

    @pl.when(inner)
    def _():
        @pl.when(row == 2)
        def _():
            loop(0, LOCAL, relay)

        side_stage()
        loop(0, LOCAL, between)

    @pl.when(edge)
    def _():
        values_stage()
        pass_stage(away)

    loop(0, LOCAL, own_others)

    def cross_head(part, h, out):
        for t in range(XS):
            slot = (row if part == 0 else pair) * XS + t
            for g in range(TOK // GROUP):
                first = idx_s[slot, 0, g * NEIGH]
                second = idx_s[slot, 0, g * NEIGH + 1]
                rows = pl.ds(g * GROUP, GROUP)
                at = cols(h)
                keys = jnp.concatenate([kd[first, :, at], kd[second, :, at]], axis=0)
                values = jnp.concatenate([vd[first, :, at], vd[second, :, at]], axis=0)
                s = lax.dot_general(qc[part, h, t, rows, :], keys, NT, preferred_element_type=jnp.float32)
                top = jnp.max(s, axis=1, keepdims=True)
                w = jnp.exp2((s - top) * EXPO)
                total = jnp.sum(w, axis=1, keepdims=True)
                o = lax.dot_general(w.astype(jnp.bfloat16), values, NN, preferred_element_type=jnp.float32)
                out[h, t, rows, :] = (o / total).astype(out.dtype)

    def merge(h, parts):
        for b in range(QB):
            at = h * QB + b
            for p in range(PER):
                rows = slice(p * TOK, (p + 1) * TOK)
                sub = b * PER + p
                top = tops[at, rows, :1]
                others = []
                for place in range(parts):
                    column = [
                        jnp.sum(jnp.where(eye, stat_in[place, h, n : n + 1], 0.0), axis=1, keepdims=True)
                        for n in (sub, XS + sub)
                    ]
                    others.append(column)
                peak = top
                for other_top, _ in others:
                    peak = jnp.maximum(peak, other_top)
                keep = jnp.exp2((top - peak) * EXPO)
                total = totals[at, rows, :1] * keep
                acc = accs[at, rows, :] * keep
                for place, (other_top, other_total) in enumerate(others):
                    w = jnp.exp2((other_top - peak) * EXPO) * other_total
                    total = total + w
                    acc = acc + part_in[place, h, sub].astype(jnp.float32) * w
                accs[at, rows, :] = acc / total

    def out_copy(h, t):
        return pltpu.make_async_remote_copy(
            mixed.at[h, t], out_ref.at[:, cols(x * LOCAL + h)], x_send.at[OUT, h, t], x_recv.at[OUT, h, x],
            device_id={"dp": dp, "ctx": row * XS + t}, device_id_type=MESH,
        )

    def own_out(h):
        return pltpu.make_async_copy(mixed.at[h, x], out_ref.at[:, cols(x * LOCAL + h)], own_sem.at[OUT, h])

    def emit(h):
        @pl.when(row == 2)
        def _():
            z_copy(ZO2, h).wait_recv()
            z_copy(ZS2, h).wait_recv()
            merge(h, 1)

        @pl.when(row == 3)
        def _():
            z_copy(ZO3, h).wait_recv()
            z_copy(ZS3, h).wait_recv()
            z_copy(ZO3B, h).wait_recv()
            z_copy(ZS3B, h).wait_recv()
            merge(h, 2)

        @pl.when(inner)
        def _():
            z_copy(ZOC, h).wait_recv()
            cross[h] = cross_out[h].astype(jnp.float32)

        self_out = accs[pl.ds(h * QB, QB)].astype(jnp.bfloat16).astype(jnp.float32).reshape(XS, TOK, HD)
        mixed[h] = (self_out + cross[h]).astype(jnp.bfloat16)
        for k in (1, 3, 2):
            out_copy(h, x_at(k)).start()
        own_out(h).start()

    @pl.when(edge)
    def _():
        last_stage()
        for kind in range(2):
            own_db(kind).wait()
        for k in range(1, XS):
            idx_copy(row, x_at(k), row * XS + x_at(k)).wait_recv()
        for k in range(XS):
            idx_copy(pair, x_at(k), pair * XS + x_at(k)).wait_recv()
        numbers = pltpu.make_async_copy(idx, idx_s, number_sem)
        numbers.start()
        numbers.wait()

        def wait_other_core(k):
            for kind in range(2):
                wait_shard(kind, 2 * k + 1 - core)

        def beside(h):
            qc_arrived(1, h)
            cross_head(1, h, cross_out)
            z_copy(ZOC, h).start()

        def here(h):
            own_copy(QC, h).wait()
            qc_arrived(0, h)
            cross_head(0, h, cross)

        loop(0, HALF, wait_other_core)
        loop(0, LOCAL, beside)
        loop(0, LOCAL, here)

    loop(0, LOCAL, emit)

    def finish(h):
        own_out(h).wait()
        for k in range(1, XS):
            peer = x_at(k)
            pltpu.make_async_remote_copy(
                mixed.at[h, peer], out_ref.at[:, cols(peer * LOCAL + h)], x_send.at[OUT, h, peer], x_recv.at[OUT, h, peer],
                device_id={"dp": dp, "ctx": row * XS + peer}, device_id_type=MESH,
            ).wait_recv()
            for kind in (KS, VS, QS):
                x_copy(kind, h, peer).wait_send()
            qc_copy(0, h, peer).wait_send()
            out_copy(h, peer).wait_send()
        @pl.when(inner)
        def _():
            qc_copy(1, h, x).wait_send()

        for at, kinds in enumerate(((ZK, ZV, ZOC), (ZO2, ZS2, ZO3, ZS3), (ZQ2, ZO3B, ZS3B), (ZQ3, ZQ3B, ZOC))):

            @pl.when(row == at)
            def _():
                for kind in kinds:
                    z_copy(kind, h).wait_send()

    @pl.when(edge)
    def _():
        for kind in range(2):
            far_copy(kind).wait_send()
            for k in (1, 3):
                y_far(kind, k).wait_send()
            y_pass(kind, away).wait_send()
            for home in (side, away):
                for k in range(4):
                    core_pass(kind, home, k).wait_send()
        for k in (1, 3):
            y_own(0, k).wait_send()
        y_pass(0, side).wait_send()

    @pl.when(inner)
    def _():
        for k in (1, 2, 3):
            side_copy(k).wait_send()
            side_pass(k).wait_send()
        idx_copy(pair, x, me).wait_send()

    for k in range(1, XS):
        idx_copy(row, x_at(k), me).wait_send()
    loop(0, LOCAL, finish)


def shards(q_self, k_self, v_self, q_cross, db_keys, db_values, nb_shard, nb_row):
    anywhere = pl.BlockSpec(memory_space=pl.ANY)
    scalars = pl.BlockSpec(memory_space=pltpu.SMEM)
    heads = pltpu.VMEM((LOCAL, XS, TOK, HD), jnp.bfloat16)
    database = pltpu.VMEM((N_DP * DB_DEV, NLEN, WIDE), jnp.bfloat16)
    both = pltpu.VMEM((2, LOCAL, XS, TOK, HD), jnp.bfloat16)
    state = pltpu.VMEM((LOCAL * QB, ROWS, HD), jnp.float32)
    parts = pltpu.VMEM((2, LOCAL, XS, TOK, HD), jnp.bfloat16)
    stats = pltpu.VMEM((2, LOCAL, 8, 128), jnp.float32)
    dma = pltpu.SemaphoreType.DMA
    out = pl.pallas_call(
        kernel,
        out_shape=jax.ShapeDtypeStruct((TOK, HEADS * HD), jnp.bfloat16),
        in_specs=[anywhere] * 6 + [scalars] * 2,
        out_specs=anywhere,
        scratch_shapes=[
            heads, heads, heads, both, heads, heads, heads, heads, database, database,
            pltpu.VMEM((4 * XS, 8, 128), jnp.int32),
            pltpu.SMEM((4 * XS, 8, 128), jnp.int32),
            pltpu.VMEM((LOCAL, XS, TOK, HD), jnp.float32),
            pltpu.VMEM((2, 2 * QB, ROWS, ROWS), jnp.float32),
            state, state, state,
            parts, stats, parts, stats, heads, heads,
            dma((5, LOCAL, XS)), dma((5, LOCAL, XS)), dma((2, LOCAL, XS)), dma((XS,)), dma((4 * XS,)),
            dma((12, LOCAL)), dma((12, LOCAL)),
            dma((2,)), dma((2, 4)), dma((2, 2, 2)), dma((2, 2)), dma((2, 2, 4)), dma((2, N_DP)), dma((5, LOCAL)), dma((2,)), dma,
            pltpu.SemaphoreType.REGULAR,
        ],
        compiler_params=pltpu.CompilerParams(
            collective_id=0, has_side_effects=True, vmem_limit_bytes=60 * 1024 * 1024
        ),
    )(q_self[0], k_self[0], v_self[0], q_cross[0], db_keys, db_values, nb_shard, nb_row)
    return out[None]


def solution(mesh):
    return jax.shard_map(
        shards,
        mesh=mesh,
        in_specs=(
            P("dp", "ctx", None),
            P("dp", "ctx", None),
            P("dp", "ctx", None),
            P("dp", "ctx", None),
            P("dp", None, None),
            P("dp", None, None),
            P("dp", "ctx", None),
            P("dp", "ctx", None),
        ),
        out_specs=P("dp", "ctx", None),
        check_vma=False,
    )
```

```python
import jax
import jax.numpy as jnp
from jax import lax
from jax.experimental import pallas as pl
from jax.experimental.pallas import tpu as pltpu
from jax.sharding import PartitionSpec as P

HEADS = 16
HD = 128
GROUP = 64
NEIGH = 2
NLEN = 128
TOK = 128
DB_DEV = 2
N_DP = 16
HALF = 8
XS = 4
LOCAL = HEADS // XS
WIDE = LOCAL * HD
ROWS = 256
PER = ROWS // TOK
QB = XS // PER
EXPO = HD**-0.5 * 1.4426950408889634
MESH = pl.DeviceIdType.MESH
NT = (((1,), (1,)), ((), ()))
NN = (((1,), (0,)), ((), ()))
QC, KS, VS, QS, OUT = range(5)
ZK, ZV, ZQ2, ZQ3, ZQ3B, ZO2, ZS2, ZO3, ZS3, ZO3B, ZS3B = range(11)


def cols(head):
    return pl.ds(pl.multiple_of(head * HD, HD), HD)


def kernel(
    qs_ref, ks_ref, vs_ref, qc_ref, kd_ref, vd_ref, shard_ref, row_ref, out_ref,
    qs, ks, vs, qc, k0, v0, q2, q3, kd, vd, idx, idx_s, cross, scores, tops, totals, accs,
    part_out, stat_out, part_in, stat_in, mixed, cross_out, kf, vf,
    x_send, x_recv, qc_send, qc_recv, idx_send, idx_recv, back_send, back_recv, z_send, z_recv,
    far_send, far_recv, y_send, core_send, db_recv, own_sem, db_own, number_sem, ready,
):
    dp = lax.axis_index("dp")
    me = lax.axis_index("ctx")
    row = me // XS
    x = lax.rem(me, XS)
    near = lax.rem(dp, HALF)
    side = dp - near
    away = HALF - side
    y = near // 2
    core = lax.rem(near, 2)
    other_core = dp + 1 - 2 * core
    far_dp = away + near
    far_ctx = (3 - row) * XS + x
    edge = (row == 0) | (row == 3)
    first_side = dp < HALF
    inner_ctx = (row // 2 + 1) * XS + x

    def x_at(k):
        return lax.rem(x + k, XS)

    def y_at(home, k):
        return home + lax.rem(near + 2 * k, HALF)

    def loop(first, last, body):
        def step(k, carry):
            body(k)
            return carry

        lax.fori_loop(first, last, step, 0)

    barrier = pltpu.get_barrier_semaphore()

    def greet(dp_of, ctx_of):
        pl.semaphore_signal(barrier, inc=1, device_id={"dp": dp_of, "ctx": ctx_of}, device_id_type=MESH)

    def plane(k):
        return lax.rem(y + k // XS, 4), x_at(lax.rem(k, XS))

    def greet_plane(k):
        to_y, to_x = plane(k)
        greet(side + 2 * to_y + core, row * XS + to_x)

    loop(1, 4 * XS, greet_plane)
    for k in range(1, 4):
        greet(dp, lax.rem(row + k, 4) * XS + x)
    greet(other_core, me)

    @pl.when(edge & first_side)
    def _():
        greet(far_dp, far_ctx)

    lane = lax.broadcasted_iota(jnp.int32, (8, 128), 1)
    tile = jnp.zeros((8, 128), jnp.int32)
    for g in range(TOK // GROUP):
        for n in range(NEIGH):
            block = shard_ref[0, g, n] * DB_DEV + row_ref[0, g, n]
            tile = jnp.where(lane == g * NEIGH + n, block, tile)
    idx[y, x] = tile

    arrays = {KS: (ks_ref, ks), VS: (vs_ref, vs), QS: (qs_ref, qs)}
    blocks = ((kd_ref, kd, kf), (vd_ref, vd, vf))
    wide = pl.ds(pl.multiple_of(x * WIDE, WIDE), WIDE)
    head = x * LOCAL + y

    def own_copy(kind, h):
        arg, buf = arrays[kind]
        return pltpu.make_async_copy(arg.at[:, cols(x * LOCAL + h)], buf.at[h, x], own_sem.at[kind, h])

    def own_qc():
        return pltpu.make_async_copy(qc_ref.at[:, cols(head)], qc.at[y, x], own_sem.at[QC, 0])

    def own_db(kind):
        arg, buf, far = blocks[kind]
        return pltpu.make_async_copy(arg.at[:, :, cols(head)], buf.at[pl.ds(dp * DB_DEV, DB_DEV)], db_own.at[kind])

    def own_far(kind):
        arg, buf, far = blocks[kind]
        return pltpu.make_async_copy(far.at[:, :, cols(y)], buf.at[pl.ds(far_dp * DB_DEV, DB_DEV)], db_own.at[2 + kind])

    def start_own(h):
        for kind in (KS, VS, QS):
            own_copy(kind, h).start()

    loop(0, LOCAL, start_own)
    own_qc().start()
    for kind in range(2):
        own_db(kind).start()

    pl.semaphore_wait(barrier, 19 + jnp.where(edge & (dp >= HALF), 1, 0))

    @pl.when(edge & (dp >= HALF))
    def _():
        pl.semaphore_signal(ready, inc=1, device_id={"dp": far_dp, "ctx": far_ctx}, device_id_type=MESH)

    def far_copy(kind):
        arg, buf, far = blocks[kind]
        return pltpu.make_async_remote_copy(
            arg.at[:, :, wide], far, far_send.at[kind], far_recv.at[kind],
            device_id={"dp": far_dp, "ctx": far_ctx}, device_id_type=MESH,
        )

    def inner_copy(kind):
        far = blocks[kind][2]
        return pltpu.make_async_remote_copy(
            far, far, far_send.at[2 + kind], far_recv.at[kind],
            device_id={"dp": dp, "ctx": inner_ctx}, device_id_type=MESH,
        )

    def shard_copy(kind, shard, src, send, target):
        part = blocks[kind][1].at[pl.ds(shard * DB_DEV, DB_DEV)]
        return pltpu.make_async_remote_copy(
            part if src is None else src, part, send, db_recv.at[kind, shard],
            device_id={"dp": target, "ctx": me}, device_id_type=MESH,
        )

    def y_copy(kind, far, k):
        to_y = lax.rem(y + k, 4)
        src = blocks[kind][2].at[:, :, cols(to_y)] if far else blocks[kind][0].at[:, :, cols(x * LOCAL + to_y)]
        return shard_copy(kind, far_dp if far else dp, src, y_send.at[kind, far, k], y_at(side, k))

    def core_pass(kind, far, k):
        src = None
        if k == 0:
            src = blocks[kind][2].at[:, :, cols(y)] if far else blocks[kind][0].at[:, :, cols(head)]
        return shard_copy(kind, y_at(away if far else side, k), src, core_send.at[kind, far, k], other_core)

    def wait_shard(kind, shard):
        shard_copy(kind, shard, None, far_send.at[kind], other_core).wait_recv()

    def qc_copy(k):
        to_y, to_x = plane(k)
        return pltpu.make_async_remote_copy(
            qc_ref.at[:, cols(to_x * LOCAL + to_y)], qc.at[y, x], qc_send.at[k], qc_recv.at[y, x],
            device_id={"dp": side + 2 * to_y + core, "ctx": row * XS + to_x}, device_id_type=MESH,
        )

    def idx_copy(k):
        to_y, to_x = plane(k)
        return pltpu.make_async_remote_copy(
            idx.at[y, x], idx.at[y, x], idx_send.at[k], idx_recv.at[y, x],
            device_id={"dp": side + 2 * to_y + core, "ctx": row * XS + to_x}, device_id_type=MESH,
        )

    def wait_plane(k):
        from_y, from_x = plane(k)
        for buf, sent, received in ((idx, idx_send, idx_recv), (qc, qc_send, qc_recv)):
            there = buf.at[from_y, from_x]
            pltpu.make_async_remote_copy(
                there, there, sent.at[k], received.at[from_y, from_x],
                device_id={"dp": side + 2 * from_y + core, "ctx": row * XS + from_x}, device_id_type=MESH,
            ).wait_recv()

    def back_copy(k):
        to_y = lax.rem(y + k, 4)
        return pltpu.make_async_remote_copy(
            cross_out.at[to_y], cross.at[y], back_send.at[k], back_recv.at[y],
            device_id={"dp": y_at(side, k), "ctx": me}, device_id_type=MESH,
        )

    def own_back():
        return pltpu.make_async_copy(cross_out.at[y], cross.at[y], own_sem.at[QC, 1])

    def x_copy(kind, h, to):
        arg, buf = arrays[kind]
        return pltpu.make_async_remote_copy(
            arg.at[:, cols(to * LOCAL + h)], buf.at[h, x], x_send.at[kind, h, to], x_recv.at[kind, h, x],
            device_id={"dp": dp, "ctx": row * XS + to}, device_id_type=MESH,
        )

    def arrived(kind, h):
        own_copy(kind, h).wait()
        for k in range(1, XS):
            source = x_at(k)
            buf = arrays[kind][1].at[h, source]
            pltpu.make_async_remote_copy(
                buf, buf, x_send.at[kind, h, source], x_recv.at[kind, h, source],
                device_id={"dp": dp, "ctx": row * XS + source}, device_id_type=MESH,
            ).wait_recv()

    def start_x(kinds):
        def step(h):
            for k in (1, 3, 2):
                for kind in kinds:
                    x_copy(kind, h, x_at(k)).start()

        loop(0, LOCAL, step)

    def start_plane(k):
        idx_copy(k).start()
        qc_copy(k).start()

    @pl.when(edge & (dp >= HALF))
    def _():
        for kind in range(2):
            far_copy(kind).start()

    for kind in range(2):
        for k in (1, 3, 2):
            y_copy(kind, 0, k).start()

    @pl.when(row < 2)
    def _():
        start_x((KS, VS))
        loop(1, 4 * XS, start_plane)
        start_x((QS,))

    @pl.when(row >= 2)
    def _():
        start_x((QS,))
        loop(1, 4 * XS, start_plane)
        start_x((KS, VS))

    for kind in range(2):
        core_pass(kind, 0, 0).start()

    @pl.when(edge & first_side)
    def _():
        pl.semaphore_wait(ready, 1)
        for kind in range(2):
            far_copy(kind).start()

    def z_copy(kind, h):
        src, dst, to = {
            ZK: (ks.at[h], k0.at[h], 1),
            ZV: (vs.at[h], v0.at[h], 1),
            ZQ2: (qs.at[h], q2.at[h], 1),
            ZQ3: (qs.at[h], q3.at[h], 1),
            ZQ3B: (qs.at[h], q3.at[h], 2),
            ZO2: (part_out.at[0, h], part_in.at[0, h], 2),
            ZS2: (stat_out.at[0, h], stat_in.at[0, h], 2),
            ZO3: (part_out.at[1, h], part_in.at[0, h], 3),
            ZS3: (stat_out.at[1, h], stat_in.at[0, h], 3),
            ZO3B: (part_out.at[1, h], part_in.at[1, h], 3),
            ZS3B: (stat_out.at[1, h], stat_in.at[1, h], 3),
        }[kind]
        return pltpu.make_async_remote_copy(
            src, dst, z_send.at[kind, h], z_recv.at[kind, h],
            device_id={"dp": dp, "ctx": to * XS + x}, device_id_type=MESH,
        )

    def relay(h):
        @pl.when(row == 0)
        def _():
            arrived(KS, h)
            z_copy(ZK, h).start()
            arrived(VS, h)
            z_copy(ZV, h).start()

        @pl.when(row == 2)
        def _():
            arrived(QS, h)
            z_copy(ZQ2, h).start()

        @pl.when(row == 3)
        def _():
            arrived(QS, h)
            z_copy(ZQ3, h).start()

    def far_stage():
        for kind in range(2):
            far_copy(kind).wait_recv()

            @pl.when(edge)
            def _():
                inner_copy(kind).start()

            for k in (1, 3, 2):
                y_copy(kind, 1, k).start()
            core_pass(kind, 1, 0).start()
            own_far(kind).start()

    def core_stage():
        for far in range(2):
            for kind in range(2):
                for k in (1, 3, 2):
                    wait_shard(kind, y_at(away if far else side, k))
                    core_pass(kind, far, k).start()

    diagonal = lax.broadcasted_iota(jnp.int32, (ROWS, ROWS), 0) >= lax.broadcasted_iota(jnp.int32, (ROWS, ROWS), 1)
    eye = lax.broadcasted_iota(jnp.int32, (TOK, TOK), 0) == lax.broadcasted_iota(jnp.int32, (TOK, TOK), 1)

    def attend(queries, h, b, chunks, slot):
        q = queries[h, pl.ds(b * PER, PER)].reshape(ROWS, HD)
        peak = None
        for j, (keys, values, c, masked) in enumerate(chunks):
            k = keys[h, pl.ds(c * PER, PER)].reshape(ROWS, HD)
            s = lax.dot_general(q, k, NT, preferred_element_type=jnp.float32)
            if masked:
                s = jnp.where(diagonal, s, -1e30)
            scores[slot, j] = s
            folded = jnp.maximum(s[:, :HD], s[:, HD:])
            peak = folded if peak is None else jnp.maximum(peak, folded)
        top = jnp.max(peak, axis=1, keepdims=True)
        total = jnp.zeros((ROWS, HD), jnp.float32)
        acc = jnp.zeros((ROWS, HD), jnp.float32)
        for j, (keys, values, c, masked) in enumerate(chunks):
            w = jnp.exp2((scores[slot, j] - top) * EXPO)
            total = total + (w[:, :HD] + w[:, HD:])
            v = values[h, pl.ds(c * PER, PER)].reshape(ROWS, HD)
            acc = acc + lax.dot_general(w.astype(jnp.bfloat16), v, NN, preferred_element_type=jnp.float32)
        return top, jnp.sum(total, axis=1, keepdims=True), acc

    def partial(queries, h, chunks, place):
        for b in range(QB):
            top, total, acc = attend(queries, h, b, chunks, b)
            part_out[place, h, pl.ds(b * PER, PER)] = (acc / total).astype(jnp.bfloat16).reshape(PER, TOK, HD)
            for p in range(PER):
                rows = slice(p * TOK, (p + 1) * TOK)
                at = b * PER + p
                stat_out[place, h, at : at + 1] = jnp.sum(jnp.where(eye, top[rows], 0.0), axis=0, keepdims=True)
                stat_out[place, h, XS + at : XS + at + 1] = jnp.sum(jnp.where(eye, total[rows], 0.0), axis=0, keepdims=True)

    def own_rows(h, extra, final):
        for b in range(QB):
            chunks = extra + [(ks, vs, c, c == b) for c in range(b + 1)]
            top, total, acc = attend(qs, h, b, chunks, b)
            at = h * QB + b
            if final:
                accs[at] = acc / total
            else:
                accs[at] = acc
                tops[at] = jnp.broadcast_to(top, (ROWS, HD))
                totals[at] = jnp.broadcast_to(total, (ROWS, HD))

    whole_own = [(ks, vs, c, False) for c in range(QB)]
    whole_first = [(k0, v0, c, False) for c in range(QB)]

    def between(h):
        @pl.when(row == 1)
        def _():
            arrived(KS, h)
            arrived(VS, h)
            z_copy(ZK, h).wait_recv()
            z_copy(ZV, h).wait_recv()
            z_copy(ZQ2, h).wait_recv()
            partial(q2, h, whole_first + whole_own, 0)
            z_copy(ZO2, h).start()
            z_copy(ZS2, h).start()
            z_copy(ZQ3, h).wait_recv()
            partial(q3, h, whole_first + whole_own, 1)
            z_copy(ZO3, h).start()
            z_copy(ZS3, h).start()
            arrived(QS, h)
            own_rows(h, whole_first, True)

        @pl.when(row == 2)
        def _():
            arrived(KS, h)
            arrived(VS, h)
            z_copy(ZQ3B, h).wait_recv()
            partial(q3, h, whole_own, 1)
            z_copy(ZO3B, h).start()
            z_copy(ZS3B, h).start()

    def own_others(h):
        @pl.when(row == 0)
        def _():
            arrived(QS, h)
            own_rows(h, [], True)

        @pl.when(row == 2)
        def _():
            own_rows(h, [], False)

        @pl.when(row == 3)
        def _():
            arrived(KS, h)
            arrived(VS, h)
            own_rows(h, [], False)

    def cross_document(k):
        doc = lax.rem(y + k, 4)
        for t in range(XS):
            for g in range(TOK // GROUP):
                first = idx_s[doc, t, 0, g * NEIGH]
                second = idx_s[doc, t, 0, g * NEIGH + 1]
                rows = pl.ds(g * GROUP, GROUP)
                keys = jnp.concatenate([kd[first], kd[second]], axis=0)
                values = jnp.concatenate([vd[first], vd[second]], axis=0)
                s = lax.dot_general(qc[doc, t, rows, :], keys, NT, preferred_element_type=jnp.float32)
                top = jnp.max(s, axis=1, keepdims=True)
                w = jnp.exp2((s - top) * EXPO)
                total = jnp.sum(w, axis=1, keepdims=True)
                o = lax.dot_general(w.astype(jnp.bfloat16), values, NN, preferred_element_type=jnp.float32)
                cross_out[doc, t, rows, :] = (o / total).astype(jnp.bfloat16)

        @pl.when(k > 0)
        def _():
            back_copy(k).start()

        @pl.when(k == 0)
        def _():
            own_back().start()

    def cross_stage():
        own_qc().wait()
        for kind in range(2):
            own_db(kind).wait()
            own_far(kind).wait()
        loop(1, 4 * XS, wait_plane)
        numbers = pltpu.make_async_copy(idx, idx_s, number_sem)
        numbers.start()
        numbers.wait()

        def wait_other_core(k):
            for kind in range(2):
                wait_shard(kind, 2 * k + 1 - core)

        loop(0, HALF, wait_other_core)
        loop(0, 4, lambda k: cross_document(3 - k))

    @pl.when(row == 0)
    def _():
        relay(0)
        relay(1)
        far_stage()
        relay(2)
        relay(3)

    @pl.when(row >= 2)
    def _():
        loop(0, LOCAL, relay)
        far_stage()

        @pl.when(row == 3)
        def _():
            loop(0, LOCAL, lambda h: z_copy(ZQ3B, h).start())

    @pl.when(row != 1)
    def _():
        core_stage()

    def between_step(h):
        between(h)
        for at, stage in enumerate((far_stage, core_stage, cross_stage)):
            pl.when((row == 1) & (h == at))(stage)

    loop(0, LOCAL, between_step)

    @pl.when(row != 1)
    def _():
        loop(0, LOCAL, own_others)
        cross_stage()

    def merge(h, parts):
        for b in range(QB):
            at = h * QB + b
            for p in range(PER):
                rows = slice(p * TOK, (p + 1) * TOK)
                sub = b * PER + p
                top = tops[at, rows, :1]
                others = []
                for place in range(parts):
                    column = [
                        jnp.sum(jnp.where(eye, stat_in[place, h, n : n + 1], 0.0), axis=1, keepdims=True)
                        for n in (sub, XS + sub)
                    ]
                    others.append(column)
                peak = top
                for other_top, _ in others:
                    peak = jnp.maximum(peak, other_top)
                keep = jnp.exp2((top - peak) * EXPO)
                total = totals[at, rows, :1] * keep
                acc = accs[at, rows, :] * keep
                for place, (other_top, other_total) in enumerate(others):
                    w = jnp.exp2((other_top - peak) * EXPO) * other_total
                    total = total + w
                    acc = acc + part_in[place, h, sub].astype(jnp.float32) * w
                accs[at, rows, :] = acc / total

    def out_copy(h, t):
        return pltpu.make_async_remote_copy(
            mixed.at[h, t], out_ref.at[:, cols(x * LOCAL + h)], x_send.at[OUT, h, t], x_recv.at[OUT, h, x],
            device_id={"dp": dp, "ctx": row * XS + t}, device_id_type=MESH,
        )

    def own_out(h):
        return pltpu.make_async_copy(mixed.at[h, x], out_ref.at[:, cols(x * LOCAL + h)], own_sem.at[OUT, h])

    def emit(h):
        @pl.when(row == 2)
        def _():
            z_copy(ZO2, h).wait_recv()
            z_copy(ZS2, h).wait_recv()
            merge(h, 1)

        @pl.when(row == 3)
        def _():
            z_copy(ZO3, h).wait_recv()
            z_copy(ZS3, h).wait_recv()
            z_copy(ZO3B, h).wait_recv()
            z_copy(ZS3B, h).wait_recv()
            merge(h, 2)

        @pl.when(h != y)
        def _():
            there = cross.at[h]
            pltpu.make_async_remote_copy(
                there, there, back_send.at[0], back_recv.at[h], device_id={"dp": side + 2 * h + core, "ctx": me}, device_id_type=MESH
            ).wait_recv()

        @pl.when(h == y)
        def _():
            own_back().wait()

        self_out = accs[pl.ds(h * QB, QB)].astype(jnp.bfloat16).astype(jnp.float32).reshape(XS, TOK, HD)
        mixed[h] = (self_out + cross[h].astype(jnp.float32)).astype(jnp.bfloat16)
        for k in (1, 3, 2):
            out_copy(h, x_at(k)).start()
        own_out(h).start()

    loop(0, LOCAL, emit)

    def finish(h):
        own_out(h).wait()
        for k in range(1, XS):
            peer = x_at(k)
            pltpu.make_async_remote_copy(
                mixed.at[h, peer], out_ref.at[:, cols(peer * LOCAL + h)], x_send.at[OUT, h, peer], x_recv.at[OUT, h, peer],
                device_id={"dp": dp, "ctx": row * XS + peer}, device_id_type=MESH,
            ).wait_recv()
            for kind in (KS, VS, QS):
                x_copy(kind, h, peer).wait_send()
            out_copy(h, peer).wait_send()
        for at, kinds in enumerate(((ZK, ZV), (ZO2, ZS2, ZO3, ZS3), (ZQ2, ZO3B, ZS3B), (ZQ3, ZQ3B))):

            @pl.when(row == at)
            def _():
                for kind in kinds:
                    z_copy(kind, h).wait_send()

    @pl.when(edge)
    def _():
        for kind in range(2):
            far_copy(kind).wait_send()
            inner_copy(kind).wait_send()

    for kind in range(2):
        for far in range(2):
            for k in range(1, 4):
                y_copy(kind, far, k).wait_send()
            for k in range(4):
                core_pass(kind, far, k).wait_send()

    def finish_plane(k):
        idx_copy(k).wait_send()
        qc_copy(k).wait_send()

    loop(1, 4 * XS, finish_plane)
    for k in range(1, 4):
        back_copy(k).wait_send()
    loop(0, LOCAL, finish)


def shards(q_self, k_self, v_self, q_cross, db_keys, db_values, nb_shard, nb_row):
    anywhere = pl.BlockSpec(memory_space=pl.ANY)
    scalars = pl.BlockSpec(memory_space=pltpu.SMEM)
    heads = pltpu.VMEM((LOCAL, XS, TOK, HD), jnp.bfloat16)
    database = pltpu.VMEM((N_DP * DB_DEV, NLEN, HD), jnp.bfloat16)
    shard = pltpu.VMEM((DB_DEV, NLEN, WIDE), jnp.bfloat16)
    state = pltpu.VMEM((LOCAL * QB, ROWS, HD), jnp.float32)
    parts = pltpu.VMEM((2, LOCAL, XS, TOK, HD), jnp.bfloat16)
    stats = pltpu.VMEM((2, LOCAL, 8, 128), jnp.float32)
    dma = pltpu.SemaphoreType.DMA
    out = pl.pallas_call(
        kernel,
        out_shape=jax.ShapeDtypeStruct((TOK, HEADS * HD), jnp.bfloat16),
        in_specs=[anywhere] * 6 + [scalars] * 2,
        out_specs=anywhere,
        scratch_shapes=[
            heads, heads, heads, heads, heads, heads, heads, heads, database, database,
            pltpu.VMEM((4, XS, 8, 128), jnp.int32),
            pltpu.SMEM((4, XS, 8, 128), jnp.int32),
            heads,
            pltpu.VMEM((2, 2 * QB, ROWS, ROWS), jnp.float32),
            state, state, state,
            parts, stats, parts, stats, heads, heads, shard, shard,
            dma((5, LOCAL, XS)), dma((5, LOCAL, XS)), dma((4 * XS,)), dma((4, XS)), dma((4 * XS,)), dma((4, XS)),
            dma((4,)), dma((4,)), dma((11, LOCAL)), dma((11, LOCAL)),
            dma((4,)), dma((2,)), dma((2, 2, 4)), dma((2, 2, 4)), dma((2, N_DP)), dma((5, LOCAL)), dma((4,)), dma,
            pltpu.SemaphoreType.REGULAR,
        ],
        compiler_params=pltpu.CompilerParams(
            collective_id=0, has_side_effects=True, vmem_limit_bytes=60 * 1024 * 1024
        ),
    )(q_self[0], k_self[0], v_self[0], q_cross[0], db_keys, db_values, nb_shard, nb_row)
    return out[None]


def solution(mesh):
    return jax.shard_map(
        shards,
        mesh=mesh,
        in_specs=(
            P("dp", "ctx", None),
            P("dp", "ctx", None),
            P("dp", "ctx", None),
            P("dp", "ctx", None),
            P("dp", None, None),
            P("dp", None, None),
            P("dp", "ctx", None),
            P("dp", "ctx", None),
        ),
        out_specs=P("dp", "ctx", None),
        check_vma=False,
    )
```

```python
import jax
import jax.numpy as jnp
from jax import lax
from jax.experimental import pallas as pl
from jax.experimental.pallas import tpu as pltpu
from jax.sharding import PartitionSpec as P

HEADS = 16
HD = 128
GROUP = 64
NEIGH = 2
NLEN = 128
TOK = 128
DB_DEV = 2
N_DP = 16
HALF = 8
XS = 4
LOCAL = HEADS // XS
WIDE = LOCAL * HD
PART = 2 * HD
ROWS = 256
PER = ROWS // TOK
QB = XS // PER
EXPO = HD**-0.5 * 1.4426950408889634
MESH = pl.DeviceIdType.MESH
NT = (((1,), (1,)), ((), ()))
NN = (((1,), (0,)), ((), ()))
QC, KS, VS, QS = range(4)
ZK, ZV, ZQ2, ZQ3, ZQ3B, ZO2, ZS2, ZO3, ZS3, ZO3B, ZS3B = range(11)


def cols(head):
    return pl.ds(pl.multiple_of(head * HD, HD), HD)


def kernel(
    qs_ref, ks_ref, vs_ref, qc_ref, kd_ref, vd_ref, shard_ref, row_ref, out_ref,
    qs, ks, vs, qc, k0, v0, q2, q3, kd, vd, idx, idx_s, cross, scores, tops, totals, accs,
    part_out, stat_out, part_in, stat_in, mixed, cross_out, kf, vf, qx, transit,
    x_send, x_recv, transit_recv, out_send, out_recv, own_out_sem, qc_send, qc_recv, idx_send, idx_recv, back_send, back_recv, z_send, z_recv,
    far_send, far_recv, y_send, core_send, db_recv, own_sem, db_own, number_sem, ready,
):
    dp = lax.axis_index("dp")
    me = lax.axis_index("ctx")
    row = me // XS
    x = lax.rem(me, XS)
    near = lax.rem(dp, HALF)
    side = dp - near
    away = HALF - side
    y = near // 2
    core = lax.rem(near, 2)
    other_core = dp + 1 - 2 * core
    far_dp = away + near
    far_ctx = (3 - row) * XS + x
    edge = (row == 0) | (row == 3)
    first_side = dp < HALF
    inner_ctx = jnp.where(row == 3, 2, 1) * XS + x

    def x_at(k):
        return lax.rem(x + k, XS)

    def y_at(home, k):
        return home + lax.rem(near + 2 * k, HALF)

    def loop(first, last, body):
        def step(k, carry):
            body(k)
            return carry

        lax.fori_loop(first, last, step, 0)

    barrier = pltpu.get_barrier_semaphore()

    def greet(dp_of, ctx_of):
        pl.semaphore_signal(barrier, inc=1, device_id={"dp": dp_of, "ctx": ctx_of}, device_id_type=MESH)

    for k in range(1, 4):
        greet(dp, row * XS + x_at(k))
        greet(y_at(side, k), me)
        greet(dp, lax.rem(row + k, 4) * XS + x)
    greet(other_core, me)

    @pl.when(edge & first_side)
    def _():
        greet(far_dp, far_ctx)

    lane = lax.broadcasted_iota(jnp.int32, (8, 128), 1)
    tile = jnp.zeros((8, 128), jnp.int32)
    for g in range(TOK // GROUP):
        for n in range(NEIGH):
            block = shard_ref[0, g, n] * DB_DEV + row_ref[0, g, n]
            tile = jnp.where(lane == g * NEIGH + n, block, tile)
    idx[y, x] = tile

    arrays = {QC: (qc_ref, qx), KS: (ks_ref, ks), VS: (vs_ref, vs), QS: (qs_ref, qs)}
    blocks = ((kd_ref, kd, kf), (vd_ref, vd, vf))
    wide = pl.ds(pl.multiple_of(x * WIDE, WIDE), WIDE)
    head = x * LOCAL + y

    def own_copy(kind):
        arg, buf = arrays[kind]
        return pltpu.make_async_copy(arg.at[:, wide], buf.at[x], own_sem.at[kind])

    def own_db(kind):
        arg, buf, far = blocks[kind]
        return pltpu.make_async_copy(arg.at[:, :, cols(head)], buf.at[pl.ds(dp * DB_DEV, DB_DEV)], db_own.at[kind])

    def own_far(kind):
        arg, buf, far = blocks[kind]
        return pltpu.make_async_copy(far.at[:, :, cols(y)], buf.at[pl.ds(far_dp * DB_DEV, DB_DEV)], db_own.at[2 + kind])

    for kind in (KS, VS, QS, QC):
        own_copy(kind).start()
    for kind in range(2):
        own_db(kind).start()

    pl.semaphore_wait(barrier, 10 + jnp.where(edge & (dp >= HALF), 1, 0))

    @pl.when(edge & (dp >= HALF))
    def _():
        pl.semaphore_signal(ready, inc=1, device_id={"dp": far_dp, "ctx": far_ctx}, device_id_type=MESH)

    def far_copy(kind):
        arg, buf, far = blocks[kind]
        return pltpu.make_async_remote_copy(
            arg.at[:, :, wide], far, far_send.at[kind], far_recv.at[kind],
            device_id={"dp": far_dp, "ctx": far_ctx}, device_id_type=MESH,
        )

    def inner_copy(kind):
        far = blocks[kind][2]
        return pltpu.make_async_remote_copy(
            far, far, far_send.at[2 + kind], far_recv.at[kind],
            device_id={"dp": dp, "ctx": inner_ctx}, device_id_type=MESH,
        )

    def shard_copy(kind, shard, src, send, target):
        part = blocks[kind][1].at[pl.ds(shard * DB_DEV, DB_DEV)]
        return pltpu.make_async_remote_copy(
            part if src is None else src, part, send, db_recv.at[kind, shard],
            device_id={"dp": target, "ctx": me}, device_id_type=MESH,
        )

    def y_copy(kind, far, k):
        to_y = lax.rem(y + k, 4)
        src = blocks[kind][2].at[:, :, cols(to_y)] if far else blocks[kind][0].at[:, :, cols(x * LOCAL + to_y)]
        return shard_copy(kind, far_dp if far else dp, src, y_send.at[kind, far, k], y_at(side, k))

    def core_pass(kind, far, k):
        src = None
        if k == 0:
            src = blocks[kind][2].at[:, :, cols(y)] if far else blocks[kind][0].at[:, :, cols(head)]
        return shard_copy(kind, y_at(away if far else side, k), src, core_send.at[kind, far, k], other_core)

    def wait_shard(kind, shard):
        shard_copy(kind, shard, None, far_send.at[kind], other_core).wait_recv()

    def half(to, p):
        return pl.ds(pl.multiple_of(to * WIDE + p * PART, PART), PART)

    def x_copy(kind, p, k):
        arg, buf = arrays[kind]
        to = x_at(k)
        return pltpu.make_async_remote_copy(
            arg.at[:, half(to, p)], buf.at[x, :, pl.ds(p * PART, PART)], x_send.at[kind, p, k], x_recv.at[kind, p, x],
            device_id={"dp": dp, "ctx": row * XS + to}, device_id_type=MESH,
        )

    def via(p):
        return 1 if p == 0 else 3

    def two_copy(kind, p):
        there = transit.at[kind, :, pl.ds(p * PART, PART)]
        return pltpu.make_async_remote_copy(
            arrays[kind][0].at[:, half(x_at(2), p)], there, x_send.at[kind, p, 2], transit_recv.at[kind, p],
            device_id={"dp": dp, "ctx": row * XS + x_at(via(p))}, device_id_type=MESH,
        )

    def pass_copy(kind, p):
        origin = x_at(4 - via(p))
        return pltpu.make_async_remote_copy(
            transit.at[kind, :, pl.ds(p * PART, PART)], arrays[kind][1].at[origin, :, pl.ds(p * PART, PART)],
            x_send.at[kind, p, 0], x_recv.at[kind, p, origin],
            device_id={"dp": dp, "ctx": row * XS + x_at(via(p))}, device_id_type=MESH,
        )

    def pass_on(kinds, p):
        for kind in kinds:
            two_copy(kind, p).wait_recv()
            pass_copy(kind, p).start()

    def arrived(kind, p):
        if p == 0:
            own_copy(kind).wait()
        for k in range(1, XS):
            source = x_at(k)
            buf = arrays[kind][1].at[source, :, pl.ds(p * PART, PART)]
            pltpu.make_async_remote_copy(
                buf, buf, x_send.at[kind, p, k], x_recv.at[kind, p, source],
                device_id={"dp": dp, "ctx": row * XS + source}, device_id_type=MESH,
            ).wait_recv()

    def start_x(kinds):
        for p in range(2):
            for kind in kinds:
                two_copy(kind, p).start()
                for k in (1, 3):
                    x_copy(kind, p, k).start()

    def qc_copy(k):
        to_y = lax.rem(y + k, 4)
        return pltpu.make_async_remote_copy(
            qx.at[:, :, cols(to_y)], qc.at[y], qc_send.at[k], qc_recv.at[y],
            device_id={"dp": y_at(side, k), "ctx": me}, device_id_type=MESH,
        )

    def own_qc():
        return pltpu.make_async_copy(qx.at[:, :, cols(y)], qc.at[y], own_sem.at[QC])

    def idx_x(k):
        return pltpu.make_async_remote_copy(
            idx.at[y, x], idx.at[y, x], idx_send.at[0, k], idx_recv.at[0, x],
            device_id={"dp": dp, "ctx": row * XS + x_at(k)}, device_id_type=MESH,
        )

    def idx_y(k):
        return pltpu.make_async_remote_copy(
            idx.at[y], idx.at[y], idx_send.at[1, k], idx_recv.at[1, y],
            device_id={"dp": y_at(side, k), "ctx": me}, device_id_type=MESH,
        )

    def from_y(k):
        source = lax.rem(y + k, 4)
        for buf, sent, received in ((idx, idx_send.at[1, k], idx_recv.at[1, source]), (qc, qc_send.at[k], qc_recv.at[source])):
            there = buf.at[source]
            pltpu.make_async_remote_copy(
                there, there, sent, received, device_id={"dp": y_at(side, k), "ctx": me}, device_id_type=MESH
            ).wait_recv()

    def qc_stage():
        for p in range(2):
            pass_on((QC,), p)
        for k in range(1, 4):
            source = x_at(k)
            there = idx.at[y, source]
            pltpu.make_async_remote_copy(
                there, there, idx_send.at[0, k], idx_recv.at[0, source],
                device_id={"dp": dp, "ctx": row * XS + source}, device_id_type=MESH,
            ).wait_recv()
        for p in range(2):
            arrived(QC, p)
        for k in (1, 3, 2):
            idx_y(k).start()
            qc_copy(k).start()
        own_qc().start()

    def back_copy(k):
        to_y = lax.rem(y + k, 4)
        return pltpu.make_async_remote_copy(
            cross_out.at[to_y], cross.at[y], back_send.at[k], back_recv.at[y],
            device_id={"dp": y_at(side, k), "ctx": me}, device_id_type=MESH,
        )

    def own_back():
        return pltpu.make_async_copy(cross_out.at[y], cross.at[y], own_sem.at[4])

    @pl.when(edge & (dp >= HALF))
    def _():
        for kind in range(2):
            far_copy(kind).start()

    for kind in range(2):
        for k in (1, 3, 2):
            y_copy(kind, 0, k).start()

    @pl.when(row < 2)
    def _():
        start_x((KS, VS))
        start_x((QS,))

    @pl.when(row >= 2)
    def _():
        start_x((QS,))
        start_x((KS, VS))

    for k in range(1, 4):
        idx_x(k).start()
    start_x((QC,))
    for kind in range(2):
        core_pass(kind, 0, 0).start()

    @pl.when(edge & first_side)
    def _():
        pl.semaphore_wait(ready, 1)
        for kind in range(2):
            far_copy(kind).start()

    def z_copy(kind, h):
        src, dst, to = {
            ZK: (ks.at[:, :, cols(h)], k0.at[h], 1),
            ZV: (vs.at[:, :, cols(h)], v0.at[h], 1),
            ZQ2: (qs.at[:, :, cols(h)], q2.at[h], 1),
            ZQ3: (q3.at[h], q3.at[h], 1),
            ZQ3B: (qs.at[:, :, cols(h)], q3.at[h], 2),
            ZO2: (part_out.at[0, h], part_in.at[0, h], 2),
            ZS2: (stat_out.at[0, h], stat_in.at[0, h], 2),
            ZO3: (part_out.at[1, h], part_in.at[0, h], 3),
            ZS3: (stat_out.at[1, h], stat_in.at[0, h], 3),
            ZO3B: (part_out.at[1, h], part_in.at[1, h], 3),
            ZS3B: (stat_out.at[1, h], stat_in.at[1, h], 3),
        }[kind]
        return pltpu.make_async_remote_copy(
            src, dst, z_send.at[kind, h], z_recv.at[kind, h],
            device_id={"dp": dp, "ctx": to * XS + x}, device_id_type=MESH,
        )

    def relay(kinds, h):
        for kind in kinds:
            z_copy(kind, h).start()

    def relay_third(h):
        z_copy(ZQ3B, h).wait_recv()
        z_copy(ZQ3, h).start()

    def far_stage():
        for kind in range(2):
            far_copy(kind).wait_recv()

            @pl.when(edge if kind == 0 else row >= 2)
            def _():
                inner_copy(kind).start()

            for k in (1, 3, 2):
                y_copy(kind, 1, k).start()
            core_pass(kind, 1, 0).start()
            own_far(kind).start()

    def core_stage():
        for far in range(2):
            for kind in range(2):
                for k in (1, 3, 2):
                    wait_shard(kind, y_at(away if far else side, k))
                    core_pass(kind, far, k).start()

    diagonal = lax.broadcasted_iota(jnp.int32, (ROWS, ROWS), 0) >= lax.broadcasted_iota(jnp.int32, (ROWS, ROWS), 1)
    eye = lax.broadcasted_iota(jnp.int32, (TOK, TOK), 0) == lax.broadcasted_iota(jnp.int32, (TOK, TOK), 1)

    def by_head(buf):
        return lambda h, b: buf[h, pl.ds(b * PER, PER)]

    def by_source(buf):
        return lambda h, b: buf[pl.ds(b * PER, PER), :, cols(h)]

    own_q, own_k, own_v = by_source(qs), by_source(ks), by_source(vs)

    def attend(queries, h, b, chunks, slot):
        q = queries(h, b).reshape(ROWS, HD)
        peak = None
        for j, (keys, values, c, masked) in enumerate(chunks):
            k = keys(h, c).reshape(ROWS, HD)
            s = lax.dot_general(q, k, NT, preferred_element_type=jnp.float32)
            if masked:
                s = jnp.where(diagonal, s, -1e30)
            scores[slot, j] = s
            folded = jnp.maximum(s[:, :HD], s[:, HD:])
            peak = folded if peak is None else jnp.maximum(peak, folded)
        top = jnp.max(peak, axis=1, keepdims=True)
        total = jnp.zeros((ROWS, HD), jnp.float32)
        acc = jnp.zeros((ROWS, HD), jnp.float32)
        for j, (keys, values, c, masked) in enumerate(chunks):
            w = jnp.exp2((scores[slot, j] - top) * EXPO)
            total = total + (w[:, :HD] + w[:, HD:])
            v = values(h, c).reshape(ROWS, HD)
            acc = acc + lax.dot_general(w.astype(jnp.bfloat16), v, NN, preferred_element_type=jnp.float32)
        return top, jnp.sum(total, axis=1, keepdims=True), acc

    def partial(queries, h, chunks, place):
        for b in range(QB):
            top, total, acc = attend(queries, h, b, chunks, b)
            part_out[place, h, pl.ds(b * PER, PER)] = (acc / total).astype(jnp.bfloat16).reshape(PER, TOK, HD)
            for p in range(PER):
                rows = slice(p * TOK, (p + 1) * TOK)
                at = b * PER + p
                stat_out[place, h, at : at + 1] = jnp.sum(jnp.where(eye, top[rows], 0.0), axis=0, keepdims=True)
                stat_out[place, h, XS + at : XS + at + 1] = jnp.sum(jnp.where(eye, total[rows], 0.0), axis=0, keepdims=True)

    def own_rows(h, extra, final):
        for b in range(QB):
            chunks = extra + [(own_k, own_v, c, c == b) for c in range(b + 1)]
            top, total, acc = attend(own_q, h, b, chunks, b)
            at = h * QB + b
            if final:
                accs[at] = acc / total
            else:
                accs[at] = acc
                tops[at] = jnp.broadcast_to(top, (ROWS, HD))
                totals[at] = jnp.broadcast_to(total, (ROWS, HD))

    whole_own = [(own_k, own_v, c, False) for c in range(QB)]
    whole_first = [(by_head(k0), by_head(v0), c, False) for c in range(QB)]

    def between(h):
        @pl.when(row == 1)
        def _():
            z_copy(ZK, h).wait_recv()
            z_copy(ZV, h).wait_recv()
            z_copy(ZQ2, h).wait_recv()
            partial(by_head(q2), h, whole_first + whole_own, 0)
            z_copy(ZO2, h).start()
            z_copy(ZS2, h).start()
            z_copy(ZQ3, h).wait_recv()
            partial(by_head(q3), h, whole_first + whole_own, 1)
            z_copy(ZO3, h).start()
            z_copy(ZS3, h).start()
            own_rows(h, whole_first, True)

        @pl.when(row == 2)
        def _():
            partial(by_head(q3), h, whole_own, 1)
            z_copy(ZO3B, h).start()
            z_copy(ZS3B, h).start()

    def own_others(h):
        @pl.when(row == 0)
        def _():
            own_rows(h, [], True)

        @pl.when(row >= 2)
        def _():
            own_rows(h, [], False)

    def cross_document(k):
        doc = lax.rem(y + k, 4)
        for t in range(XS):
            for g in range(TOK // GROUP):
                first = idx_s[doc, t, 0, g * NEIGH]
                second = idx_s[doc, t, 0, g * NEIGH + 1]
                rows = pl.ds(g * GROUP, GROUP)
                keys = jnp.concatenate([kd[first], kd[second]], axis=0)
                values = jnp.concatenate([vd[first], vd[second]], axis=0)
                s = lax.dot_general(qc[doc, t, rows, :], keys, NT, preferred_element_type=jnp.float32)
                top = jnp.max(s, axis=1, keepdims=True)
                w = jnp.exp2((s - top) * EXPO)
                total = jnp.sum(w, axis=1, keepdims=True)
                o = lax.dot_general(w.astype(jnp.bfloat16), values, NN, preferred_element_type=jnp.float32)
                cross_out[doc, t, rows, :] = (o / total).astype(jnp.bfloat16)

        @pl.when(k > 0)
        def _():
            back_copy(k).start()

        @pl.when(k == 0)
        def _():
            own_back().start()

    def cross_stage():
        own_qc().wait()
        for kind in range(2):
            own_db(kind).wait()
            own_far(kind).wait()
        for k in range(1, 4):
            from_y(k)
        numbers = pltpu.make_async_copy(idx, idx_s, number_sem)
        numbers.start()
        numbers.wait()

        def wait_other_core(k):
            for kind in range(2):
                wait_shard(kind, 2 * k + 1 - core)

        loop(0, HALF, wait_other_core)
        loop(0, 4, lambda k: cross_document(3 - k))

    def take(kinds):
        for p in range(2):
            for kind in kinds:
                arrived(kind, p)

    @pl.when(row == 0)
    def _():
        for p in range(2):
            pass_on((KS, VS), p)
            arrived(KS, p)
            arrived(VS, p)
            loop(2 * p, 2 * p + 2, lambda h: relay((ZK, ZV), h))
        far_stage()
        for p in range(2):
            pass_on((QS,), p)
        qc_stage()
        core_stage()
        take((QS,))

    @pl.when(row == 1)
    def _():
        for p in range(2):
            pass_on((KS, VS), p)
        for p in range(2):
            pass_on((QS,), p)
        take((KS, VS, QS))

    @pl.when(row == 2)
    def _():
        for p in range(2):
            pass_on((QS,), p)
            arrived(QS, p)
            loop(2 * p, 2 * p + 2, lambda h: relay((ZQ2,), h))
        loop(0, 2, relay_third)
        for p in range(2):
            pass_on((KS, VS), p)
        loop(2, 4, relay_third)
        far_stage()
        qc_stage()
        core_stage()
        take((KS, VS))

    @pl.when(row == 3)
    def _():
        for p in range(2):
            pass_on((QS,), p)
            arrived(QS, p)
            loop(2 * p, 2 * p + 2, lambda h: relay((ZQ3B,), h))
        far_stage()
        for p in range(2):
            pass_on((KS, VS), p)
        qc_stage()
        core_stage()
        take((KS, VS))

    def between_step(h):
        between(h)

        @pl.when((row == 1) & (h == 0))
        def _():
            qc_stage()
            far_stage()

        pl.when((row == 1) & (h == 1))(core_stage)
        pl.when((row == 1) & (h == 2))(cross_stage)

    loop(0, LOCAL, between_step)

    @pl.when(row != 1)
    def _():
        loop(0, LOCAL, own_others)
        cross_stage()

    def merge(h, parts):
        for b in range(QB):
            at = h * QB + b
            for p in range(PER):
                rows = slice(p * TOK, (p + 1) * TOK)
                sub = b * PER + p
                top = tops[at, rows, :1]
                others = []
                for place in range(parts):
                    column = [
                        jnp.sum(jnp.where(eye, stat_in[place, h, n : n + 1], 0.0), axis=1, keepdims=True)
                        for n in (sub, XS + sub)
                    ]
                    others.append(column)
                peak = top
                for other_top, _ in others:
                    peak = jnp.maximum(peak, other_top)
                keep = jnp.exp2((top - peak) * EXPO)
                total = totals[at, rows, :1] * keep
                acc = accs[at, rows, :] * keep
                for place, (other_top, other_total) in enumerate(others):
                    w = jnp.exp2((other_top - peak) * EXPO) * other_total
                    total = total + w
                    acc = acc + part_in[place, h, sub].astype(jnp.float32) * w
                accs[at, rows, :] = acc / total

    def out_copy(h, t):
        return pltpu.make_async_remote_copy(
            mixed.at[h, t], out_ref.at[:, cols(x * LOCAL + h)], out_send.at[h, t], out_recv.at[h, x],
            device_id={"dp": dp, "ctx": row * XS + t}, device_id_type=MESH,
        )

    def own_out(h):
        return pltpu.make_async_copy(mixed.at[h, x], out_ref.at[:, cols(x * LOCAL + h)], own_out_sem.at[h])

    def emit(h):
        @pl.when(row == 2)
        def _():
            z_copy(ZO2, h).wait_recv()
            z_copy(ZS2, h).wait_recv()
            merge(h, 1)

        @pl.when(row == 3)
        def _():
            z_copy(ZO3, h).wait_recv()
            z_copy(ZS3, h).wait_recv()
            z_copy(ZO3B, h).wait_recv()
            z_copy(ZS3B, h).wait_recv()
            merge(h, 2)

        @pl.when(h != y)
        def _():
            there = cross.at[h]
            pltpu.make_async_remote_copy(
                there, there, back_send.at[0], back_recv.at[h], device_id={"dp": side + 2 * h + core, "ctx": me}, device_id_type=MESH
            ).wait_recv()

        @pl.when(h == y)
        def _():
            own_back().wait()

        self_out = accs[pl.ds(h * QB, QB)].astype(jnp.bfloat16).astype(jnp.float32).reshape(XS, TOK, HD)
        mixed[h] = (self_out + cross[h].astype(jnp.float32)).astype(jnp.bfloat16)
        for k in (1, 3, 2):
            out_copy(h, x_at(k)).start()
        own_out(h).start()

    loop(0, LOCAL, emit)

    def finish(h):
        own_out(h).wait()
        for k in range(1, XS):
            peer = x_at(k)
            pltpu.make_async_remote_copy(
                mixed.at[h, peer], out_ref.at[:, cols(peer * LOCAL + h)], out_send.at[h, peer], out_recv.at[h, peer],
                device_id={"dp": dp, "ctx": row * XS + peer}, device_id_type=MESH,
            ).wait_recv()
            out_copy(h, peer).wait_send()
        for at, kinds in enumerate(((ZK, ZV), (ZO2, ZS2, ZO3, ZS3), (ZQ2, ZQ3, ZO3B, ZS3B), (ZQ3B,))):

            @pl.when(row == at)
            def _():
                for kind in kinds:
                    z_copy(kind, h).wait_send()

    @pl.when(edge)
    def _():
        for kind in range(2):
            far_copy(kind).wait_send()
        inner_copy(0).wait_send()

    @pl.when(row >= 2)
    def _():
        inner_copy(1).wait_send()

    for kind in range(2):
        for far in range(2):
            for k in range(1, 4):
                y_copy(kind, far, k).wait_send()
            for k in range(4):
                core_pass(kind, far, k).wait_send()

    for kind in range(4):
        for p in range(2):
            two_copy(kind, p).wait_send()
            pass_copy(kind, p).wait_send()
            for k in (1, 3):
                x_copy(kind, p, k).wait_send()
    for k in range(1, 4):
        idx_x(k).wait_send()
        idx_y(k).wait_send()
        qc_copy(k).wait_send()
    for k in range(1, 4):
        back_copy(k).wait_send()
    loop(0, LOCAL, finish)


def shards(q_self, k_self, v_self, q_cross, db_keys, db_values, nb_shard, nb_row):
    anywhere = pl.BlockSpec(memory_space=pl.ANY)
    scalars = pl.BlockSpec(memory_space=pltpu.SMEM)
    heads = pltpu.VMEM((LOCAL, XS, TOK, HD), jnp.bfloat16)
    sources = pltpu.VMEM((XS, TOK, WIDE), jnp.bfloat16)
    database = pltpu.VMEM((N_DP * DB_DEV, NLEN, HD), jnp.bfloat16)
    shard = pltpu.VMEM((DB_DEV, NLEN, WIDE), jnp.bfloat16)
    state = pltpu.VMEM((LOCAL * QB, ROWS, HD), jnp.float32)
    parts = pltpu.VMEM((2, LOCAL, XS, TOK, HD), jnp.bfloat16)
    stats = pltpu.VMEM((2, LOCAL, 8, 128), jnp.float32)
    dma = pltpu.SemaphoreType.DMA
    out = pl.pallas_call(
        kernel,
        out_shape=jax.ShapeDtypeStruct((TOK, HEADS * HD), jnp.bfloat16),
        in_specs=[anywhere] * 6 + [scalars] * 2,
        out_specs=anywhere,
        scratch_shapes=[
            sources, sources, sources, heads, heads, heads, heads, heads, database, database,
            pltpu.VMEM((4, XS, 8, 128), jnp.int32),
            pltpu.SMEM((4, XS, 8, 128), jnp.int32),
            heads,
            pltpu.VMEM((2, 2 * QB, ROWS, ROWS), jnp.float32),
            state, state, state,
            parts, stats, parts, stats, heads, heads, shard, shard, sources,
            pltpu.VMEM((4, TOK, WIDE), jnp.bfloat16),
            dma((4, 2, 4)), dma((4, 2, XS)), dma((4, 2)), dma((LOCAL, XS)), dma((LOCAL, XS)), dma((LOCAL,)),
            dma((4,)), dma((4,)), dma((2, 4)), dma((2, 4)),
            dma((4,)), dma((4,)), dma((11, LOCAL)), dma((11, LOCAL)),
            dma((4,)), dma((2,)), dma((2, 2, 4)), dma((2, 2, 4)), dma((2, N_DP)), dma((5,)), dma((4,)), dma,
            pltpu.SemaphoreType.REGULAR,
        ],
        compiler_params=pltpu.CompilerParams(
            collective_id=0, has_side_effects=True, vmem_limit_bytes=60 * 1024 * 1024
        ),
    )(q_self[0], k_self[0], v_self[0], q_cross[0], db_keys, db_values, nb_shard, nb_row)
    return out[None]


def solution(mesh):
    return jax.shard_map(
        shards,
        mesh=mesh,
        in_specs=(
            P("dp", "ctx", None),
            P("dp", "ctx", None),
            P("dp", "ctx", None),
            P("dp", "ctx", None),
            P("dp", None, None),
            P("dp", None, None),
            P("dp", "ctx", None),
            P("dp", "ctx", None),
        ),
        out_specs=P("dp", "ctx", None),
        check_vma=False,
    )
```

```python
import jax
import jax.numpy as jnp
from jax import lax
from jax.experimental import pallas as pl
from jax.experimental.pallas import tpu as pltpu
from jax.sharding import PartitionSpec as P

HEADS = 16
HD = 128
GROUP = 64
NEIGH = 2
NLEN = 128
TOK = 128
DB_DEV = 2
N_DP = 16
HALF = 8
XS = 4
LOCAL = HEADS // XS
WIDE = LOCAL * HD
ROWS = 256
PER = ROWS // TOK
QB = XS // PER
EXPO = HD**-0.5 * 1.4426950408889634
MESH = pl.DeviceIdType.MESH
NT = (((1,), (1,)), ((), ()))
NN = (((1,), (0,)), ((), ()))
QC, KS, VS, QS, OUT = range(5)
ZK, ZV, ZQ2, ZQ3, ZQ3B, ZO2, ZS2, ZO3, ZS3, ZO3B, ZS3B = range(11)


def cols(head):
    return pl.ds(pl.multiple_of(head * HD, HD), HD)


def kernel(
    qs_ref, ks_ref, vs_ref, qc_ref, kd_ref, vd_ref, shard_ref, row_ref, out_ref,
    qs, ks, vs, qc, k0, v0, q2, q3, kd, vd, idx, idx_s, cross, scores, tops, totals, accs,
    part_out, stat_out, part_in, stat_in, mixed, cross_out, kf, vf,
    x_send, x_recv, qc_send, qc_recv, idx_send, idx_recv, back_send, back_recv, z_send, z_recv,
    far_send, far_recv, y_send, core_send, db_recv, own_sem, db_own, number_sem, ready,
):
    dp = lax.axis_index("dp")
    me = lax.axis_index("ctx")
    row = me // XS
    x = lax.rem(me, XS)
    near = lax.rem(dp, HALF)
    side = dp - near
    away = HALF - side
    y = near // 2
    core = lax.rem(near, 2)
    other_core = dp + 1 - 2 * core
    far_dp = away + near
    far_ctx = (3 - row) * XS + x
    edge = (row == 0) | (row == 3)
    first_side = dp < HALF
    inner_ctx = (row // 2 + 1) * XS + x

    def x_at(k):
        return lax.rem(x + k, XS)

    def y_at(home, k):
        return home + lax.rem(near + 2 * k, HALF)

    def loop(first, last, body):
        def step(k, carry):
            body(k)
            return carry

        lax.fori_loop(first, last, step, 0)

    barrier = pltpu.get_barrier_semaphore()

    def greet(dp_of, ctx_of):
        pl.semaphore_signal(barrier, inc=1, device_id={"dp": dp_of, "ctx": ctx_of}, device_id_type=MESH)

    def plane(k):
        return lax.rem(y + k // XS, 4), x_at(lax.rem(k, XS))

    def greet_plane(k):
        to_y, to_x = plane(k)
        greet(side + 2 * to_y + core, row * XS + to_x)

    loop(1, 4 * XS, greet_plane)
    for k in range(1, 4):
        greet(dp, lax.rem(row + k, 4) * XS + x)
    greet(other_core, me)

    @pl.when(edge & first_side)
    def _():
        greet(far_dp, far_ctx)

    lane = lax.broadcasted_iota(jnp.int32, (8, 128), 1)
    tile = jnp.zeros((8, 128), jnp.int32)
    for g in range(TOK // GROUP):
        for n in range(NEIGH):
            block = shard_ref[0, g, n] * DB_DEV + row_ref[0, g, n]
            tile = jnp.where(lane == g * NEIGH + n, block, tile)
    idx[y, x] = tile

    arrays = {KS: (ks_ref, ks), VS: (vs_ref, vs), QS: (qs_ref, qs)}
    blocks = ((kd_ref, kd, kf), (vd_ref, vd, vf))
    wide = pl.ds(pl.multiple_of(x * WIDE, WIDE), WIDE)
    head = x * LOCAL + y

    def own_copy(kind, h):
        arg, buf = arrays[kind]
        return pltpu.make_async_copy(arg.at[:, cols(x * LOCAL + h)], buf.at[h, x], own_sem.at[kind, h])

    def own_qc():
        return pltpu.make_async_copy(qc_ref.at[:, cols(head)], qc.at[y, x], own_sem.at[QC, 0])

    def own_db(kind):
        arg, buf, far = blocks[kind]
        return pltpu.make_async_copy(arg.at[:, :, cols(head)], buf.at[pl.ds(dp * DB_DEV, DB_DEV)], db_own.at[kind])

    def own_far(kind):
        arg, buf, far = blocks[kind]
        return pltpu.make_async_copy(far.at[:, :, cols(y)], buf.at[pl.ds(far_dp * DB_DEV, DB_DEV)], db_own.at[2 + kind])

    def start_own(h):
        for kind in (KS, VS, QS):
            own_copy(kind, h).start()

    loop(0, LOCAL, start_own)
    own_qc().start()
    for kind in range(2):
        own_db(kind).start()

    pl.semaphore_wait(barrier, 19 + jnp.where(edge & (dp >= HALF), 1, 0))

    @pl.when(edge & (dp >= HALF))
    def _():
        pl.semaphore_signal(ready, inc=1, device_id={"dp": far_dp, "ctx": far_ctx}, device_id_type=MESH)

    def far_copy(kind):
        arg, buf, far = blocks[kind]
        return pltpu.make_async_remote_copy(
            arg.at[:, :, wide], far, far_send.at[kind], far_recv.at[kind],
            device_id={"dp": far_dp, "ctx": far_ctx}, device_id_type=MESH,
        )

    def inner_copy(kind):
        far = blocks[kind][2]
        return pltpu.make_async_remote_copy(
            far, far, far_send.at[2 + kind], far_recv.at[kind],
            device_id={"dp": dp, "ctx": inner_ctx}, device_id_type=MESH,
        )

    def shard_copy(kind, shard, src, send, target):
        part = blocks[kind][1].at[pl.ds(shard * DB_DEV, DB_DEV)]
        return pltpu.make_async_remote_copy(
            part if src is None else src, part, send, db_recv.at[kind, shard],
            device_id={"dp": target, "ctx": me}, device_id_type=MESH,
        )

    def y_copy(kind, far, k):
        to_y = lax.rem(y + k, 4)
        src = blocks[kind][2].at[:, :, cols(to_y)] if far else blocks[kind][0].at[:, :, cols(x * LOCAL + to_y)]
        return shard_copy(kind, far_dp if far else dp, src, y_send.at[kind, far, k], y_at(side, k))

    def core_pass(kind, far, k):
        src = None
        if k == 0:
            src = blocks[kind][2].at[:, :, cols(y)] if far else blocks[kind][0].at[:, :, cols(head)]
        return shard_copy(kind, y_at(away if far else side, k), src, core_send.at[kind, far, k], other_core)

    def wait_shard(kind, shard):
        shard_copy(kind, shard, None, far_send.at[kind], other_core).wait_recv()

    def qc_copy(k):
        to_y, to_x = plane(k)
        return pltpu.make_async_remote_copy(
            qc_ref.at[:, cols(to_x * LOCAL + to_y)], qc.at[y, x], qc_send.at[k], qc_recv.at[y, x],
            device_id={"dp": side + 2 * to_y + core, "ctx": row * XS + to_x}, device_id_type=MESH,
        )

    def idx_copy(k):
        to_y, to_x = plane(k)
        return pltpu.make_async_remote_copy(
            idx.at[y, x], idx.at[y, x], idx_send.at[k], idx_recv.at[y, x],
            device_id={"dp": side + 2 * to_y + core, "ctx": row * XS + to_x}, device_id_type=MESH,
        )

    def wait_plane(k):
        from_y, from_x = plane(k)
        for buf, sent, received in ((idx, idx_send, idx_recv), (qc, qc_send, qc_recv)):
            there = buf.at[from_y, from_x]
            pltpu.make_async_remote_copy(
                there, there, sent.at[k], received.at[from_y, from_x],
                device_id={"dp": side + 2 * from_y + core, "ctx": row * XS + from_x}, device_id_type=MESH,
            ).wait_recv()

    def back_copy(k):
        to_y = lax.rem(y + k, 4)
        return pltpu.make_async_remote_copy(
            cross_out.at[to_y], cross.at[y], back_send.at[k], back_recv.at[y],
            device_id={"dp": y_at(side, k), "ctx": me}, device_id_type=MESH,
        )

    def own_back():
        return pltpu.make_async_copy(cross_out.at[y], cross.at[y], own_sem.at[QC, 1])

    def x_copy(kind, h, to):
        arg, buf = arrays[kind]
        return pltpu.make_async_remote_copy(
            arg.at[:, cols(to * LOCAL + h)], buf.at[h, x], x_send.at[kind, h, to], x_recv.at[kind, h, x],
            device_id={"dp": dp, "ctx": row * XS + to}, device_id_type=MESH,
        )

    def arrived(kind, h):
        own_copy(kind, h).wait()
        for k in range(1, XS):
            source = x_at(k)
            buf = arrays[kind][1].at[h, source]
            pltpu.make_async_remote_copy(
                buf, buf, x_send.at[kind, h, source], x_recv.at[kind, h, source],
                device_id={"dp": dp, "ctx": row * XS + source}, device_id_type=MESH,
            ).wait_recv()

    def start_x(kinds, h):
        for k in (1, 3, 2):
            for kind in kinds:
                x_copy(kind, h, x_at(k)).start()

    def start_plane():
        def step(k):
            idx_copy(k).start()
            qc_copy(k).start()

        loop(1, 4 * XS, step)

    def start_far():
        for kind in range(2):
            far_copy(kind).start()

    def start_near():
        for kind in range(2):
            for k in (1, 3, 2):
                y_copy(kind, 0, k).start()
            core_pass(kind, 0, 0).start()

    def start_far_first():
        pl.when(dp >= HALF)(start_far)

    def start_far_second():
        @pl.when(first_side)
        def _():
            pl.semaphore_wait(ready, 1)
            start_far()

    def z_copy(kind, h):
        src, dst, to = {
            ZK: (ks.at[h], k0.at[h], 1),
            ZV: (vs.at[h], v0.at[h], 1),
            ZQ2: (qs.at[h], q2.at[h], 1),
            ZQ3: (qs.at[h], q3.at[h], 1),
            ZQ3B: (qs.at[h], q3.at[h], 2),
            ZO2: (part_out.at[0, h], part_in.at[0, h], 2),
            ZS2: (stat_out.at[0, h], stat_in.at[0, h], 2),
            ZO3: (part_out.at[1, h], part_in.at[0, h], 3),
            ZS3: (stat_out.at[1, h], stat_in.at[0, h], 3),
            ZO3B: (part_out.at[1, h], part_in.at[1, h], 3),
            ZS3B: (stat_out.at[1, h], stat_in.at[1, h], 3),
        }[kind]
        return pltpu.make_async_remote_copy(
            src, dst, z_send.at[kind, h], z_recv.at[kind, h],
            device_id={"dp": dp, "ctx": to * XS + x}, device_id_type=MESH,
        )

    def relay(h):
        @pl.when(row == 0)
        def _():
            arrived(KS, h)
            z_copy(ZK, h).start()
            arrived(VS, h)
            z_copy(ZV, h).start()

        @pl.when(row == 2)
        def _():
            arrived(QS, h)
            z_copy(ZQ2, h).start()

        @pl.when(row == 3)
        def _():
            arrived(QS, h)
            z_copy(ZQ3, h).start()

    def far_stage():
        for kind in range(2):
            far_copy(kind).wait_recv()

            @pl.when(edge)
            def _():
                inner_copy(kind).start()

            for k in (1, 3, 2):
                y_copy(kind, 1, k).start()
            core_pass(kind, 1, 0).start()
            own_far(kind).start()

    def core_stage():
        for far in range(2):
            for kind in range(2):
                for k in (1, 3, 2):
                    wait_shard(kind, y_at(away if far else side, k))
                    core_pass(kind, far, k).start()

    diagonal = lax.broadcasted_iota(jnp.int32, (ROWS, ROWS), 0) >= lax.broadcasted_iota(jnp.int32, (ROWS, ROWS), 1)
    eye = lax.broadcasted_iota(jnp.int32, (TOK, TOK), 0) == lax.broadcasted_iota(jnp.int32, (TOK, TOK), 1)

    def attend(queries, h, b, chunks, slot):
        q = queries[h, pl.ds(b * PER, PER)].reshape(ROWS, HD)
        peak = None
        for j, (keys, values, c, masked) in enumerate(chunks):
            k = keys[h, pl.ds(c * PER, PER)].reshape(ROWS, HD)
            s = lax.dot_general(q, k, NT, preferred_element_type=jnp.float32)
            if masked:
                s = jnp.where(diagonal, s, -1e30)
            scores[slot, j] = s
            folded = jnp.maximum(s[:, :HD], s[:, HD:])
            peak = folded if peak is None else jnp.maximum(peak, folded)
        top = jnp.max(peak, axis=1, keepdims=True)
        total = jnp.zeros((ROWS, HD), jnp.float32)
        acc = jnp.zeros((ROWS, HD), jnp.float32)
        for j, (keys, values, c, masked) in enumerate(chunks):
            w = jnp.exp2((scores[slot, j] - top) * EXPO)
            total = total + (w[:, :HD] + w[:, HD:])
            v = values[h, pl.ds(c * PER, PER)].reshape(ROWS, HD)
            acc = acc + lax.dot_general(w.astype(jnp.bfloat16), v, NN, preferred_element_type=jnp.float32)
        return top, jnp.sum(total, axis=1, keepdims=True), acc

    def partial(queries, h, chunks, place):
        for b in range(QB):
            top, total, acc = attend(queries, h, b, chunks, b)
            part_out[place, h, pl.ds(b * PER, PER)] = (acc / total).astype(jnp.bfloat16).reshape(PER, TOK, HD)
            for p in range(PER):
                rows = slice(p * TOK, (p + 1) * TOK)
                at = b * PER + p
                stat_out[place, h, at : at + 1] = jnp.sum(jnp.where(eye, top[rows], 0.0), axis=0, keepdims=True)
                stat_out[place, h, XS + at : XS + at + 1] = jnp.sum(jnp.where(eye, total[rows], 0.0), axis=0, keepdims=True)

    def own_rows(h, extra, final):
        for b in range(QB):
            chunks = extra + [(ks, vs, c, c == b) for c in range(b + 1)]
            top, total, acc = attend(qs, h, b, chunks, b)
            at = h * QB + b
            if final:
                accs[at] = acc / total
            else:
                accs[at] = acc
                tops[at] = jnp.broadcast_to(top, (ROWS, HD))
                totals[at] = jnp.broadcast_to(total, (ROWS, HD))

    whole_own = [(ks, vs, c, False) for c in range(QB)]
    whole_first = [(k0, v0, c, False) for c in range(QB)]

    def between(h):
        @pl.when(row == 1)
        def _():
            arrived(KS, h)
            arrived(VS, h)
            z_copy(ZK, h).wait_recv()
            z_copy(ZV, h).wait_recv()
            z_copy(ZQ2, h).wait_recv()
            partial(q2, h, whole_first + whole_own, 0)
            z_copy(ZO2, h).start()
            z_copy(ZS2, h).start()
            z_copy(ZQ3, h).wait_recv()
            partial(q3, h, whole_first + whole_own, 1)
            z_copy(ZO3, h).start()
            z_copy(ZS3, h).start()
            arrived(QS, h)
            own_rows(h, whole_first, True)

        @pl.when(row == 2)
        def _():
            arrived(KS, h)
            arrived(VS, h)
            z_copy(ZQ3B, h).wait_recv()
            partial(q3, h, whole_own, 1)
            z_copy(ZO3B, h).start()
            z_copy(ZS3B, h).start()

    def own_others(h):
        @pl.when(row == 0)
        def _():
            arrived(QS, h)
            own_rows(h, [], True)

        @pl.when(row == 2)
        def _():
            own_rows(h, [], False)

        @pl.when(row == 3)
        def _():
            arrived(KS, h)
            arrived(VS, h)
            own_rows(h, [], False)

    def cross_document(k):
        doc = lax.rem(y + k, 4)
        for t in range(XS):
            for g in range(TOK // GROUP):
                first = idx_s[doc, t, 0, g * NEIGH]
                second = idx_s[doc, t, 0, g * NEIGH + 1]
                rows = pl.ds(g * GROUP, GROUP)
                keys = jnp.concatenate([kd[first], kd[second]], axis=0)
                values = jnp.concatenate([vd[first], vd[second]], axis=0)
                s = lax.dot_general(qc[doc, t, rows, :], keys, NT, preferred_element_type=jnp.float32)
                top = jnp.max(s, axis=1, keepdims=True)
                w = jnp.exp2((s - top) * EXPO)
                total = jnp.sum(w, axis=1, keepdims=True)
                o = lax.dot_general(w.astype(jnp.bfloat16), values, NN, preferred_element_type=jnp.float32)
                cross_out[doc, t, rows, :] = (o / total).astype(jnp.bfloat16)

        @pl.when(k > 0)
        def _():
            back_copy(k).start()

        @pl.when(k == 0)
        def _():
            own_back().start()

    def cross_stage():
        own_qc().wait()
        for kind in range(2):
            own_db(kind).wait()
            own_far(kind).wait()
        loop(1, 4 * XS, wait_plane)
        numbers = pltpu.make_async_copy(idx, idx_s, number_sem)
        numbers.start()
        numbers.wait()

        def wait_other_core(k):
            for kind in range(2):
                wait_shard(kind, 2 * k + 1 - core)

        loop(0, HALF, wait_other_core)
        loop(0, 4, lambda k: cross_document(3 - k))

    @pl.when(row == 0)
    def _():
        start_x((KS, VS), 0)
        start_far_first()
        start_x((KS, VS), 1)
        relay(0)
        start_x((KS, VS), 2)
        relay(1)
        start_x((KS, VS), 3)
        start_far_second()
        relay(2)
        start_near()
        relay(3)
        start_plane()
        loop(0, LOCAL, lambda h: start_x((QS,), h))
        far_stage()

    @pl.when(row == 1)
    def _():
        loop(0, LOCAL, lambda h: start_x((KS, VS), h))
        loop(0, LOCAL, lambda h: start_x((QS,), h))
        start_near()
        start_plane()

    @pl.when(row == 2)
    def _():
        loop(0, LOCAL, lambda h: start_x((QS,), h))
        loop(0, LOCAL, relay)
        start_near()
        start_plane()
        loop(0, LOCAL, lambda h: start_x((KS, VS), h))
        far_stage()

    @pl.when(row == 3)
    def _():
        loop(0, LOCAL, lambda h: start_x((QS,), h))
        start_far_first()
        loop(0, LOCAL, relay)
        start_far_second()
        start_near()
        loop(0, LOCAL, lambda h: start_x((KS, VS), h))
        far_stage()
        loop(0, LOCAL, lambda h: z_copy(ZQ3B, h).start())
        start_plane()

    @pl.when(row != 1)
    def _():
        core_stage()

    def between_step(h):
        between(h)
        for at, stage in enumerate((far_stage, core_stage, cross_stage)):
            pl.when((row == 1) & (h == at))(stage)

    loop(0, LOCAL, between_step)

    @pl.when(row != 1)
    def _():
        loop(0, LOCAL, own_others)
        cross_stage()

    def merge(h, parts):
        for b in range(QB):
            at = h * QB + b
            for p in range(PER):
                rows = slice(p * TOK, (p + 1) * TOK)
                sub = b * PER + p
                top = tops[at, rows, :1]
                others = []
                for place in range(parts):
                    column = [
                        jnp.sum(jnp.where(eye, stat_in[place, h, n : n + 1], 0.0), axis=1, keepdims=True)
                        for n in (sub, XS + sub)
                    ]
                    others.append(column)
                peak = top
                for other_top, _ in others:
                    peak = jnp.maximum(peak, other_top)
                keep = jnp.exp2((top - peak) * EXPO)
                total = totals[at, rows, :1] * keep
                acc = accs[at, rows, :] * keep
                for place, (other_top, other_total) in enumerate(others):
                    w = jnp.exp2((other_top - peak) * EXPO) * other_total
                    total = total + w
                    acc = acc + part_in[place, h, sub].astype(jnp.float32) * w
                accs[at, rows, :] = acc / total

    def out_copy(h, t):
        return pltpu.make_async_remote_copy(
            mixed.at[h, t], out_ref.at[:, cols(x * LOCAL + h)], x_send.at[OUT, h, t], x_recv.at[OUT, h, x],
            device_id={"dp": dp, "ctx": row * XS + t}, device_id_type=MESH,
        )

    def own_out(h):
        return pltpu.make_async_copy(mixed.at[h, x], out_ref.at[:, cols(x * LOCAL + h)], own_sem.at[OUT, h])

    def emit(h):
        @pl.when(row == 2)
        def _():
            z_copy(ZO2, h).wait_recv()
            z_copy(ZS2, h).wait_recv()
            merge(h, 1)

        @pl.when(row == 3)
        def _():
            z_copy(ZO3, h).wait_recv()
            z_copy(ZS3, h).wait_recv()
            z_copy(ZO3B, h).wait_recv()
            z_copy(ZS3B, h).wait_recv()
            merge(h, 2)

        @pl.when(h != y)
        def _():
            there = cross.at[h]
            pltpu.make_async_remote_copy(
                there, there, back_send.at[0], back_recv.at[h], device_id={"dp": side + 2 * h + core, "ctx": me}, device_id_type=MESH
            ).wait_recv()

        @pl.when(h == y)
        def _():
            own_back().wait()

        self_out = accs[pl.ds(h * QB, QB)].astype(jnp.bfloat16).astype(jnp.float32).reshape(XS, TOK, HD)
        mixed[h] = (self_out + cross[h].astype(jnp.float32)).astype(jnp.bfloat16)
        for k in (1, 3, 2):
            out_copy(h, x_at(k)).start()
        own_out(h).start()

    loop(0, LOCAL, emit)

    def finish(h):
        own_out(h).wait()
        for k in range(1, XS):
            peer = x_at(k)
            pltpu.make_async_remote_copy(
                mixed.at[h, peer], out_ref.at[:, cols(peer * LOCAL + h)], x_send.at[OUT, h, peer], x_recv.at[OUT, h, peer],
                device_id={"dp": dp, "ctx": row * XS + peer}, device_id_type=MESH,
            ).wait_recv()
            for kind in (KS, VS, QS):
                x_copy(kind, h, peer).wait_send()
            out_copy(h, peer).wait_send()
        for at, kinds in enumerate(((ZK, ZV), (ZO2, ZS2, ZO3, ZS3), (ZQ2, ZO3B, ZS3B), (ZQ3, ZQ3B))):

            @pl.when(row == at)
            def _():
                for kind in kinds:
                    z_copy(kind, h).wait_send()

    @pl.when(edge)
    def _():
        for kind in range(2):
            far_copy(kind).wait_send()
            inner_copy(kind).wait_send()

    for kind in range(2):
        for far in range(2):
            for k in range(1, 4):
                y_copy(kind, far, k).wait_send()
            for k in range(4):
                core_pass(kind, far, k).wait_send()

    def finish_plane(k):
        idx_copy(k).wait_send()
        qc_copy(k).wait_send()

    loop(1, 4 * XS, finish_plane)
    for k in range(1, 4):
        back_copy(k).wait_send()
    loop(0, LOCAL, finish)


def shards(q_self, k_self, v_self, q_cross, db_keys, db_values, nb_shard, nb_row):
    anywhere = pl.BlockSpec(memory_space=pl.ANY)
    scalars = pl.BlockSpec(memory_space=pltpu.SMEM)
    heads = pltpu.VMEM((LOCAL, XS, TOK, HD), jnp.bfloat16)
    database = pltpu.VMEM((N_DP * DB_DEV, NLEN, HD), jnp.bfloat16)
    shard = pltpu.VMEM((DB_DEV, NLEN, WIDE), jnp.bfloat16)
    state = pltpu.VMEM((LOCAL * QB, ROWS, HD), jnp.float32)
    parts = pltpu.VMEM((2, LOCAL, XS, TOK, HD), jnp.bfloat16)
    stats = pltpu.VMEM((2, LOCAL, 8, 128), jnp.float32)
    dma = pltpu.SemaphoreType.DMA
    out = pl.pallas_call(
        kernel,
        out_shape=jax.ShapeDtypeStruct((TOK, HEADS * HD), jnp.bfloat16),
        in_specs=[anywhere] * 6 + [scalars] * 2,
        out_specs=anywhere,
        scratch_shapes=[
            heads, heads, heads, heads, heads, heads, heads, heads, database, database,
            pltpu.VMEM((4, XS, 8, 128), jnp.int32),
            pltpu.SMEM((4, XS, 8, 128), jnp.int32),
            heads,
            pltpu.VMEM((2, 2 * QB, ROWS, ROWS), jnp.float32),
            state, state, state,
            parts, stats, parts, stats, heads, heads, shard, shard,
            dma((5, LOCAL, XS)), dma((5, LOCAL, XS)), dma((4 * XS,)), dma((4, XS)), dma((4 * XS,)), dma((4, XS)),
            dma((4,)), dma((4,)), dma((11, LOCAL)), dma((11, LOCAL)),
            dma((4,)), dma((2,)), dma((2, 2, 4)), dma((2, 2, 4)), dma((2, N_DP)), dma((5, LOCAL)), dma((4,)), dma,
            pltpu.SemaphoreType.REGULAR,
        ],
        compiler_params=pltpu.CompilerParams(
            collective_id=0, has_side_effects=True, vmem_limit_bytes=60 * 1024 * 1024
        ),
    )(q_self[0], k_self[0], v_self[0], q_cross[0], db_keys, db_values, nb_shard, nb_row)
    return out[None]


def solution(mesh):
    return jax.shard_map(
        shards,
        mesh=mesh,
        in_specs=(
            P("dp", "ctx", None),
            P("dp", "ctx", None),
            P("dp", "ctx", None),
            P("dp", "ctx", None),
            P("dp", None, None),
            P("dp", None, None),
            P("dp", "ctx", None),
            P("dp", "ctx", None),
        ),
        out_specs=P("dp", "ctx", None),
        check_vma=False,
    )
```

```python
import jax
import jax.numpy as jnp
from jax import lax
from jax.experimental import pallas as pl
from jax.experimental.pallas import tpu as pltpu
from jax.sharding import PartitionSpec as P

HEADS = 16
HD = 128
GROUP = 64
NEIGH = 2
NLEN = 128
TOK = 128
DB_DEV = 2
N_DP = 16
HALF = 8
XS = 4
LOCAL = HEADS // XS
WIDE = LOCAL * HD
ROWS = 256
PER = ROWS // TOK
QB = XS // PER
EXPO = HD**-0.5 * 1.4426950408889634
MESH = pl.DeviceIdType.MESH
NT = (((1,), (1,)), ((), ()))
NN = (((1,), (0,)), ((), ()))
QC, KS, VS, QS, OUT = range(5)
ZK, ZV, ZQ2, ZQ3, ZQ3B, ZO2, ZS2, ZO3, ZS3, ZO3B, ZS3B = range(11)


def cols(head):
    return pl.ds(pl.multiple_of(head * HD, HD), HD)


def kernel(
    qs_ref, ks_ref, vs_ref, qc_ref, kd_ref, vd_ref, shard_ref, row_ref, out_ref,
    qs, ks, vs, qc, k0, v0, q2, q3, kd, vd, idx, idx_s, cross, scores, tops, totals, accs,
    part_out, stat_out, part_in, stat_in, mixed, cross_out, kf, vf,
    x_send, x_recv, qc_send, qc_recv, idx_send, idx_recv, back_send, back_recv, z_send, z_recv,
    far_send, far_recv, y_send, core_send, db_recv, own_sem, db_own, number_sem, ready,
):
    dp = lax.axis_index("dp")
    me = lax.axis_index("ctx")
    row = me // XS
    x = lax.rem(me, XS)
    near = lax.rem(dp, HALF)
    side = dp - near
    away = HALF - side
    y = near // 2
    core = lax.rem(near, 2)
    other_core = dp + 1 - 2 * core
    far_dp = away + near
    far_ctx = (3 - row) * XS + x
    edge = (row == 0) | (row == 3)
    first_side = dp < HALF
    inner = (row == 1) | (row == 2)
    pair = row + 1 - 2 * lax.rem(row, 2)
    cross_row = jnp.where(inner, pair, row)
    cross_part = jnp.where(inner, 1, 0)

    def x_at(k):
        return lax.rem(x + k, XS)

    def y_at(home, k):
        return home + lax.rem(near + 2 * k, HALF)

    def loop(first, last, body):
        def step(k, carry):
            body(k)
            return carry

        lax.fori_loop(first, last, step, 0)

    barrier = pltpu.get_barrier_semaphore()

    def greet(dp_of, ctx_of):
        pl.semaphore_signal(barrier, inc=1, device_id={"dp": dp_of, "ctx": ctx_of}, device_id_type=MESH)

    def plane(k):
        return lax.rem(y + k // XS, 4), x_at(lax.rem(k, XS))

    def greet_plane(of_row):
        def step(k):
            to_y, to_x = plane(k)
            greet(side + 2 * to_y + core, of_row * XS + to_x)

        return step

    loop(1, jnp.where(edge, 4 * XS, XS), greet_plane(row))
    loop(1, 4 * XS, greet_plane(pair))
    for k in range(1, 4):
        greet(dp, lax.rem(row + k, 4) * XS + x)

    @pl.when(edge)
    def _():
        greet(other_core, me)

    @pl.when(edge & first_side)
    def _():
        greet(far_dp, far_ctx)

    lane = lax.broadcasted_iota(jnp.int32, (8, 128), 1)
    tile = jnp.zeros((8, 128), jnp.int32)
    for g in range(TOK // GROUP):
        for n in range(NEIGH):
            block = shard_ref[0, g, n] * DB_DEV + row_ref[0, g, n]
            tile = jnp.where(lane == g * NEIGH + n, block, tile)
    idx[cross_part, y, x] = tile

    arrays = {KS: (ks_ref, ks), VS: (vs_ref, vs), QS: (qs_ref, qs)}
    blocks = ((kd_ref, kd, kf), (vd_ref, vd, vf))
    wide = pl.ds(pl.multiple_of(x * WIDE, WIDE), WIDE)
    head = x * LOCAL + y

    def own_copy(kind, h):
        arg, buf = arrays[kind]
        return pltpu.make_async_copy(arg.at[:, cols(x * LOCAL + h)], buf.at[h, x], own_sem.at[kind, h])

    def own_qc():
        return pltpu.make_async_copy(qc_ref.at[:, cols(head)], qc.at[0, y, x], own_sem.at[QC, 0])

    def own_db(kind):
        arg, buf, far = blocks[kind]
        return pltpu.make_async_copy(arg.at[:, :, cols(head)], buf.at[pl.ds(dp * DB_DEV, DB_DEV)], db_own.at[kind])

    def own_far(kind):
        arg, buf, far = blocks[kind]
        return pltpu.make_async_copy(far.at[:, :, cols(y)], buf.at[pl.ds(far_dp * DB_DEV, DB_DEV)], db_own.at[2 + kind])

    def start_own(h):
        for kind in (KS, VS, QS):
            own_copy(kind, h).start()

    loop(0, LOCAL, start_own)

    @pl.when(edge)
    def _():
        own_qc().start()
        for kind in range(2):
            own_db(kind).start()

    pl.semaphore_wait(barrier, 21 + jnp.where(edge, 13, 0) + jnp.where(edge & (dp >= HALF), 1, 0))

    @pl.when(edge & (dp >= HALF))
    def _():
        pl.semaphore_signal(ready, inc=1, device_id={"dp": far_dp, "ctx": far_ctx}, device_id_type=MESH)

    def far_copy(kind):
        arg, buf, far = blocks[kind]
        return pltpu.make_async_remote_copy(
            arg.at[:, :, wide], far, far_send.at[kind], far_recv.at[kind],
            device_id={"dp": far_dp, "ctx": far_ctx}, device_id_type=MESH,
        )

    def shard_copy(kind, shard, src, send, target):
        part = blocks[kind][1].at[pl.ds(shard * DB_DEV, DB_DEV)]
        return pltpu.make_async_remote_copy(
            part if src is None else src, part, send, db_recv.at[kind, shard],
            device_id={"dp": target, "ctx": me}, device_id_type=MESH,
        )

    def y_copy(kind, far, k):
        to_y = lax.rem(y + k, 4)
        src = blocks[kind][2].at[:, :, cols(to_y)] if far else blocks[kind][0].at[:, :, cols(x * LOCAL + to_y)]
        return shard_copy(kind, far_dp if far else dp, src, y_send.at[kind, far, k], y_at(side, k))

    def core_pass(kind, far, k):
        src = None
        if k == 0:
            src = blocks[kind][2].at[:, :, cols(y)] if far else blocks[kind][0].at[:, :, cols(head)]
        return shard_copy(kind, y_at(away if far else side, k), src, core_send.at[kind, far, k], other_core)

    def wait_shard(kind, shard):
        shard_copy(kind, shard, None, far_send.at[kind], other_core).wait_recv()

    def qc_copy(k):
        to_y, to_x = plane(k)
        return pltpu.make_async_remote_copy(
            qc_ref.at[:, cols(to_x * LOCAL + to_y)], qc.at[cross_part, y, x], qc_send.at[k], qc_recv.at[cross_part, y, x],
            device_id={"dp": side + 2 * to_y + core, "ctx": cross_row * XS + to_x}, device_id_type=MESH,
        )

    def idx_copy(k):
        to_y, to_x = plane(k)
        return pltpu.make_async_remote_copy(
            idx.at[cross_part, y, x], idx.at[cross_part, y, x], idx_send.at[k], idx_recv.at[cross_part, y, x],
            device_id={"dp": side + 2 * to_y + core, "ctx": cross_row * XS + to_x}, device_id_type=MESH,
        )

    def wait_plane(part):
        def step(k):
            from_y, from_x = plane(k)
            for buf, sent, received in ((idx, idx_send, idx_recv), (qc, qc_send, qc_recv)):
                there = buf.at[part, from_y, from_x]
                pltpu.make_async_remote_copy(
                    there, there, sent.at[k], received.at[part, from_y, from_x],
                    device_id={"dp": side + 2 * from_y + core, "ctx": jnp.where(part == 1, pair, row) * XS + from_x},
                    device_id_type=MESH,
                ).wait_recv()

        return step

    def back_copy(part, k):
        to_y = lax.rem(y + k, 4)
        return pltpu.make_async_remote_copy(
            cross_out.at[part, to_y], cross.at[y], back_send.at[part, k], back_recv.at[y],
            device_id={"dp": y_at(side, k), "ctx": jnp.where(part == 1, pair, row) * XS + x}, device_id_type=MESH,
        )

    def own_back():
        return pltpu.make_async_copy(cross_out.at[0, y], cross.at[y], own_sem.at[QC, 1])

    def x_copy(kind, h, to):
        arg, buf = arrays[kind]
        return pltpu.make_async_remote_copy(
            arg.at[:, cols(to * LOCAL + h)], buf.at[h, x], x_send.at[kind, h, to], x_recv.at[kind, h, x],
            device_id={"dp": dp, "ctx": row * XS + to}, device_id_type=MESH,
        )

    def arrived(kind, h):
        own_copy(kind, h).wait()
        for k in range(1, XS):
            source = x_at(k)
            buf = arrays[kind][1].at[h, source]
            pltpu.make_async_remote_copy(
                buf, buf, x_send.at[kind, h, source], x_recv.at[kind, h, source],
                device_id={"dp": dp, "ctx": row * XS + source}, device_id_type=MESH,
            ).wait_recv()

    def start_x(kinds):
        def step(h):
            for k in (1, 3, 2):
                for kind in kinds:
                    x_copy(kind, h, x_at(k)).start()

        loop(0, LOCAL, step)

    def start_plane(k):
        idx_copy(k).start()
        qc_copy(k).start()

    @pl.when(edge & (dp >= HALF))
    def _():
        for kind in range(2):
            far_copy(kind).start()

    first_plane = jnp.where(inner, 0, 1)

    @pl.when(row < 2)
    def _():
        start_x((KS, VS))
        loop(first_plane, 4 * XS, start_plane)
        start_x((QS,))

    @pl.when(row >= 2)
    def _():
        start_x((QS,))
        loop(first_plane, 4 * XS, start_plane)
        start_x((KS, VS))

    @pl.when(edge)
    def _():
        for kind in range(2):
            for k in (1, 3, 2):
                y_copy(kind, 0, k).start()
            core_pass(kind, 0, 0).start()

    @pl.when(edge & first_side)
    def _():
        pl.semaphore_wait(ready, 1)
        for kind in range(2):
            far_copy(kind).start()

    def z_copy(kind, h):
        src, dst, to = {
            ZK: (ks.at[h], k0.at[h], 1),
            ZV: (vs.at[h], v0.at[h], 1),
            ZQ2: (qs.at[h], q2.at[h], 1),
            ZQ3: (qs.at[h], q3.at[h], 1),
            ZQ3B: (qs.at[h], q3.at[h], 2),
            ZO2: (part_out.at[0, h], part_in.at[0, h], 2),
            ZS2: (stat_out.at[0, h], stat_in.at[0, h], 2),
            ZO3: (part_out.at[1, h], part_in.at[0, h], 3),
            ZS3: (stat_out.at[1, h], stat_in.at[0, h], 3),
            ZO3B: (part_out.at[1, h], part_in.at[1, h], 3),
            ZS3B: (stat_out.at[1, h], stat_in.at[1, h], 3),
        }[kind]
        return pltpu.make_async_remote_copy(
            src, dst, z_send.at[kind, h], z_recv.at[kind, h],
            device_id={"dp": dp, "ctx": to * XS + x}, device_id_type=MESH,
        )

    def relay(h):
        @pl.when(row == 0)
        def _():
            arrived(KS, h)
            z_copy(ZK, h).start()
            arrived(VS, h)
            z_copy(ZV, h).start()

        @pl.when(row == 2)
        def _():
            arrived(QS, h)
            z_copy(ZQ2, h).start()

        @pl.when(row == 3)
        def _():
            arrived(QS, h)
            z_copy(ZQ3, h).start()
            z_copy(ZQ3B, h).start()

    def far_stage():
        for kind in range(2):
            far_copy(kind).wait_recv()
            for k in (1, 3, 2):
                y_copy(kind, 1, k).start()
            core_pass(kind, 1, 0).start()
            own_far(kind).start()

    def core_stage():
        for far in range(2):
            for kind in range(2):
                for k in (1, 3, 2):
                    wait_shard(kind, y_at(away if far else side, k))
                    core_pass(kind, far, k).start()

    diagonal = lax.broadcasted_iota(jnp.int32, (ROWS, ROWS), 0) >= lax.broadcasted_iota(jnp.int32, (ROWS, ROWS), 1)
    eye = lax.broadcasted_iota(jnp.int32, (TOK, TOK), 0) == lax.broadcasted_iota(jnp.int32, (TOK, TOK), 1)

    def attend(queries, h, b, chunks, slot):
        q = queries[h, pl.ds(b * PER, PER)].reshape(ROWS, HD)
        peak = None
        for j, (keys, values, c, masked) in enumerate(chunks):
            k = keys[h, pl.ds(c * PER, PER)].reshape(ROWS, HD)
            s = lax.dot_general(q, k, NT, preferred_element_type=jnp.float32)
            if masked:
                s = jnp.where(diagonal, s, -1e30)
            scores[slot, j] = s
            folded = jnp.maximum(s[:, :HD], s[:, HD:])
            peak = folded if peak is None else jnp.maximum(peak, folded)
        top = jnp.max(peak, axis=1, keepdims=True)
        total = jnp.zeros((ROWS, HD), jnp.float32)
        acc = jnp.zeros((ROWS, HD), jnp.float32)
        for j, (keys, values, c, masked) in enumerate(chunks):
            w = jnp.exp2((scores[slot, j] - top) * EXPO)
            total = total + (w[:, :HD] + w[:, HD:])
            v = values[h, pl.ds(c * PER, PER)].reshape(ROWS, HD)
            acc = acc + lax.dot_general(w.astype(jnp.bfloat16), v, NN, preferred_element_type=jnp.float32)
        return top, jnp.sum(total, axis=1, keepdims=True), acc

    def partial(queries, h, chunks, place):
        for b in range(QB):
            top, total, acc = attend(queries, h, b, chunks, b)
            part_out[place, h, pl.ds(b * PER, PER)] = (acc / total).astype(jnp.bfloat16).reshape(PER, TOK, HD)
            for p in range(PER):
                rows = slice(p * TOK, (p + 1) * TOK)
                at = b * PER + p
                stat_out[place, h, at : at + 1] = jnp.sum(jnp.where(eye, top[rows], 0.0), axis=0, keepdims=True)
                stat_out[place, h, XS + at : XS + at + 1] = jnp.sum(jnp.where(eye, total[rows], 0.0), axis=0, keepdims=True)

    def own_rows(h, extra, final):
        for b in range(QB):
            chunks = extra + [(ks, vs, c, c == b) for c in range(b + 1)]
            top, total, acc = attend(qs, h, b, chunks, b)
            at = h * QB + b
            if final:
                accs[at] = acc / total
            else:
                accs[at] = acc
                tops[at] = jnp.broadcast_to(top, (ROWS, HD))
                totals[at] = jnp.broadcast_to(total, (ROWS, HD))

    whole_own = [(ks, vs, c, False) for c in range(QB)]
    whole_first = [(k0, v0, c, False) for c in range(QB)]

    def between(h):
        @pl.when(row == 1)
        def _():
            arrived(KS, h)
            arrived(VS, h)
            z_copy(ZK, h).wait_recv()
            z_copy(ZV, h).wait_recv()
            z_copy(ZQ2, h).wait_recv()
            partial(q2, h, whole_first + whole_own, 0)
            z_copy(ZO2, h).start()
            z_copy(ZS2, h).start()
            z_copy(ZQ3, h).wait_recv()
            partial(q3, h, whole_first + whole_own, 1)
            z_copy(ZO3, h).start()
            z_copy(ZS3, h).start()
            arrived(QS, h)
            own_rows(h, whole_first, True)

        @pl.when(row == 2)
        def _():
            arrived(KS, h)
            arrived(VS, h)
            z_copy(ZQ3B, h).wait_recv()
            partial(q3, h, whole_own, 1)
            z_copy(ZO3B, h).start()
            z_copy(ZS3B, h).start()

    def own_others(h):
        @pl.when(row == 0)
        def _():
            arrived(QS, h)
            own_rows(h, [], True)

        @pl.when(row == 2)
        def _():
            own_rows(h, [], False)

        @pl.when(row == 3)
        def _():
            arrived(KS, h)
            arrived(VS, h)
            own_rows(h, [], False)

    def cross_document(part, k):
        doc = lax.rem(y + k, 4)
        for t in range(XS):
            for g in range(TOK // GROUP):
                first = idx_s[part, doc, t, 0, g * NEIGH]
                second = idx_s[part, doc, t, 0, g * NEIGH + 1]
                rows = pl.ds(g * GROUP, GROUP)
                keys = jnp.concatenate([kd[first], kd[second]], axis=0)
                values = jnp.concatenate([vd[first], vd[second]], axis=0)
                s = lax.dot_general(qc[part, doc, t, rows, :], keys, NT, preferred_element_type=jnp.float32)
                top = jnp.max(s, axis=1, keepdims=True)
                w = jnp.exp2((s - top) * EXPO)
                total = jnp.sum(w, axis=1, keepdims=True)
                o = lax.dot_general(w.astype(jnp.bfloat16), values, NN, preferred_element_type=jnp.float32)
                cross_out[part, doc, t, rows, :] = (o / total).astype(jnp.bfloat16)

        here = (part == 0) & (k == 0)

        @pl.when(jnp.logical_not(here))
        def _():
            back_copy(part, k).start()

        @pl.when(here)
        def _():
            own_back().start()

    def cross_stage():
        own_qc().wait()
        for kind in range(2):
            own_db(kind).wait()
            own_far(kind).wait()

        def wait_other_core(k):
            for kind in range(2):
                wait_shard(kind, 2 * k + 1 - core)

        loop(0, HALF, wait_other_core)

        def cross_row_of(n):
            part = 1 - n
            loop(n, 4 * XS, wait_plane(part))
            numbers = pltpu.make_async_copy(idx.at[part], idx_s.at[part], number_sem)
            numbers.start()
            numbers.wait()
            loop(0, 4, lambda k: cross_document(part, 3 - k))

        loop(0, 2, cross_row_of)

    @pl.when(row == 0)
    def _():
        relay(0)
        relay(1)
        far_stage()
        relay(2)
        relay(3)

    @pl.when(row >= 2)
    def _():
        loop(0, LOCAL, relay)

    pl.when(row == 3)(far_stage)

    @pl.when(edge)
    def _():
        core_stage()
        cross_stage()

    loop(0, LOCAL, between)
    loop(0, LOCAL, own_others)

    def merge(h, parts):
        for b in range(QB):
            at = h * QB + b
            for p in range(PER):
                rows = slice(p * TOK, (p + 1) * TOK)
                sub = b * PER + p
                top = tops[at, rows, :1]
                others = []
                for place in range(parts):
                    column = [
                        jnp.sum(jnp.where(eye, stat_in[place, h, n : n + 1], 0.0), axis=1, keepdims=True)
                        for n in (sub, XS + sub)
                    ]
                    others.append(column)
                peak = top
                for other_top, _ in others:
                    peak = jnp.maximum(peak, other_top)
                keep = jnp.exp2((top - peak) * EXPO)
                total = totals[at, rows, :1] * keep
                acc = accs[at, rows, :] * keep
                for place, (other_top, other_total) in enumerate(others):
                    w = jnp.exp2((other_top - peak) * EXPO) * other_total
                    total = total + w
                    acc = acc + part_in[place, h, sub].astype(jnp.float32) * w
                accs[at, rows, :] = acc / total

    def out_copy(h, t):
        return pltpu.make_async_remote_copy(
            mixed.at[h, t], out_ref.at[:, cols(x * LOCAL + h)], x_send.at[OUT, h, t], x_recv.at[OUT, h, x],
            device_id={"dp": dp, "ctx": row * XS + t}, device_id_type=MESH,
        )

    def own_out(h):
        return pltpu.make_async_copy(mixed.at[h, x], out_ref.at[:, cols(x * LOCAL + h)], own_sem.at[OUT, h])

    def emit(h):
        @pl.when(row == 2)
        def _():
            z_copy(ZO2, h).wait_recv()
            z_copy(ZS2, h).wait_recv()
            merge(h, 1)

        @pl.when(row == 3)
        def _():
            z_copy(ZO3, h).wait_recv()
            z_copy(ZS3, h).wait_recv()
            z_copy(ZO3B, h).wait_recv()
            z_copy(ZS3B, h).wait_recv()
            merge(h, 2)

        @pl.when((h != y) | inner)
        def _():
            there = cross.at[h]
            pltpu.make_async_remote_copy(
                there, there, back_send.at[0, 0], back_recv.at[h],
                device_id={"dp": side + 2 * h + core, "ctx": cross_row * XS + x}, device_id_type=MESH,
            ).wait_recv()

        @pl.when((h == y) & edge)
        def _():
            own_back().wait()

        self_out = accs[pl.ds(h * QB, QB)].astype(jnp.bfloat16).astype(jnp.float32).reshape(XS, TOK, HD)
        mixed[h] = (self_out + cross[h].astype(jnp.float32)).astype(jnp.bfloat16)
        for k in (1, 3, 2):
            out_copy(h, x_at(k)).start()
        own_out(h).start()

    loop(0, LOCAL, emit)

    def finish(h):
        own_out(h).wait()
        for k in range(1, XS):
            peer = x_at(k)
            pltpu.make_async_remote_copy(
                mixed.at[h, peer], out_ref.at[:, cols(peer * LOCAL + h)], x_send.at[OUT, h, peer], x_recv.at[OUT, h, peer],
                device_id={"dp": dp, "ctx": row * XS + peer}, device_id_type=MESH,
            ).wait_recv()
            for kind in (KS, VS, QS):
                x_copy(kind, h, peer).wait_send()
            out_copy(h, peer).wait_send()
        for at, kinds in enumerate(((ZK, ZV), (ZO2, ZS2, ZO3, ZS3), (ZQ2, ZO3B, ZS3B), (ZQ3, ZQ3B))):

            @pl.when(row == at)
            def _():
                for kind in kinds:
                    z_copy(kind, h).wait_send()

    @pl.when(edge)
    def _():
        for kind in range(2):
            far_copy(kind).wait_send()
            for far in range(2):
                for k in range(1, 4):
                    y_copy(kind, far, k).wait_send()
                for k in range(4):
                    core_pass(kind, far, k).wait_send()
        for k in range(1, 4):
            back_copy(0, k).wait_send()
        for k in range(4):
            back_copy(1, k).wait_send()

    def finish_plane(k):
        idx_copy(k).wait_send()
        qc_copy(k).wait_send()

    loop(first_plane, 4 * XS, finish_plane)
    loop(0, LOCAL, finish)


def shards(q_self, k_self, v_self, q_cross, db_keys, db_values, nb_shard, nb_row):
    anywhere = pl.BlockSpec(memory_space=pl.ANY)
    scalars = pl.BlockSpec(memory_space=pltpu.SMEM)
    heads = pltpu.VMEM((LOCAL, XS, TOK, HD), jnp.bfloat16)
    database = pltpu.VMEM((N_DP * DB_DEV, NLEN, HD), jnp.bfloat16)
    shard = pltpu.VMEM((DB_DEV, NLEN, WIDE), jnp.bfloat16)
    state = pltpu.VMEM((LOCAL * QB, ROWS, HD), jnp.float32)
    parts = pltpu.VMEM((2, LOCAL, XS, TOK, HD), jnp.bfloat16)
    stats = pltpu.VMEM((2, LOCAL, 8, 128), jnp.float32)
    dma = pltpu.SemaphoreType.DMA
    out = pl.pallas_call(
        kernel,
        out_shape=jax.ShapeDtypeStruct((TOK, HEADS * HD), jnp.bfloat16),
        in_specs=[anywhere] * 6 + [scalars] * 2,
        out_specs=anywhere,
        scratch_shapes=[
            heads, heads, heads, parts, heads, heads, heads, heads, database, database,
            pltpu.VMEM((2, 4, XS, 8, 128), jnp.int32),
            pltpu.SMEM((2, 4, XS, 8, 128), jnp.int32),
            heads,
            pltpu.VMEM((2, 2 * QB, ROWS, ROWS), jnp.float32),
            state, state, state,
            parts, stats, parts, stats, heads, parts, shard, shard,
            dma((5, LOCAL, XS)), dma((5, LOCAL, XS)), dma((4 * XS,)), dma((2, 4, XS)), dma((4 * XS,)), dma((2, 4, XS)),
            dma((2, 4)), dma((4,)), dma((11, LOCAL)), dma((11, LOCAL)),
            dma((2,)), dma((2,)), dma((2, 2, 4)), dma((2, 2, 4)), dma((2, N_DP)), dma((5, LOCAL)), dma((4,)), dma,
            pltpu.SemaphoreType.REGULAR,
        ],
        compiler_params=pltpu.CompilerParams(
            collective_id=0, has_side_effects=True, vmem_limit_bytes=60 * 1024 * 1024
        ),
    )(q_self[0], k_self[0], v_self[0], q_cross[0], db_keys, db_values, nb_shard, nb_row)
    return out[None]


def solution(mesh):
    return jax.shard_map(
        shards,
        mesh=mesh,
        in_specs=(
            P("dp", "ctx", None),
            P("dp", "ctx", None),
            P("dp", "ctx", None),
            P("dp", "ctx", None),
            P("dp", None, None),
            P("dp", None, None),
            P("dp", "ctx", None),
            P("dp", "ctx", None),
        ),
        out_specs=P("dp", "ctx", None),
        check_vma=False,
    )
```

```python
import jax
import jax.numpy as jnp
from jax import lax
from jax.experimental import pallas as pl
from jax.experimental.pallas import tpu as pltpu
from jax.sharding import PartitionSpec as P

HEADS = 16
HD = 128
GROUP = 64
NEIGH = 2
NLEN = 128
TOK = 128
DB_DEV = 2
N_DP = 16
HALF = 8
XS = 4
LOCAL = HEADS // XS
WIDE = LOCAL * HD
ROWS = 256
PER = ROWS // TOK
QB = XS // PER
EXPO = HD**-0.5 * 1.4426950408889634
MESH = pl.DeviceIdType.MESH
NT = (((1,), (1,)), ((), ()))
NN = (((1,), (0,)), ((), ()))
QC, KS, VS, QS, OUT = range(5)
ZK, ZV, ZQ2, ZQ3, ZQ3B, ZO2, ZS2, ZO3, ZS3, ZO3B, ZS3B = range(11)


def cols(head):
    return pl.ds(pl.multiple_of(head * HD, HD), HD)


def kernel(
    qs_ref, ks_ref, vs_ref, qc_ref, kd_ref, vd_ref, shard_ref, row_ref, out_ref,
    qs, ks, vs, qc, k0, v0, q2, q3, kd, vd, idx, idx_s, cross, scores, tops, totals, accs,
    part_out, stat_out, part_in, stat_in, mixed, cross_out, kf, vf,
    x_send, x_recv, qc_send, qc_recv, idx_send, idx_recv, back_send, back_recv, z_send, z_recv,
    far_send, far_recv, y_send, core_send, db_recv, own_sem, db_own, number_sem, ready,
):
    dp = lax.axis_index("dp")
    me = lax.axis_index("ctx")
    row = me // XS
    x = lax.rem(me, XS)
    near = lax.rem(dp, HALF)
    side = dp - near
    away = HALF - side
    y = near // 2
    core = lax.rem(near, 2)
    other_core = dp + 1 - 2 * core
    far_dp = away + near
    far_ctx = (3 - row) * XS + x
    edge = (row == 0) | (row == 3)
    first_side = dp < HALF
    inner = (row == 1) | (row == 2)
    pair = row + 1 - 2 * lax.rem(row, 2)
    cross_row = jnp.where(inner, pair, row)
    cross_part = jnp.where(inner, 1, 0)

    def x_at(k):
        return lax.rem(x + k, XS)

    def y_at(home, k):
        return home + lax.rem(near + 2 * k, HALF)

    def loop(first, last, body):
        def step(k, carry):
            body(k)
            return carry

        lax.fori_loop(first, last, step, 0)

    barrier = pltpu.get_barrier_semaphore()

    def greet(dp_of, ctx_of):
        pl.semaphore_signal(barrier, inc=1, device_id={"dp": dp_of, "ctx": ctx_of}, device_id_type=MESH)

    def plane(k):
        return lax.rem(y + k // XS, 4), x_at(lax.rem(k, XS))

    def greet_plane(of_row):
        def step(k):
            to_y, to_x = plane(k)
            greet(side + 2 * to_y + core, of_row * XS + to_x)

        return step

    loop(1, jnp.where(edge, 4 * XS, XS), greet_plane(row))
    loop(1, 4 * XS, greet_plane(pair))
    for k in range(1, 4):
        greet(dp, lax.rem(row + k, 4) * XS + x)

    @pl.when(edge)
    def _():
        greet(other_core, me)

    @pl.when(edge & first_side)
    def _():
        greet(far_dp, far_ctx)

    lane = lax.broadcasted_iota(jnp.int32, (8, 128), 1)
    tile = jnp.zeros((8, 128), jnp.int32)
    for g in range(TOK // GROUP):
        for n in range(NEIGH):
            block = shard_ref[0, g, n] * DB_DEV + row_ref[0, g, n]
            tile = jnp.where(lane == g * NEIGH + n, block, tile)
    idx[cross_part, y, x] = tile

    arrays = {KS: (ks_ref, ks), VS: (vs_ref, vs), QS: (qs_ref, qs)}
    blocks = ((kd_ref, kd, kf), (vd_ref, vd, vf))
    wide = pl.ds(pl.multiple_of(x * WIDE, WIDE), WIDE)
    head = x * LOCAL + y

    def own_copy(kind, h):
        arg, buf = arrays[kind]
        return pltpu.make_async_copy(arg.at[:, cols(x * LOCAL + h)], buf.at[h, x], own_sem.at[kind, h])

    def own_qc():
        return pltpu.make_async_copy(qc_ref.at[:, cols(head)], qc.at[0, y, x], own_sem.at[QC, 0])

    def own_db(kind):
        arg, buf, far = blocks[kind]
        return pltpu.make_async_copy(arg.at[:, :, cols(head)], buf.at[pl.ds(dp * DB_DEV, DB_DEV)], db_own.at[kind])

    def own_far(kind):
        arg, buf, far = blocks[kind]
        return pltpu.make_async_copy(far.at[:, :, cols(y)], buf.at[pl.ds(far_dp * DB_DEV, DB_DEV)], db_own.at[2 + kind])

    def start_own(h):
        for kind in (KS, VS, QS):
            own_copy(kind, h).start()

    loop(0, LOCAL, start_own)

    @pl.when(edge)
    def _():
        own_qc().start()
        for kind in range(2):
            own_db(kind).start()

    pl.semaphore_wait(barrier, 21 + jnp.where(edge, 13, 0) + jnp.where(edge & (dp >= HALF), 1, 0))

    @pl.when(edge & (dp >= HALF))
    def _():
        pl.semaphore_signal(ready, inc=1, device_id={"dp": far_dp, "ctx": far_ctx}, device_id_type=MESH)

    def far_copy(kind):
        arg, buf, far = blocks[kind]
        return pltpu.make_async_remote_copy(
            arg.at[:, :, wide], far, far_send.at[kind], far_recv.at[kind],
            device_id={"dp": far_dp, "ctx": far_ctx}, device_id_type=MESH,
        )

    def shard_copy(kind, shard, src, send, target):
        part = blocks[kind][1].at[pl.ds(shard * DB_DEV, DB_DEV)]
        return pltpu.make_async_remote_copy(
            part if src is None else src, part, send, db_recv.at[kind, shard],
            device_id={"dp": target, "ctx": me}, device_id_type=MESH,
        )

    def y_copy(kind, far, k):
        to_y = lax.rem(y + k, 4)
        src = blocks[kind][2].at[:, :, cols(to_y)] if far else blocks[kind][0].at[:, :, cols(x * LOCAL + to_y)]
        return shard_copy(kind, far_dp if far else dp, src, y_send.at[kind, far, k], y_at(side, k))

    def core_pass(kind, far, k):
        src = None
        if k == 0:
            src = blocks[kind][2].at[:, :, cols(y)] if far else blocks[kind][0].at[:, :, cols(head)]
        return shard_copy(kind, y_at(away if far else side, k), src, core_send.at[kind, far, k], other_core)

    def wait_shard(kind, shard):
        shard_copy(kind, shard, None, far_send.at[kind], other_core).wait_recv()

    def qc_copy(k):
        to_y, to_x = plane(k)
        return pltpu.make_async_remote_copy(
            qc_ref.at[:, cols(to_x * LOCAL + to_y)], qc.at[cross_part, y, x], qc_send.at[k], qc_recv.at[cross_part, y, x],
            device_id={"dp": side + 2 * to_y + core, "ctx": cross_row * XS + to_x}, device_id_type=MESH,
        )

    def idx_copy(k):
        to_y, to_x = plane(k)
        return pltpu.make_async_remote_copy(
            idx.at[cross_part, y, x], idx.at[cross_part, y, x], idx_send.at[k], idx_recv.at[cross_part, y, x],
            device_id={"dp": side + 2 * to_y + core, "ctx": cross_row * XS + to_x}, device_id_type=MESH,
        )

    def wait_plane(part):
        def step(k):
            from_y, from_x = plane(k)
            for buf, sent, received in ((idx, idx_send, idx_recv), (qc, qc_send, qc_recv)):
                there = buf.at[part, from_y, from_x]
                pltpu.make_async_remote_copy(
                    there, there, sent.at[k], received.at[part, from_y, from_x],
                    device_id={"dp": side + 2 * from_y + core, "ctx": jnp.where(part == 1, pair, row) * XS + from_x},
                    device_id_type=MESH,
                ).wait_recv()

        return step

    def back_copy(part, k):
        to_y = lax.rem(y + k, 4)
        return pltpu.make_async_remote_copy(
            cross_out.at[part, to_y], cross.at[y], back_send.at[part, k], back_recv.at[y],
            device_id={"dp": y_at(side, k), "ctx": jnp.where(part == 1, pair, row) * XS + x}, device_id_type=MESH,
        )

    def own_back():
        return pltpu.make_async_copy(cross_out.at[0, y], cross.at[y], own_sem.at[QC, 1])

    def x_copy(kind, h, to):
        arg, buf = arrays[kind]
        return pltpu.make_async_remote_copy(
            arg.at[:, cols(to * LOCAL + h)], buf.at[h, x], x_send.at[kind, h, to], x_recv.at[kind, h, x],
            device_id={"dp": dp, "ctx": row * XS + to}, device_id_type=MESH,
        )

    def arrived(kind, h):
        own_copy(kind, h).wait()
        for k in range(1, XS):
            source = x_at(k)
            buf = arrays[kind][1].at[h, source]
            pltpu.make_async_remote_copy(
                buf, buf, x_send.at[kind, h, source], x_recv.at[kind, h, source],
                device_id={"dp": dp, "ctx": row * XS + source}, device_id_type=MESH,
            ).wait_recv()

    def start_x(kinds):
        def step(h):
            for k in (1, 3, 2):
                for kind in kinds:
                    x_copy(kind, h, x_at(k)).start()

        loop(0, LOCAL, step)

    def start_plane(k):
        idx_copy(k).start()
        qc_copy(k).start()

    @pl.when(edge & (dp >= HALF))
    def _():
        for kind in range(2):
            far_copy(kind).start()

    first_plane = jnp.where(inner, 0, 1)

    @pl.when(row < 2)
    def _():
        start_x((KS, VS))
        loop(first_plane, 4 * XS, start_plane)
        start_x((QS,))

    @pl.when(row >= 2)
    def _():
        start_x((QS,))
        loop(first_plane, 4 * XS, start_plane)
        start_x((KS, VS))

    @pl.when(edge)
    def _():
        for kind in range(2):
            for k in (1, 3, 2):
                y_copy(kind, 0, k).start()
            core_pass(kind, 0, 0).start()

    @pl.when(edge & first_side)
    def _():
        pl.semaphore_wait(ready, 1)
        for kind in range(2):
            far_copy(kind).start()

    def z_copy(kind, h):
        src, dst, to = {
            ZK: (ks.at[h], k0.at[h], 1),
            ZV: (vs.at[h], v0.at[h], 1),
            ZQ2: (qs.at[h], q2.at[h], 1),
            ZQ3: (qs.at[h], q3.at[h], 1),
            ZQ3B: (qs.at[h], q3.at[h], 2),
            ZO2: (part_out.at[0, h], part_in.at[0, h], 2),
            ZS2: (stat_out.at[0, h], stat_in.at[0, h], 2),
            ZO3: (part_out.at[1, h], part_in.at[0, h], 3),
            ZS3: (stat_out.at[1, h], stat_in.at[0, h], 3),
            ZO3B: (part_out.at[1, h], part_in.at[1, h], 3),
            ZS3B: (stat_out.at[1, h], stat_in.at[1, h], 3),
        }[kind]
        return pltpu.make_async_remote_copy(
            src, dst, z_send.at[kind, h], z_recv.at[kind, h],
            device_id={"dp": dp, "ctx": to * XS + x}, device_id_type=MESH,
        )

    def relay(h):
        @pl.when(row == 0)
        def _():
            arrived(KS, h)
            z_copy(ZK, h).start()
            arrived(VS, h)
            z_copy(ZV, h).start()

        @pl.when(row == 2)
        def _():
            arrived(QS, h)
            z_copy(ZQ2, h).start()

        @pl.when(row == 3)
        def _():
            arrived(QS, h)
            z_copy(ZQ3, h).start()
            z_copy(ZQ3B, h).start()

    def far_stage():
        for kind in range(2):
            far_copy(kind).wait_recv()
            for k in (1, 3, 2):
                y_copy(kind, 1, k).start()
            core_pass(kind, 1, 0).start()
            own_far(kind).start()

    def core_stage():
        for far in range(2):
            for kind in range(2):
                for k in (1, 3, 2):
                    wait_shard(kind, y_at(away if far else side, k))
                    core_pass(kind, far, k).start()

    diagonal = lax.broadcasted_iota(jnp.int32, (ROWS, ROWS), 0) >= lax.broadcasted_iota(jnp.int32, (ROWS, ROWS), 1)
    eye = lax.broadcasted_iota(jnp.int32, (TOK, TOK), 0) == lax.broadcasted_iota(jnp.int32, (TOK, TOK), 1)

    def score_block(queries, h, b, chunks, slot):
        q = queries[h, pl.ds(b * PER, PER)].reshape(ROWS, HD)
        peak = None
        for j, (keys, values, c, masked) in enumerate(chunks):
            k = keys[h, pl.ds(c * PER, PER)].reshape(ROWS, HD)
            s = lax.dot_general(q, k, NT, preferred_element_type=jnp.float32)
            if masked:
                s = jnp.where(diagonal, s, -1e30)
            scores[slot, j] = s
            folded = jnp.maximum(s[:, :HD], s[:, HD:])
            peak = folded if peak is None else jnp.maximum(peak, folded)
        return jnp.max(peak, axis=1, keepdims=True)

    def weigh_block(h, chunks, slot, top):
        total = jnp.zeros((ROWS, HD), jnp.float32)
        acc = jnp.zeros((ROWS, HD), jnp.float32)
        for j, (keys, values, c, masked) in enumerate(chunks):
            w = jnp.exp2((scores[slot, j] - top) * EXPO)
            total = total + (w[:, :HD] + w[:, HD:])
            v = values[h, pl.ds(c * PER, PER)].reshape(ROWS, HD)
            acc = acc + lax.dot_general(w.astype(jnp.bfloat16), v, NN, preferred_element_type=jnp.float32)
        return jnp.sum(total, axis=1, keepdims=True), acc

    def attend(h, jobs):
        tops_of = []
        for n in range(len(jobs) + 1):
            if n < len(jobs):
                queries, b, chunks, done = jobs[n]
                tops_of.append(score_block(queries, h, b, chunks, n % 3))
            if n >= 1:
                queries, b, chunks, done = jobs[n - 1]
                done(b, tops_of[n - 1], *weigh_block(h, chunks, (n - 1) % 3, tops_of[n - 1]))

    def partial(queries, h, chunks, place):
        def done(b, top, total, acc):
            part_out[place, h, pl.ds(b * PER, PER)] = (acc / total).astype(jnp.bfloat16).reshape(PER, TOK, HD)
            for p in range(PER):
                rows = slice(p * TOK, (p + 1) * TOK)
                at = b * PER + p
                stat_out[place, h, at : at + 1] = jnp.sum(jnp.where(eye, top[rows], 0.0), axis=0, keepdims=True)
                stat_out[place, h, XS + at : XS + at + 1] = jnp.sum(jnp.where(eye, total[rows], 0.0), axis=0, keepdims=True)

        return [(queries, b, chunks, done) for b in range(QB)]

    def own_rows(h, extra, final):
        def done(b, top, total, acc):
            at = h * QB + b
            if final:
                accs[at] = acc / total
            else:
                accs[at] = acc
                tops[at] = jnp.broadcast_to(top, (ROWS, HD))
                totals[at] = jnp.broadcast_to(total, (ROWS, HD))

        return [(qs, b, extra + [(ks, vs, c, c == b) for c in range(b + 1)], done) for b in range(QB)]

    whole_own = [(ks, vs, c, False) for c in range(QB)]
    whole_first = [(k0, v0, c, False) for c in range(QB)]

    def between(h):
        @pl.when(row == 1)
        def _():
            arrived(KS, h)
            arrived(VS, h)
            z_copy(ZK, h).wait_recv()
            z_copy(ZV, h).wait_recv()
            z_copy(ZQ2, h).wait_recv()
            z_copy(ZQ3, h).wait_recv()
            attend(h, partial(q2, h, whole_first + whole_own, 0) + partial(q3, h, whole_first + whole_own, 1))
            z_copy(ZO2, h).start()
            z_copy(ZS2, h).start()
            z_copy(ZO3, h).start()
            z_copy(ZS3, h).start()
            arrived(QS, h)
            attend(h, own_rows(h, whole_first, True))

        @pl.when(row == 2)
        def _():
            arrived(KS, h)
            arrived(VS, h)
            z_copy(ZQ3B, h).wait_recv()
            attend(h, partial(q3, h, whole_own, 1))
            z_copy(ZO3B, h).start()
            z_copy(ZS3B, h).start()

    def own_others(h):
        @pl.when(row == 0)
        def _():
            arrived(QS, h)
            attend(h, own_rows(h, [], True))

        @pl.when(row == 2)
        def _():
            attend(h, own_rows(h, [], False))

        @pl.when(row == 3)
        def _():
            arrived(KS, h)
            arrived(VS, h)
            attend(h, own_rows(h, [], False))

    def cross_document(part, k):
        doc = lax.rem(y + k, 4)
        groups = [(t, g) for t in range(XS) for g in range(TOK // GROUP)]
        picks = [[idx_s[part, doc, t, 0, g * NEIGH + n] for n in range(NEIGH)] for t, g in groups]
        s = []
        for (t, g), pick in zip(groups, picks):
            keys = jnp.concatenate([kd[block] for block in pick], axis=0)
            q = qc[part, doc, t, pl.ds(g * GROUP, GROUP), :]
            s.append(lax.dot_general(q, keys, NT, preferred_element_type=jnp.float32))
        top = [jnp.max(one, axis=1, keepdims=True) for one in s]
        w = [jnp.exp2((one - high) * EXPO) for one, high in zip(s, top)]
        total = [jnp.sum(one, axis=1, keepdims=True) for one in w]
        o = []
        for one, pick in zip(w, picks):
            values = jnp.concatenate([vd[block] for block in pick], axis=0)
            o.append(lax.dot_general(one.astype(jnp.bfloat16), values, NN, preferred_element_type=jnp.float32))
        for (t, g), one, whole in zip(groups, o, total):
            cross_out[part, doc, t, pl.ds(g * GROUP, GROUP), :] = (one / whole).astype(jnp.bfloat16)

        here = (part == 0) & (k == 0)

        @pl.when(jnp.logical_not(here))
        def _():
            back_copy(part, k).start()

        @pl.when(here)
        def _():
            own_back().start()

    def cross_stage():
        own_qc().wait()
        for kind in range(2):
            own_db(kind).wait()
            own_far(kind).wait()

        def wait_other_core(k):
            for kind in range(2):
                wait_shard(kind, 2 * k + 1 - core)

        loop(0, HALF, wait_other_core)

        def cross_row_of(n):
            part = 1 - n
            loop(n, 4 * XS, wait_plane(part))
            numbers = pltpu.make_async_copy(idx.at[part], idx_s.at[part], number_sem)
            numbers.start()
            numbers.wait()
            loop(0, 4, lambda k: cross_document(part, 3 - k))

        loop(0, 2, cross_row_of)

    @pl.when(row == 0)
    def _():
        relay(0)
        relay(1)
        far_stage()
        relay(2)
        relay(3)

    @pl.when(row >= 2)
    def _():
        loop(0, LOCAL, relay)

    pl.when(row == 3)(far_stage)

    @pl.when(edge)
    def _():
        core_stage()
        cross_stage()

    loop(0, LOCAL, between)
    loop(0, LOCAL, own_others)

    def merge(h, parts):
        for b in range(QB):
            at = h * QB + b
            for p in range(PER):
                rows = slice(p * TOK, (p + 1) * TOK)
                sub = b * PER + p
                top = tops[at, rows, :1]
                others = []
                for place in range(parts):
                    column = [
                        jnp.sum(jnp.where(eye, stat_in[place, h, n : n + 1], 0.0), axis=1, keepdims=True)
                        for n in (sub, XS + sub)
                    ]
                    others.append(column)
                peak = top
                for other_top, _ in others:
                    peak = jnp.maximum(peak, other_top)
                keep = jnp.exp2((top - peak) * EXPO)
                total = totals[at, rows, :1] * keep
                acc = accs[at, rows, :] * keep
                for place, (other_top, other_total) in enumerate(others):
                    w = jnp.exp2((other_top - peak) * EXPO) * other_total
                    total = total + w
                    acc = acc + part_in[place, h, sub].astype(jnp.float32) * w
                accs[at, rows, :] = acc / total

    def out_copy(h, t):
        return pltpu.make_async_remote_copy(
            mixed.at[h, t], out_ref.at[:, cols(x * LOCAL + h)], x_send.at[OUT, h, t], x_recv.at[OUT, h, x],
            device_id={"dp": dp, "ctx": row * XS + t}, device_id_type=MESH,
        )

    def own_out(h):
        return pltpu.make_async_copy(mixed.at[h, x], out_ref.at[:, cols(x * LOCAL + h)], own_sem.at[OUT, h])

    def emit(h):
        @pl.when(row == 2)
        def _():
            z_copy(ZO2, h).wait_recv()
            z_copy(ZS2, h).wait_recv()
            merge(h, 1)

        @pl.when(row == 3)
        def _():
            z_copy(ZO3, h).wait_recv()
            z_copy(ZS3, h).wait_recv()
            z_copy(ZO3B, h).wait_recv()
            z_copy(ZS3B, h).wait_recv()
            merge(h, 2)

        @pl.when((h != y) | inner)
        def _():
            there = cross.at[h]
            pltpu.make_async_remote_copy(
                there, there, back_send.at[0, 0], back_recv.at[h],
                device_id={"dp": side + 2 * h + core, "ctx": cross_row * XS + x}, device_id_type=MESH,
            ).wait_recv()

        @pl.when((h == y) & edge)
        def _():
            own_back().wait()

        self_out = accs[pl.ds(h * QB, QB)].astype(jnp.bfloat16).astype(jnp.float32).reshape(XS, TOK, HD)
        mixed[h] = (self_out + cross[h].astype(jnp.float32)).astype(jnp.bfloat16)
        for k in (1, 3, 2):
            out_copy(h, x_at(k)).start()
        own_out(h).start()

    loop(0, LOCAL, emit)

    def finish(h):
        own_out(h).wait()
        for k in range(1, XS):
            peer = x_at(k)
            pltpu.make_async_remote_copy(
                mixed.at[h, peer], out_ref.at[:, cols(peer * LOCAL + h)], x_send.at[OUT, h, peer], x_recv.at[OUT, h, peer],
                device_id={"dp": dp, "ctx": row * XS + peer}, device_id_type=MESH,
            ).wait_recv()
            for kind in (KS, VS, QS):
                x_copy(kind, h, peer).wait_send()
            out_copy(h, peer).wait_send()
        for at, kinds in enumerate(((ZK, ZV), (ZO2, ZS2, ZO3, ZS3), (ZQ2, ZO3B, ZS3B), (ZQ3, ZQ3B))):

            @pl.when(row == at)
            def _():
                for kind in kinds:
                    z_copy(kind, h).wait_send()

    @pl.when(edge)
    def _():
        for kind in range(2):
            far_copy(kind).wait_send()
            for far in range(2):
                for k in range(1, 4):
                    y_copy(kind, far, k).wait_send()
                for k in range(4):
                    core_pass(kind, far, k).wait_send()
        for k in range(1, 4):
            back_copy(0, k).wait_send()
        for k in range(4):
            back_copy(1, k).wait_send()

    def finish_plane(k):
        idx_copy(k).wait_send()
        qc_copy(k).wait_send()

    loop(first_plane, 4 * XS, finish_plane)
    loop(0, LOCAL, finish)


def shards(q_self, k_self, v_self, q_cross, db_keys, db_values, nb_shard, nb_row):
    anywhere = pl.BlockSpec(memory_space=pl.ANY)
    scalars = pl.BlockSpec(memory_space=pltpu.SMEM)
    heads = pltpu.VMEM((LOCAL, XS, TOK, HD), jnp.bfloat16)
    database = pltpu.VMEM((N_DP * DB_DEV, NLEN, HD), jnp.bfloat16)
    shard = pltpu.VMEM((DB_DEV, NLEN, WIDE), jnp.bfloat16)
    state = pltpu.VMEM((LOCAL * QB, ROWS, HD), jnp.float32)
    parts = pltpu.VMEM((2, LOCAL, XS, TOK, HD), jnp.bfloat16)
    stats = pltpu.VMEM((2, LOCAL, 8, 128), jnp.float32)
    dma = pltpu.SemaphoreType.DMA
    out = pl.pallas_call(
        kernel,
        out_shape=jax.ShapeDtypeStruct((TOK, HEADS * HD), jnp.bfloat16),
        in_specs=[anywhere] * 6 + [scalars] * 2,
        out_specs=anywhere,
        scratch_shapes=[
            heads, heads, heads, parts, heads, heads, heads, heads, database, database,
            pltpu.VMEM((2, 4, XS, 8, 128), jnp.int32),
            pltpu.SMEM((2, 4, XS, 8, 128), jnp.int32),
            heads,
            pltpu.VMEM((3, 2 * QB, ROWS, ROWS), jnp.float32),
            state, state, state,
            parts, stats, parts, stats, heads, parts, shard, shard,
            dma((5, LOCAL, XS)), dma((5, LOCAL, XS)), dma((4 * XS,)), dma((2, 4, XS)), dma((4 * XS,)), dma((2, 4, XS)),
            dma((2, 4)), dma((4,)), dma((11, LOCAL)), dma((11, LOCAL)),
            dma((2,)), dma((2,)), dma((2, 2, 4)), dma((2, 2, 4)), dma((2, N_DP)), dma((5, LOCAL)), dma((4,)), dma,
            pltpu.SemaphoreType.REGULAR,
        ],
        compiler_params=pltpu.CompilerParams(
            collective_id=0, has_side_effects=True, vmem_limit_bytes=60 * 1024 * 1024
        ),
    )(q_self[0], k_self[0], v_self[0], q_cross[0], db_keys, db_values, nb_shard, nb_row)
    return out[None]


def solution(mesh):
    return jax.shard_map(
        shards,
        mesh=mesh,
        in_specs=(
            P("dp", "ctx", None),
            P("dp", "ctx", None),
            P("dp", "ctx", None),
            P("dp", "ctx", None),
            P("dp", None, None),
            P("dp", None, None),
            P("dp", "ctx", None),
            P("dp", "ctx", None),
        ),
        out_specs=P("dp", "ctx", None),
        check_vma=False,
    )
```

```python
import jax
import jax.numpy as jnp
from jax import lax
from jax.experimental import pallas as pl
from jax.experimental.pallas import tpu as pltpu
from jax.sharding import PartitionSpec as P

HEADS = 16
HD = 128
GROUP = 64
NEIGH = 2
NLEN = 128
TOK = 128
DB_DEV = 2
N_DP = 16
HALF = 8
XS = 4
LOCAL = HEADS // XS
WIDE = LOCAL * HD
ROWS = 256
PER = ROWS // TOK
QB = XS // PER
EXPO = HD**-0.5 * 1.4426950408889634
MESH = pl.DeviceIdType.MESH
NT = (((1,), (1,)), ((), ()))
NN = (((1,), (0,)), ((), ()))
QC, KS, VS, QS, OUT = range(5)
ZK, ZV, ZQ2, ZQ3, ZQ3B, ZO2, ZS2, ZO3, ZS3, ZO3B, ZS3B = range(11)


def cols(head):
    return pl.ds(pl.multiple_of(head * HD, HD), HD)


def kernel(
    qs_ref, ks_ref, vs_ref, qc_ref, kd_ref, vd_ref, shard_ref, row_ref, out_ref,
    qs, ks, vs, qc, k0, v0, q2, q3, kd, vd, idx, idx_s, cross, scores, tops, totals, accs,
    part_out, stat_out, part_in, stat_in, mixed, cross_out, kf, vf,
    x_send, x_recv, qc_send, qc_recv, idx_send, idx_recv, back_send, back_recv, z_send, z_recv,
    far_send, far_recv, y_send, core_send, db_recv, own_sem, db_own, number_sem, ready,
):
    dp = lax.axis_index("dp")
    me = lax.axis_index("ctx")
    row = me // XS
    x = lax.rem(me, XS)
    near = lax.rem(dp, HALF)
    side = dp - near
    away = HALF - side
    y = near // 2
    core = lax.rem(near, 2)
    other_core = dp + 1 - 2 * core
    far_dp = away + near
    far_ctx = (3 - row) * XS + x
    edge = (row == 0) | (row == 3)
    first_side = dp < HALF
    inner = (row == 1) | (row == 2)
    pair = row + 1 - 2 * lax.rem(row, 2)
    cross_row = jnp.where(inner, pair, row)
    cross_part = jnp.where(inner, 1, 0)

    def x_at(k):
        return lax.rem(x + k, XS)

    def y_at(home, k):
        return home + lax.rem(near + 2 * k, HALF)

    def loop(first, last, body):
        def step(k, carry):
            body(k)
            return carry

        lax.fori_loop(first, last, step, 0)

    barrier = pltpu.get_barrier_semaphore()

    def greet(dp_of, ctx_of):
        pl.semaphore_signal(barrier, inc=1, device_id={"dp": dp_of, "ctx": ctx_of}, device_id_type=MESH)

    def plane(k):
        return lax.rem(y + k // XS, 4), x_at(lax.rem(k, XS))

    def greet_plane(of_row):
        def step(k):
            to_y, to_x = plane(k)
            greet(side + 2 * to_y + core, of_row * XS + to_x)

        return step

    loop(1, jnp.where(edge, 4 * XS, XS), greet_plane(row))
    loop(1, 4 * XS, greet_plane(pair))
    for k in range(1, 4):
        greet(dp, lax.rem(row + k, 4) * XS + x)

    @pl.when(edge)
    def _():
        greet(other_core, me)

    @pl.when(edge & first_side)
    def _():
        greet(far_dp, far_ctx)

    lane = lax.broadcasted_iota(jnp.int32, (8, 128), 1)
    tile = jnp.zeros((8, 128), jnp.int32)
    for g in range(TOK // GROUP):
        for n in range(NEIGH):
            block = shard_ref[0, g, n] * DB_DEV + row_ref[0, g, n]
            tile = jnp.where(lane == g * NEIGH + n, block, tile)
    idx[cross_part, y, x] = tile

    arrays = {KS: (ks_ref, ks), VS: (vs_ref, vs), QS: (qs_ref, qs)}
    blocks = ((kd_ref, kd, kf), (vd_ref, vd, vf))
    wide = pl.ds(pl.multiple_of(x * WIDE, WIDE), WIDE)
    head = x * LOCAL + y

    def own_copy(kind, h):
        arg, buf = arrays[kind]
        return pltpu.make_async_copy(arg.at[:, cols(x * LOCAL + h)], buf.at[h, x], own_sem.at[kind, h])

    def own_qc():
        return pltpu.make_async_copy(qc_ref.at[:, cols(head)], qc.at[0, y, x], own_sem.at[QC, 0])

    def own_db(kind):
        arg, buf, far = blocks[kind]
        return pltpu.make_async_copy(arg.at[:, :, cols(head)], buf.at[pl.ds(dp * DB_DEV, DB_DEV)], db_own.at[kind])

    def own_far(kind):
        arg, buf, far = blocks[kind]
        return pltpu.make_async_copy(far.at[:, :, cols(y)], buf.at[pl.ds(far_dp * DB_DEV, DB_DEV)], db_own.at[2 + kind])

    def start_own(h):
        for kind in (KS, VS, QS):
            own_copy(kind, h).start()

    loop(0, LOCAL, start_own)

    @pl.when(edge)
    def _():
        own_qc().start()
        for kind in range(2):
            own_db(kind).start()

    pl.semaphore_wait(barrier, 21 + jnp.where(edge, 13, 0) + jnp.where(edge & (dp >= HALF), 1, 0))

    @pl.when(edge & (dp >= HALF))
    def _():
        pl.semaphore_signal(ready, inc=1, device_id={"dp": far_dp, "ctx": far_ctx}, device_id_type=MESH)

    def far_copy(kind):
        arg, buf, far = blocks[kind]
        return pltpu.make_async_remote_copy(
            arg.at[:, :, wide], far, far_send.at[kind], far_recv.at[kind],
            device_id={"dp": far_dp, "ctx": far_ctx}, device_id_type=MESH,
        )

    def shard_copy(kind, shard, src, send, target):
        part = blocks[kind][1].at[pl.ds(shard * DB_DEV, DB_DEV)]
        return pltpu.make_async_remote_copy(
            part if src is None else src, part, send, db_recv.at[kind, shard],
            device_id={"dp": target, "ctx": me}, device_id_type=MESH,
        )

    def y_copy(kind, far, k):
        to_y = lax.rem(y + k, 4)
        src = blocks[kind][2].at[:, :, cols(to_y)] if far else blocks[kind][0].at[:, :, cols(x * LOCAL + to_y)]
        return shard_copy(kind, far_dp if far else dp, src, y_send.at[kind, far, k], y_at(side, k))

    def core_pass(kind, far, k):
        src = None
        if k == 0:
            src = blocks[kind][2].at[:, :, cols(y)] if far else blocks[kind][0].at[:, :, cols(head)]
        return shard_copy(kind, y_at(away if far else side, k), src, core_send.at[kind, far, k], other_core)

    def wait_shard(kind, shard):
        shard_copy(kind, shard, None, far_send.at[kind], other_core).wait_recv()

    def qc_copy(k):
        to_y, to_x = plane(k)
        return pltpu.make_async_remote_copy(
            qc_ref.at[:, cols(to_x * LOCAL + to_y)], qc.at[cross_part, y, x], qc_send.at[k], qc_recv.at[cross_part, y, x],
            device_id={"dp": side + 2 * to_y + core, "ctx": cross_row * XS + to_x}, device_id_type=MESH,
        )

    def idx_copy(k):
        to_y, to_x = plane(k)
        return pltpu.make_async_remote_copy(
            idx.at[cross_part, y, x], idx.at[cross_part, y, x], idx_send.at[k], idx_recv.at[cross_part, y, x],
            device_id={"dp": side + 2 * to_y + core, "ctx": cross_row * XS + to_x}, device_id_type=MESH,
        )

    def wait_plane(part):
        def step(k):
            from_y, from_x = plane(k)
            for buf, sent, received in ((idx, idx_send, idx_recv), (qc, qc_send, qc_recv)):
                there = buf.at[part, from_y, from_x]
                pltpu.make_async_remote_copy(
                    there, there, sent.at[k], received.at[part, from_y, from_x],
                    device_id={"dp": side + 2 * from_y + core, "ctx": jnp.where(part == 1, pair, row) * XS + from_x},
                    device_id_type=MESH,
                ).wait_recv()

        return step

    def back_copy(part, k):
        to_y = lax.rem(y + k, 4)
        return pltpu.make_async_remote_copy(
            cross_out.at[part, to_y], cross.at[y], back_send.at[part, k], back_recv.at[y],
            device_id={"dp": y_at(side, k), "ctx": jnp.where(part == 1, pair, row) * XS + x}, device_id_type=MESH,
        )

    def own_back():
        return pltpu.make_async_copy(cross_out.at[0, y], cross.at[y], own_sem.at[QC, 1])

    def x_copy(kind, h, to):
        arg, buf = arrays[kind]
        return pltpu.make_async_remote_copy(
            arg.at[:, cols(to * LOCAL + h)], buf.at[h, x], x_send.at[kind, h, to], x_recv.at[kind, h, x],
            device_id={"dp": dp, "ctx": row * XS + to}, device_id_type=MESH,
        )

    def arrived(kind, h):
        own_copy(kind, h).wait()
        for k in range(1, XS):
            source = x_at(k)
            buf = arrays[kind][1].at[h, source]
            pltpu.make_async_remote_copy(
                buf, buf, x_send.at[kind, h, source], x_recv.at[kind, h, source],
                device_id={"dp": dp, "ctx": row * XS + source}, device_id_type=MESH,
            ).wait_recv()

    def start_x(kinds):
        def step(h):
            for k in (1, 3, 2):
                for kind in kinds:
                    x_copy(kind, h, x_at(k)).start()

        loop(0, LOCAL, step)

    def start_plane(k):
        idx_copy(k).start()
        qc_copy(k).start()

    @pl.when(edge & (dp >= HALF))
    def _():
        for kind in range(2):
            far_copy(kind).start()

    first_plane = jnp.where(inner, 0, 1)

    @pl.when(row < 2)
    def _():
        start_x((KS, VS))
        loop(first_plane, 4 * XS, start_plane)
        start_x((QS,))

    @pl.when(row >= 2)
    def _():
        start_x((QS,))
        loop(first_plane, 4 * XS, start_plane)
        start_x((KS, VS))

    @pl.when(edge)
    def _():
        for kind in range(2):
            for k in (1, 3, 2):
                y_copy(kind, 0, k).start()
            core_pass(kind, 0, 0).start()

    @pl.when(edge & first_side)
    def _():
        pl.semaphore_wait(ready, 1)
        for kind in range(2):
            far_copy(kind).start()

    def z_copy(kind, h):
        src, dst, to = {
            ZK: (ks.at[h], k0.at[h], 1),
            ZV: (vs.at[h], v0.at[h], 1),
            ZQ2: (qs.at[h], q2.at[h], 1),
            ZQ3: (qs.at[h], q3.at[h], 1),
            ZQ3B: (qs.at[h], q3.at[h], 2),
            ZO2: (part_out.at[0, h], part_in.at[0, h], 2),
            ZS2: (stat_out.at[0, h], stat_in.at[0, h], 2),
            ZO3: (part_out.at[1, h], part_in.at[0, h], 3),
            ZS3: (stat_out.at[1, h], stat_in.at[0, h], 3),
            ZO3B: (part_out.at[1, h], part_in.at[1, h], 3),
            ZS3B: (stat_out.at[1, h], stat_in.at[1, h], 3),
        }[kind]
        return pltpu.make_async_remote_copy(
            src, dst, z_send.at[kind, h], z_recv.at[kind, h],
            device_id={"dp": dp, "ctx": to * XS + x}, device_id_type=MESH,
        )

    def relay(h):
        @pl.when(row == 0)
        def _():
            arrived(KS, h)
            z_copy(ZK, h).start()
            arrived(VS, h)
            z_copy(ZV, h).start()

        @pl.when(row == 2)
        def _():
            arrived(QS, h)
            z_copy(ZQ2, h).start()

        @pl.when(row == 3)
        def _():
            arrived(QS, h)
            z_copy(ZQ3, h).start()
            z_copy(ZQ3B, h).start()

    def far_stage():
        for kind in range(2):
            far_copy(kind).wait_recv()
            for k in (1, 3, 2):
                y_copy(kind, 1, k).start()
            core_pass(kind, 1, 0).start()
            own_far(kind).start()

    def core_stage():
        for far in range(2):
            for kind in range(2):
                for k in (1, 3, 2):
                    wait_shard(kind, y_at(away if far else side, k))
                    core_pass(kind, far, k).start()

    diagonal = lax.broadcasted_iota(jnp.int32, (ROWS, ROWS), 0) >= lax.broadcasted_iota(jnp.int32, (ROWS, ROWS), 1)
    eye = lax.broadcasted_iota(jnp.int32, (TOK, TOK), 0) == lax.broadcasted_iota(jnp.int32, (TOK, TOK), 1)

    def score_block(queries, h, b, chunks, slot):
        q = queries[h, pl.ds(b * PER, PER)].reshape(ROWS, HD)
        peak = None
        for j, (keys, values, c, masked) in enumerate(chunks):
            k = keys[h, pl.ds(c * PER, PER)].reshape(ROWS, HD)
            s = lax.dot_general(q, k, NT, preferred_element_type=jnp.float32)
            if masked:
                s = jnp.where(diagonal, s, -1e30)
            scores[slot, j] = s
            folded = jnp.maximum(s[:, :HD], s[:, HD:])
            peak = folded if peak is None else jnp.maximum(peak, folded)
        return jnp.max(peak, axis=1, keepdims=True)

    def weigh_block(h, chunks, slot, top):
        total = jnp.zeros((ROWS, HD), jnp.float32)
        acc = jnp.zeros((ROWS, HD), jnp.float32)
        for j, (keys, values, c, masked) in enumerate(chunks):
            w = jnp.exp2((scores[slot, j] - top) * EXPO)
            total = total + (w[:, :HD] + w[:, HD:])
            v = values[h, pl.ds(c * PER, PER)].reshape(ROWS, HD)
            acc = acc + lax.dot_general(w.astype(jnp.bfloat16), v, NN, preferred_element_type=jnp.float32)
        return jnp.sum(total, axis=1, keepdims=True), acc

    def attend(h, jobs):
        tops_of = []
        for n in range(len(jobs) + 1):
            if n < len(jobs):
                queries, b, chunks, done = jobs[n]
                tops_of.append(score_block(queries, h, b, chunks, n % 3))
            if n >= 1:
                queries, b, chunks, done = jobs[n - 1]
                done(b, tops_of[n - 1], *weigh_block(h, chunks, (n - 1) % 3, tops_of[n - 1]))

    def partial(queries, h, chunks, place):
        def done(b, top, total, acc):
            part_out[place, h, pl.ds(b * PER, PER)] = (acc / total).astype(jnp.bfloat16).reshape(PER, TOK, HD)
            for p in range(PER):
                rows = slice(p * TOK, (p + 1) * TOK)
                at = b * PER + p
                stat_out[place, h, at : at + 1] = jnp.sum(jnp.where(eye, top[rows], 0.0), axis=0, keepdims=True)
                stat_out[place, h, XS + at : XS + at + 1] = jnp.sum(jnp.where(eye, total[rows], 0.0), axis=0, keepdims=True)

        return [(queries, b, chunks, done) for b in range(QB)]

    def own_rows(h, extra, final):
        def done(b, top, total, acc):
            at = h * QB + b
            if final:
                accs[at] = acc / total
            else:
                accs[at] = acc
                tops[at] = jnp.broadcast_to(top, (ROWS, HD))
                totals[at] = jnp.broadcast_to(total, (ROWS, HD))

        return [(qs, b, extra + [(ks, vs, c, c == b) for c in range(b + 1)], done) for b in range(QB)]

    whole_own = [(ks, vs, c, False) for c in range(QB)]
    whole_first = [(k0, v0, c, False) for c in range(QB)]

    def between(h):
        @pl.when(row == 1)
        def _():
            arrived(KS, h)
            arrived(VS, h)
            z_copy(ZK, h).wait_recv()
            z_copy(ZV, h).wait_recv()
            z_copy(ZQ2, h).wait_recv()
            z_copy(ZQ3, h).wait_recv()
            attend(h, partial(q2, h, whole_first + whole_own, 0) + partial(q3, h, whole_first + whole_own, 1))
            z_copy(ZO2, h).start()
            z_copy(ZS2, h).start()
            z_copy(ZO3, h).start()
            z_copy(ZS3, h).start()
            arrived(QS, h)
            attend(h, own_rows(h, whole_first, True))

        @pl.when(row == 2)
        def _():
            arrived(KS, h)
            arrived(VS, h)
            z_copy(ZQ3B, h).wait_recv()
            attend(h, partial(q3, h, whole_own, 1))
            z_copy(ZO3B, h).start()
            z_copy(ZS3B, h).start()

    def own_others(h):
        @pl.when(row == 0)
        def _():
            arrived(QS, h)
            attend(h, own_rows(h, [], True))

        @pl.when(row == 2)
        def _():
            attend(h, own_rows(h, [], False))

        @pl.when(row == 3)
        def _():
            arrived(KS, h)
            arrived(VS, h)
            attend(h, own_rows(h, [], False))

    def cross_document(part, k):
        doc = lax.rem(y + k, 4)
        groups = [(t, g) for t in range(XS) for g in range(TOK // GROUP)]
        picks = [[idx_s[part, doc, t, 0, g * NEIGH + n] for n in range(NEIGH)] for t, g in groups]
        s = []
        for (t, g), pick in zip(groups, picks):
            keys = jnp.concatenate([kd[block] for block in pick], axis=0)
            q = qc[part, doc, t, pl.ds(g * GROUP, GROUP), :]
            s.append(lax.dot_general(q, keys, NT, preferred_element_type=jnp.float32))
        top = [jnp.max(one, axis=1, keepdims=True) for one in s]
        w = [jnp.exp2((one - high) * EXPO) for one, high in zip(s, top)]
        total = [jnp.sum(one, axis=1, keepdims=True) for one in w]
        o = []
        for one, pick in zip(w, picks):
            values = jnp.concatenate([vd[block] for block in pick], axis=0)
            o.append(lax.dot_general(one.astype(jnp.bfloat16), values, NN, preferred_element_type=jnp.float32))
        for (t, g), one, whole in zip(groups, o, total):
            cross_out[part, doc, t, pl.ds(g * GROUP, GROUP), :] = (one / whole).astype(jnp.bfloat16)

        here = (part == 0) & (k == 0)

        @pl.when(jnp.logical_not(here))
        def _():
            back_copy(part, k).start()

        @pl.when(here)
        def _():
            own_back().start()

    def cross_stage():
        own_qc().wait()
        for kind in range(2):
            own_db(kind).wait()
            own_far(kind).wait()

        def wait_other_core(k):
            for kind in range(2):
                wait_shard(kind, 2 * k + 1 - core)

        loop(0, HALF, wait_other_core)

        def cross_row_of(n):
            part = 1 - n
            loop(n, 4 * XS, wait_plane(part))
            numbers = pltpu.make_async_copy(idx.at[part], idx_s.at[part], number_sem)
            numbers.start()
            numbers.wait()
            loop(0, 4, lambda k: cross_document(part, 3 - k))

        loop(0, 2, cross_row_of)

    @pl.when(row == 0)
    def _():
        relay(0)
        relay(1)
        far_stage()
        relay(2)
        relay(3)

    @pl.when(row >= 2)
    def _():
        loop(0, LOCAL, relay)

    pl.when(row == 3)(far_stage)

    @pl.when(edge)
    def _():
        core_stage()
        cross_stage()

    loop(0, LOCAL, between)

    def merge(h, parts):
        for b in range(QB):
            at = h * QB + b
            for p in range(PER):
                rows = slice(p * TOK, (p + 1) * TOK)
                sub = b * PER + p
                top = tops[at, rows, :1]
                others = []
                for place in range(parts):
                    column = [
                        jnp.sum(jnp.where(eye, stat_in[place, h, n : n + 1], 0.0), axis=1, keepdims=True)
                        for n in (sub, XS + sub)
                    ]
                    others.append(column)
                peak = top
                for other_top, _ in others:
                    peak = jnp.maximum(peak, other_top)
                keep = jnp.exp2((top - peak) * EXPO)
                total = totals[at, rows, :1] * keep
                acc = accs[at, rows, :] * keep
                for place, (other_top, other_total) in enumerate(others):
                    w = jnp.exp2((other_top - peak) * EXPO) * other_total
                    total = total + w
                    acc = acc + part_in[place, h, sub].astype(jnp.float32) * w
                accs[at, rows, :] = acc / total

    def out_copy(h, t):
        return pltpu.make_async_remote_copy(
            mixed.at[h, t], out_ref.at[:, cols(x * LOCAL + h)], x_send.at[OUT, h, t], x_recv.at[OUT, h, x],
            device_id={"dp": dp, "ctx": row * XS + t}, device_id_type=MESH,
        )

    def own_out(h):
        return pltpu.make_async_copy(mixed.at[h, x], out_ref.at[:, cols(x * LOCAL + h)], own_sem.at[OUT, h])

    def emit(h):
        @pl.when(row == 2)
        def _():
            z_copy(ZO2, h).wait_recv()
            z_copy(ZS2, h).wait_recv()
            merge(h, 1)

        @pl.when(row == 3)
        def _():
            z_copy(ZO3, h).wait_recv()
            z_copy(ZS3, h).wait_recv()
            z_copy(ZO3B, h).wait_recv()
            z_copy(ZS3B, h).wait_recv()
            merge(h, 2)

        @pl.when((h != y) | inner)
        def _():
            there = cross.at[h]
            pltpu.make_async_remote_copy(
                there, there, back_send.at[0, 0], back_recv.at[h],
                device_id={"dp": side + 2 * h + core, "ctx": cross_row * XS + x}, device_id_type=MESH,
            ).wait_recv()

        @pl.when((h == y) & edge)
        def _():
            own_back().wait()

        self_out = accs[pl.ds(h * QB, QB)].astype(jnp.bfloat16).astype(jnp.float32).reshape(XS, TOK, HD)
        mixed[h] = (self_out + cross[h].astype(jnp.float32)).astype(jnp.bfloat16)
        for k in (1, 3, 2):
            out_copy(h, x_at(k)).start()
        own_out(h).start()

    def own_and_emit(h):
        own_others(h)
        emit(h)

    loop(0, LOCAL, own_and_emit)

    @pl.when(edge)
    def _():
        for kind in range(2):
            far_copy(kind).wait_send()
            for far in range(2):
                for k in range(1, 4):
                    y_copy(kind, far, k).wait_send()
                for k in range(4):
                    core_pass(kind, far, k).wait_send()
        for k in range(1, 4):
            back_copy(0, k).wait_send()
        for k in range(4):
            back_copy(1, k).wait_send()

    def finish_plane(k):
        idx_copy(k).wait_send()
        qc_copy(k).wait_send()

    loop(first_plane, 4 * XS, finish_plane)
    def finish(h):
        for k in range(1, XS):
            peer = x_at(k)
            for kind in (KS, VS, QS):
                x_copy(kind, h, peer).wait_send()
        for at, kinds in enumerate(((ZK, ZV), (ZO2, ZS2, ZO3, ZS3), (ZQ2, ZO3B, ZS3B), (ZQ3, ZQ3B))):

            @pl.when(row == at)
            def _():
                for kind in kinds:
                    z_copy(kind, h).wait_send()

    def finish_out(h):
        own_out(h).wait()
        for k in range(1, XS):
            peer = x_at(k)
            out_copy(h, peer).wait_send()
            pltpu.make_async_remote_copy(
                mixed.at[h, peer], out_ref.at[:, cols(peer * LOCAL + h)], x_send.at[OUT, h, peer], x_recv.at[OUT, h, peer],
                device_id={"dp": dp, "ctx": row * XS + peer}, device_id_type=MESH,
            ).wait_recv()

    loop(0, LOCAL, finish)
    loop(0, LOCAL, finish_out)


def shards(q_self, k_self, v_self, q_cross, db_keys, db_values, nb_shard, nb_row):
    anywhere = pl.BlockSpec(memory_space=pl.ANY)
    scalars = pl.BlockSpec(memory_space=pltpu.SMEM)
    heads = pltpu.VMEM((LOCAL, XS, TOK, HD), jnp.bfloat16)
    database = pltpu.VMEM((N_DP * DB_DEV, NLEN, HD), jnp.bfloat16)
    shard = pltpu.VMEM((DB_DEV, NLEN, WIDE), jnp.bfloat16)
    state = pltpu.VMEM((LOCAL * QB, ROWS, HD), jnp.float32)
    parts = pltpu.VMEM((2, LOCAL, XS, TOK, HD), jnp.bfloat16)
    stats = pltpu.VMEM((2, LOCAL, 8, 128), jnp.float32)
    dma = pltpu.SemaphoreType.DMA
    out = pl.pallas_call(
        kernel,
        out_shape=jax.ShapeDtypeStruct((TOK, HEADS * HD), jnp.bfloat16),
        in_specs=[anywhere] * 6 + [scalars] * 2,
        out_specs=anywhere,
        scratch_shapes=[
            heads, heads, heads, parts, heads, heads, heads, heads, database, database,
            pltpu.VMEM((2, 4, XS, 8, 128), jnp.int32),
            pltpu.SMEM((2, 4, XS, 8, 128), jnp.int32),
            heads,
            pltpu.VMEM((3, 2 * QB, ROWS, ROWS), jnp.float32),
            state, state, state,
            parts, stats, parts, stats, heads, parts, shard, shard,
            dma((5, LOCAL, XS)), dma((5, LOCAL, XS)), dma((4 * XS,)), dma((2, 4, XS)), dma((4 * XS,)), dma((2, 4, XS)),
            dma((2, 4)), dma((4,)), dma((11, LOCAL)), dma((11, LOCAL)),
            dma((2,)), dma((2,)), dma((2, 2, 4)), dma((2, 2, 4)), dma((2, N_DP)), dma((5, LOCAL)), dma((4,)), dma,
            pltpu.SemaphoreType.REGULAR,
        ],
        compiler_params=pltpu.CompilerParams(
            collective_id=0, has_side_effects=True, vmem_limit_bytes=60 * 1024 * 1024
        ),
    )(q_self[0], k_self[0], v_self[0], q_cross[0], db_keys, db_values, nb_shard, nb_row)
    return out[None]


def solution(mesh):
    return jax.shard_map(
        shards,
        mesh=mesh,
        in_specs=(
            P("dp", "ctx", None),
            P("dp", "ctx", None),
            P("dp", "ctx", None),
            P("dp", "ctx", None),
            P("dp", None, None),
            P("dp", None, None),
            P("dp", "ctx", None),
            P("dp", "ctx", None),
        ),
        out_specs=P("dp", "ctx", None),
        check_vma=False,
    )
```

```python
import jax
import jax.numpy as jnp
from jax import lax
from jax.experimental import pallas as pl
from jax.experimental.pallas import tpu as pltpu
from jax.sharding import PartitionSpec as P

HEADS = 16
HD = 128
GROUP = 64
NEIGH = 2
NLEN = 128
TOK = 128
DB_DEV = 2
N_DP = 16
HALF = 8
XS = 4
LOCAL = HEADS // XS
WIDE = LOCAL * HD
ROWS = 256
PER = ROWS // TOK
QB = XS // PER
EXPO = HD**-0.5 * 1.4426950408889634
MESH = pl.DeviceIdType.MESH
NT = (((1,), (1,)), ((), ()))
NN = (((1,), (0,)), ((), ()))
QC, KS, VS, QS, OUT = range(5)
ZK, ZV, ZQ2, ZQ3, ZQ3B, ZO2, ZS2, ZO3, ZS3, ZO3B, ZS3B = range(11)


def cols(head):
    return pl.ds(pl.multiple_of(head * HD, HD), HD)


def kernel(
    qs_ref, ks_ref, vs_ref, qc_ref, kd_ref, vd_ref, shard_ref, row_ref, out_ref,
    qs, ks, vs, qc, k0, v0, q2, q3, kd, vd, idx, idx_s, cross, scores, tops, totals, accs,
    part_out, stat_out, part_in, stat_in, mixed, cross_out, kf, vf,
    x_send, x_recv, qc_send, qc_recv, idx_send, idx_recv, back_send, back_recv, z_send, z_recv,
    far_send, far_recv, y_send, core_send, db_recv, own_sem, db_own, number_sem, ready,
):
    dp = lax.axis_index("dp")
    me = lax.axis_index("ctx")
    row = me // XS
    x = lax.rem(me, XS)
    near = lax.rem(dp, HALF)
    side = dp - near
    away = HALF - side
    y = near // 2
    core = lax.rem(near, 2)
    other_core = dp + 1 - 2 * core
    far_dp = away + near
    far_ctx = (3 - row) * XS + x
    edge = (row == 0) | (row == 3)
    first_side = dp < HALF
    inner = (row == 1) | (row == 2)
    pair = row + 1 - 2 * lax.rem(row, 2)
    cross_row = jnp.where(inner, pair, row)
    cross_part = jnp.where(inner, 1, 0)

    def x_at(k):
        return lax.rem(x + k, XS)

    def y_at(home, k):
        return home + lax.rem(near + 2 * k, HALF)

    def loop(first, last, body):
        def step(k, carry):
            body(k)
            return carry

        lax.fori_loop(first, last, step, 0)

    barrier = pltpu.get_barrier_semaphore()

    def greet(dp_of, ctx_of):
        pl.semaphore_signal(barrier, inc=1, device_id={"dp": dp_of, "ctx": ctx_of}, device_id_type=MESH)

    def plane(k):
        return lax.rem(y + k // XS, 4), x_at(lax.rem(k, XS))

    def greet_plane(of_row):
        def step(k):
            to_y, to_x = plane(k)
            greet(side + 2 * to_y + core, of_row * XS + to_x)

        return step

    loop(1, jnp.where(edge, 4 * XS, XS), greet_plane(row))
    loop(1, 4 * XS, greet_plane(pair))
    for k in range(1, 4):
        greet(dp, lax.rem(row + k, 4) * XS + x)

    @pl.when(edge)
    def _():
        greet(other_core, me)

    @pl.when(edge & first_side)
    def _():
        greet(far_dp, far_ctx)

    lane = lax.broadcasted_iota(jnp.int32, (8, 128), 1)
    tile = jnp.zeros((8, 128), jnp.int32)
    for g in range(TOK // GROUP):
        for n in range(NEIGH):
            block = shard_ref[0, g, n] * DB_DEV + row_ref[0, g, n]
            tile = jnp.where(lane == g * NEIGH + n, block, tile)
    idx[cross_part, y, x] = tile

    arrays = {KS: (ks_ref, ks), VS: (vs_ref, vs), QS: (qs_ref, qs)}
    blocks = ((kd_ref, kd, kf), (vd_ref, vd, vf))
    wide = pl.ds(pl.multiple_of(x * WIDE, WIDE), WIDE)
    head = x * LOCAL + y

    def own_copy(kind, h):
        arg, buf = arrays[kind]
        return pltpu.make_async_copy(arg.at[:, cols(x * LOCAL + h)], buf.at[h, x], own_sem.at[kind, h])

    def own_qc():
        return pltpu.make_async_copy(qc_ref.at[:, cols(head)], qc.at[0, y, x], own_sem.at[QC, 0])

    def own_db(kind):
        arg, buf, far = blocks[kind]
        return pltpu.make_async_copy(arg.at[:, :, cols(head)], buf.at[pl.ds(dp * DB_DEV, DB_DEV)], db_own.at[kind])

    def own_far(kind):
        arg, buf, far = blocks[kind]
        return pltpu.make_async_copy(far.at[:, :, cols(y)], buf.at[pl.ds(far_dp * DB_DEV, DB_DEV)], db_own.at[2 + kind])

    def start_own(h):
        for kind in (KS, VS, QS):
            own_copy(kind, h).start()

    loop(0, LOCAL, start_own)

    @pl.when(edge)
    def _():
        own_qc().start()
        for kind in range(2):
            own_db(kind).start()

    pl.semaphore_wait(barrier, 21 + jnp.where(edge, 13, 0) + jnp.where(edge & (dp >= HALF), 1, 0))

    @pl.when(edge & (dp >= HALF))
    def _():
        pl.semaphore_signal(ready, inc=1, device_id={"dp": far_dp, "ctx": far_ctx}, device_id_type=MESH)

    def far_copy(kind):
        arg, buf, far = blocks[kind]
        return pltpu.make_async_remote_copy(
            arg.at[:, :, wide], far, far_send.at[kind], far_recv.at[kind],
            device_id={"dp": far_dp, "ctx": far_ctx}, device_id_type=MESH,
        )

    def shard_copy(kind, shard, src, send, target):
        part = blocks[kind][1].at[pl.ds(shard * DB_DEV, DB_DEV)]
        return pltpu.make_async_remote_copy(
            part if src is None else src, part, send, db_recv.at[kind, shard],
            device_id={"dp": target, "ctx": me}, device_id_type=MESH,
        )

    def y_copy(kind, far, k):
        to_y = lax.rem(y + k, 4)
        src = blocks[kind][2].at[:, :, cols(to_y)] if far else blocks[kind][0].at[:, :, cols(x * LOCAL + to_y)]
        return shard_copy(kind, far_dp if far else dp, src, y_send.at[kind, far, k], y_at(side, k))

    def core_pass(kind, far, k):
        src = None
        if k == 0:
            src = blocks[kind][2].at[:, :, cols(y)] if far else blocks[kind][0].at[:, :, cols(head)]
        return shard_copy(kind, y_at(away if far else side, k), src, core_send.at[kind, far, k], other_core)

    def wait_shard(kind, shard):
        shard_copy(kind, shard, None, far_send.at[kind], other_core).wait_recv()

    def qc_copy(k):
        to_y, to_x = plane(k)
        return pltpu.make_async_remote_copy(
            qc_ref.at[:, cols(to_x * LOCAL + to_y)], qc.at[cross_part, y, x], qc_send.at[k], qc_recv.at[cross_part, y, x],
            device_id={"dp": side + 2 * to_y + core, "ctx": cross_row * XS + to_x}, device_id_type=MESH,
        )

    def idx_copy(k):
        to_y, to_x = plane(k)
        return pltpu.make_async_remote_copy(
            idx.at[cross_part, y, x], idx.at[cross_part, y, x], idx_send.at[k], idx_recv.at[cross_part, y, x],
            device_id={"dp": side + 2 * to_y + core, "ctx": cross_row * XS + to_x}, device_id_type=MESH,
        )

    def wait_plane(part):
        def step(k):
            from_y, from_x = plane(k)
            for buf, sent, received in ((idx, idx_send, idx_recv), (qc, qc_send, qc_recv)):
                there = buf.at[part, from_y, from_x]
                pltpu.make_async_remote_copy(
                    there, there, sent.at[k], received.at[part, from_y, from_x],
                    device_id={"dp": side + 2 * from_y + core, "ctx": jnp.where(part == 1, pair, row) * XS + from_x},
                    device_id_type=MESH,
                ).wait_recv()

        return step

    def back_copy(part, k):
        to_y = lax.rem(y + k, 4)
        return pltpu.make_async_remote_copy(
            cross_out.at[part, to_y], cross.at[y], back_send.at[part, k], back_recv.at[y],
            device_id={"dp": y_at(side, k), "ctx": jnp.where(part == 1, pair, row) * XS + x}, device_id_type=MESH,
        )

    def own_back():
        return pltpu.make_async_copy(cross_out.at[0, y], cross.at[y], own_sem.at[QC, 1])

    def x_copy(kind, h, to):
        arg, buf = arrays[kind]
        return pltpu.make_async_remote_copy(
            arg.at[:, cols(to * LOCAL + h)], buf.at[h, x], x_send.at[kind, h, to], x_recv.at[kind, h, x],
            device_id={"dp": dp, "ctx": row * XS + to}, device_id_type=MESH,
        )

    def arrived(kind, h):
        own_copy(kind, h).wait()
        for k in range(1, XS):
            source = x_at(k)
            buf = arrays[kind][1].at[h, source]
            pltpu.make_async_remote_copy(
                buf, buf, x_send.at[kind, h, source], x_recv.at[kind, h, source],
                device_id={"dp": dp, "ctx": row * XS + source}, device_id_type=MESH,
            ).wait_recv()

    def start_x(kinds, first=0, last=LOCAL):
        def step(h):
            for k in (1, 3, 2):
                for kind in kinds:
                    x_copy(kind, h, x_at(k)).start()

        loop(first, last, step)

    first_plane = jnp.where(inner, 0, 1)

    def start_plane():
        def step(k):
            idx_copy(k).start()
            qc_copy(k).start()

        loop(first_plane, 4 * XS, step)

    def start_near():
        for kind in range(2):
            for k in (1, 3, 2):
                y_copy(kind, 0, k).start()
            core_pass(kind, 0, 0).start()

    def start_far_first():
        @pl.when(dp >= HALF)
        def _():
            for kind in range(2):
                far_copy(kind).start()

    def start_far_second():
        @pl.when(first_side)
        def _():
            pl.semaphore_wait(ready, 1)
            for kind in range(2):
                far_copy(kind).start()

    @pl.when(row == 0)
    def _():
        start_far_first()
        start_x((KS, VS), 0, 1)
        start_near()
        start_x((KS, VS), 1, 3)
        start_plane()
        start_far_second()
        start_x((KS, VS), 3, 4)
        start_x((QS,))

    @pl.when(row == 1)
    def _():
        start_plane()
        start_x((KS, VS))
        start_x((QS,))

    @pl.when(row == 2)
    def _():
        start_x((QS,))
        start_plane()
        start_x((KS, VS))

    @pl.when(row == 3)
    def _():
        start_far_first()
        start_x((QS,))
        start_near()
        start_plane()
        start_far_second()
        start_x((KS, VS))

    def z_copy(kind, h):
        src, dst, to = {
            ZK: (ks.at[h], k0.at[h], 1),
            ZV: (vs.at[h], v0.at[h], 1),
            ZQ2: (qs.at[h], q2.at[h], 1),
            ZQ3: (qs.at[h], q3.at[h], 1),
            ZQ3B: (qs.at[h], q3.at[h], 2),
            ZO2: (part_out.at[0, h], part_in.at[0, h], 2),
            ZS2: (stat_out.at[0, h], stat_in.at[0, h], 2),
            ZO3: (part_out.at[1, h], part_in.at[0, h], 3),
            ZS3: (stat_out.at[1, h], stat_in.at[0, h], 3),
            ZO3B: (part_out.at[1, h], part_in.at[1, h], 3),
            ZS3B: (stat_out.at[1, h], stat_in.at[1, h], 3),
        }[kind]
        return pltpu.make_async_remote_copy(
            src, dst, z_send.at[kind, h], z_recv.at[kind, h],
            device_id={"dp": dp, "ctx": to * XS + x}, device_id_type=MESH,
        )

    def relay(h):
        @pl.when(row == 0)
        def _():
            arrived(KS, h)
            z_copy(ZK, h).start()
            arrived(VS, h)
            z_copy(ZV, h).start()

        @pl.when(row == 2)
        def _():
            arrived(QS, h)
            z_copy(ZQ2, h).start()

        @pl.when(row == 3)
        def _():
            arrived(QS, h)
            z_copy(ZQ3, h).start()
            z_copy(ZQ3B, h).start()

    def far_stage():
        for kind in range(2):
            far_copy(kind).wait_recv()
            for k in (1, 3, 2):
                y_copy(kind, 1, k).start()
            core_pass(kind, 1, 0).start()
            own_far(kind).start()

    def core_stage():
        for far in range(2):
            for kind in range(2):
                for k in (1, 3, 2):
                    wait_shard(kind, y_at(away if far else side, k))
                    core_pass(kind, far, k).start()

    diagonal = lax.broadcasted_iota(jnp.int32, (ROWS, ROWS), 0) >= lax.broadcasted_iota(jnp.int32, (ROWS, ROWS), 1)
    eye = lax.broadcasted_iota(jnp.int32, (TOK, TOK), 0) == lax.broadcasted_iota(jnp.int32, (TOK, TOK), 1)

    def score_block(queries, h, b, chunks, slot):
        q = queries[h, pl.ds(b * PER, PER)].reshape(ROWS, HD)
        peak = None
        for j, (keys, values, c, masked) in enumerate(chunks):
            k = keys[h, pl.ds(c * PER, PER)].reshape(ROWS, HD)
            s = lax.dot_general(q, k, NT, preferred_element_type=jnp.float32)
            if masked:
                s = jnp.where(diagonal, s, -1e30)
            scores[slot, j] = s
            folded = jnp.maximum(s[:, :HD], s[:, HD:])
            peak = folded if peak is None else jnp.maximum(peak, folded)
        return jnp.max(peak, axis=1, keepdims=True)

    def weigh_block(h, chunks, slot, top):
        total = jnp.zeros((ROWS, HD), jnp.float32)
        acc = jnp.zeros((ROWS, HD), jnp.float32)
        for j, (keys, values, c, masked) in enumerate(chunks):
            w = jnp.exp2((scores[slot, j] - top) * EXPO)
            total = total + (w[:, :HD] + w[:, HD:])
            v = values[h, pl.ds(c * PER, PER)].reshape(ROWS, HD)
            acc = acc + lax.dot_general(w.astype(jnp.bfloat16), v, NN, preferred_element_type=jnp.float32)
        return jnp.sum(total, axis=1, keepdims=True), acc

    def attend(h, jobs):
        tops_of = []
        for n in range(len(jobs) + 1):
            if n < len(jobs):
                queries, b, chunks, done = jobs[n]
                tops_of.append(score_block(queries, h, b, chunks, n % 3))
            if n >= 1:
                queries, b, chunks, done = jobs[n - 1]
                done(b, tops_of[n - 1], *weigh_block(h, chunks, (n - 1) % 3, tops_of[n - 1]))

    def partial(queries, h, chunks, place):
        def done(b, top, total, acc):
            part_out[place, h, pl.ds(b * PER, PER)] = (acc / total).astype(jnp.bfloat16).reshape(PER, TOK, HD)
            for p in range(PER):
                rows = slice(p * TOK, (p + 1) * TOK)
                at = b * PER + p
                stat_out[place, h, at : at + 1] = jnp.sum(jnp.where(eye, top[rows], 0.0), axis=0, keepdims=True)
                stat_out[place, h, XS + at : XS + at + 1] = jnp.sum(jnp.where(eye, total[rows], 0.0), axis=0, keepdims=True)

        return [(queries, b, chunks, done) for b in range(QB)]

    def own_rows(h, extra, final):
        def done(b, top, total, acc):
            at = h * QB + b
            if final:
                accs[at] = acc / total
            else:
                accs[at] = acc
                tops[at] = jnp.broadcast_to(top, (ROWS, HD))
                totals[at] = jnp.broadcast_to(total, (ROWS, HD))

        return [(qs, b, extra + [(ks, vs, c, c == b) for c in range(b + 1)], done) for b in range(QB)]

    whole_own = [(ks, vs, c, False) for c in range(QB)]
    whole_first = [(k0, v0, c, False) for c in range(QB)]

    def between(h):
        @pl.when(row == 1)
        def _():
            arrived(KS, h)
            arrived(VS, h)
            z_copy(ZK, h).wait_recv()
            z_copy(ZV, h).wait_recv()
            z_copy(ZQ2, h).wait_recv()
            z_copy(ZQ3, h).wait_recv()
            attend(h, partial(q2, h, whole_first + whole_own, 0) + partial(q3, h, whole_first + whole_own, 1))
            z_copy(ZO2, h).start()
            z_copy(ZS2, h).start()
            z_copy(ZO3, h).start()
            z_copy(ZS3, h).start()
            arrived(QS, h)
            attend(h, own_rows(h, whole_first, True))

        @pl.when(row == 2)
        def _():
            arrived(KS, h)
            arrived(VS, h)
            z_copy(ZQ3B, h).wait_recv()
            attend(h, partial(q3, h, whole_own, 1))
            z_copy(ZO3B, h).start()
            z_copy(ZS3B, h).start()

    def own_others(h):
        @pl.when(row == 0)
        def _():
            arrived(QS, h)
            attend(h, own_rows(h, [], True))

        @pl.when(row == 2)
        def _():
            attend(h, own_rows(h, [], False))

        @pl.when(row == 3)
        def _():
            arrived(KS, h)
            arrived(VS, h)
            attend(h, own_rows(h, [], False))

    def cross_document(part, k):
        doc = lax.rem(y + k, 4)
        groups = [(t, g) for t in range(XS) for g in range(TOK // GROUP)]
        picks = [[idx_s[part, doc, t, 0, g * NEIGH + n] for n in range(NEIGH)] for t, g in groups]
        s = []
        for (t, g), pick in zip(groups, picks):
            keys = jnp.concatenate([kd[block] for block in pick], axis=0)
            q = qc[part, doc, t, pl.ds(g * GROUP, GROUP), :]
            s.append(lax.dot_general(q, keys, NT, preferred_element_type=jnp.float32))
        top = [jnp.max(one, axis=1, keepdims=True) for one in s]
        w = [jnp.exp2((one - high) * EXPO) for one, high in zip(s, top)]
        total = [jnp.sum(one, axis=1, keepdims=True) for one in w]
        o = []
        for one, pick in zip(w, picks):
            values = jnp.concatenate([vd[block] for block in pick], axis=0)
            o.append(lax.dot_general(one.astype(jnp.bfloat16), values, NN, preferred_element_type=jnp.float32))
        for (t, g), one, whole in zip(groups, o, total):
            cross_out[part, doc, t, pl.ds(g * GROUP, GROUP), :] = (one / whole).astype(jnp.bfloat16)

        here = (part == 0) & (k == 0)

        @pl.when(jnp.logical_not(here))
        def _():
            back_copy(part, k).start()

        @pl.when(here)
        def _():
            own_back().start()

    def cross_stage():
        own_qc().wait()
        for kind in range(2):
            own_db(kind).wait()
            own_far(kind).wait()

        def wait_other_core(k):
            for kind in range(2):
                wait_shard(kind, 2 * k + 1 - core)

        loop(0, HALF, wait_other_core)

        def cross_row_of(n):
            part = 1 - n
            loop(n, 4 * XS, wait_plane(part))
            numbers = pltpu.make_async_copy(idx.at[part], idx_s.at[part], number_sem)
            numbers.start()
            numbers.wait()
            loop(0, 4, lambda k: cross_document(part, 3 - k))

            @pl.when((row == 0) & (n == 0))
            def _():
                relay(3)

        loop(0, 2, cross_row_of)

    @pl.when(row == 0)
    def _():
        relay(0)
        relay(1)
        far_stage()
        relay(2)

    @pl.when(row >= 2)
    def _():
        loop(0, LOCAL, relay)

    pl.when(row == 3)(far_stage)

    @pl.when(edge)
    def _():
        core_stage()
        cross_stage()

    loop(0, LOCAL, between)

    def merge(h, parts):
        for b in range(QB):
            at = h * QB + b
            for p in range(PER):
                rows = slice(p * TOK, (p + 1) * TOK)
                sub = b * PER + p
                top = tops[at, rows, :1]
                others = []
                for place in range(parts):
                    column = [
                        jnp.sum(jnp.where(eye, stat_in[place, h, n : n + 1], 0.0), axis=1, keepdims=True)
                        for n in (sub, XS + sub)
                    ]
                    others.append(column)
                peak = top
                for other_top, _ in others:
                    peak = jnp.maximum(peak, other_top)
                keep = jnp.exp2((top - peak) * EXPO)
                total = totals[at, rows, :1] * keep
                acc = accs[at, rows, :] * keep
                for place, (other_top, other_total) in enumerate(others):
                    w = jnp.exp2((other_top - peak) * EXPO) * other_total
                    total = total + w
                    acc = acc + part_in[place, h, sub].astype(jnp.float32) * w
                accs[at, rows, :] = acc / total

    def out_copy(h, t):
        return pltpu.make_async_remote_copy(
            mixed.at[h, t], out_ref.at[:, cols(x * LOCAL + h)], x_send.at[OUT, h, t], x_recv.at[OUT, h, x],
            device_id={"dp": dp, "ctx": row * XS + t}, device_id_type=MESH,
        )

    def own_out(h):
        return pltpu.make_async_copy(mixed.at[h, x], out_ref.at[:, cols(x * LOCAL + h)], own_sem.at[OUT, h])

    def emit(h):
        @pl.when(row == 2)
        def _():
            z_copy(ZO2, h).wait_recv()
            z_copy(ZS2, h).wait_recv()
            merge(h, 1)

        @pl.when(row == 3)
        def _():
            z_copy(ZO3, h).wait_recv()
            z_copy(ZS3, h).wait_recv()
            z_copy(ZO3B, h).wait_recv()
            z_copy(ZS3B, h).wait_recv()
            merge(h, 2)

        @pl.when((h != y) | inner)
        def _():
            there = cross.at[h]
            pltpu.make_async_remote_copy(
                there, there, back_send.at[0, 0], back_recv.at[h],
                device_id={"dp": side + 2 * h + core, "ctx": cross_row * XS + x}, device_id_type=MESH,
            ).wait_recv()

        @pl.when((h == y) & edge)
        def _():
            own_back().wait()

        self_out = accs[pl.ds(h * QB, QB)].astype(jnp.bfloat16).astype(jnp.float32).reshape(XS, TOK, HD)
        mixed[h] = (self_out + cross[h].astype(jnp.float32)).astype(jnp.bfloat16)
        for k in (1, 3, 2):
            out_copy(h, x_at(k)).start()
        own_out(h).start()

    def own_and_emit(h):
        own_others(h)
        emit(h)

    loop(0, LOCAL, own_and_emit)

    @pl.when(edge)
    def _():
        for kind in range(2):
            far_copy(kind).wait_send()
            for far in range(2):
                for k in range(1, 4):
                    y_copy(kind, far, k).wait_send()
                for k in range(4):
                    core_pass(kind, far, k).wait_send()
        for k in range(1, 4):
            back_copy(0, k).wait_send()
        for k in range(4):
            back_copy(1, k).wait_send()

    def finish_plane(k):
        idx_copy(k).wait_send()
        qc_copy(k).wait_send()

    loop(first_plane, 4 * XS, finish_plane)
    def finish(h):
        for k in range(1, XS):
            peer = x_at(k)
            for kind in (KS, VS, QS):
                x_copy(kind, h, peer).wait_send()
        for at, kinds in enumerate(((ZK, ZV), (ZO2, ZS2, ZO3, ZS3), (ZQ2, ZO3B, ZS3B), (ZQ3, ZQ3B))):

            @pl.when(row == at)
            def _():
                for kind in kinds:
                    z_copy(kind, h).wait_send()

    def finish_out(h):
        own_out(h).wait()
        for k in range(1, XS):
            peer = x_at(k)
            out_copy(h, peer).wait_send()
            pltpu.make_async_remote_copy(
                mixed.at[h, peer], out_ref.at[:, cols(peer * LOCAL + h)], x_send.at[OUT, h, peer], x_recv.at[OUT, h, peer],
                device_id={"dp": dp, "ctx": row * XS + peer}, device_id_type=MESH,
            ).wait_recv()

    loop(0, LOCAL, finish)
    loop(0, LOCAL, finish_out)


def shards(q_self, k_self, v_self, q_cross, db_keys, db_values, nb_shard, nb_row):
    anywhere = pl.BlockSpec(memory_space=pl.ANY)
    scalars = pl.BlockSpec(memory_space=pltpu.SMEM)
    heads = pltpu.VMEM((LOCAL, XS, TOK, HD), jnp.bfloat16)
    database = pltpu.VMEM((N_DP * DB_DEV, NLEN, HD), jnp.bfloat16)
    shard = pltpu.VMEM((DB_DEV, NLEN, WIDE), jnp.bfloat16)
    state = pltpu.VMEM((LOCAL * QB, ROWS, HD), jnp.float32)
    parts = pltpu.VMEM((2, LOCAL, XS, TOK, HD), jnp.bfloat16)
    stats = pltpu.VMEM((2, LOCAL, 8, 128), jnp.float32)
    dma = pltpu.SemaphoreType.DMA
    out = pl.pallas_call(
        kernel,
        out_shape=jax.ShapeDtypeStruct((TOK, HEADS * HD), jnp.bfloat16),
        in_specs=[anywhere] * 6 + [scalars] * 2,
        out_specs=anywhere,
        scratch_shapes=[
            heads, heads, heads, parts, heads, heads, heads, heads, database, database,
            pltpu.VMEM((2, 4, XS, 8, 128), jnp.int32),
            pltpu.SMEM((2, 4, XS, 8, 128), jnp.int32),
            heads,
            pltpu.VMEM((3, 2 * QB, ROWS, ROWS), jnp.float32),
            state, state, state,
            parts, stats, parts, stats, heads, parts, shard, shard,
            dma((5, LOCAL, XS)), dma((5, LOCAL, XS)), dma((4 * XS,)), dma((2, 4, XS)), dma((4 * XS,)), dma((2, 4, XS)),
            dma((2, 4)), dma((4,)), dma((11, LOCAL)), dma((11, LOCAL)),
            dma((2,)), dma((2,)), dma((2, 2, 4)), dma((2, 2, 4)), dma((2, N_DP)), dma((5, LOCAL)), dma((4,)), dma,
            pltpu.SemaphoreType.REGULAR,
        ],
        compiler_params=pltpu.CompilerParams(
            collective_id=0, has_side_effects=True, vmem_limit_bytes=60 * 1024 * 1024
        ),
    )(q_self[0], k_self[0], v_self[0], q_cross[0], db_keys, db_values, nb_shard, nb_row)
    return out[None]


def solution(mesh):
    return jax.shard_map(
        shards,
        mesh=mesh,
        in_specs=(
            P("dp", "ctx", None),
            P("dp", "ctx", None),
            P("dp", "ctx", None),
            P("dp", "ctx", None),
            P("dp", None, None),
            P("dp", None, None),
            P("dp", "ctx", None),
            P("dp", "ctx", None),
        ),
        out_specs=P("dp", "ctx", None),
        check_vma=False,
    )
```

```python
import jax
import jax.numpy as jnp
from jax import lax
from jax.experimental import pallas as pl
from jax.experimental.pallas import tpu as pltpu
from jax.sharding import PartitionSpec as P

HEADS = 16
HD = 128
GROUP = 64
NEIGH = 2
NLEN = 128
TOK = 128
DB_DEV = 2
N_DP = 16
HALF = 8
XS = 4
LOCAL = HEADS // XS
WIDE = LOCAL * HD
ROWS = 256
PER = ROWS // TOK
QB = XS // PER
EXPO = HD**-0.5 * 1.4426950408889634
MESH = pl.DeviceIdType.MESH
NT = (((1,), (1,)), ((), ()))
NN = (((1,), (0,)), ((), ()))
QC, KS, VS, QS, OUT = range(5)
ZK, ZV, ZQ2, ZQ3, ZQ3B, ZO2, ZS2, ZO3, ZS3, ZO3B, ZS3B = range(11)


def cols(head):
    return pl.ds(pl.multiple_of(head * HD, HD), HD)


def kernel(
    qs_ref, ks_ref, vs_ref, qc_ref, kd_ref, vd_ref, shard_ref, row_ref, out_ref,
    qs, ks, vs, qc, k0, v0, q2, q3, kd, vd, idx, idx_s, cross, scores, tops, totals, accs,
    part_out, stat_out, part_in, stat_in, mixed, cross_out, kf, vf,
    x_send, x_recv, qc_send, qc_recv, idx_send, idx_recv, back_send, back_recv, z_send, z_recv,
    far_send, far_recv, y_send, core_send, db_recv, own_sem, db_own, number_sem, ready,
):
    dp = lax.axis_index("dp")
    me = lax.axis_index("ctx")
    row = me // XS
    x = lax.rem(me, XS)
    near = lax.rem(dp, HALF)
    side = dp - near
    away = HALF - side
    y = near // 2
    core = lax.rem(near, 2)
    other_core = dp + 1 - 2 * core
    far_dp = away + near
    far_ctx = (3 - row) * XS + x
    edge = (row == 0) | (row == 3)
    first_side = dp < HALF
    inner = (row == 1) | (row == 2)
    pair = row + 1 - 2 * lax.rem(row, 2)
    cross_row = jnp.where(inner, pair, row)
    cross_part = jnp.where(inner, 1, 0)

    def x_at(k):
        return lax.rem(x + k, XS)

    def y_at(home, k):
        return home + lax.rem(near + 2 * k, HALF)

    def loop(first, last, body):
        def step(k, carry):
            body(k)
            return carry

        lax.fori_loop(first, last, step, 0)

    barrier = pltpu.get_barrier_semaphore()

    def greet(dp_of, ctx_of):
        pl.semaphore_signal(barrier, inc=1, device_id={"dp": dp_of, "ctx": ctx_of}, device_id_type=MESH)

    def plane(k):
        return lax.rem(y + k // XS, 4), x_at(lax.rem(k, XS))

    def greet_plane(of_row):
        def step(k):
            to_y, to_x = plane(k)
            greet(side + 2 * to_y + core, of_row * XS + to_x)

        return step

    loop(1, jnp.where(edge, 4 * XS, XS), greet_plane(row))
    loop(1, 4 * XS, greet_plane(pair))
    for k in range(1, 4):
        greet(dp, lax.rem(row + k, 4) * XS + x)

    @pl.when(edge)
    def _():
        greet(other_core, me)

    @pl.when(edge & first_side)
    def _():
        greet(far_dp, far_ctx)

    lane = lax.broadcasted_iota(jnp.int32, (8, 128), 1)
    tile = jnp.zeros((8, 128), jnp.int32)
    for g in range(TOK // GROUP):
        for n in range(NEIGH):
            block = shard_ref[0, g, n] * DB_DEV + row_ref[0, g, n]
            tile = jnp.where(lane == g * NEIGH + n, block, tile)
    idx[cross_part, y, x] = tile

    arrays = {KS: (ks_ref, ks), VS: (vs_ref, vs), QS: (qs_ref, qs)}
    blocks = ((kd_ref, kd, kf), (vd_ref, vd, vf))
    wide = pl.ds(pl.multiple_of(x * WIDE, WIDE), WIDE)
    head = x * LOCAL + y

    def own_copy(kind, h):
        arg, buf = arrays[kind]
        return pltpu.make_async_copy(arg.at[:, cols(x * LOCAL + h)], buf.at[h, x], own_sem.at[kind, h])

    def own_qc():
        return pltpu.make_async_copy(qc_ref.at[:, cols(head)], qc.at[0, y, x], own_sem.at[QC, 0])

    def own_db(kind):
        arg, buf, far = blocks[kind]
        return pltpu.make_async_copy(arg.at[:, :, cols(head)], buf.at[pl.ds(dp * DB_DEV, DB_DEV)], db_own.at[kind])

    def own_far(kind):
        arg, buf, far = blocks[kind]
        return pltpu.make_async_copy(far.at[:, :, cols(y)], buf.at[pl.ds(far_dp * DB_DEV, DB_DEV)], db_own.at[2 + kind])

    def start_own(h):
        for kind in (KS, VS, QS):
            own_copy(kind, h).start()

    loop(0, LOCAL, start_own)

    @pl.when(edge)
    def _():
        own_qc().start()
        for kind in range(2):
            own_db(kind).start()

    pl.semaphore_wait(barrier, 21 + jnp.where(edge, 13, 0) + jnp.where(edge & (dp >= HALF), 1, 0))

    @pl.when(edge & (dp >= HALF))
    def _():
        pl.semaphore_signal(ready, inc=1, device_id={"dp": far_dp, "ctx": far_ctx}, device_id_type=MESH)

    def far_copy(kind):
        arg, buf, far = blocks[kind]
        return pltpu.make_async_remote_copy(
            arg.at[:, :, wide], far, far_send.at[kind], far_recv.at[kind],
            device_id={"dp": far_dp, "ctx": far_ctx}, device_id_type=MESH,
        )

    def shard_copy(kind, shard, src, send, target):
        part = blocks[kind][1].at[pl.ds(shard * DB_DEV, DB_DEV)]
        return pltpu.make_async_remote_copy(
            part if src is None else src, part, send, db_recv.at[kind, shard],
            device_id={"dp": target, "ctx": me}, device_id_type=MESH,
        )

    def y_copy(kind, far, k):
        to_y = lax.rem(y + k, 4)
        src = blocks[kind][2].at[:, :, cols(to_y)] if far else blocks[kind][0].at[:, :, cols(x * LOCAL + to_y)]
        return shard_copy(kind, far_dp if far else dp, src, y_send.at[kind, far, k], y_at(side, k))

    def core_pass(kind, far, k):
        src = None
        if k == 0:
            src = blocks[kind][2].at[:, :, cols(y)] if far else blocks[kind][0].at[:, :, cols(head)]
        return shard_copy(kind, y_at(away if far else side, k), src, core_send.at[kind, far, k], other_core)

    def wait_shard(kind, shard):
        shard_copy(kind, shard, None, far_send.at[kind], other_core).wait_recv()

    def qc_copy(k):
        to_y, to_x = plane(k)
        return pltpu.make_async_remote_copy(
            qc_ref.at[:, cols(to_x * LOCAL + to_y)], qc.at[cross_part, y, x], qc_send.at[k], qc_recv.at[cross_part, y, x],
            device_id={"dp": side + 2 * to_y + core, "ctx": cross_row * XS + to_x}, device_id_type=MESH,
        )

    def idx_copy(k):
        to_y, to_x = plane(k)
        return pltpu.make_async_remote_copy(
            idx.at[cross_part, y, x], idx.at[cross_part, y, x], idx_send.at[k], idx_recv.at[cross_part, y, x],
            device_id={"dp": side + 2 * to_y + core, "ctx": cross_row * XS + to_x}, device_id_type=MESH,
        )

    def wait_plane(part):
        def step(k):
            from_y, from_x = plane(k)
            for buf, sent, received in ((idx, idx_send, idx_recv), (qc, qc_send, qc_recv)):
                there = buf.at[part, from_y, from_x]
                pltpu.make_async_remote_copy(
                    there, there, sent.at[k], received.at[part, from_y, from_x],
                    device_id={"dp": side + 2 * from_y + core, "ctx": jnp.where(part == 1, pair, row) * XS + from_x},
                    device_id_type=MESH,
                ).wait_recv()

        return step

    def back_copy(part, k):
        to_y = lax.rem(y + k, 4)
        return pltpu.make_async_remote_copy(
            cross_out.at[part, to_y], cross.at[y], back_send.at[part, k], back_recv.at[y],
            device_id={"dp": y_at(side, k), "ctx": jnp.where(part == 1, pair, row) * XS + x}, device_id_type=MESH,
        )

    def own_back():
        return pltpu.make_async_copy(cross_out.at[0, y], cross.at[y], own_sem.at[QC, 1])

    def x_copy(kind, h, to):
        arg, buf = arrays[kind]
        return pltpu.make_async_remote_copy(
            arg.at[:, cols(to * LOCAL + h)], buf.at[h, x], x_send.at[kind, h, to], x_recv.at[kind, h, x],
            device_id={"dp": dp, "ctx": row * XS + to}, device_id_type=MESH,
        )

    def arrived(kind, h):
        own_copy(kind, h).wait()
        for k in range(1, XS):
            source = x_at(k)
            buf = arrays[kind][1].at[h, source]
            pltpu.make_async_remote_copy(
                buf, buf, x_send.at[kind, h, source], x_recv.at[kind, h, source],
                device_id={"dp": dp, "ctx": row * XS + source}, device_id_type=MESH,
            ).wait_recv()

    def start_x(kinds):
        def step(h):
            for k in (1, 3, 2):
                for kind in kinds:
                    x_copy(kind, h, x_at(k)).start()

        loop(0, LOCAL, step)

    def start_plane(k):
        idx_copy(k).start()
        qc_copy(k).start()

    @pl.when(edge & (dp >= HALF))
    def _():
        for kind in range(2):
            far_copy(kind).start()

    first_plane = jnp.where(inner, 0, 1)

    @pl.when(row < 2)
    def _():
        start_x((KS, VS))
        loop(first_plane, 4 * XS, start_plane)
        start_x((QS,))

    @pl.when(row >= 2)
    def _():
        start_x((QS,))
        loop(first_plane, 4 * XS, start_plane)
        start_x((KS, VS))

    @pl.when(edge)
    def _():
        for kind in range(2):
            for k in (1, 3, 2):
                y_copy(kind, 0, k).start()
            core_pass(kind, 0, 0).start()

    @pl.when(edge & first_side)
    def _():
        pl.semaphore_wait(ready, 1)
        for kind in range(2):
            far_copy(kind).start()

    def z_copy(kind, h):
        src, dst, to = {
            ZK: (ks.at[h], k0.at[h], 1),
            ZV: (vs.at[h], v0.at[h], 1),
            ZQ2: (qs.at[h], q2.at[h], 1),
            ZQ3: (qs.at[h], q3.at[h], 1),
            ZQ3B: (qs.at[h], q3.at[h], 2),
            ZO2: (part_out.at[0, h], part_in.at[0, h], 2),
            ZS2: (stat_out.at[0, h], stat_in.at[0, h], 2),
            ZO3: (part_out.at[1, h], part_in.at[0, h], 3),
            ZS3: (stat_out.at[1, h], stat_in.at[0, h], 3),
            ZO3B: (part_out.at[1, h], part_in.at[1, h], 3),
            ZS3B: (stat_out.at[1, h], stat_in.at[1, h], 3),
        }[kind]
        return pltpu.make_async_remote_copy(
            src, dst, z_send.at[kind, h], z_recv.at[kind, h],
            device_id={"dp": dp, "ctx": to * XS + x}, device_id_type=MESH,
        )

    def relay(h):
        @pl.when(row == 0)
        def _():
            arrived(KS, h)
            z_copy(ZK, h).start()
            arrived(VS, h)
            z_copy(ZV, h).start()

        @pl.when(row == 2)
        def _():
            arrived(QS, h)
            z_copy(ZQ2, h).start()

        @pl.when(row == 3)
        def _():
            arrived(QS, h)
            z_copy(ZQ3, h).start()
            z_copy(ZQ3B, h).start()

    def far_stage():
        for kind in range(2):
            far_copy(kind).wait_recv()
            for k in (1, 3, 2):
                y_copy(kind, 1, k).start()
            core_pass(kind, 1, 0).start()
            own_far(kind).start()

    def core_stage():
        for far in range(2):
            for kind in range(2):
                for k in (1, 3, 2):
                    wait_shard(kind, y_at(away if far else side, k))
                    core_pass(kind, far, k).start()

    diagonal = lax.broadcasted_iota(jnp.int32, (ROWS, ROWS), 0) >= lax.broadcasted_iota(jnp.int32, (ROWS, ROWS), 1)
    eye = lax.broadcasted_iota(jnp.int32, (TOK, TOK), 0) == lax.broadcasted_iota(jnp.int32, (TOK, TOK), 1)

    def score_block(queries, h, b, chunks, slot):
        q = queries[h, pl.ds(b * PER, PER)].reshape(ROWS, HD)
        peak = None
        for j, (keys, values, c, masked) in enumerate(chunks):
            k = keys[h, pl.ds(c * PER, PER)].reshape(ROWS, HD)
            s = lax.dot_general(q, k, NT, preferred_element_type=jnp.float32)
            if masked:
                s = jnp.where(diagonal, s, -1e30)
            scores[slot, j] = s
            folded = jnp.maximum(s[:, :HD], s[:, HD:])
            peak = folded if peak is None else jnp.maximum(peak, folded)
        return jnp.max(peak, axis=1, keepdims=True)

    def weigh_block(h, chunks, slot, top):
        total = jnp.zeros((ROWS, HD), jnp.float32)
        acc = jnp.zeros((ROWS, HD), jnp.float32)
        for j, (keys, values, c, masked) in enumerate(chunks):
            w = jnp.exp2((scores[slot, j] - top) * EXPO)
            total = total + (w[:, :HD] + w[:, HD:])
            v = values[h, pl.ds(c * PER, PER)].reshape(ROWS, HD)
            acc = acc + lax.dot_general(w.astype(jnp.bfloat16), v, NN, preferred_element_type=jnp.float32)
        return jnp.sum(total, axis=1, keepdims=True), acc

    def attend(h, jobs):
        tops_of = []
        for n in range(len(jobs) + 1):
            if n < len(jobs):
                queries, b, chunks, done = jobs[n]
                tops_of.append(score_block(queries, h, b, chunks, n % 3))
            if n >= 1:
                queries, b, chunks, done = jobs[n - 1]
                done(b, tops_of[n - 1], *weigh_block(h, chunks, (n - 1) % 3, tops_of[n - 1]))

    def partial(queries, h, chunks, place):
        def done(b, top, total, acc):
            part_out[place, h, pl.ds(b * PER, PER)] = (acc / total).astype(jnp.bfloat16).reshape(PER, TOK, HD)
            for p in range(PER):
                rows = slice(p * TOK, (p + 1) * TOK)
                at = b * PER + p
                stat_out[place, h, at : at + 1] = jnp.sum(jnp.where(eye, top[rows], 0.0), axis=0, keepdims=True)
                stat_out[place, h, XS + at : XS + at + 1] = jnp.sum(jnp.where(eye, total[rows], 0.0), axis=0, keepdims=True)

        return [(queries, b, chunks, done) for b in range(QB)]

    def own_rows(h, extra, final):
        def done(b, top, total, acc):
            at = h * QB + b
            if final:
                accs[at] = acc / total
            else:
                accs[at] = acc
                tops[at] = jnp.broadcast_to(top, (ROWS, HD))
                totals[at] = jnp.broadcast_to(total, (ROWS, HD))

        return [(qs, b, extra + [(ks, vs, c, c == b) for c in range(b + 1)], done) for b in range(QB)]

    whole_own = [(ks, vs, c, False) for c in range(QB)]
    whole_first = [(k0, v0, c, False) for c in range(QB)]

    def between(h):
        @pl.when(row == 1)
        def _():
            arrived(KS, h)
            arrived(VS, h)
            z_copy(ZK, h).wait_recv()
            z_copy(ZV, h).wait_recv()
            z_copy(ZQ2, h).wait_recv()
            z_copy(ZQ3, h).wait_recv()
            attend(h, partial(q2, h, whole_first + whole_own, 0) + partial(q3, h, whole_first + whole_own, 1))
            z_copy(ZO2, h).start()
            z_copy(ZS2, h).start()
            z_copy(ZO3, h).start()
            z_copy(ZS3, h).start()

        @pl.when(row == 2)
        def _():
            arrived(KS, h)
            arrived(VS, h)
            z_copy(ZQ3B, h).wait_recv()
            attend(h, partial(q3, h, whole_own, 1))
            z_copy(ZO3B, h).start()
            z_copy(ZS3B, h).start()

    def own_others(h):
        @pl.when(row == 0)
        def _():
            arrived(QS, h)
            attend(h, own_rows(h, [], True))

        @pl.when(row == 1)
        def _():
            arrived(QS, h)
            attend(h, own_rows(h, whole_first, True))

        @pl.when(row == 2)
        def _():
            attend(h, own_rows(h, [], False))

        @pl.when(row == 3)
        def _():
            arrived(KS, h)
            arrived(VS, h)
            attend(h, own_rows(h, [], False))

    def cross_document(part, k):
        doc = lax.rem(y + k, 4)
        groups = [(t, g) for t in range(XS) for g in range(TOK // GROUP)]
        picks = [[idx_s[part, doc, t, 0, g * NEIGH + n] for n in range(NEIGH)] for t, g in groups]
        s = []
        for (t, g), pick in zip(groups, picks):
            keys = jnp.concatenate([kd[block] for block in pick], axis=0)
            q = qc[part, doc, t, pl.ds(g * GROUP, GROUP), :]
            s.append(lax.dot_general(q, keys, NT, preferred_element_type=jnp.float32))
        top = [jnp.max(one, axis=1, keepdims=True) for one in s]
        w = [jnp.exp2((one - high) * EXPO) for one, high in zip(s, top)]
        total = [jnp.sum(one, axis=1, keepdims=True) for one in w]
        o = []
        for one, pick in zip(w, picks):
            values = jnp.concatenate([vd[block] for block in pick], axis=0)
            o.append(lax.dot_general(one.astype(jnp.bfloat16), values, NN, preferred_element_type=jnp.float32))
        for (t, g), one, whole in zip(groups, o, total):
            cross_out[part, doc, t, pl.ds(g * GROUP, GROUP), :] = (one / whole).astype(jnp.bfloat16)

        here = (part == 0) & (k == 0)

        @pl.when(jnp.logical_not(here))
        def _():
            back_copy(part, k).start()

        @pl.when(here)
        def _():
            own_back().start()

    def cross_stage():
        own_qc().wait()
        for kind in range(2):
            own_db(kind).wait()
            own_far(kind).wait()

        def wait_other_core(k):
            for kind in range(2):
                wait_shard(kind, 2 * k + 1 - core)

        loop(0, HALF, wait_other_core)

        def cross_row_of(n):
            part = 1 - n
            loop(n, 4 * XS, wait_plane(part))
            numbers = pltpu.make_async_copy(idx.at[part], idx_s.at[part], number_sem)
            numbers.start()
            numbers.wait()
            loop(0, 4, lambda k: cross_document(part, 3 - k))

        loop(0, 2, cross_row_of)

    @pl.when(row == 0)
    def _():
        relay(0)
        relay(1)
        far_stage()
        relay(2)
        relay(3)

    @pl.when(row >= 2)
    def _():
        loop(0, LOCAL, relay)

    pl.when(row == 3)(far_stage)

    @pl.when(edge)
    def _():
        core_stage()
        cross_stage()

    loop(0, LOCAL, between)

    def merge(h, parts):
        for b in range(QB):
            at = h * QB + b
            for p in range(PER):
                rows = slice(p * TOK, (p + 1) * TOK)
                sub = b * PER + p
                top = tops[at, rows, :1]
                others = []
                for place in range(parts):
                    column = [
                        jnp.sum(jnp.where(eye, stat_in[place, h, n : n + 1], 0.0), axis=1, keepdims=True)
                        for n in (sub, XS + sub)
                    ]
                    others.append(column)
                peak = top
                for other_top, _ in others:
                    peak = jnp.maximum(peak, other_top)
                keep = jnp.exp2((top - peak) * EXPO)
                total = totals[at, rows, :1] * keep
                acc = accs[at, rows, :] * keep
                for place, (other_top, other_total) in enumerate(others):
                    w = jnp.exp2((other_top - peak) * EXPO) * other_total
                    total = total + w
                    acc = acc + part_in[place, h, sub].astype(jnp.float32) * w
                accs[at, rows, :] = acc / total

    def out_copy(h, t):
        return pltpu.make_async_remote_copy(
            mixed.at[h, t], out_ref.at[:, cols(x * LOCAL + h)], x_send.at[OUT, h, t], x_recv.at[OUT, h, x],
            device_id={"dp": dp, "ctx": row * XS + t}, device_id_type=MESH,
        )

    def own_out(h):
        return pltpu.make_async_copy(mixed.at[h, x], out_ref.at[:, cols(x * LOCAL + h)], own_sem.at[OUT, h])

    def emit(h):
        @pl.when(row == 2)
        def _():
            z_copy(ZO2, h).wait_recv()
            z_copy(ZS2, h).wait_recv()
            merge(h, 1)

        @pl.when(row == 3)
        def _():
            z_copy(ZO3, h).wait_recv()
            z_copy(ZS3, h).wait_recv()
            z_copy(ZO3B, h).wait_recv()
            z_copy(ZS3B, h).wait_recv()
            merge(h, 2)

        @pl.when((h != y) | inner)
        def _():
            there = cross.at[h]
            pltpu.make_async_remote_copy(
                there, there, back_send.at[0, 0], back_recv.at[h],
                device_id={"dp": side + 2 * h + core, "ctx": cross_row * XS + x}, device_id_type=MESH,
            ).wait_recv()

        @pl.when((h == y) & edge)
        def _():
            own_back().wait()

        self_out = accs[pl.ds(h * QB, QB)].astype(jnp.bfloat16).astype(jnp.float32).reshape(XS, TOK, HD)
        mixed[h] = (self_out + cross[h].astype(jnp.float32)).astype(jnp.bfloat16)
        for k in (1, 3, 2):
            out_copy(h, x_at(k)).start()
        own_out(h).start()

    def own_and_emit(h):
        own_others(h)
        emit(h)

    loop(0, LOCAL, own_and_emit)

    @pl.when(edge)
    def _():
        for kind in range(2):
            far_copy(kind).wait_send()
            for far in range(2):
                for k in range(1, 4):
                    y_copy(kind, far, k).wait_send()
                for k in range(4):
                    core_pass(kind, far, k).wait_send()
        for k in range(1, 4):
            back_copy(0, k).wait_send()
        for k in range(4):
            back_copy(1, k).wait_send()

    def finish_plane(k):
        idx_copy(k).wait_send()
        qc_copy(k).wait_send()

    loop(first_plane, 4 * XS, finish_plane)
    def finish(h):
        for k in range(1, XS):
            peer = x_at(k)
            for kind in (KS, VS, QS):
                x_copy(kind, h, peer).wait_send()
        for at, kinds in enumerate(((ZK, ZV), (ZO2, ZS2, ZO3, ZS3), (ZQ2, ZO3B, ZS3B), (ZQ3, ZQ3B))):

            @pl.when(row == at)
            def _():
                for kind in kinds:
                    z_copy(kind, h).wait_send()

    def finish_out(h):
        own_out(h).wait()
        for k in range(1, XS):
            peer = x_at(k)
            out_copy(h, peer).wait_send()
            pltpu.make_async_remote_copy(
                mixed.at[h, peer], out_ref.at[:, cols(peer * LOCAL + h)], x_send.at[OUT, h, peer], x_recv.at[OUT, h, peer],
                device_id={"dp": dp, "ctx": row * XS + peer}, device_id_type=MESH,
            ).wait_recv()

    loop(0, LOCAL, finish)
    loop(0, LOCAL, finish_out)


def shards(q_self, k_self, v_self, q_cross, db_keys, db_values, nb_shard, nb_row):
    anywhere = pl.BlockSpec(memory_space=pl.ANY)
    scalars = pl.BlockSpec(memory_space=pltpu.SMEM)
    heads = pltpu.VMEM((LOCAL, XS, TOK, HD), jnp.bfloat16)
    database = pltpu.VMEM((N_DP * DB_DEV, NLEN, HD), jnp.bfloat16)
    shard = pltpu.VMEM((DB_DEV, NLEN, WIDE), jnp.bfloat16)
    state = pltpu.VMEM((LOCAL * QB, ROWS, HD), jnp.float32)
    parts = pltpu.VMEM((2, LOCAL, XS, TOK, HD), jnp.bfloat16)
    stats = pltpu.VMEM((2, LOCAL, 8, 128), jnp.float32)
    dma = pltpu.SemaphoreType.DMA
    out = pl.pallas_call(
        kernel,
        out_shape=jax.ShapeDtypeStruct((TOK, HEADS * HD), jnp.bfloat16),
        in_specs=[anywhere] * 6 + [scalars] * 2,
        out_specs=anywhere,
        scratch_shapes=[
            heads, heads, heads, parts, heads, heads, heads, heads, database, database,
            pltpu.VMEM((2, 4, XS, 8, 128), jnp.int32),
            pltpu.SMEM((2, 4, XS, 8, 128), jnp.int32),
            heads,
            pltpu.VMEM((3, 2 * QB, ROWS, ROWS), jnp.float32),
            state, state, state,
            parts, stats, parts, stats, heads, parts, shard, shard,
            dma((5, LOCAL, XS)), dma((5, LOCAL, XS)), dma((4 * XS,)), dma((2, 4, XS)), dma((4 * XS,)), dma((2, 4, XS)),
            dma((2, 4)), dma((4,)), dma((11, LOCAL)), dma((11, LOCAL)),
            dma((2,)), dma((2,)), dma((2, 2, 4)), dma((2, 2, 4)), dma((2, N_DP)), dma((5, LOCAL)), dma((4,)), dma,
            pltpu.SemaphoreType.REGULAR,
        ],
        compiler_params=pltpu.CompilerParams(
            collective_id=0, has_side_effects=True, vmem_limit_bytes=60 * 1024 * 1024
        ),
    )(q_self[0], k_self[0], v_self[0], q_cross[0], db_keys, db_values, nb_shard, nb_row)
    return out[None]


def solution(mesh):
    return jax.shard_map(
        shards,
        mesh=mesh,
        in_specs=(
            P("dp", "ctx", None),
            P("dp", "ctx", None),
            P("dp", "ctx", None),
            P("dp", "ctx", None),
            P("dp", None, None),
            P("dp", None, None),
            P("dp", "ctx", None),
            P("dp", "ctx", None),
        ),
        out_specs=P("dp", "ctx", None),
        check_vma=False,
    )
```

```python
import jax
import jax.numpy as jnp
from jax import lax
from jax.experimental import pallas as pl
from jax.experimental.pallas import tpu as pltpu
from jax.sharding import PartitionSpec as P

HEADS = 16
HD = 128
GROUP = 64
NEIGH = 2
NLEN = 128
TOK = 128
DB_DEV = 2
N_DP = 16
HALF = 8
XS = 4
LOCAL = HEADS // XS
WIDE = LOCAL * HD
ROWS = 256
PER = ROWS // TOK
QB = XS // PER
EXPO = HD**-0.5 * 1.4426950408889634
MESH = pl.DeviceIdType.MESH
NT = (((1,), (1,)), ((), ()))
NN = (((1,), (0,)), ((), ()))
QC, KS, VS, QS, OUT = range(5)
ZK, ZV, ZQ2, ZQ3, ZQ3B, ZO2, ZS2, ZO3, ZS3, ZO3B, ZS3B = range(11)


def cols(head):
    return pl.ds(pl.multiple_of(head * HD, HD), HD)


def kernel(
    qs_ref, ks_ref, vs_ref, qc_ref, kd_ref, vd_ref, shard_ref, row_ref, out_ref,
    qs, ks, vs, qc, k0, v0, q2, q3, kd, vd, idx, idx_s, cross, scores, tops, totals, accs,
    part_out, stat_out, part_in, stat_in, mixed, cross_out, kf, vf,
    x_send, x_recv, qc_send, qc_recv, idx_send, idx_recv, back_send, back_recv, z_send, z_recv,
    far_send, far_recv, y_send, core_send, db_recv, own_sem, db_own, number_sem, ready,
):
    dp = lax.axis_index("dp")
    me = lax.axis_index("ctx")
    row = me // XS
    x = lax.rem(me, XS)
    near = lax.rem(dp, HALF)
    side = dp - near
    away = HALF - side
    y = near // 2
    core = lax.rem(near, 2)
    other_core = dp + 1 - 2 * core
    far_dp = away + near
    far_ctx = (3 - row) * XS + x
    edge = (row == 0) | (row == 3)
    first_side = dp < HALF
    inner = (row == 1) | (row == 2)
    pair = row + 1 - 2 * lax.rem(row, 2)
    cross_row = jnp.where(inner, pair, row)
    cross_part = jnp.where(inner, 1, 0)

    def x_at(k):
        return lax.rem(x + k, XS)

    def y_at(home, k):
        return home + lax.rem(near + 2 * k, HALF)

    def loop(first, last, body):
        def step(k, carry):
            body(k)
            return carry

        lax.fori_loop(first, last, step, 0)

    barrier = pltpu.get_barrier_semaphore()

    def greet(dp_of, ctx_of):
        pl.semaphore_signal(barrier, inc=1, device_id={"dp": dp_of, "ctx": ctx_of}, device_id_type=MESH)

    def plane(k):
        return lax.rem(y + k // XS, 4), x_at(lax.rem(k, XS))

    def greet_plane(of_row):
        def step(k):
            to_y, to_x = plane(k)
            greet(side + 2 * to_y + core, of_row * XS + to_x)

        return step

    loop(1, jnp.where(edge, 4 * XS, XS), greet_plane(row))
    loop(1, 4 * XS, greet_plane(pair))
    for k in range(1, 4):
        greet(dp, lax.rem(row + k, 4) * XS + x)

    @pl.when(edge)
    def _():
        greet(other_core, me)

    @pl.when(edge & first_side)
    def _():
        greet(far_dp, far_ctx)

    lane = lax.broadcasted_iota(jnp.int32, (8, 128), 1)
    tile = jnp.zeros((8, 128), jnp.int32)
    for g in range(TOK // GROUP):
        for n in range(NEIGH):
            block = shard_ref[0, g, n] * DB_DEV + row_ref[0, g, n]
            tile = jnp.where(lane == g * NEIGH + n, block, tile)
    idx[cross_part, y, x] = tile

    arrays = {KS: (ks_ref, ks), VS: (vs_ref, vs), QS: (qs_ref, qs)}
    blocks = ((kd_ref, kd, kf), (vd_ref, vd, vf))
    wide = pl.ds(pl.multiple_of(x * WIDE, WIDE), WIDE)
    head = x * LOCAL + y

    def own_copy(kind, h):
        arg, buf = arrays[kind]
        return pltpu.make_async_copy(arg.at[:, cols(x * LOCAL + h)], buf.at[h, x], own_sem.at[kind, h])

    def own_qc():
        return pltpu.make_async_copy(qc_ref.at[:, cols(head)], qc.at[0, y, x], own_sem.at[QC, 0])

    def own_db(kind):
        arg, buf, far = blocks[kind]
        return pltpu.make_async_copy(arg.at[:, :, cols(head)], buf.at[pl.ds(dp * DB_DEV, DB_DEV)], db_own.at[kind])

    def own_far(kind):
        arg, buf, far = blocks[kind]
        return pltpu.make_async_copy(far.at[:, :, cols(y)], buf.at[pl.ds(far_dp * DB_DEV, DB_DEV)], db_own.at[2 + kind])

    def start_own(h):
        for kind in (KS, VS, QS):
            own_copy(kind, h).start()

    loop(0, LOCAL, start_own)

    @pl.when(edge)
    def _():
        own_qc().start()
        for kind in range(2):
            own_db(kind).start()

    pl.semaphore_wait(barrier, 21 + jnp.where(edge, 13, 0) + jnp.where(edge & (dp >= HALF), 1, 0))

    @pl.when(edge & (dp >= HALF))
    def _():
        pl.semaphore_signal(ready, inc=1, device_id={"dp": far_dp, "ctx": far_ctx}, device_id_type=MESH)

    def far_copy(kind):
        arg, buf, far = blocks[kind]
        return pltpu.make_async_remote_copy(
            arg.at[:, :, wide], far, far_send.at[kind], far_recv.at[kind],
            device_id={"dp": far_dp, "ctx": far_ctx}, device_id_type=MESH,
        )

    def shard_copy(kind, shard, src, send, target):
        part = blocks[kind][1].at[pl.ds(shard * DB_DEV, DB_DEV)]
        return pltpu.make_async_remote_copy(
            part if src is None else src, part, send, db_recv.at[kind, shard],
            device_id={"dp": target, "ctx": me}, device_id_type=MESH,
        )

    def y_copy(kind, far, k):
        to_y = lax.rem(y + k, 4)
        src = blocks[kind][2].at[:, :, cols(to_y)] if far else blocks[kind][0].at[:, :, cols(x * LOCAL + to_y)]
        return shard_copy(kind, far_dp if far else dp, src, y_send.at[kind, far, k], y_at(side, k))

    def core_pass(kind, far, k):
        src = None
        if k == 0:
            src = blocks[kind][2].at[:, :, cols(y)] if far else blocks[kind][0].at[:, :, cols(head)]
        return shard_copy(kind, y_at(away if far else side, k), src, core_send.at[kind, far, k], other_core)

    def wait_shard(kind, shard):
        shard_copy(kind, shard, None, far_send.at[kind], other_core).wait_recv()

    def qc_copy(k):
        to_y, to_x = plane(k)
        return pltpu.make_async_remote_copy(
            qc_ref.at[:, cols(to_x * LOCAL + to_y)], qc.at[cross_part, y, x], qc_send.at[k], qc_recv.at[cross_part, y, x],
            device_id={"dp": side + 2 * to_y + core, "ctx": cross_row * XS + to_x}, device_id_type=MESH,
        )

    def idx_copy(k):
        to_y, to_x = plane(k)
        return pltpu.make_async_remote_copy(
            idx.at[cross_part, y, x], idx.at[cross_part, y, x], idx_send.at[k], idx_recv.at[cross_part, y, x],
            device_id={"dp": side + 2 * to_y + core, "ctx": cross_row * XS + to_x}, device_id_type=MESH,
        )

    def wait_plane(part):
        def step(k):
            from_y, from_x = plane(k)
            for buf, sent, received in ((idx, idx_send, idx_recv), (qc, qc_send, qc_recv)):
                there = buf.at[part, from_y, from_x]
                pltpu.make_async_remote_copy(
                    there, there, sent.at[k], received.at[part, from_y, from_x],
                    device_id={"dp": side + 2 * from_y + core, "ctx": jnp.where(part == 1, pair, row) * XS + from_x},
                    device_id_type=MESH,
                ).wait_recv()

        return step

    def back_copy(part, k):
        to_y = lax.rem(y + k, 4)
        return pltpu.make_async_remote_copy(
            cross_out.at[part, to_y], cross.at[y], back_send.at[part, k], back_recv.at[y],
            device_id={"dp": y_at(side, k), "ctx": jnp.where(part == 1, pair, row) * XS + x}, device_id_type=MESH,
        )

    def own_back():
        return pltpu.make_async_copy(cross_out.at[0, y], cross.at[y], own_sem.at[QC, 1])

    def x_copy(kind, h, to):
        arg, buf = arrays[kind]
        return pltpu.make_async_remote_copy(
            arg.at[:, cols(to * LOCAL + h)], buf.at[h, x], x_send.at[kind, h, to], x_recv.at[kind, h, x],
            device_id={"dp": dp, "ctx": row * XS + to}, device_id_type=MESH,
        )

    def arrived(kind, h):
        own_copy(kind, h).wait()
        for k in range(1, XS):
            source = x_at(k)
            buf = arrays[kind][1].at[h, source]
            pltpu.make_async_remote_copy(
                buf, buf, x_send.at[kind, h, source], x_recv.at[kind, h, source],
                device_id={"dp": dp, "ctx": row * XS + source}, device_id_type=MESH,
            ).wait_recv()

    def start_x(kinds):
        def step(h):
            for k in (1, 3, 2):
                for kind in kinds:
                    x_copy(kind, h, x_at(k)).start()

        loop(0, LOCAL, step)

    first_plane = jnp.where(inner, 0, 1)

    def start_plane():
        def step(k):
            idx_copy(k).start()
            qc_copy(k).start()

        loop(first_plane, 4 * XS, step)

    def start_near():
        for kind in range(2):
            for k in (1, 3, 2):
                y_copy(kind, 0, k).start()
            core_pass(kind, 0, 0).start()

    def start_far_first():
        @pl.when(dp >= HALF)
        def _():
            for kind in range(2):
                far_copy(kind).start()

    def start_far_second():
        @pl.when(first_side)
        def _():
            pl.semaphore_wait(ready, 1)
            for kind in range(2):
                far_copy(kind).start()

    @pl.when(row == 0)
    def _():
        start_far_first()
        start_x((KS, VS))
        start_near()
        start_plane()
        start_far_second()
        start_x((QS,))

    @pl.when(row == 1)
    def _():
        start_plane()
        start_x((KS, VS))
        start_x((QS,))

    @pl.when(row == 2)
    def _():
        start_x((QS,))
        start_plane()
        start_x((KS, VS))

    @pl.when(row == 3)
    def _():
        start_far_first()
        start_x((QS,))
        start_near()
        start_plane()
        start_far_second()
        start_x((KS, VS))

    def z_copy(kind, h):
        src, dst, to = {
            ZK: (ks.at[h], k0.at[h], 1),
            ZV: (vs.at[h], v0.at[h], 1),
            ZQ2: (qs.at[h], q2.at[h], 1),
            ZQ3: (qs.at[h], q3.at[h], 1),
            ZQ3B: (qs.at[h], q3.at[h], 2),
            ZO2: (part_out.at[0, h], part_in.at[0, h], 2),
            ZS2: (stat_out.at[0, h], stat_in.at[0, h], 2),
            ZO3: (part_out.at[1, h], part_in.at[0, h], 3),
            ZS3: (stat_out.at[1, h], stat_in.at[0, h], 3),
            ZO3B: (part_out.at[1, h], part_in.at[1, h], 3),
            ZS3B: (stat_out.at[1, h], stat_in.at[1, h], 3),
        }[kind]
        return pltpu.make_async_remote_copy(
            src, dst, z_send.at[kind, h], z_recv.at[kind, h],
            device_id={"dp": dp, "ctx": to * XS + x}, device_id_type=MESH,
        )

    def relay(h):
        @pl.when(row == 0)
        def _():
            arrived(KS, h)
            z_copy(ZK, h).start()
            arrived(VS, h)
            z_copy(ZV, h).start()

        @pl.when(row == 2)
        def _():
            arrived(QS, h)
            z_copy(ZQ2, h).start()

        @pl.when(row == 3)
        def _():
            arrived(QS, h)
            z_copy(ZQ3, h).start()
            z_copy(ZQ3B, h).start()

    def far_stage():
        for kind in range(2):
            far_copy(kind).wait_recv()
            for k in (1, 3, 2):
                y_copy(kind, 1, k).start()
            core_pass(kind, 1, 0).start()
            own_far(kind).start()

    def core_stage():
        for far in range(2):
            for kind in range(2):
                for k in (1, 3, 2):
                    wait_shard(kind, y_at(away if far else side, k))
                    core_pass(kind, far, k).start()

    diagonal = lax.broadcasted_iota(jnp.int32, (ROWS, ROWS), 0) >= lax.broadcasted_iota(jnp.int32, (ROWS, ROWS), 1)
    eye = lax.broadcasted_iota(jnp.int32, (TOK, TOK), 0) == lax.broadcasted_iota(jnp.int32, (TOK, TOK), 1)

    def score_block(queries, h, b, chunks, slot):
        q = queries[h, pl.ds(b * PER, PER)].reshape(ROWS, HD)
        peak = None
        for j, (keys, values, c, masked) in enumerate(chunks):
            k = keys[h, pl.ds(c * PER, PER)].reshape(ROWS, HD)
            s = lax.dot_general(q, k, NT, preferred_element_type=jnp.float32)
            if masked:
                s = jnp.where(diagonal, s, -1e30)
            scores[slot, j] = s
            folded = jnp.maximum(s[:, :HD], s[:, HD:])
            peak = folded if peak is None else jnp.maximum(peak, folded)
        return jnp.max(peak, axis=1, keepdims=True)

    def weigh_block(h, chunks, slot, top):
        total = jnp.zeros((ROWS, HD), jnp.float32)
        acc = jnp.zeros((ROWS, HD), jnp.float32)
        for j, (keys, values, c, masked) in enumerate(chunks):
            w = jnp.exp2((scores[slot, j] - top) * EXPO)
            total = total + (w[:, :HD] + w[:, HD:])
            v = values[h, pl.ds(c * PER, PER)].reshape(ROWS, HD)
            acc = acc + lax.dot_general(w.astype(jnp.bfloat16), v, NN, preferred_element_type=jnp.float32)
        return jnp.sum(total, axis=1, keepdims=True), acc

    def attend(h, jobs):
        tops_of = []
        for n in range(len(jobs) + 1):
            if n < len(jobs):
                queries, b, chunks, done = jobs[n]
                tops_of.append(score_block(queries, h, b, chunks, n % 3))
            if n >= 1:
                queries, b, chunks, done = jobs[n - 1]
                done(b, tops_of[n - 1], *weigh_block(h, chunks, (n - 1) % 3, tops_of[n - 1]))

    def partial(queries, h, chunks, place):
        def done(b, top, total, acc):
            part_out[place, h, pl.ds(b * PER, PER)] = (acc / total).astype(jnp.bfloat16).reshape(PER, TOK, HD)
            for p in range(PER):
                rows = slice(p * TOK, (p + 1) * TOK)
                at = b * PER + p
                stat_out[place, h, at : at + 1] = jnp.sum(jnp.where(eye, top[rows], 0.0), axis=0, keepdims=True)
                stat_out[place, h, XS + at : XS + at + 1] = jnp.sum(jnp.where(eye, total[rows], 0.0), axis=0, keepdims=True)

        return [(queries, b, chunks, done) for b in range(QB)]

    def own_rows(h, extra, final):
        def done(b, top, total, acc):
            at = h * QB + b
            if final:
                accs[at] = acc / total
            else:
                accs[at] = acc
                tops[at] = jnp.broadcast_to(top, (ROWS, HD))
                totals[at] = jnp.broadcast_to(total, (ROWS, HD))

        return [(qs, b, extra + [(ks, vs, c, c == b) for c in range(b + 1)], done) for b in range(QB)]

    whole_own = [(ks, vs, c, False) for c in range(QB)]
    whole_first = [(k0, v0, c, False) for c in range(QB)]

    def between(h):
        @pl.when(row == 1)
        def _():
            arrived(KS, h)
            arrived(VS, h)
            z_copy(ZK, h).wait_recv()
            z_copy(ZV, h).wait_recv()
            z_copy(ZQ2, h).wait_recv()
            z_copy(ZQ3, h).wait_recv()
            attend(h, partial(q2, h, whole_first + whole_own, 0) + partial(q3, h, whole_first + whole_own, 1))
            z_copy(ZO2, h).start()
            z_copy(ZS2, h).start()
            z_copy(ZO3, h).start()
            z_copy(ZS3, h).start()

        @pl.when(row == 2)
        def _():
            arrived(KS, h)
            arrived(VS, h)
            z_copy(ZQ3B, h).wait_recv()
            attend(h, partial(q3, h, whole_own, 1))
            z_copy(ZO3B, h).start()
            z_copy(ZS3B, h).start()

    def own_others(h):
        @pl.when(row == 0)
        def _():
            arrived(QS, h)
            attend(h, own_rows(h, [], True))

        @pl.when(row == 1)
        def _():
            arrived(QS, h)
            attend(h, own_rows(h, whole_first, True))

        @pl.when(row == 2)
        def _():
            attend(h, own_rows(h, [], False))

        @pl.when(row == 3)
        def _():
            arrived(KS, h)
            arrived(VS, h)
            attend(h, own_rows(h, [], False))

    def cross_document(part, k):
        doc = lax.rem(y + k, 4)
        groups = [(t, g) for t in range(XS) for g in range(TOK // GROUP)]
        picks = [[idx_s[part, doc, t, 0, g * NEIGH + n] for n in range(NEIGH)] for t, g in groups]
        s = []
        for (t, g), pick in zip(groups, picks):
            keys = jnp.concatenate([kd[block] for block in pick], axis=0)
            q = qc[part, doc, t, pl.ds(g * GROUP, GROUP), :]
            s.append(lax.dot_general(q, keys, NT, preferred_element_type=jnp.float32))
        top = [jnp.max(one, axis=1, keepdims=True) for one in s]
        w = [jnp.exp2((one - high) * EXPO) for one, high in zip(s, top)]
        total = [jnp.sum(one, axis=1, keepdims=True) for one in w]
        o = []
        for one, pick in zip(w, picks):
            values = jnp.concatenate([vd[block] for block in pick], axis=0)
            o.append(lax.dot_general(one.astype(jnp.bfloat16), values, NN, preferred_element_type=jnp.float32))
        for (t, g), one, whole in zip(groups, o, total):
            cross_out[part, doc, t, pl.ds(g * GROUP, GROUP), :] = (one / whole).astype(jnp.bfloat16)

        here = (part == 0) & (k == 0)

        @pl.when(jnp.logical_not(here))
        def _():
            back_copy(part, k).start()

        @pl.when(here)
        def _():
            own_back().start()

    def cross_stage():
        own_qc().wait()
        for kind in range(2):
            own_db(kind).wait()
            own_far(kind).wait()

        def wait_other_core(k):
            for kind in range(2):
                wait_shard(kind, 2 * k + 1 - core)

        loop(0, HALF, wait_other_core)

        def cross_row_of(n):
            part = 1 - n
            loop(n, 4 * XS, wait_plane(part))
            numbers = pltpu.make_async_copy(idx.at[part], idx_s.at[part], number_sem)
            numbers.start()
            numbers.wait()
            loop(0, 4, lambda k: cross_document(part, 3 - k))

        loop(0, 2, cross_row_of)

    @pl.when(row == 0)
    def _():
        relay(0)
        relay(1)
        far_stage()
        relay(2)
        relay(3)

    @pl.when(row >= 2)
    def _():
        loop(0, LOCAL, relay)

    pl.when(row == 3)(far_stage)

    @pl.when(edge)
    def _():
        core_stage()
        cross_stage()

    loop(0, LOCAL, between)

    def merge(h, parts):
        for b in range(QB):
            at = h * QB + b
            for p in range(PER):
                rows = slice(p * TOK, (p + 1) * TOK)
                sub = b * PER + p
                top = tops[at, rows, :1]
                others = []
                for place in range(parts):
                    column = [
                        jnp.sum(jnp.where(eye, stat_in[place, h, n : n + 1], 0.0), axis=1, keepdims=True)
                        for n in (sub, XS + sub)
                    ]
                    others.append(column)
                peak = top
                for other_top, _ in others:
                    peak = jnp.maximum(peak, other_top)
                keep = jnp.exp2((top - peak) * EXPO)
                total = totals[at, rows, :1] * keep
                acc = accs[at, rows, :] * keep
                for place, (other_top, other_total) in enumerate(others):
                    w = jnp.exp2((other_top - peak) * EXPO) * other_total
                    total = total + w
                    acc = acc + part_in[place, h, sub].astype(jnp.float32) * w
                accs[at, rows, :] = acc / total

    def out_copy(h, t):
        return pltpu.make_async_remote_copy(
            mixed.at[h, t], out_ref.at[:, cols(x * LOCAL + h)], x_send.at[OUT, h, t], x_recv.at[OUT, h, x],
            device_id={"dp": dp, "ctx": row * XS + t}, device_id_type=MESH,
        )

    def own_out(h):
        return pltpu.make_async_copy(mixed.at[h, x], out_ref.at[:, cols(x * LOCAL + h)], own_sem.at[OUT, h])

    def emit(h):
        @pl.when(row == 2)
        def _():
            z_copy(ZO2, h).wait_recv()
            z_copy(ZS2, h).wait_recv()
            merge(h, 1)

        @pl.when(row == 3)
        def _():
            z_copy(ZO3, h).wait_recv()
            z_copy(ZS3, h).wait_recv()
            z_copy(ZO3B, h).wait_recv()
            z_copy(ZS3B, h).wait_recv()
            merge(h, 2)

        @pl.when((h != y) | inner)
        def _():
            there = cross.at[h]
            pltpu.make_async_remote_copy(
                there, there, back_send.at[0, 0], back_recv.at[h],
                device_id={"dp": side + 2 * h + core, "ctx": cross_row * XS + x}, device_id_type=MESH,
            ).wait_recv()

        @pl.when((h == y) & edge)
        def _():
            own_back().wait()

        self_out = accs[pl.ds(h * QB, QB)].astype(jnp.bfloat16).astype(jnp.float32).reshape(XS, TOK, HD)
        mixed[h] = (self_out + cross[h].astype(jnp.float32)).astype(jnp.bfloat16)
        for k in (1, 3, 2):
            out_copy(h, x_at(k)).start()
        own_out(h).start()

    def own_and_emit(h):
        own_others(h)
        emit(h)

    loop(0, LOCAL, own_and_emit)

    @pl.when(edge)
    def _():
        for kind in range(2):
            far_copy(kind).wait_send()
            for far in range(2):
                for k in range(1, 4):
                    y_copy(kind, far, k).wait_send()
                for k in range(4):
                    core_pass(kind, far, k).wait_send()
        for k in range(1, 4):
            back_copy(0, k).wait_send()
        for k in range(4):
            back_copy(1, k).wait_send()

    def finish_plane(k):
        idx_copy(k).wait_send()
        qc_copy(k).wait_send()

    loop(first_plane, 4 * XS, finish_plane)
    def finish(h):
        for k in range(1, XS):
            peer = x_at(k)
            for kind in (KS, VS, QS):
                x_copy(kind, h, peer).wait_send()
        for at, kinds in enumerate(((ZK, ZV), (ZO2, ZS2, ZO3, ZS3), (ZQ2, ZO3B, ZS3B), (ZQ3, ZQ3B))):

            @pl.when(row == at)
            def _():
                for kind in kinds:
                    z_copy(kind, h).wait_send()

    def finish_out(h):
        own_out(h).wait()
        for k in range(1, XS):
            peer = x_at(k)
            out_copy(h, peer).wait_send()
            pltpu.make_async_remote_copy(
                mixed.at[h, peer], out_ref.at[:, cols(peer * LOCAL + h)], x_send.at[OUT, h, peer], x_recv.at[OUT, h, peer],
                device_id={"dp": dp, "ctx": row * XS + peer}, device_id_type=MESH,
            ).wait_recv()

    loop(0, LOCAL, finish)
    loop(0, LOCAL, finish_out)


def shards(q_self, k_self, v_self, q_cross, db_keys, db_values, nb_shard, nb_row):
    anywhere = pl.BlockSpec(memory_space=pl.ANY)
    scalars = pl.BlockSpec(memory_space=pltpu.SMEM)
    heads = pltpu.VMEM((LOCAL, XS, TOK, HD), jnp.bfloat16)
    database = pltpu.VMEM((N_DP * DB_DEV, NLEN, HD), jnp.bfloat16)
    shard = pltpu.VMEM((DB_DEV, NLEN, WIDE), jnp.bfloat16)
    state = pltpu.VMEM((LOCAL * QB, ROWS, HD), jnp.float32)
    parts = pltpu.VMEM((2, LOCAL, XS, TOK, HD), jnp.bfloat16)
    stats = pltpu.VMEM((2, LOCAL, 8, 128), jnp.float32)
    dma = pltpu.SemaphoreType.DMA
    out = pl.pallas_call(
        kernel,
        out_shape=jax.ShapeDtypeStruct((TOK, HEADS * HD), jnp.bfloat16),
        in_specs=[anywhere] * 6 + [scalars] * 2,
        out_specs=anywhere,
        scratch_shapes=[
            heads, heads, heads, parts, heads, heads, heads, heads, database, database,
            pltpu.VMEM((2, 4, XS, 8, 128), jnp.int32),
            pltpu.SMEM((2, 4, XS, 8, 128), jnp.int32),
            heads,
            pltpu.VMEM((3, 2 * QB, ROWS, ROWS), jnp.float32),
            state, state, state,
            parts, stats, parts, stats, heads, parts, shard, shard,
            dma((5, LOCAL, XS)), dma((5, LOCAL, XS)), dma((4 * XS,)), dma((2, 4, XS)), dma((4 * XS,)), dma((2, 4, XS)),
            dma((2, 4)), dma((4,)), dma((11, LOCAL)), dma((11, LOCAL)),
            dma((2,)), dma((2,)), dma((2, 2, 4)), dma((2, 2, 4)), dma((2, N_DP)), dma((5, LOCAL)), dma((4,)), dma,
            pltpu.SemaphoreType.REGULAR,
        ],
        compiler_params=pltpu.CompilerParams(
            collective_id=0, has_side_effects=True, vmem_limit_bytes=60 * 1024 * 1024
        ),
    )(q_self[0], k_self[0], v_self[0], q_cross[0], db_keys, db_values, nb_shard, nb_row)
    return out[None]


def solution(mesh):
    return jax.shard_map(
        shards,
        mesh=mesh,
        in_specs=(
            P("dp", "ctx", None),
            P("dp", "ctx", None),
            P("dp", "ctx", None),
            P("dp", "ctx", None),
            P("dp", None, None),
            P("dp", None, None),
            P("dp", "ctx", None),
            P("dp", "ctx", None),
        ),
        out_specs=P("dp", "ctx", None),
        check_vma=False,
    )
```

```python
import jax
import jax.numpy as jnp
from jax import lax
from jax.experimental import pallas as pl
from jax.experimental.pallas import tpu as pltpu
from jax.sharding import PartitionSpec as P

HEADS = 16
HD = 128
GROUP = 64
NEIGH = 2
NLEN = 128
TOK = 128
DB_DEV = 2
N_DP = 16
HALF = 8
XS = 4
LOCAL = HEADS // XS
ROWS = 256
PER = ROWS // TOK
QB = XS // PER
EXPO = HD**-0.5 * 1.4426950408889634
MESH = pl.DeviceIdType.MESH
NT = (((1,), (1,)), ((), ()))
NN = (((1,), (0,)), ((), ()))
QC, KS, VS, QS, OUT = range(5)
ZK, ZV, ZQ2, ZQ3, ZQ3B, ZO2, ZS2, ZO3, ZS3, ZO3B, ZS3B = range(11)


def cols(head):
    return pl.ds(pl.multiple_of(head * HD, HD), HD)


def kernel(
    qs_ref, ks_ref, vs_ref, qc_ref, kd_ref, vd_ref, shard_ref, row_ref, out_ref,
    qs, ks, vs, qc, k0, v0, q2, q3, kd, vd, idx, idx_s, cross, scores, tops, totals, accs,
    part_out, stat_out, part_in, stat_in, mixed, cross_out,
    x_send, x_recv, qc_send, qc_recv, idx_send, idx_recv, back_send, back_recv, z_send, z_recv,
    y_send, core_send, db_recv, own_sem, db_own, number_sem, ready,
):
    dp = lax.axis_index("dp")
    me = lax.axis_index("ctx")
    row = me // XS
    x = lax.rem(me, XS)
    near = lax.rem(dp, HALF)
    side = dp - near
    away = HALF - side
    y = near // 2
    core = lax.rem(near, 2)
    other_core = dp + 1 - 2 * core
    far_ctx = (3 - row) * XS + x
    edge = (row == 0) | (row == 3)
    first_side = dp < HALF
    inner = (row == 1) | (row == 2)
    pair = row + 1 - 2 * lax.rem(row, 2)
    cross_row = jnp.where(inner, pair, row)
    cross_part = jnp.where(inner, 1, 0)

    def x_at(k):
        return lax.rem(x + k, XS)

    def y_at(home, k):
        return home + lax.rem(near + 2 * k, HALF)

    def loop(first, last, body):
        def step(k, carry):
            body(k)
            return carry

        lax.fori_loop(first, last, step, 0)

    barrier = pltpu.get_barrier_semaphore()

    def greet(dp_of, ctx_of):
        pl.semaphore_signal(barrier, inc=1, device_id={"dp": dp_of, "ctx": ctx_of}, device_id_type=MESH)

    def plane(k):
        return lax.rem(y + k // XS, 4), x_at(lax.rem(k, XS))

    def greet_plane(of_row):
        def step(k):
            to_y, to_x = plane(k)
            greet(side + 2 * to_y + core, of_row * XS + to_x)

        return step

    loop(1, jnp.where(edge, 4 * XS, XS), greet_plane(row))
    loop(1, 4 * XS, greet_plane(pair))
    for k in range(1, 4):
        greet(dp, lax.rem(row + k, 4) * XS + x)

    @pl.when(edge)
    def _():
        greet(other_core, me)

    @pl.when(edge & first_side)
    def _():
        for k in range(4):
            greet(y_at(away, k), far_ctx)

    lane = lax.broadcasted_iota(jnp.int32, (8, 128), 1)
    tile = jnp.zeros((8, 128), jnp.int32)
    for g in range(TOK // GROUP):
        for n in range(NEIGH):
            block = shard_ref[0, g, n] * DB_DEV + row_ref[0, g, n]
            tile = jnp.where(lane == g * NEIGH + n, block, tile)
    idx[cross_part, y, x] = tile

    arrays = {KS: (ks_ref, ks), VS: (vs_ref, vs), QS: (qs_ref, qs)}
    blocks = ((kd_ref, kd), (vd_ref, vd))
    head = x * LOCAL + y

    def own_copy(kind, h):
        arg, buf = arrays[kind]
        return pltpu.make_async_copy(arg.at[:, cols(x * LOCAL + h)], buf.at[h, x], own_sem.at[kind, h])

    def own_qc():
        return pltpu.make_async_copy(qc_ref.at[:, cols(head)], qc.at[0, y, x], own_sem.at[QC, 0])

    def own_db(kind):
        arg, buf = blocks[kind]
        return pltpu.make_async_copy(arg.at[:, :, cols(head)], buf.at[pl.ds(dp * DB_DEV, DB_DEV)], db_own.at[kind])

    def start_own(h):
        for kind in (KS, VS, QS):
            own_copy(kind, h).start()

    loop(0, LOCAL, start_own)

    @pl.when(edge)
    def _():
        own_qc().start()
        for kind in range(2):
            own_db(kind).start()

    pl.semaphore_wait(barrier, 21 + jnp.where(edge, 13, 0) + jnp.where(edge & (dp >= HALF), 4, 0))

    @pl.when(edge & (dp >= HALF))
    def _():
        for k in range(4):
            pl.semaphore_signal(ready, inc=1, device_id={"dp": y_at(away, k), "ctx": far_ctx}, device_id_type=MESH)

    def shard_copy(kind, shard, src, send, target, target_ctx):
        part = blocks[kind][1].at[pl.ds(shard * DB_DEV, DB_DEV)]
        return pltpu.make_async_remote_copy(
            part if src is None else src, part, send, db_recv.at[kind, shard],
            device_id={"dp": target, "ctx": target_ctx}, device_id_type=MESH,
        )

    def y_copy(kind, far, k):
        src = blocks[kind][0].at[:, :, cols(x * LOCAL + lax.rem(y + k, 4))]
        target = y_at(away if far else side, k)
        return shard_copy(kind, dp, src, y_send.at[kind, far, k], target, far_ctx if far else me)

    def core_pass(kind, far, k):
        src = blocks[kind][0].at[:, :, cols(head)] if (far, k) == (0, 0) else None
        return shard_copy(kind, y_at(away if far else side, k), src, core_send.at[kind, far, k], other_core, me)

    def wait_shard(kind, shard):
        shard_copy(kind, shard, None, y_send.at[kind, 0, 0], other_core, me).wait_recv()

    def qc_copy(k):
        to_y, to_x = plane(k)
        return pltpu.make_async_remote_copy(
            qc_ref.at[:, cols(to_x * LOCAL + to_y)], qc.at[cross_part, y, x], qc_send.at[k], qc_recv.at[cross_part, y, x],
            device_id={"dp": side + 2 * to_y + core, "ctx": cross_row * XS + to_x}, device_id_type=MESH,
        )

    def idx_copy(k):
        to_y, to_x = plane(k)
        return pltpu.make_async_remote_copy(
            idx.at[cross_part, y, x], idx.at[cross_part, y, x], idx_send.at[k], idx_recv.at[cross_part, y, x],
            device_id={"dp": side + 2 * to_y + core, "ctx": cross_row * XS + to_x}, device_id_type=MESH,
        )

    def wait_plane(part):
        def step(k):
            from_y, from_x = plane(k)
            for buf, sent, received in ((idx, idx_send, idx_recv), (qc, qc_send, qc_recv)):
                there = buf.at[part, from_y, from_x]
                pltpu.make_async_remote_copy(
                    there, there, sent.at[k], received.at[part, from_y, from_x],
                    device_id={"dp": side + 2 * from_y + core, "ctx": jnp.where(part == 1, pair, row) * XS + from_x},
                    device_id_type=MESH,
                ).wait_recv()

        return step

    def back_copy(part, k):
        to_y = lax.rem(y + k, 4)
        return pltpu.make_async_remote_copy(
            cross_out.at[part, to_y], cross.at[y], back_send.at[part, k], back_recv.at[y],
            device_id={"dp": y_at(side, k), "ctx": jnp.where(part == 1, pair, row) * XS + x}, device_id_type=MESH,
        )

    def own_back():
        return pltpu.make_async_copy(cross_out.at[0, y], cross.at[y], own_sem.at[QC, 1])

    def x_copy(kind, h, to):
        arg, buf = arrays[kind]
        return pltpu.make_async_remote_copy(
            arg.at[:, cols(to * LOCAL + h)], buf.at[h, x], x_send.at[kind, h, to], x_recv.at[kind, h, x],
            device_id={"dp": dp, "ctx": row * XS + to}, device_id_type=MESH,
        )

    def arrived(kind, h):
        own_copy(kind, h).wait()
        for k in range(1, XS):
            source = x_at(k)
            buf = arrays[kind][1].at[h, source]
            pltpu.make_async_remote_copy(
                buf, buf, x_send.at[kind, h, source], x_recv.at[kind, h, source],
                device_id={"dp": dp, "ctx": row * XS + source}, device_id_type=MESH,
            ).wait_recv()

    def start_x(kinds):
        def step(h):
            for k in (1, 3, 2):
                for kind in kinds:
                    x_copy(kind, h, x_at(k)).start()

        loop(0, LOCAL, step)

    first_plane = jnp.where(inner, 0, 1)

    def start_plane():
        def step(k):
            idx_copy(k).start()
            qc_copy(k).start()

        loop(first_plane, 4 * XS, step)

    def start_near():
        for kind in range(2):
            for k in (1, 3, 2):
                y_copy(kind, 0, k).start()
            core_pass(kind, 0, 0).start()

    def start_far_first():
        @pl.when(dp >= HALF)
        def _():
            for kind in range(2):
                for k in range(4):
                    y_copy(kind, 1, k).start()

    def start_far_second():
        @pl.when(first_side)
        def _():
            pl.semaphore_wait(ready, 4)
            for kind in range(2):
                for k in range(4):
                    y_copy(kind, 1, k).start()

    @pl.when(row == 0)
    def _():
        start_far_first()
        start_x((KS, VS))
        start_near()
        start_plane()
        start_far_second()
        start_x((QS,))

    @pl.when(row == 1)
    def _():
        start_plane()
        start_x((KS, VS))
        start_x((QS,))

    @pl.when(row == 2)
    def _():
        start_x((QS,))
        start_plane()
        start_x((KS, VS))

    @pl.when(row == 3)
    def _():
        start_far_first()
        start_x((QS,))
        start_near()
        start_plane()
        start_far_second()
        start_x((KS, VS))

    def z_copy(kind, h):
        src, dst, to = {
            ZK: (ks.at[h], k0.at[h], 1),
            ZV: (vs.at[h], v0.at[h], 1),
            ZQ2: (qs.at[h], q2.at[h], 1),
            ZQ3: (qs.at[h], q3.at[h], 1),
            ZQ3B: (qs.at[h], q3.at[h], 2),
            ZO2: (part_out.at[0, h], part_in.at[0, h], 2),
            ZS2: (stat_out.at[0, h], stat_in.at[0, h], 2),
            ZO3: (part_out.at[1, h], part_in.at[0, h], 3),
            ZS3: (stat_out.at[1, h], stat_in.at[0, h], 3),
            ZO3B: (part_out.at[1, h], part_in.at[1, h], 3),
            ZS3B: (stat_out.at[1, h], stat_in.at[1, h], 3),
        }[kind]
        return pltpu.make_async_remote_copy(
            src, dst, z_send.at[kind, h], z_recv.at[kind, h],
            device_id={"dp": dp, "ctx": to * XS + x}, device_id_type=MESH,
        )

    def relay(h):
        @pl.when(row == 0)
        def _():
            arrived(KS, h)
            z_copy(ZK, h).start()
            arrived(VS, h)
            z_copy(ZV, h).start()

        @pl.when(row == 2)
        def _():
            arrived(QS, h)
            z_copy(ZQ2, h).start()

        @pl.when(row == 3)
        def _():
            arrived(QS, h)
            z_copy(ZQ3, h).start()
            z_copy(ZQ3B, h).start()

    def core_stage():
        for far in range(2):
            for kind in range(2):
                for k in (0, 1, 3, 2)[1 - far :]:
                    wait_shard(kind, y_at(away if far else side, k))
                    core_pass(kind, far, k).start()

    diagonal = lax.broadcasted_iota(jnp.int32, (ROWS, ROWS), 0) >= lax.broadcasted_iota(jnp.int32, (ROWS, ROWS), 1)
    eye = lax.broadcasted_iota(jnp.int32, (TOK, TOK), 0) == lax.broadcasted_iota(jnp.int32, (TOK, TOK), 1)

    def score_block(queries, h, b, chunks, slot):
        q = queries[h, pl.ds(b * PER, PER)].reshape(ROWS, HD)
        peak = None
        for j, (keys, values, c, masked) in enumerate(chunks):
            k = keys[h, pl.ds(c * PER, PER)].reshape(ROWS, HD)
            s = lax.dot_general(q, k, NT, preferred_element_type=jnp.float32)
            if masked:
                s = jnp.where(diagonal, s, -1e30)
            scores[slot, j] = s
            folded = jnp.maximum(s[:, :HD], s[:, HD:])
            peak = folded if peak is None else jnp.maximum(peak, folded)
        return jnp.max(peak, axis=1, keepdims=True)

    def weigh_block(h, chunks, slot, top):
        total = jnp.zeros((ROWS, HD), jnp.float32)
        acc = jnp.zeros((ROWS, HD), jnp.float32)
        for j, (keys, values, c, masked) in enumerate(chunks):
            w = jnp.exp2((scores[slot, j] - top) * EXPO)
            total = total + (w[:, :HD] + w[:, HD:])
            v = values[h, pl.ds(c * PER, PER)].reshape(ROWS, HD)
            acc = acc + lax.dot_general(w.astype(jnp.bfloat16), v, NN, preferred_element_type=jnp.float32)
        return jnp.sum(total, axis=1, keepdims=True), acc

    def attend(h, jobs):
        tops_of = []
        for n in range(len(jobs) + 1):
            if n < len(jobs):
                queries, b, chunks, done = jobs[n]
                tops_of.append(score_block(queries, h, b, chunks, n % 3))
            if n >= 1:
                queries, b, chunks, done = jobs[n - 1]
                done(b, tops_of[n - 1], *weigh_block(h, chunks, (n - 1) % 3, tops_of[n - 1]))

    def partial(queries, h, chunks, place):
        def done(b, top, total, acc):
            part_out[place, h, pl.ds(b * PER, PER)] = (acc / total).astype(jnp.bfloat16).reshape(PER, TOK, HD)
            for p in range(PER):
                rows = slice(p * TOK, (p + 1) * TOK)
                at = b * PER + p
                stat_out[place, h, at : at + 1] = jnp.sum(jnp.where(eye, top[rows], 0.0), axis=0, keepdims=True)
                stat_out[place, h, XS + at : XS + at + 1] = jnp.sum(jnp.where(eye, total[rows], 0.0), axis=0, keepdims=True)

        return [(queries, b, chunks, done) for b in range(QB)]

    def own_rows(h, extra, final):
        def done(b, top, total, acc):
            at = h * QB + b
            if final:
                accs[at] = acc / total
            else:
                accs[at] = acc
                tops[at] = jnp.broadcast_to(top, (ROWS, HD))
                totals[at] = jnp.broadcast_to(total, (ROWS, HD))

        return [(qs, b, extra + [(ks, vs, c, c == b) for c in range(b + 1)], done) for b in range(QB)]

    whole_own = [(ks, vs, c, False) for c in range(QB)]
    whole_first = [(k0, v0, c, False) for c in range(QB)]

    def between(h):
        @pl.when(row == 1)
        def _():
            arrived(KS, h)
            arrived(VS, h)
            z_copy(ZK, h).wait_recv()
            z_copy(ZV, h).wait_recv()
            z_copy(ZQ2, h).wait_recv()
            z_copy(ZQ3, h).wait_recv()
            attend(h, partial(q2, h, whole_first + whole_own, 0) + partial(q3, h, whole_first + whole_own, 1))
            z_copy(ZO2, h).start()
            z_copy(ZS2, h).start()
            z_copy(ZO3, h).start()
            z_copy(ZS3, h).start()

        @pl.when(row == 2)
        def _():
            arrived(KS, h)
            arrived(VS, h)
            z_copy(ZQ3B, h).wait_recv()
            attend(h, partial(q3, h, whole_own, 1))
            z_copy(ZO3B, h).start()
            z_copy(ZS3B, h).start()

    def own_others(h):
        @pl.when(row == 0)
        def _():
            arrived(QS, h)
            attend(h, own_rows(h, [], True))

        @pl.when(row == 1)
        def _():
            arrived(QS, h)
            attend(h, own_rows(h, whole_first, True))

        @pl.when(row == 2)
        def _():
            attend(h, own_rows(h, [], False))

        @pl.when(row == 3)
        def _():
            arrived(KS, h)
            arrived(VS, h)
            attend(h, own_rows(h, [], False))

    def cross_document(part, k):
        doc = lax.rem(y + k, 4)
        groups = [(t, g) for t in range(XS) for g in range(TOK // GROUP)]
        picks = [[idx_s[part, doc, t, 0, g * NEIGH + n] for n in range(NEIGH)] for t, g in groups]
        s = []
        for (t, g), pick in zip(groups, picks):
            keys = jnp.concatenate([kd[block] for block in pick], axis=0)
            q = qc[part, doc, t, pl.ds(g * GROUP, GROUP), :]
            s.append(lax.dot_general(q, keys, NT, preferred_element_type=jnp.float32))
        top = [jnp.max(one, axis=1, keepdims=True) for one in s]
        w = [jnp.exp2((one - high) * EXPO) for one, high in zip(s, top)]
        total = [jnp.sum(one, axis=1, keepdims=True) for one in w]
        o = []
        for one, pick in zip(w, picks):
            values = jnp.concatenate([vd[block] for block in pick], axis=0)
            o.append(lax.dot_general(one.astype(jnp.bfloat16), values, NN, preferred_element_type=jnp.float32))
        for (t, g), one, whole in zip(groups, o, total):
            cross_out[part, doc, t, pl.ds(g * GROUP, GROUP), :] = (one / whole).astype(jnp.bfloat16)

        here = (part == 0) & (k == 0)

        @pl.when(jnp.logical_not(here))
        def _():
            back_copy(part, k).start()

        @pl.when(here)
        def _():
            own_back().start()

    def cross_stage():
        own_qc().wait()
        for kind in range(2):
            own_db(kind).wait()

        def wait_other_core(k):
            for kind in range(2):
                wait_shard(kind, 2 * k + 1 - core)

        loop(0, HALF, wait_other_core)

        def cross_row_of(n):
            part = 1 - n
            loop(n, 4 * XS, wait_plane(part))
            numbers = pltpu.make_async_copy(idx.at[part], idx_s.at[part], number_sem)
            numbers.start()
            numbers.wait()
            loop(0, 4, lambda k: cross_document(part, 3 - k))

        loop(0, 2, cross_row_of)

    @pl.when(row == 0)
    def _():
        loop(0, LOCAL, relay)

    @pl.when(row >= 2)
    def _():
        loop(0, LOCAL, relay)

    @pl.when(edge)
    def _():
        core_stage()
        cross_stage()

    loop(0, LOCAL, between)

    def merge(h, parts):
        for b in range(QB):
            at = h * QB + b
            for p in range(PER):
                rows = slice(p * TOK, (p + 1) * TOK)
                sub = b * PER + p
                top = tops[at, rows, :1]
                others = []
                for place in range(parts):
                    column = [
                        jnp.sum(jnp.where(eye, stat_in[place, h, n : n + 1], 0.0), axis=1, keepdims=True)
                        for n in (sub, XS + sub)
                    ]
                    others.append(column)
                peak = top
                for other_top, _ in others:
                    peak = jnp.maximum(peak, other_top)
                keep = jnp.exp2((top - peak) * EXPO)
                total = totals[at, rows, :1] * keep
                acc = accs[at, rows, :] * keep
                for place, (other_top, other_total) in enumerate(others):
                    w = jnp.exp2((other_top - peak) * EXPO) * other_total
                    total = total + w
                    acc = acc + part_in[place, h, sub].astype(jnp.float32) * w
                accs[at, rows, :] = acc / total

    def out_copy(h, t):
        return pltpu.make_async_remote_copy(
            mixed.at[h, t], out_ref.at[:, cols(x * LOCAL + h)], x_send.at[OUT, h, t], x_recv.at[OUT, h, x],
            device_id={"dp": dp, "ctx": row * XS + t}, device_id_type=MESH,
        )

    def own_out(h):
        return pltpu.make_async_copy(mixed.at[h, x], out_ref.at[:, cols(x * LOCAL + h)], own_sem.at[OUT, h])

    def emit(h):
        @pl.when(row == 2)
        def _():
            z_copy(ZO2, h).wait_recv()
            z_copy(ZS2, h).wait_recv()
            merge(h, 1)

        @pl.when(row == 3)
        def _():
            z_copy(ZO3, h).wait_recv()
            z_copy(ZS3, h).wait_recv()
            z_copy(ZO3B, h).wait_recv()
            z_copy(ZS3B, h).wait_recv()
            merge(h, 2)

        @pl.when((h != y) | inner)
        def _():
            there = cross.at[h]
            pltpu.make_async_remote_copy(
                there, there, back_send.at[0, 0], back_recv.at[h],
                device_id={"dp": side + 2 * h + core, "ctx": cross_row * XS + x}, device_id_type=MESH,
            ).wait_recv()

        @pl.when((h == y) & edge)
        def _():
            own_back().wait()

        self_out = accs[pl.ds(h * QB, QB)].astype(jnp.bfloat16).astype(jnp.float32).reshape(XS, TOK, HD)
        mixed[h] = (self_out + cross[h].astype(jnp.float32)).astype(jnp.bfloat16)
        for k in (1, 3, 2):
            out_copy(h, x_at(k)).start()
        own_out(h).start()

    def own_and_emit(h):
        own_others(h)
        emit(h)

    loop(0, LOCAL, own_and_emit)

    @pl.when(edge)
    def _():
        for kind in range(2):
            for far in range(2):
                for k in range(1 - far, 4):
                    y_copy(kind, far, k).wait_send()
                for k in range(4):
                    core_pass(kind, far, k).wait_send()
        for k in range(1, 4):
            back_copy(0, k).wait_send()
        for k in range(4):
            back_copy(1, k).wait_send()

    def finish_plane(k):
        idx_copy(k).wait_send()
        qc_copy(k).wait_send()

    loop(first_plane, 4 * XS, finish_plane)
    def finish(h):
        for k in range(1, XS):
            peer = x_at(k)
            for kind in (KS, VS, QS):
                x_copy(kind, h, peer).wait_send()
        for at, kinds in enumerate(((ZK, ZV), (ZO2, ZS2, ZO3, ZS3), (ZQ2, ZO3B, ZS3B), (ZQ3, ZQ3B))):

            @pl.when(row == at)
            def _():
                for kind in kinds:
                    z_copy(kind, h).wait_send()

    def finish_out(h):
        own_out(h).wait()
        for k in range(1, XS):
            peer = x_at(k)
            out_copy(h, peer).wait_send()
            pltpu.make_async_remote_copy(
                mixed.at[h, peer], out_ref.at[:, cols(peer * LOCAL + h)], x_send.at[OUT, h, peer], x_recv.at[OUT, h, peer],
                device_id={"dp": dp, "ctx": row * XS + peer}, device_id_type=MESH,
            ).wait_recv()

    loop(0, LOCAL, finish)
    loop(0, LOCAL, finish_out)


def shards(q_self, k_self, v_self, q_cross, db_keys, db_values, nb_shard, nb_row):
    anywhere = pl.BlockSpec(memory_space=pl.ANY)
    scalars = pl.BlockSpec(memory_space=pltpu.SMEM)
    heads = pltpu.VMEM((LOCAL, XS, TOK, HD), jnp.bfloat16)
    database = pltpu.VMEM((N_DP * DB_DEV, NLEN, HD), jnp.bfloat16)
    state = pltpu.VMEM((LOCAL * QB, ROWS, HD), jnp.float32)
    parts = pltpu.VMEM((2, LOCAL, XS, TOK, HD), jnp.bfloat16)
    stats = pltpu.VMEM((2, LOCAL, 8, 128), jnp.float32)
    dma = pltpu.SemaphoreType.DMA
    out = pl.pallas_call(
        kernel,
        out_shape=jax.ShapeDtypeStruct((TOK, HEADS * HD), jnp.bfloat16),
        in_specs=[anywhere] * 6 + [scalars] * 2,
        out_specs=anywhere,
        scratch_shapes=[
            heads, heads, heads, parts, heads, heads, heads, heads, database, database,
            pltpu.VMEM((2, 4, XS, 8, 128), jnp.int32),
            pltpu.SMEM((2, 4, XS, 8, 128), jnp.int32),
            heads,
            pltpu.VMEM((3, 2 * QB, ROWS, ROWS), jnp.float32),
            state, state, state,
            parts, stats, parts, stats, heads, parts,
            dma((5, LOCAL, XS)), dma((5, LOCAL, XS)), dma((4 * XS,)), dma((2, 4, XS)), dma((4 * XS,)), dma((2, 4, XS)),
            dma((2, 4)), dma((4,)), dma((11, LOCAL)), dma((11, LOCAL)),
            dma((2, 2, 4)), dma((2, 2, 4)), dma((2, N_DP)), dma((5, LOCAL)), dma((2,)), dma,
            pltpu.SemaphoreType.REGULAR,
        ],
        compiler_params=pltpu.CompilerParams(
            collective_id=0, has_side_effects=True, vmem_limit_bytes=60 * 1024 * 1024
        ),
    )(q_self[0], k_self[0], v_self[0], q_cross[0], db_keys, db_values, nb_shard, nb_row)
    return out[None]


def solution(mesh):
    return jax.shard_map(
        shards,
        mesh=mesh,
        in_specs=(
            P("dp", "ctx", None),
            P("dp", "ctx", None),
            P("dp", "ctx", None),
            P("dp", "ctx", None),
            P("dp", None, None),
            P("dp", None, None),
            P("dp", "ctx", None),
            P("dp", "ctx", None),
        ),
        out_specs=P("dp", "ctx", None),
        check_vma=False,
    )
```

```python
import jax
import jax.numpy as jnp
from jax import lax
from jax.experimental import pallas as pl
from jax.experimental.pallas import tpu as pltpu
from jax.sharding import PartitionSpec as P

HEADS = 16
HD = 128
GROUP = 64
NEIGH = 2
NLEN = 128
TOK = 128
DB_DEV = 2
N_DP = 16
HALF = 8
XS = 4
LOCAL = HEADS // XS
ROWS = 256
PER = ROWS // TOK
QB = XS // PER
EXPO = HD**-0.5 * 1.4426950408889634
MESH = pl.DeviceIdType.MESH
NT = (((1,), (1,)), ((), ()))
NN = (((1,), (0,)), ((), ()))
QC, KS, VS, QS, OUT = range(5)
ZK, ZV, ZQ2, ZQ3, ZQ3B, ZO2, ZS2, ZO3, ZS3, ZO3B, ZS3B = range(11)


def cols(head):
    return pl.ds(pl.multiple_of(head * HD, HD), HD)


def kernel(
    qs_ref, ks_ref, vs_ref, qc_ref, kd_ref, vd_ref, shard_ref, row_ref, out_ref,
    qs, ks, vs, qc, k0, v0, q2, q3, kd, vd, idx, idx_s, cross, scores, tops, totals, accs,
    part_out, stat_out, part_in, stat_in, mixed, cross_out, transit,
    x_send, x_recv, transit_recv, pass_send, qc_send, qc_recv, idx_send, idx_recv, back_send, back_recv, z_send, z_recv,
    y_send, core_send, db_recv, own_sem, db_own, number_sem, ready,
):
    dp = lax.axis_index("dp")
    me = lax.axis_index("ctx")
    row = me // XS
    x = lax.rem(me, XS)
    near = lax.rem(dp, HALF)
    side = dp - near
    away = HALF - side
    y = near // 2
    core = lax.rem(near, 2)
    other_core = dp + 1 - 2 * core
    far_ctx = (3 - row) * XS + x
    edge = (row == 0) | (row == 3)
    first_side = dp < HALF
    inner = (row == 1) | (row == 2)
    pair = row + 1 - 2 * lax.rem(row, 2)
    cross_row = jnp.where(inner, pair, row)
    cross_part = jnp.where(inner, 1, 0)

    def x_at(k):
        return lax.rem(x + k, XS)

    def y_at(home, k):
        return home + lax.rem(near + 2 * k, HALF)

    def loop(first, last, body):
        def step(k, carry):
            body(k)
            return carry

        lax.fori_loop(first, last, step, 0)

    barrier = pltpu.get_barrier_semaphore()

    def greet(dp_of, ctx_of):
        pl.semaphore_signal(barrier, inc=1, device_id={"dp": dp_of, "ctx": ctx_of}, device_id_type=MESH)

    def plane(k):
        return lax.rem(y + k // XS, 4), x_at(lax.rem(k, XS))

    def greet_plane(of_row):
        def step(k):
            to_y, to_x = plane(k)
            greet(side + 2 * to_y + core, of_row * XS + to_x)

        return step

    loop(1, jnp.where(edge, 4 * XS, XS), greet_plane(row))
    loop(1, 4 * XS, greet_plane(pair))
    for k in range(1, 4):
        greet(dp, lax.rem(row + k, 4) * XS + x)

    @pl.when(edge)
    def _():
        greet(other_core, me)

    @pl.when(edge & first_side)
    def _():
        for k in range(4):
            greet(y_at(away, k), far_ctx)

    lane = lax.broadcasted_iota(jnp.int32, (8, 128), 1)
    tile = jnp.zeros((8, 128), jnp.int32)
    for g in range(TOK // GROUP):
        for n in range(NEIGH):
            block = shard_ref[0, g, n] * DB_DEV + row_ref[0, g, n]
            tile = jnp.where(lane == g * NEIGH + n, block, tile)
    idx[cross_part, y, x] = tile

    arrays = {KS: (ks_ref, ks), VS: (vs_ref, vs), QS: (qs_ref, qs)}
    blocks = ((kd_ref, kd), (vd_ref, vd))
    head = x * LOCAL + y

    def own_copy(kind, h):
        arg, buf = arrays[kind]
        return pltpu.make_async_copy(arg.at[:, cols(x * LOCAL + h)], buf.at[h, x], own_sem.at[kind, h])

    def own_qc():
        return pltpu.make_async_copy(qc_ref.at[:, cols(head)], qc.at[0, y, x], own_sem.at[QC, 0])

    def own_db(kind):
        arg, buf = blocks[kind]
        return pltpu.make_async_copy(arg.at[:, :, cols(head)], buf.at[pl.ds(dp * DB_DEV, DB_DEV)], db_own.at[kind])

    def start_own(h):
        for kind in (KS, VS, QS):
            own_copy(kind, h).start()

    loop(0, LOCAL, start_own)

    @pl.when(edge)
    def _():
        own_qc().start()
        for kind in range(2):
            own_db(kind).start()

    pl.semaphore_wait(barrier, 21 + jnp.where(edge, 13, 0) + jnp.where(edge & (dp >= HALF), 4, 0))

    @pl.when(edge & (dp >= HALF))
    def _():
        for k in range(4):
            pl.semaphore_signal(ready, inc=1, device_id={"dp": y_at(away, k), "ctx": far_ctx}, device_id_type=MESH)

    def shard_copy(kind, shard, src, send, target, target_ctx):
        part = blocks[kind][1].at[pl.ds(shard * DB_DEV, DB_DEV)]
        return pltpu.make_async_remote_copy(
            part if src is None else src, part, send, db_recv.at[kind, shard],
            device_id={"dp": target, "ctx": target_ctx}, device_id_type=MESH,
        )

    def y_copy(kind, far, k):
        src = blocks[kind][0].at[:, :, cols(x * LOCAL + lax.rem(y + k, 4))]
        target = y_at(away if far else side, k)
        return shard_copy(kind, dp, src, y_send.at[kind, far, k], target, far_ctx if far else me)

    def core_pass(kind, far, k):
        src = blocks[kind][0].at[:, :, cols(head)] if (far, k) == (0, 0) else None
        return shard_copy(kind, y_at(away if far else side, k), src, core_send.at[kind, far, k], other_core, me)

    def wait_shard(kind, shard):
        shard_copy(kind, shard, None, y_send.at[kind, 0, 0], other_core, me).wait_recv()

    def qc_copy(k):
        to_y, to_x = plane(k)
        return pltpu.make_async_remote_copy(
            qc_ref.at[:, cols(to_x * LOCAL + to_y)], qc.at[cross_part, y, x], qc_send.at[k], qc_recv.at[cross_part, y, x],
            device_id={"dp": side + 2 * to_y + core, "ctx": cross_row * XS + to_x}, device_id_type=MESH,
        )

    def idx_copy(k):
        to_y, to_x = plane(k)
        return pltpu.make_async_remote_copy(
            idx.at[cross_part, y, x], idx.at[cross_part, y, x], idx_send.at[k], idx_recv.at[cross_part, y, x],
            device_id={"dp": side + 2 * to_y + core, "ctx": cross_row * XS + to_x}, device_id_type=MESH,
        )

    def wait_plane(part):
        def step(k):
            from_y, from_x = plane(k)
            for buf, sent, received in ((idx, idx_send, idx_recv), (qc, qc_send, qc_recv)):
                there = buf.at[part, from_y, from_x]
                pltpu.make_async_remote_copy(
                    there, there, sent.at[k], received.at[part, from_y, from_x],
                    device_id={"dp": side + 2 * from_y + core, "ctx": jnp.where(part == 1, pair, row) * XS + from_x},
                    device_id_type=MESH,
                ).wait_recv()

        return step

    def back_copy(part, k):
        to_y = lax.rem(y + k, 4)
        return pltpu.make_async_remote_copy(
            cross_out.at[part, to_y], cross.at[y], back_send.at[part, k], back_recv.at[y],
            device_id={"dp": y_at(side, k), "ctx": jnp.where(part == 1, pair, row) * XS + x}, device_id_type=MESH,
        )

    def own_back():
        return pltpu.make_async_copy(cross_out.at[0, y], cross.at[y], own_sem.at[QC, 1])

    def x_copy(kind, h, to):
        arg, buf = arrays[kind]
        return pltpu.make_async_remote_copy(
            arg.at[:, cols(to * LOCAL + h)], buf.at[h, x], x_send.at[kind, h, to], x_recv.at[kind, h, x],
            device_id={"dp": dp, "ctx": row * XS + to}, device_id_type=MESH,
        )

    def via(h):
        return 1 + 2 * lax.rem(h, 2)

    def two_copy(kind, h):
        to = x_at(2)
        return pltpu.make_async_remote_copy(
            arrays[kind][0].at[:, cols(to * LOCAL + h)], transit.at[kind - 1, h], x_send.at[kind, h, to], transit_recv.at[kind - 1, h],
            device_id={"dp": dp, "ctx": row * XS + x_at(via(h))}, device_id_type=MESH,
        )

    def pass_copy(kind, h):
        origin = x_at(4 - via(h))
        return pltpu.make_async_remote_copy(
            transit.at[kind - 1, h], arrays[kind][1].at[h, origin], pass_send.at[kind - 1, h], x_recv.at[kind, h, origin],
            device_id={"dp": dp, "ctx": row * XS + x_at(via(h))}, device_id_type=MESH,
        )

    def pass_on(kind, h):
        two_copy(kind, h).wait_recv()
        pass_copy(kind, h).start()

    def arrived(kind, h):
        own_copy(kind, h).wait()
        for k in range(1, XS):
            source = x_at(k)
            buf = arrays[kind][1].at[h, source]
            pltpu.make_async_remote_copy(
                buf, buf, x_send.at[kind, h, source], x_recv.at[kind, h, source],
                device_id={"dp": dp, "ctx": row * XS + source}, device_id_type=MESH,
            ).wait_recv()

    def start_x(kinds, passed=True):
        def step(h):
            if passed:
                for kind in kinds:
                    two_copy(kind, h).start()
            for k in (1, 3) if passed else (1, 3, 2):
                for kind in kinds:
                    x_copy(kind, h, x_at(k)).start()

        loop(0, LOCAL, step)

    first_plane = jnp.where(inner, 0, 1)

    def start_plane():
        def step(k):
            idx_copy(k).start()
            qc_copy(k).start()

        loop(first_plane, 4 * XS, step)

    def start_near():
        for kind in range(2):
            for k in (1, 3, 2):
                y_copy(kind, 0, k).start()
            core_pass(kind, 0, 0).start()

    def start_far_first():
        @pl.when(dp >= HALF)
        def _():
            for kind in range(2):
                for k in range(4):
                    y_copy(kind, 1, k).start()

    def start_far_second():
        @pl.when(first_side)
        def _():
            pl.semaphore_wait(ready, 4)
            for kind in range(2):
                for k in range(4):
                    y_copy(kind, 1, k).start()

    @pl.when(row == 0)
    def _():
        start_far_first()
        start_x((KS, VS))
        start_near()
        start_plane()
        start_far_second()
        start_x((QS,), False)

    @pl.when(row == 1)
    def _():
        start_plane()
        start_x((KS, VS))
        start_x((QS,), False)

    @pl.when(row == 2)
    def _():
        start_x((QS,))
        start_plane()
        start_x((KS, VS))

    @pl.when(row == 3)
    def _():
        start_far_first()
        start_x((QS,))
        start_near()
        start_plane()
        start_far_second()
        start_x((KS, VS))

    def z_copy(kind, h):
        src, dst, to = {
            ZK: (ks.at[h], k0.at[h], 1),
            ZV: (vs.at[h], v0.at[h], 1),
            ZQ2: (qs.at[h], q2.at[h], 1),
            ZQ3: (qs.at[h], q3.at[h], 1),
            ZQ3B: (qs.at[h], q3.at[h], 2),
            ZO2: (part_out.at[0, h], part_in.at[0, h], 2),
            ZS2: (stat_out.at[0, h], stat_in.at[0, h], 2),
            ZO3: (part_out.at[1, h], part_in.at[0, h], 3),
            ZS3: (stat_out.at[1, h], stat_in.at[0, h], 3),
            ZO3B: (part_out.at[1, h], part_in.at[1, h], 3),
            ZS3B: (stat_out.at[1, h], stat_in.at[1, h], 3),
        }[kind]
        return pltpu.make_async_remote_copy(
            src, dst, z_send.at[kind, h], z_recv.at[kind, h],
            device_id={"dp": dp, "ctx": to * XS + x}, device_id_type=MESH,
        )

    def relay(h):
        @pl.when(row == 0)
        def _():
            pass_on(KS, h)
            pass_on(VS, h)
            arrived(KS, h)
            z_copy(ZK, h).start()
            arrived(VS, h)
            z_copy(ZV, h).start()

        @pl.when(row == 2)
        def _():
            pass_on(QS, h)
            arrived(QS, h)
            z_copy(ZQ2, h).start()

        @pl.when(row == 3)
        def _():
            pass_on(QS, h)
            arrived(QS, h)
            z_copy(ZQ3, h).start()
            z_copy(ZQ3B, h).start()

    def core_stage():
        for far in range(2):
            for kind in range(2):
                for k in (0, 1, 3, 2)[1 - far :]:
                    wait_shard(kind, y_at(away if far else side, k))
                    core_pass(kind, far, k).start()

    diagonal = lax.broadcasted_iota(jnp.int32, (ROWS, ROWS), 0) >= lax.broadcasted_iota(jnp.int32, (ROWS, ROWS), 1)
    eye = lax.broadcasted_iota(jnp.int32, (TOK, TOK), 0) == lax.broadcasted_iota(jnp.int32, (TOK, TOK), 1)

    def score_block(queries, h, b, chunks, slot):
        q = queries[h, pl.ds(b * PER, PER)].reshape(ROWS, HD)
        peak = None
        for j, (keys, values, c, masked) in enumerate(chunks):
            k = keys[h, pl.ds(c * PER, PER)].reshape(ROWS, HD)
            s = lax.dot_general(q, k, NT, preferred_element_type=jnp.float32)
            if masked:
                s = jnp.where(diagonal, s, -1e30)
            scores[slot, j] = s
            folded = jnp.maximum(s[:, :HD], s[:, HD:])
            peak = folded if peak is None else jnp.maximum(peak, folded)
        return jnp.max(peak, axis=1, keepdims=True)

    def weigh_block(h, chunks, slot, top):
        total = jnp.zeros((ROWS, HD), jnp.float32)
        acc = jnp.zeros((ROWS, HD), jnp.float32)
        for j, (keys, values, c, masked) in enumerate(chunks):
            w = jnp.exp2((scores[slot, j] - top) * EXPO)
            total = total + (w[:, :HD] + w[:, HD:])
            v = values[h, pl.ds(c * PER, PER)].reshape(ROWS, HD)
            acc = acc + lax.dot_general(w.astype(jnp.bfloat16), v, NN, preferred_element_type=jnp.float32)
        return jnp.sum(total, axis=1, keepdims=True), acc

    def attend(h, jobs):
        tops_of = []
        for n in range(len(jobs) + 1):
            if n < len(jobs):
                queries, b, chunks, done = jobs[n]
                tops_of.append(score_block(queries, h, b, chunks, n % 3))
            if n >= 1:
                queries, b, chunks, done = jobs[n - 1]
                done(b, tops_of[n - 1], *weigh_block(h, chunks, (n - 1) % 3, tops_of[n - 1]))

    def partial(queries, h, chunks, place):
        def done(b, top, total, acc):
            part_out[place, h, pl.ds(b * PER, PER)] = (acc / total).astype(jnp.bfloat16).reshape(PER, TOK, HD)
            for p in range(PER):
                rows = slice(p * TOK, (p + 1) * TOK)
                at = b * PER + p
                stat_out[place, h, at : at + 1] = jnp.sum(jnp.where(eye, top[rows], 0.0), axis=0, keepdims=True)
                stat_out[place, h, XS + at : XS + at + 1] = jnp.sum(jnp.where(eye, total[rows], 0.0), axis=0, keepdims=True)

        return [(queries, b, chunks, done) for b in range(QB)]

    def own_rows(h, extra, final):
        def done(b, top, total, acc):
            at = h * QB + b
            if final:
                accs[at] = acc / total
            else:
                accs[at] = acc
                tops[at] = jnp.broadcast_to(top, (ROWS, HD))
                totals[at] = jnp.broadcast_to(total, (ROWS, HD))

        return [(qs, b, extra + [(ks, vs, c, c == b) for c in range(b + 1)], done) for b in range(QB)]

    whole_own = [(ks, vs, c, False) for c in range(QB)]
    whole_first = [(k0, v0, c, False) for c in range(QB)]

    def between(h):
        @pl.when(row == 1)
        def _():
            arrived(KS, h)
            arrived(VS, h)
            z_copy(ZK, h).wait_recv()
            z_copy(ZV, h).wait_recv()
            z_copy(ZQ2, h).wait_recv()
            z_copy(ZQ3, h).wait_recv()
            attend(h, partial(q2, h, whole_first + whole_own, 0) + partial(q3, h, whole_first + whole_own, 1))
            z_copy(ZO2, h).start()
            z_copy(ZS2, h).start()
            z_copy(ZO3, h).start()
            z_copy(ZS3, h).start()

        @pl.when(row == 2)
        def _():
            arrived(KS, h)
            arrived(VS, h)
            z_copy(ZQ3B, h).wait_recv()
            attend(h, partial(q3, h, whole_own, 1))
            z_copy(ZO3B, h).start()
            z_copy(ZS3B, h).start()

    def own_others(h):
        @pl.when(row == 0)
        def _():
            arrived(QS, h)
            attend(h, own_rows(h, [], True))

        @pl.when(row == 1)
        def _():
            arrived(QS, h)
            attend(h, own_rows(h, whole_first, True))

        @pl.when(row == 2)
        def _():
            attend(h, own_rows(h, [], False))

        @pl.when(row == 3)
        def _():
            arrived(KS, h)
            arrived(VS, h)
            attend(h, own_rows(h, [], False))

    def cross_document(part, k):
        doc = lax.rem(y + k, 4)
        groups = [(t, g) for t in range(XS) for g in range(TOK // GROUP)]
        picks = [[idx_s[part, doc, t, 0, g * NEIGH + n] for n in range(NEIGH)] for t, g in groups]
        s = []
        for (t, g), pick in zip(groups, picks):
            keys = jnp.concatenate([kd[block] for block in pick], axis=0)
            q = qc[part, doc, t, pl.ds(g * GROUP, GROUP), :]
            s.append(lax.dot_general(q, keys, NT, preferred_element_type=jnp.float32))
        top = [jnp.max(one, axis=1, keepdims=True) for one in s]
        w = [jnp.exp2((one - high) * EXPO) for one, high in zip(s, top)]
        total = [jnp.sum(one, axis=1, keepdims=True) for one in w]
        o = []
        for one, pick in zip(w, picks):
            values = jnp.concatenate([vd[block] for block in pick], axis=0)
            o.append(lax.dot_general(one.astype(jnp.bfloat16), values, NN, preferred_element_type=jnp.float32))
        for (t, g), one, whole in zip(groups, o, total):
            cross_out[part, doc, t, pl.ds(g * GROUP, GROUP), :] = (one / whole).astype(jnp.bfloat16)

        here = (part == 0) & (k == 0)

        @pl.when(jnp.logical_not(here))
        def _():
            back_copy(part, k).start()

        @pl.when(here)
        def _():
            own_back().start()

    def cross_stage():
        own_qc().wait()
        for kind in range(2):
            own_db(kind).wait()

        def wait_other_core(k):
            for kind in range(2):
                wait_shard(kind, 2 * k + 1 - core)

        loop(0, HALF, wait_other_core)

        def cross_row_of(n):
            part = 1 - n
            loop(n, 4 * XS, wait_plane(part))
            numbers = pltpu.make_async_copy(idx.at[part], idx_s.at[part], number_sem)
            numbers.start()
            numbers.wait()
            def document(k):
                cross_document(part, 3 - k)
                for kind, parity in ((KS, 0), (VS, 1)):

                    @pl.when((row == 3) & (lax.rem(k, 2) == parity))
                    def _():
                        pass_on(kind, 2 * n + k // 2)

            loop(0, 4, document)

        loop(0, 2, cross_row_of)

    @pl.when(row == 0)
    def _():
        loop(0, LOCAL, relay)

    @pl.when(row >= 2)
    def _():
        loop(0, LOCAL, relay)

    @pl.when(edge)
    def _():
        core_stage()
        cross_stage()

    def pass_both(h):
        pass_on(KS, h)
        pass_on(VS, h)

    @pl.when(inner)
    def _():
        loop(0, 2, pass_both)

    def between_step(h):
        @pl.when(inner & (h < 2))
        def _():
            pass_both(h + 2)

        between(h)

    loop(0, LOCAL, between_step)

    def merge(h, parts):
        for b in range(QB):
            at = h * QB + b
            for p in range(PER):
                rows = slice(p * TOK, (p + 1) * TOK)
                sub = b * PER + p
                top = tops[at, rows, :1]
                others = []
                for place in range(parts):
                    column = [
                        jnp.sum(jnp.where(eye, stat_in[place, h, n : n + 1], 0.0), axis=1, keepdims=True)
                        for n in (sub, XS + sub)
                    ]
                    others.append(column)
                peak = top
                for other_top, _ in others:
                    peak = jnp.maximum(peak, other_top)
                keep = jnp.exp2((top - peak) * EXPO)
                total = totals[at, rows, :1] * keep
                acc = accs[at, rows, :] * keep
                for place, (other_top, other_total) in enumerate(others):
                    w = jnp.exp2((other_top - peak) * EXPO) * other_total
                    total = total + w
                    acc = acc + part_in[place, h, sub].astype(jnp.float32) * w
                accs[at, rows, :] = acc / total

    def out_copy(h, t):
        return pltpu.make_async_remote_copy(
            mixed.at[h, t], out_ref.at[:, cols(x * LOCAL + h)], x_send.at[OUT, h, t], x_recv.at[OUT, h, x],
            device_id={"dp": dp, "ctx": row * XS + t}, device_id_type=MESH,
        )

    def own_out(h):
        return pltpu.make_async_copy(mixed.at[h, x], out_ref.at[:, cols(x * LOCAL + h)], own_sem.at[OUT, h])

    def emit(h):
        @pl.when(row == 2)
        def _():
            z_copy(ZO2, h).wait_recv()
            z_copy(ZS2, h).wait_recv()
            merge(h, 1)

        @pl.when(row == 3)
        def _():
            z_copy(ZO3, h).wait_recv()
            z_copy(ZS3, h).wait_recv()
            z_copy(ZO3B, h).wait_recv()
            z_copy(ZS3B, h).wait_recv()
            merge(h, 2)

        @pl.when((h != y) | inner)
        def _():
            there = cross.at[h]
            pltpu.make_async_remote_copy(
                there, there, back_send.at[0, 0], back_recv.at[h],
                device_id={"dp": side + 2 * h + core, "ctx": cross_row * XS + x}, device_id_type=MESH,
            ).wait_recv()

        @pl.when((h == y) & edge)
        def _():
            own_back().wait()

        self_out = accs[pl.ds(h * QB, QB)].astype(jnp.bfloat16).astype(jnp.float32).reshape(XS, TOK, HD)
        mixed[h] = (self_out + cross[h].astype(jnp.float32)).astype(jnp.bfloat16)
        for k in (1, 3, 2):
            out_copy(h, x_at(k)).start()
        own_out(h).start()

    def own_and_emit(h):
        own_others(h)
        emit(h)

    loop(0, LOCAL, own_and_emit)

    @pl.when(edge)
    def _():
        for kind in range(2):
            for far in range(2):
                for k in range(1 - far, 4):
                    y_copy(kind, far, k).wait_send()
                for k in range(4):
                    core_pass(kind, far, k).wait_send()
        for k in range(1, 4):
            back_copy(0, k).wait_send()
        for k in range(4):
            back_copy(1, k).wait_send()

    def finish_plane(k):
        idx_copy(k).wait_send()
        qc_copy(k).wait_send()

    loop(first_plane, 4 * XS, finish_plane)
    def finish(h):
        for k in range(1, XS):
            peer = x_at(k)
            for kind in (KS, VS, QS):
                x_copy(kind, h, peer).wait_send()
        for kind in (KS, VS):
            pass_copy(kind, h).wait_send()

        @pl.when(row >= 2)
        def _():
            pass_copy(QS, h).wait_send()

        for at, kinds in enumerate(((ZK, ZV), (ZO2, ZS2, ZO3, ZS3), (ZQ2, ZO3B, ZS3B), (ZQ3, ZQ3B))):

            @pl.when(row == at)
            def _():
                for kind in kinds:
                    z_copy(kind, h).wait_send()

    def finish_out(h):
        own_out(h).wait()
        for k in range(1, XS):
            peer = x_at(k)
            out_copy(h, peer).wait_send()
            pltpu.make_async_remote_copy(
                mixed.at[h, peer], out_ref.at[:, cols(peer * LOCAL + h)], x_send.at[OUT, h, peer], x_recv.at[OUT, h, peer],
                device_id={"dp": dp, "ctx": row * XS + peer}, device_id_type=MESH,
            ).wait_recv()

    loop(0, LOCAL, finish)
    loop(0, LOCAL, finish_out)


def shards(q_self, k_self, v_self, q_cross, db_keys, db_values, nb_shard, nb_row):
    anywhere = pl.BlockSpec(memory_space=pl.ANY)
    scalars = pl.BlockSpec(memory_space=pltpu.SMEM)
    heads = pltpu.VMEM((LOCAL, XS, TOK, HD), jnp.bfloat16)
    database = pltpu.VMEM((N_DP * DB_DEV, NLEN, HD), jnp.bfloat16)
    state = pltpu.VMEM((LOCAL * QB, ROWS, HD), jnp.float32)
    parts = pltpu.VMEM((2, LOCAL, XS, TOK, HD), jnp.bfloat16)
    stats = pltpu.VMEM((2, LOCAL, 8, 128), jnp.float32)
    dma = pltpu.SemaphoreType.DMA
    out = pl.pallas_call(
        kernel,
        out_shape=jax.ShapeDtypeStruct((TOK, HEADS * HD), jnp.bfloat16),
        in_specs=[anywhere] * 6 + [scalars] * 2,
        out_specs=anywhere,
        scratch_shapes=[
            heads, heads, heads, parts, heads, heads, heads, heads, database, database,
            pltpu.VMEM((2, 4, XS, 8, 128), jnp.int32),
            pltpu.SMEM((2, 4, XS, 8, 128), jnp.int32),
            heads,
            pltpu.VMEM((3, 2 * QB, ROWS, ROWS), jnp.float32),
            state, state, state,
            parts, stats, parts, stats, heads, parts,
            pltpu.VMEM((3, LOCAL, TOK, HD), jnp.bfloat16),
            dma((5, LOCAL, XS)), dma((5, LOCAL, XS)), dma((3, LOCAL)), dma((3, LOCAL)), dma((4 * XS,)), dma((2, 4, XS)), dma((4 * XS,)), dma((2, 4, XS)),
            dma((2, 4)), dma((4,)), dma((11, LOCAL)), dma((11, LOCAL)),
            dma((2, 2, 4)), dma((2, 2, 4)), dma((2, N_DP)), dma((5, LOCAL)), dma((2,)), dma,
            pltpu.SemaphoreType.REGULAR,
        ],
        compiler_params=pltpu.CompilerParams(
            collective_id=0, has_side_effects=True, vmem_limit_bytes=60 * 1024 * 1024
        ),
    )(q_self[0], k_self[0], v_self[0], q_cross[0], db_keys, db_values, nb_shard, nb_row)
    return out[None]


def solution(mesh):
    return jax.shard_map(
        shards,
        mesh=mesh,
        in_specs=(
            P("dp", "ctx", None),
            P("dp", "ctx", None),
            P("dp", "ctx", None),
            P("dp", "ctx", None),
            P("dp", None, None),
            P("dp", None, None),
            P("dp", "ctx", None),
            P("dp", "ctx", None),
        ),
        out_specs=P("dp", "ctx", None),
        check_vma=False,
    )
```

```python
import jax
import jax.numpy as jnp
from jax import lax
from jax.experimental import pallas as pl
from jax.experimental.pallas import tpu as pltpu
from jax.sharding import PartitionSpec as P

HEADS = 16
HD = 128
GROUP = 64
NEIGH = 2
NLEN = 128
TOK = 128
DB_DEV = 2
N_DP = 16
HALF = 8
XS = 4
LOCAL = HEADS // XS
ROWS = 256
PER = ROWS // TOK
QB = XS // PER
EXPO = HD**-0.5 * 1.4426950408889634
MESH = pl.DeviceIdType.MESH
NT = (((1,), (1,)), ((), ()))
NN = (((1,), (0,)), ((), ()))
QC, KS, VS, QS, OUT = range(5)
ZK, ZV, ZQ2, ZQ3, ZQ3B, ZO2, ZS2, ZO3, ZS3, ZO3B, ZS3B = range(11)


def cols(head):
    return pl.ds(pl.multiple_of(head * HD, HD), HD)


def kernel(
    qs_ref, ks_ref, vs_ref, qc_ref, kd_ref, vd_ref, shard_ref, row_ref, out_ref,
    qs, ks, vs, qc, k0, v0, q2, q3, kd, vd, idx, idx_s, cross, scores, tops, totals, accs,
    part_out, stat_out, part_in, stat_in, mixed, cross_out,
    x_send, x_recv, qc_send, qc_recv, idx_send, idx_recv, back_send, back_recv, z_send, z_recv,
    y_send, core_send, db_recv, own_sem, db_own, number_sem, ready,
):
    dp = lax.axis_index("dp")
    me = lax.axis_index("ctx")
    row = me // XS
    x = lax.rem(me, XS)
    near = lax.rem(dp, HALF)
    side = dp - near
    away = HALF - side
    y = near // 2
    core = lax.rem(near, 2)
    other_core = dp + 1 - 2 * core
    far_ctx = (3 - row) * XS + x
    edge = (row == 0) | (row == 3)
    first_side = dp < HALF
    inner = (row == 1) | (row == 2)
    pair = row + 1 - 2 * lax.rem(row, 2)
    cross_row = jnp.where(inner, pair, row)
    cross_part = jnp.where(inner, 1, 0)

    def x_at(k):
        return lax.rem(x + k, XS)

    def y_at(home, k):
        return home + lax.rem(near + 2 * k, HALF)

    def loop(first, last, body):
        def step(k, carry):
            body(k)
            return carry

        lax.fori_loop(first, last, step, 0)

    barrier = pltpu.get_barrier_semaphore()

    def greet(dp_of, ctx_of):
        pl.semaphore_signal(barrier, inc=1, device_id={"dp": dp_of, "ctx": ctx_of}, device_id_type=MESH)

    def plane(k):
        return lax.rem(y + k // XS, 4), x_at(lax.rem(k, XS))

    def greet_plane(of_row):
        def step(k):
            to_y, to_x = plane(k)
            greet(side + 2 * to_y + core, of_row * XS + to_x)

        return step

    loop(1, jnp.where(edge, 4 * XS, XS), greet_plane(row))
    loop(1, 4 * XS, greet_plane(pair))
    for k in range(1, 4):
        greet(dp, lax.rem(row + k, 4) * XS + x)

    @pl.when(edge)
    def _():
        greet(other_core, me)

    @pl.when(edge & first_side)
    def _():
        for k in range(4):
            greet(y_at(away, k), far_ctx)

    lane = lax.broadcasted_iota(jnp.int32, (8, 128), 1)
    tile = jnp.zeros((8, 128), jnp.int32)
    for g in range(TOK // GROUP):
        for n in range(NEIGH):
            block = shard_ref[0, g, n] * DB_DEV + row_ref[0, g, n]
            tile = jnp.where(lane == g * NEIGH + n, block, tile)
    idx[cross_part, y, x] = tile

    arrays = {KS: (ks_ref, ks), VS: (vs_ref, vs), QS: (qs_ref, qs)}
    blocks = ((kd_ref, kd), (vd_ref, vd))
    head = x * LOCAL + y

    def own_copy(kind, h):
        arg, buf = arrays[kind]
        return pltpu.make_async_copy(arg.at[:, cols(x * LOCAL + h)], buf.at[h, x], own_sem.at[kind, h])

    def own_qc():
        return pltpu.make_async_copy(qc_ref.at[:, cols(head)], qc.at[0, y, x], own_sem.at[QC, 0])

    def own_db(kind):
        arg, buf = blocks[kind]
        return pltpu.make_async_copy(arg.at[:, :, cols(head)], buf.at[pl.ds(dp * DB_DEV, DB_DEV)], db_own.at[kind])

    def start_own(h):
        for kind in (KS, VS, QS):
            own_copy(kind, h).start()

    loop(0, LOCAL, start_own)

    @pl.when(edge)
    def _():
        own_qc().start()
        for kind in range(2):
            own_db(kind).start()

    pl.semaphore_wait(barrier, 21 + jnp.where(edge, 13, 0) + jnp.where(edge & (dp >= HALF), 4, 0))

    @pl.when(edge & (dp >= HALF))
    def _():
        for k in range(4):
            pl.semaphore_signal(ready, inc=1, device_id={"dp": y_at(away, k), "ctx": far_ctx}, device_id_type=MESH)

    def shard_copy(kind, shard, src, send, target, target_ctx):
        part = blocks[kind][1].at[pl.ds(shard * DB_DEV, DB_DEV)]
        return pltpu.make_async_remote_copy(
            part if src is None else src, part, send, db_recv.at[kind, shard],
            device_id={"dp": target, "ctx": target_ctx}, device_id_type=MESH,
        )

    def y_copy(kind, far, k):
        src = blocks[kind][0].at[:, :, cols(x * LOCAL + lax.rem(y + k, 4))]
        target = y_at(away if far else side, k)
        return shard_copy(kind, dp, src, y_send.at[kind, far, k], target, far_ctx if far else me)

    def core_pass(kind, far, k):
        src = blocks[kind][0].at[:, :, cols(head)] if (far, k) == (0, 0) else None
        return shard_copy(kind, y_at(away if far else side, k), src, core_send.at[kind, far, k], other_core, me)

    def wait_shard(kind, shard):
        shard_copy(kind, shard, None, y_send.at[kind, 0, 0], other_core, me).wait_recv()

    def qc_copy(k):
        to_y, to_x = plane(k)
        return pltpu.make_async_remote_copy(
            qc_ref.at[:, cols(to_x * LOCAL + to_y)], qc.at[cross_part, y, x], qc_send.at[k], qc_recv.at[cross_part, y, x],
            device_id={"dp": side + 2 * to_y + core, "ctx": cross_row * XS + to_x}, device_id_type=MESH,
        )

    def idx_copy(k):
        to_y, to_x = plane(k)
        return pltpu.make_async_remote_copy(
            idx.at[cross_part, y, x], idx.at[cross_part, y, x], idx_send.at[k], idx_recv.at[cross_part, y, x],
            device_id={"dp": side + 2 * to_y + core, "ctx": cross_row * XS + to_x}, device_id_type=MESH,
        )

    def wait_plane(part):
        def step(k):
            from_y, from_x = plane(k)
            for buf, sent, received in ((idx, idx_send, idx_recv), (qc, qc_send, qc_recv)):
                there = buf.at[part, from_y, from_x]
                pltpu.make_async_remote_copy(
                    there, there, sent.at[k], received.at[part, from_y, from_x],
                    device_id={"dp": side + 2 * from_y + core, "ctx": jnp.where(part == 1, pair, row) * XS + from_x},
                    device_id_type=MESH,
                ).wait_recv()

        return step

    def back_copy(part, k):
        to_y = lax.rem(y + k, 4)
        return pltpu.make_async_remote_copy(
            cross_out.at[part, to_y], cross.at[y], back_send.at[part, k], back_recv.at[y],
            device_id={"dp": y_at(side, k), "ctx": jnp.where(part == 1, pair, row) * XS + x}, device_id_type=MESH,
        )

    def own_back():
        return pltpu.make_async_copy(cross_out.at[0, y], cross.at[y], own_sem.at[QC, 1])

    def x_copy(kind, h, to):
        arg, buf = arrays[kind]
        return pltpu.make_async_remote_copy(
            arg.at[:, cols(to * LOCAL + h)], buf.at[h, x], x_send.at[kind, h, to], x_recv.at[kind, h, x],
            device_id={"dp": dp, "ctx": row * XS + to}, device_id_type=MESH,
        )

    def arrived(kind, h):
        own_copy(kind, h).wait()
        for k in range(1, XS):
            source = x_at(k)
            buf = arrays[kind][1].at[h, source]
            pltpu.make_async_remote_copy(
                buf, buf, x_send.at[kind, h, source], x_recv.at[kind, h, source],
                device_id={"dp": dp, "ctx": row * XS + source}, device_id_type=MESH,
            ).wait_recv()

    def start_x(kinds):
        def step(h):
            for k in (1, 3, 2):
                for kind in kinds:
                    x_copy(kind, h, x_at(k)).start()

        loop(0, LOCAL, step)

    first_plane = jnp.where(inner, 0, 1)

    def start_plane():
        def step(k):
            idx_copy(k).start()
            qc_copy(k).start()

        loop(first_plane, 4 * XS, step)

    def start_near():
        for kind in range(2):
            for k in (1, 3, 2):
                y_copy(kind, 0, k).start()
            core_pass(kind, 0, 0).start()

    def start_far_first():
        @pl.when(dp >= HALF)
        def _():
            for kind in range(2):
                for k in range(4):
                    y_copy(kind, 1, k).start()

    def start_far_second():
        @pl.when(first_side)
        def _():
            pl.semaphore_wait(ready, 4)
            for kind in range(2):
                for k in range(4):
                    y_copy(kind, 1, k).start()

    def z_copy(kind, h):
        src, dst, to = {
            ZK: (ks.at[h], k0.at[h], 1),
            ZV: (vs.at[h], v0.at[h], 1),
            ZQ2: (qs.at[h], q2.at[h], 1),
            ZQ3: (qs.at[h], q3.at[h], 1),
            ZQ3B: (qs.at[h], q3.at[h], 2),
            ZO2: (part_out.at[0, h], part_in.at[0, h], 2),
            ZS2: (stat_out.at[0, h], stat_in.at[0, h], 2),
            ZO3: (part_out.at[1, h], part_in.at[0, h], 3),
            ZS3: (stat_out.at[1, h], stat_in.at[0, h], 3),
            ZO3B: (part_out.at[1, h], part_in.at[1, h], 3),
            ZS3B: (stat_out.at[1, h], stat_in.at[1, h], 3),
        }[kind]
        return pltpu.make_async_remote_copy(
            src, dst, z_send.at[kind, h], z_recv.at[kind, h],
            device_id={"dp": dp, "ctx": to * XS + x}, device_id_type=MESH,
        )

    def relay(h):
        @pl.when(row == 0)
        def _():
            arrived(KS, h)
            z_copy(ZK, h).start()
            arrived(VS, h)
            z_copy(ZV, h).start()

        @pl.when(row == 2)
        def _():
            arrived(QS, h)
            z_copy(ZQ2, h).start()

        @pl.when(row == 3)
        def _():
            arrived(QS, h)
            z_copy(ZQ3, h).start()

    def core_stage():
        for far in range(2):
            for kind in range(2):
                for k in (0, 1, 3, 2)[1 - far :]:
                    wait_shard(kind, y_at(away if far else side, k))
                    core_pass(kind, far, k).start()

    diagonal = lax.broadcasted_iota(jnp.int32, (ROWS, ROWS), 0) >= lax.broadcasted_iota(jnp.int32, (ROWS, ROWS), 1)
    eye = lax.broadcasted_iota(jnp.int32, (TOK, TOK), 0) == lax.broadcasted_iota(jnp.int32, (TOK, TOK), 1)

    def score_block(queries, h, b, chunks, slot):
        q = queries[h, pl.ds(b * PER, PER)].reshape(ROWS, HD)
        peak = None
        for j, (keys, values, c, masked) in enumerate(chunks):
            k = keys[h, pl.ds(c * PER, PER)].reshape(ROWS, HD)
            s = lax.dot_general(q, k, NT, preferred_element_type=jnp.float32)
            if masked:
                s = jnp.where(diagonal, s, -1e30)
            scores[slot, j] = s
            folded = jnp.maximum(s[:, :HD], s[:, HD:])
            peak = folded if peak is None else jnp.maximum(peak, folded)
        return jnp.max(peak, axis=1, keepdims=True)

    def weigh_block(h, chunks, slot, top):
        total = jnp.zeros((ROWS, HD), jnp.float32)
        acc = jnp.zeros((ROWS, HD), jnp.float32)
        for j, (keys, values, c, masked) in enumerate(chunks):
            w = jnp.exp2((scores[slot, j] - top) * EXPO)
            total = total + (w[:, :HD] + w[:, HD:])
            v = values[h, pl.ds(c * PER, PER)].reshape(ROWS, HD)
            acc = acc + lax.dot_general(w.astype(jnp.bfloat16), v, NN, preferred_element_type=jnp.float32)
        return jnp.sum(total, axis=1, keepdims=True), acc

    def attend(h, jobs):
        tops_of = []
        for n in range(len(jobs) + 1):
            if n < len(jobs):
                queries, b, chunks, done = jobs[n]
                tops_of.append(score_block(queries, h, b, chunks, n % 3))
            if n >= 1:
                queries, b, chunks, done = jobs[n - 1]
                done(b, tops_of[n - 1], *weigh_block(h, chunks, (n - 1) % 3, tops_of[n - 1]))

    def partial(queries, h, chunks, place):
        def done(b, top, total, acc):
            part_out[place, h, pl.ds(b * PER, PER)] = (acc / total).astype(jnp.bfloat16).reshape(PER, TOK, HD)
            for p in range(PER):
                rows = slice(p * TOK, (p + 1) * TOK)
                at = b * PER + p
                stat_out[place, h, at : at + 1] = jnp.sum(jnp.where(eye, top[rows], 0.0), axis=0, keepdims=True)
                stat_out[place, h, XS + at : XS + at + 1] = jnp.sum(jnp.where(eye, total[rows], 0.0), axis=0, keepdims=True)

        return [(queries, b, chunks, done) for b in range(QB)]

    def own_rows(h, extra, final):
        def done(b, top, total, acc):
            at = h * QB + b
            if final:
                accs[at] = acc / total
            else:
                accs[at] = acc
                tops[at] = jnp.broadcast_to(top, (ROWS, HD))
                totals[at] = jnp.broadcast_to(total, (ROWS, HD))

        return [(qs, b, extra + [(ks, vs, c, c == b) for c in range(b + 1)], done) for b in range(QB)]

    whole_own = [(ks, vs, c, False) for c in range(QB)]
    whole_first = [(k0, v0, c, False) for c in range(QB)]

    def between(h):
        @pl.when(row == 1)
        def _():
            arrived(KS, h)
            arrived(VS, h)
            z_copy(ZK, h).wait_recv()
            z_copy(ZV, h).wait_recv()
            z_copy(ZQ2, h).wait_recv()
            z_copy(ZQ3, h).wait_recv()
            attend(h, partial(q2, h, whole_first + whole_own, 0) + partial(q3, h, whole_first + whole_own, 1))
            z_copy(ZO2, h).start()
            z_copy(ZS2, h).start()
            z_copy(ZO3, h).start()
            z_copy(ZS3, h).start()

        @pl.when(row == 2)
        def _():
            arrived(KS, h)
            arrived(VS, h)
            z_copy(ZQ3B, h).wait_recv()
            attend(h, partial(q3, h, whole_own, 1))
            z_copy(ZO3B, h).start()
            z_copy(ZS3B, h).start()

    def own_others(h):
        @pl.when(row == 0)
        def _():
            arrived(QS, h)
            attend(h, own_rows(h, [], True))

        @pl.when(row == 1)
        def _():
            arrived(QS, h)
            attend(h, own_rows(h, whole_first, True))

        @pl.when(row == 2)
        def _():
            attend(h, own_rows(h, [], False))

        @pl.when(row == 3)
        def _():
            arrived(KS, h)
            arrived(VS, h)
            attend(h, own_rows(h, [], False))

    def cross_document(part, k):
        doc = lax.rem(y + k, 4)
        groups = [(t, g) for t in range(XS) for g in range(TOK // GROUP)]
        picks = [[idx_s[part, doc, t, 0, g * NEIGH + n] for n in range(NEIGH)] for t, g in groups]
        s = []
        for (t, g), pick in zip(groups, picks):
            keys = jnp.concatenate([kd[block] for block in pick], axis=0)
            q = qc[part, doc, t, pl.ds(g * GROUP, GROUP), :]
            s.append(lax.dot_general(q, keys, NT, preferred_element_type=jnp.float32))
        top = [jnp.max(one, axis=1, keepdims=True) for one in s]
        w = [jnp.exp2((one - high) * EXPO) for one, high in zip(s, top)]
        total = [jnp.sum(one, axis=1, keepdims=True) for one in w]
        o = []
        for one, pick in zip(w, picks):
            values = jnp.concatenate([vd[block] for block in pick], axis=0)
            o.append(lax.dot_general(one.astype(jnp.bfloat16), values, NN, preferred_element_type=jnp.float32))
        for (t, g), one, whole in zip(groups, o, total):
            cross_out[part, doc, t, pl.ds(g * GROUP, GROUP), :] = (one / whole).astype(jnp.bfloat16)

        here = (part == 0) & (k == 0)

        @pl.when(jnp.logical_not(here))
        def _():
            back_copy(part, k).start()

        @pl.when(here)
        def _():
            own_back().start()

    def cross_stage():
        own_qc().wait()
        for kind in range(2):
            own_db(kind).wait()

        def wait_other_core(k):
            for kind in range(2):
                wait_shard(kind, 2 * k + 1 - core)

        loop(0, HALF, wait_other_core)

        def cross_row_of(n):
            part = 1 - n
            loop(n, 4 * XS, wait_plane(part))
            numbers = pltpu.make_async_copy(idx.at[part], idx_s.at[part], number_sem)
            numbers.start()
            numbers.wait()
            loop(0, 4, lambda k: cross_document(part, 3 - k))

        loop(0, 2, cross_row_of)

    @pl.when(row == 0)
    def _():
        start_far_first()
        start_x((KS, VS))
        start_near()
        relay(0)
        start_far_second()
        start_plane()
        loop(1, LOCAL, relay)
        start_x((QS,))

    @pl.when(row == 1)
    def _():
        start_plane()
        start_x((KS, VS))
        start_x((QS,))

    @pl.when(row == 2)
    def _():
        start_x((QS,))
        loop(0, LOCAL, relay)
        start_plane()
        start_x((KS, VS))

    @pl.when(row == 3)
    def _():
        start_far_first()
        start_x((QS,))
        start_near()
        loop(0, LOCAL, relay)
        start_far_second()
        start_plane()
        loop(0, LOCAL, lambda h: z_copy(ZQ3B, h).start())
        start_x((KS, VS))

    @pl.when(edge)
    def _():
        core_stage()
        cross_stage()

    loop(0, LOCAL, between)

    def merge(h, parts):
        for b in range(QB):
            at = h * QB + b
            for p in range(PER):
                rows = slice(p * TOK, (p + 1) * TOK)
                sub = b * PER + p
                top = tops[at, rows, :1]
                others = []
                for place in range(parts):
                    column = [
                        jnp.sum(jnp.where(eye, stat_in[place, h, n : n + 1], 0.0), axis=1, keepdims=True)
                        for n in (sub, XS + sub)
                    ]
                    others.append(column)
                peak = top
                for other_top, _ in others:
                    peak = jnp.maximum(peak, other_top)
                keep = jnp.exp2((top - peak) * EXPO)
                total = totals[at, rows, :1] * keep
                acc = accs[at, rows, :] * keep
                for place, (other_top, other_total) in enumerate(others):
                    w = jnp.exp2((other_top - peak) * EXPO) * other_total
                    total = total + w
                    acc = acc + part_in[place, h, sub].astype(jnp.float32) * w
                accs[at, rows, :] = acc / total

    def out_copy(h, t):
        return pltpu.make_async_remote_copy(
            mixed.at[h, t], out_ref.at[:, cols(x * LOCAL + h)], x_send.at[OUT, h, t], x_recv.at[OUT, h, x],
            device_id={"dp": dp, "ctx": row * XS + t}, device_id_type=MESH,
        )

    def own_out(h):
        return pltpu.make_async_copy(mixed.at[h, x], out_ref.at[:, cols(x * LOCAL + h)], own_sem.at[OUT, h])

    def emit(h):
        @pl.when(row == 2)
        def _():
            z_copy(ZO2, h).wait_recv()
            z_copy(ZS2, h).wait_recv()
            merge(h, 1)

        @pl.when(row == 3)
        def _():
            z_copy(ZO3, h).wait_recv()
            z_copy(ZS3, h).wait_recv()
            z_copy(ZO3B, h).wait_recv()
            z_copy(ZS3B, h).wait_recv()
            merge(h, 2)

        @pl.when((h != y) | inner)
        def _():
            there = cross.at[h]
            pltpu.make_async_remote_copy(
                there, there, back_send.at[0, 0], back_recv.at[h],
                device_id={"dp": side + 2 * h + core, "ctx": cross_row * XS + x}, device_id_type=MESH,
            ).wait_recv()

        @pl.when((h == y) & edge)
        def _():
            own_back().wait()

        self_out = accs[pl.ds(h * QB, QB)].astype(jnp.bfloat16).astype(jnp.float32).reshape(XS, TOK, HD)
        mixed[h] = (self_out + cross[h].astype(jnp.float32)).astype(jnp.bfloat16)
        for k in (1, 3, 2):
            out_copy(h, x_at(k)).start()
        own_out(h).start()

    def own_and_emit(h):
        own_others(h)
        emit(h)

    loop(0, LOCAL, own_and_emit)

    @pl.when(edge)
    def _():
        for kind in range(2):
            for far in range(2):
                for k in range(1 - far, 4):
                    y_copy(kind, far, k).wait_send()
                for k in range(4):
                    core_pass(kind, far, k).wait_send()
        for k in range(1, 4):
            back_copy(0, k).wait_send()
        for k in range(4):
            back_copy(1, k).wait_send()

    def finish_plane(k):
        idx_copy(k).wait_send()
        qc_copy(k).wait_send()

    loop(first_plane, 4 * XS, finish_plane)
    def finish(h):
        for k in range(1, XS):
            peer = x_at(k)
            for kind in (KS, VS, QS):
                x_copy(kind, h, peer).wait_send()
        for at, kinds in enumerate(((ZK, ZV), (ZO2, ZS2, ZO3, ZS3), (ZQ2, ZO3B, ZS3B), (ZQ3, ZQ3B))):

            @pl.when(row == at)
            def _():
                for kind in kinds:
                    z_copy(kind, h).wait_send()

    def finish_out(h):
        own_out(h).wait()
        for k in range(1, XS):
            peer = x_at(k)
            out_copy(h, peer).wait_send()
            pltpu.make_async_remote_copy(
                mixed.at[h, peer], out_ref.at[:, cols(peer * LOCAL + h)], x_send.at[OUT, h, peer], x_recv.at[OUT, h, peer],
                device_id={"dp": dp, "ctx": row * XS + peer}, device_id_type=MESH,
            ).wait_recv()

    loop(0, LOCAL, finish)
    loop(0, LOCAL, finish_out)


def shards(q_self, k_self, v_self, q_cross, db_keys, db_values, nb_shard, nb_row):
    anywhere = pl.BlockSpec(memory_space=pl.ANY)
    scalars = pl.BlockSpec(memory_space=pltpu.SMEM)
    heads = pltpu.VMEM((LOCAL, XS, TOK, HD), jnp.bfloat16)
    database = pltpu.VMEM((N_DP * DB_DEV, NLEN, HD), jnp.bfloat16)
    state = pltpu.VMEM((LOCAL * QB, ROWS, HD), jnp.float32)
    parts = pltpu.VMEM((2, LOCAL, XS, TOK, HD), jnp.bfloat16)
    stats = pltpu.VMEM((2, LOCAL, 8, 128), jnp.float32)
    dma = pltpu.SemaphoreType.DMA
    out = pl.pallas_call(
        kernel,
        out_shape=jax.ShapeDtypeStruct((TOK, HEADS * HD), jnp.bfloat16),
        in_specs=[anywhere] * 6 + [scalars] * 2,
        out_specs=anywhere,
        scratch_shapes=[
            heads, heads, heads, parts, heads, heads, heads, heads, database, database,
            pltpu.VMEM((2, 4, XS, 8, 128), jnp.int32),
            pltpu.SMEM((2, 4, XS, 8, 128), jnp.int32),
            heads,
            pltpu.VMEM((3, 2 * QB, ROWS, ROWS), jnp.float32),
            state, state, state,
            parts, stats, parts, stats, heads, parts,
            dma((5, LOCAL, XS)), dma((5, LOCAL, XS)), dma((4 * XS,)), dma((2, 4, XS)), dma((4 * XS,)), dma((2, 4, XS)),
            dma((2, 4)), dma((4,)), dma((11, LOCAL)), dma((11, LOCAL)),
            dma((2, 2, 4)), dma((2, 2, 4)), dma((2, N_DP)), dma((5, LOCAL)), dma((2,)), dma,
            pltpu.SemaphoreType.REGULAR,
        ],
        compiler_params=pltpu.CompilerParams(
            collective_id=0, has_side_effects=True, vmem_limit_bytes=60 * 1024 * 1024
        ),
    )(q_self[0], k_self[0], v_self[0], q_cross[0], db_keys, db_values, nb_shard, nb_row)
    return out[None]


def solution(mesh):
    return jax.shard_map(
        shards,
        mesh=mesh,
        in_specs=(
            P("dp", "ctx", None),
            P("dp", "ctx", None),
            P("dp", "ctx", None),
            P("dp", "ctx", None),
            P("dp", None, None),
            P("dp", None, None),
            P("dp", "ctx", None),
            P("dp", "ctx", None),
        ),
        out_specs=P("dp", "ctx", None),
        check_vma=False,
    )
```

```python
import jax
import jax.numpy as jnp
from jax import lax
from jax.experimental import pallas as pl
from jax.experimental.pallas import tpu as pltpu
from jax.sharding import PartitionSpec as P

HEADS = 16
HD = 128
GROUP = 64
NEIGH = 2
NLEN = 128
TOK = 128
DB_DEV = 2
N_DP = 16
HALF = 8
XS = 4
LOCAL = HEADS // XS
ROWS = 256
PER = ROWS // TOK
QB = XS // PER
EXPO = HD**-0.5 * 1.4426950408889634
MESH = pl.DeviceIdType.MESH
NT = (((1,), (1,)), ((), ()))
NN = (((1,), (0,)), ((), ()))
QC, KS, VS, QS, OUT = range(5)
ZK, ZV, ZQ2, ZQ3, ZQ3B, ZO2, ZS2, ZO3, ZS3, ZO3B, ZS3B = range(11)


def cols(head):
    return pl.ds(pl.multiple_of(head * HD, HD), HD)


def kernel(
    qs_ref, ks_ref, vs_ref, qc_ref, kd_ref, vd_ref, shard_ref, row_ref, out_ref,
    qs, ks, vs, qc, k0, v0, q2, q3, kd, vd, idx, idx_s, cross, scores, tops, totals, accs,
    part_out, stat_out, part_in, stat_in, mixed, cross_out,
    x_send, x_recv, qc_send, qc_recv, idx_send, idx_recv, back_send, back_recv, z_send, z_recv,
    y_send, core_send, db_recv, own_sem, db_own, number_sem, ready,
):
    dp = lax.axis_index("dp")
    me = lax.axis_index("ctx")
    row = me // XS
    x = lax.rem(me, XS)
    near = lax.rem(dp, HALF)
    side = dp - near
    away = HALF - side
    y = near // 2
    core = lax.rem(near, 2)
    other_core = dp + 1 - 2 * core
    far_ctx = (3 - row) * XS + x
    edge = (row == 0) | (row == 3)
    first_side = dp < HALF
    inner = (row == 1) | (row == 2)
    pair = row + 1 - 2 * lax.rem(row, 2)
    cross_row = jnp.where(inner, pair, row)
    cross_part = jnp.where(inner, 1, 0)

    def x_at(k):
        return lax.rem(x + k, XS)

    def y_at(home, k):
        return home + lax.rem(near + 2 * k, HALF)

    def loop(first, last, body):
        def step(k, carry):
            body(k)
            return carry

        lax.fori_loop(first, last, step, 0)

    barrier = pltpu.get_barrier_semaphore()

    def greet(dp_of, ctx_of):
        pl.semaphore_signal(barrier, inc=1, device_id={"dp": dp_of, "ctx": ctx_of}, device_id_type=MESH)

    def plane(k):
        return lax.rem(y + k // XS, 4), x_at(lax.rem(k, XS))

    def greet_plane(of_row):
        def step(k):
            to_y, to_x = plane(k)
            greet(side + 2 * to_y + core, of_row * XS + to_x)

        return step

    loop(1, jnp.where(edge, 4 * XS, XS), greet_plane(row))
    loop(1, 4 * XS, greet_plane(pair))
    for k in range(1, 4):
        greet(dp, lax.rem(row + k, 4) * XS + x)

    @pl.when(edge)
    def _():
        greet(other_core, me)

    @pl.when(edge & first_side)
    def _():
        for k in range(4):
            greet(y_at(away, k), far_ctx)

    lane = lax.broadcasted_iota(jnp.int32, (8, 128), 1)
    tile = jnp.zeros((8, 128), jnp.int32)
    for g in range(TOK // GROUP):
        for n in range(NEIGH):
            block = shard_ref[0, g, n] * DB_DEV + row_ref[0, g, n]
            tile = jnp.where(lane == g * NEIGH + n, block, tile)
    idx[cross_part, y, x] = tile

    arrays = {KS: (ks_ref, ks), VS: (vs_ref, vs), QS: (qs_ref, qs)}
    blocks = ((kd_ref, kd), (vd_ref, vd))
    head = x * LOCAL + y

    def own_copy(kind, h):
        arg, buf = arrays[kind]
        return pltpu.make_async_copy(arg.at[:, cols(x * LOCAL + h)], buf.at[h, x], own_sem.at[kind, h])

    def own_qc():
        return pltpu.make_async_copy(qc_ref.at[:, cols(head)], qc.at[0, y, x], own_sem.at[QC, 0])

    def own_db(kind):
        arg, buf = blocks[kind]
        return pltpu.make_async_copy(arg.at[:, :, cols(head)], buf.at[pl.ds(dp * DB_DEV, DB_DEV)], db_own.at[kind])

    def start_own(h):
        for kind in (KS, VS, QS):
            own_copy(kind, h).start()

    loop(0, LOCAL, start_own)

    @pl.when(edge)
    def _():
        own_qc().start()
        for kind in range(2):
            own_db(kind).start()

    pl.semaphore_wait(barrier, 21 + jnp.where(edge, 13, 0) + jnp.where(edge & (dp >= HALF), 4, 0))

    @pl.when(edge & (dp >= HALF))
    def _():
        for k in range(4):
            pl.semaphore_signal(ready, inc=1, device_id={"dp": y_at(away, k), "ctx": far_ctx}, device_id_type=MESH)

    def shard_copy(kind, shard, src, send, target, target_ctx):
        part = blocks[kind][1].at[pl.ds(shard * DB_DEV, DB_DEV)]
        return pltpu.make_async_remote_copy(
            part if src is None else src, part, send, db_recv.at[kind, shard],
            device_id={"dp": target, "ctx": target_ctx}, device_id_type=MESH,
        )

    def y_copy(kind, far, k):
        src = blocks[kind][0].at[:, :, cols(x * LOCAL + lax.rem(y + k, 4))]
        target = y_at(away if far else side, k)
        return shard_copy(kind, dp, src, y_send.at[kind, far, k], target, far_ctx if far else me)

    def core_pass(kind, far, k):
        src = blocks[kind][0].at[:, :, cols(head)] if (far, k) == (0, 0) else None
        return shard_copy(kind, y_at(away if far else side, k), src, core_send.at[kind, far, k], other_core, me)

    def wait_shard(kind, shard):
        shard_copy(kind, shard, None, y_send.at[kind, 0, 0], other_core, me).wait_recv()

    def qc_copy(k):
        to_y, to_x = plane(k)
        return pltpu.make_async_remote_copy(
            qc_ref.at[:, cols(to_x * LOCAL + to_y)], qc.at[cross_part, y, x], qc_send.at[k], qc_recv.at[cross_part, y, x],
            device_id={"dp": side + 2 * to_y + core, "ctx": cross_row * XS + to_x}, device_id_type=MESH,
        )

    def idx_copy(k):
        to_y, to_x = plane(k)
        return pltpu.make_async_remote_copy(
            idx.at[cross_part, y, x], idx.at[cross_part, y, x], idx_send.at[k], idx_recv.at[cross_part, y, x],
            device_id={"dp": side + 2 * to_y + core, "ctx": cross_row * XS + to_x}, device_id_type=MESH,
        )

    def wait_plane(part):
        def step(k):
            from_y, from_x = plane(k)
            for buf, sent, received in ((idx, idx_send, idx_recv), (qc, qc_send, qc_recv)):
                there = buf.at[part, from_y, from_x]
                pltpu.make_async_remote_copy(
                    there, there, sent.at[k], received.at[part, from_y, from_x],
                    device_id={"dp": side + 2 * from_y + core, "ctx": jnp.where(part == 1, pair, row) * XS + from_x},
                    device_id_type=MESH,
                ).wait_recv()

        return step

    def back_copy(part, k):
        to_y = lax.rem(y + k, 4)
        return pltpu.make_async_remote_copy(
            cross_out.at[part, to_y], cross.at[y], back_send.at[part, k], back_recv.at[y],
            device_id={"dp": y_at(side, k), "ctx": jnp.where(part == 1, pair, row) * XS + x}, device_id_type=MESH,
        )

    def own_back():
        return pltpu.make_async_copy(cross_out.at[0, y], cross.at[y], own_sem.at[QC, 1])

    def x_copy(kind, h, to):
        arg, buf = arrays[kind]
        return pltpu.make_async_remote_copy(
            arg.at[:, cols(to * LOCAL + h)], buf.at[h, x], x_send.at[kind, h, to], x_recv.at[kind, h, x],
            device_id={"dp": dp, "ctx": row * XS + to}, device_id_type=MESH,
        )

    def arrived(kind, h):
        own_copy(kind, h).wait()
        for k in range(1, XS):
            source = x_at(k)
            buf = arrays[kind][1].at[h, source]
            pltpu.make_async_remote_copy(
                buf, buf, x_send.at[kind, h, source], x_recv.at[kind, h, source],
                device_id={"dp": dp, "ctx": row * XS + source}, device_id_type=MESH,
            ).wait_recv()

    def start_x(kinds):
        def step(h):
            for k in (1, 3, 2):
                for kind in kinds:
                    x_copy(kind, h, x_at(k)).start()

        loop(0, LOCAL, step)

    first_plane = jnp.where(inner, 0, 1)

    def start_plane():
        def step(k):
            idx_copy(k).start()
            qc_copy(k).start()

        loop(first_plane, 4 * XS, step)

    def start_near():
        for kind in range(2):
            for k in (1, 3, 2):
                y_copy(kind, 0, k).start()
            core_pass(kind, 0, 0).start()

    def start_far_first():
        @pl.when(dp >= HALF)
        def _():
            for kind in range(2):
                for k in range(4):
                    y_copy(kind, 1, k).start()

    def start_far_second():
        @pl.when(first_side)
        def _():
            pl.semaphore_wait(ready, 4)
            for kind in range(2):
                for k in range(4):
                    y_copy(kind, 1, k).start()

    @pl.when(row == 0)
    def _():
        start_far_first()
        start_x((KS, VS))
        start_near()
        start_plane()
        start_far_second()
        start_x((QS,))

    @pl.when(row == 1)
    def _():
        start_plane()
        start_x((KS, VS))
        start_x((QS,))

    @pl.when(row == 2)
    def _():
        start_x((QS,))
        start_plane()
        start_x((KS, VS))

    @pl.when(row == 3)
    def _():
        start_far_first()
        start_x((QS,))
        start_near()
        start_plane()
        start_far_second()
        start_x((KS, VS))

    def z_copy(kind, h):
        src, dst, to = {
            ZK: (ks.at[h], k0.at[h], 1),
            ZV: (vs.at[h], v0.at[h], 1),
            ZQ2: (qs.at[h], q2.at[h], 1),
            ZQ3: (qs.at[h], q3.at[h], 1),
            ZQ3B: (qs.at[h], q3.at[h], 2),
            ZO2: (part_out.at[0, h], part_in.at[0, h], 2),
            ZS2: (stat_out.at[0, h], stat_in.at[0, h], 2),
            ZO3: (part_out.at[1, h], part_in.at[0, h], 3),
            ZS3: (stat_out.at[1, h], stat_in.at[0, h], 3),
            ZO3B: (part_out.at[1, h], part_in.at[1, h], 3),
            ZS3B: (stat_out.at[1, h], stat_in.at[1, h], 3),
        }[kind]
        return pltpu.make_async_remote_copy(
            src, dst, z_send.at[kind, h], z_recv.at[kind, h],
            device_id={"dp": dp, "ctx": to * XS + x}, device_id_type=MESH,
        )

    def relay(h):
        @pl.when(row == 0)
        def _():
            arrived(KS, h)
            z_copy(ZK, h).start()
            arrived(VS, h)
            z_copy(ZV, h).start()

        @pl.when(row == 2)
        def _():
            arrived(QS, h)
            z_copy(ZQ2, h).start()

        @pl.when(row == 3)
        def _():
            arrived(QS, h)
            z_copy(ZQ3, h).start()
            z_copy(ZQ3B, h).start()

    def core_stage(far):
        for kind in range(2):
            for k in (0, 1, 3, 2)[1 - far :]:
                wait_shard(kind, y_at(away if far else side, k))
                core_pass(kind, far, k).start()

    diagonal = lax.broadcasted_iota(jnp.int32, (ROWS, ROWS), 0) >= lax.broadcasted_iota(jnp.int32, (ROWS, ROWS), 1)
    eye = lax.broadcasted_iota(jnp.int32, (TOK, TOK), 0) == lax.broadcasted_iota(jnp.int32, (TOK, TOK), 1)

    def score_block(queries, h, b, chunks, slot):
        q = queries[h, pl.ds(b * PER, PER)].reshape(ROWS, HD)
        peak = None
        for j, (keys, values, c, masked) in enumerate(chunks):
            k = keys[h, pl.ds(c * PER, PER)].reshape(ROWS, HD)
            s = lax.dot_general(q, k, NT, preferred_element_type=jnp.float32)
            if masked:
                s = jnp.where(diagonal, s, -1e30)
            scores[slot, j] = s
            folded = jnp.maximum(s[:, :HD], s[:, HD:])
            peak = folded if peak is None else jnp.maximum(peak, folded)
        return jnp.max(peak, axis=1, keepdims=True)

    def weigh_block(h, chunks, slot, top):
        total = jnp.zeros((ROWS, HD), jnp.float32)
        acc = jnp.zeros((ROWS, HD), jnp.float32)
        for j, (keys, values, c, masked) in enumerate(chunks):
            w = jnp.exp2((scores[slot, j] - top) * EXPO)
            total = total + (w[:, :HD] + w[:, HD:])
            v = values[h, pl.ds(c * PER, PER)].reshape(ROWS, HD)
            acc = acc + lax.dot_general(w.astype(jnp.bfloat16), v, NN, preferred_element_type=jnp.float32)
        return jnp.sum(total, axis=1, keepdims=True), acc

    def attend(h, jobs):
        tops_of = []
        for n in range(len(jobs) + 1):
            if n < len(jobs):
                queries, b, chunks, done = jobs[n]
                tops_of.append(score_block(queries, h, b, chunks, n % 3))
            if n >= 1:
                queries, b, chunks, done = jobs[n - 1]
                done(b, tops_of[n - 1], *weigh_block(h, chunks, (n - 1) % 3, tops_of[n - 1]))

    def partial(queries, h, chunks, place):
        def done(b, top, total, acc):
            part_out[place, h, pl.ds(b * PER, PER)] = (acc / total).astype(jnp.bfloat16).reshape(PER, TOK, HD)
            for p in range(PER):
                rows = slice(p * TOK, (p + 1) * TOK)
                at = b * PER + p
                stat_out[place, h, at : at + 1] = jnp.sum(jnp.where(eye, top[rows], 0.0), axis=0, keepdims=True)
                stat_out[place, h, XS + at : XS + at + 1] = jnp.sum(jnp.where(eye, total[rows], 0.0), axis=0, keepdims=True)

        return [(queries, b, chunks, done) for b in range(QB)]

    def own_rows(h, extra, final):
        def done(b, top, total, acc):
            at = h * QB + b
            if final:
                accs[at] = acc / total
            else:
                accs[at] = acc
                tops[at] = jnp.broadcast_to(top, (ROWS, HD))
                totals[at] = jnp.broadcast_to(total, (ROWS, HD))

        return [(qs, b, extra + [(ks, vs, c, c == b) for c in range(b + 1)], done) for b in range(QB)]

    whole_own = [(ks, vs, c, False) for c in range(QB)]
    whole_first = [(k0, v0, c, False) for c in range(QB)]

    def between(h):
        @pl.when(row == 1)
        def _():
            arrived(KS, h)
            arrived(VS, h)
            z_copy(ZK, h).wait_recv()
            z_copy(ZV, h).wait_recv()
            z_copy(ZQ2, h).wait_recv()
            z_copy(ZQ3, h).wait_recv()
            attend(h, partial(q2, h, whole_first + whole_own, 0) + partial(q3, h, whole_first + whole_own, 1))
            z_copy(ZO2, h).start()
            z_copy(ZS2, h).start()
            z_copy(ZO3, h).start()
            z_copy(ZS3, h).start()

        @pl.when(row == 2)
        def _():
            arrived(KS, h)
            arrived(VS, h)
            z_copy(ZQ3B, h).wait_recv()
            attend(h, partial(q3, h, whole_own, 1))
            z_copy(ZO3B, h).start()
            z_copy(ZS3B, h).start()

    def own_others(h):
        @pl.when(row == 0)
        def _():
            arrived(QS, h)
            attend(h, own_rows(h, [], True))

        @pl.when(row == 1)
        def _():
            arrived(QS, h)
            attend(h, own_rows(h, whole_first, True))

        @pl.when(row == 2)
        def _():
            attend(h, own_rows(h, [], False))

        @pl.when(row == 3)
        def _():
            arrived(KS, h)
            arrived(VS, h)
            attend(h, own_rows(h, [], False))

    def cross_documents(part, pairs):
        docs = [lax.rem(y + 3 - 2 * pairs - n, 4) for n in range(2)]
        groups = [(doc, t, g) for doc in docs for t in range(XS) for g in range(TOK // GROUP)]
        picks = [[idx_s[part, doc, t, 0, g * NEIGH + n] for n in range(NEIGH)] for doc, t, g in groups]
        s = []
        for (doc, t, g), pick in zip(groups, picks):
            keys = jnp.concatenate([kd[block] for block in pick], axis=0)
            q = qc[part, doc, t, pl.ds(g * GROUP, GROUP), :]
            s.append(lax.dot_general(q, keys, NT, preferred_element_type=jnp.float32))
        top = [jnp.max(one, axis=1, keepdims=True) for one in s]
        w = [jnp.exp2((one - high) * EXPO) for one, high in zip(s, top)]
        total = [jnp.sum(one, axis=1, keepdims=True) for one in w]
        o = []
        for one, pick in zip(w, picks):
            values = jnp.concatenate([vd[block] for block in pick], axis=0)
            o.append(lax.dot_general(one.astype(jnp.bfloat16), values, NN, preferred_element_type=jnp.float32))
        for (doc, t, g), one, whole in zip(groups, o, total):
            cross_out[part, doc, t, pl.ds(g * GROUP, GROUP), :] = (one / whole).astype(jnp.bfloat16)

        back_copy(part, 3 - 2 * pairs).start()
        send_back(part, 2 - 2 * pairs)

    def send_back(part, k):
        here = (part == 0) & (k == 0)

        @pl.when(jnp.logical_not(here))
        def _():
            back_copy(part, k).start()

        @pl.when(here)
        def _():
            own_back().start()

    def cross_stage():
        own_qc().wait()
        for kind in range(2):
            own_db(kind).wait()

        def wait_other_core(k):
            for kind in range(2):
                wait_shard(kind, 2 * k + 1 - core)

        loop(0, HALF, wait_other_core)

        def cross_row_of(n):
            part = 1 - n
            loop(n, 4 * XS, wait_plane(part))
            numbers = pltpu.make_async_copy(idx.at[part], idx_s.at[part], number_sem)
            numbers.start()
            numbers.wait()
            loop(0, 2, lambda pairs: cross_documents(part, pairs))

        loop(0, 2, cross_row_of)

    @pl.when(row == 0)
    def _():
        loop(0, 2, relay)
        core_stage(0)
        loop(2, LOCAL, relay)

    @pl.when(row >= 2)
    def _():
        loop(0, LOCAL, relay)

    pl.when(row == 3)(lambda: core_stage(0))

    @pl.when(edge)
    def _():
        core_stage(1)
        cross_stage()

    loop(0, LOCAL, between)

    def merge(h, parts):
        columns = [jnp.transpose(stat_in[place, h]) for place in range(parts)]
        for b in range(QB):
            at = h * QB + b
            for p in range(PER):
                rows = slice(p * TOK, (p + 1) * TOK)
                sub = b * PER + p
                top = tops[at, rows, :1]
                others = [(one[:, sub : sub + 1], one[:, XS + sub : XS + sub + 1]) for one in columns]
                peak = top
                for other_top, _ in others:
                    peak = jnp.maximum(peak, other_top)
                keep = jnp.exp2((top - peak) * EXPO)
                total = totals[at, rows, :1] * keep
                acc = accs[at, rows, :] * keep
                for place, (other_top, other_total) in enumerate(others):
                    w = jnp.exp2((other_top - peak) * EXPO) * other_total
                    total = total + w
                    acc = acc + part_in[place, h, sub].astype(jnp.float32) * w
                accs[at, rows, :] = acc / total

    def out_copy(h, t):
        return pltpu.make_async_remote_copy(
            mixed.at[h, t], out_ref.at[:, cols(x * LOCAL + h)], x_send.at[OUT, h, t], x_recv.at[OUT, h, x],
            device_id={"dp": dp, "ctx": row * XS + t}, device_id_type=MESH,
        )

    def own_out(h):
        return pltpu.make_async_copy(mixed.at[h, x], out_ref.at[:, cols(x * LOCAL + h)], own_sem.at[OUT, h])

    def emit(h):
        @pl.when(row == 2)
        def _():
            z_copy(ZO2, h).wait_recv()
            z_copy(ZS2, h).wait_recv()
            merge(h, 1)

        @pl.when(row == 3)
        def _():
            z_copy(ZO3, h).wait_recv()
            z_copy(ZS3, h).wait_recv()
            z_copy(ZO3B, h).wait_recv()
            z_copy(ZS3B, h).wait_recv()
            merge(h, 2)

        @pl.when((h != y) | inner)
        def _():
            there = cross.at[h]
            pltpu.make_async_remote_copy(
                there, there, back_send.at[0, 0], back_recv.at[h],
                device_id={"dp": side + 2 * h + core, "ctx": cross_row * XS + x}, device_id_type=MESH,
            ).wait_recv()

        @pl.when((h == y) & edge)
        def _():
            own_back().wait()

        self_out = accs[pl.ds(h * QB, QB)].astype(jnp.bfloat16).astype(jnp.float32).reshape(XS, TOK, HD)
        mixed[h] = (self_out + cross[h].astype(jnp.float32)).astype(jnp.bfloat16)
        for k in (1, 3, 2):
            out_copy(h, x_at(k)).start()
        own_out(h).start()

    def own_and_emit(h):
        own_others(h)
        emit(h)

    loop(0, LOCAL, own_and_emit)

    @pl.when(edge)
    def _():
        for kind in range(2):
            for far in range(2):
                for k in range(1 - far, 4):
                    y_copy(kind, far, k).wait_send()
                for k in range(4):
                    core_pass(kind, far, k).wait_send()
        for k in range(1, 4):
            back_copy(0, k).wait_send()
        for k in range(4):
            back_copy(1, k).wait_send()

    def finish_plane(k):
        idx_copy(k).wait_send()
        qc_copy(k).wait_send()

    loop(first_plane, 4 * XS, finish_plane)
    def finish(h):
        for k in range(1, XS):
            peer = x_at(k)
            for kind in (KS, VS, QS):
                x_copy(kind, h, peer).wait_send()
        for at, kinds in enumerate(((ZK, ZV), (ZO2, ZS2, ZO3, ZS3), (ZQ2, ZO3B, ZS3B), (ZQ3, ZQ3B))):

            @pl.when(row == at)
            def _():
                for kind in kinds:
                    z_copy(kind, h).wait_send()

    def finish_out(h):
        own_out(h).wait()
        for k in range(1, XS):
            peer = x_at(k)
            out_copy(h, peer).wait_send()
            pltpu.make_async_remote_copy(
                mixed.at[h, peer], out_ref.at[:, cols(peer * LOCAL + h)], x_send.at[OUT, h, peer], x_recv.at[OUT, h, peer],
                device_id={"dp": dp, "ctx": row * XS + peer}, device_id_type=MESH,
            ).wait_recv()

    loop(0, LOCAL, finish)
    loop(0, LOCAL, finish_out)


def shards(q_self, k_self, v_self, q_cross, db_keys, db_values, nb_shard, nb_row):
    anywhere = pl.BlockSpec(memory_space=pl.ANY)
    scalars = pl.BlockSpec(memory_space=pltpu.SMEM)
    heads = pltpu.VMEM((LOCAL, XS, TOK, HD), jnp.bfloat16)
    database = pltpu.VMEM((N_DP * DB_DEV, NLEN, HD), jnp.bfloat16)
    state = pltpu.VMEM((LOCAL * QB, ROWS, HD), jnp.float32)
    parts = pltpu.VMEM((2, LOCAL, XS, TOK, HD), jnp.bfloat16)
    stats = pltpu.VMEM((2, LOCAL, 8, 128), jnp.float32)
    dma = pltpu.SemaphoreType.DMA
    out = pl.pallas_call(
        kernel,
        out_shape=jax.ShapeDtypeStruct((TOK, HEADS * HD), jnp.bfloat16),
        in_specs=[anywhere] * 6 + [scalars] * 2,
        out_specs=anywhere,
        scratch_shapes=[
            heads, heads, heads, parts, heads, heads, heads, heads, database, database,
            pltpu.VMEM((2, 4, XS, 8, 128), jnp.int32),
            pltpu.SMEM((2, 4, XS, 8, 128), jnp.int32),
            heads,
            pltpu.VMEM((3, 2 * QB, ROWS, ROWS), jnp.float32),
            state, state, state,
            parts, stats, parts, stats, heads, parts,
            dma((5, LOCAL, XS)), dma((5, LOCAL, XS)), dma((4 * XS,)), dma((2, 4, XS)), dma((4 * XS,)), dma((2, 4, XS)),
            dma((2, 4)), dma((4,)), dma((11, LOCAL)), dma((11, LOCAL)),
            dma((2, 2, 4)), dma((2, 2, 4)), dma((2, N_DP)), dma((5, LOCAL)), dma((2,)), dma,
            pltpu.SemaphoreType.REGULAR,
        ],
        compiler_params=pltpu.CompilerParams(
            collective_id=0, has_side_effects=True, vmem_limit_bytes=60 * 1024 * 1024
        ),
    )(q_self[0], k_self[0], v_self[0], q_cross[0], db_keys, db_values, nb_shard, nb_row)
    return out[None]


def solution(mesh):
    return jax.shard_map(
        shards,
        mesh=mesh,
        in_specs=(
            P("dp", "ctx", None),
            P("dp", "ctx", None),
            P("dp", "ctx", None),
            P("dp", "ctx", None),
            P("dp", None, None),
            P("dp", None, None),
            P("dp", "ctx", None),
            P("dp", "ctx", None),
        ),
        out_specs=P("dp", "ctx", None),
        check_vma=False,
    )
```

```python
import jax
import jax.numpy as jnp
from jax import lax
from jax.experimental import pallas as pl
from jax.experimental.pallas import tpu as pltpu
from jax.sharding import PartitionSpec as P

HEADS = 16
HD = 128
GROUP = 64
NEIGH = 2
NLEN = 128
TOK = 128
DB_DEV = 2
N_DP = 16
HALF = 8
XS = 4
LOCAL = HEADS // XS
ROWS = 256
WIDE = LOCAL * HD
PART = 2 * HD
PER = ROWS // TOK
QB = XS // PER
EXPO = HD**-0.5 * 1.4426950408889634
MESH = pl.DeviceIdType.MESH
NT = (((1,), (1,)), ((), ()))
NN = (((1,), (0,)), ((), ()))
QC, KS, VS, QS, OUT = range(5)
ZK, ZV, ZQ2, ZQ3, ZQ3B, ZO2, ZS2, ZO3, ZS3, ZO3B, ZS3B = range(11)


def cols(head):
    return pl.ds(pl.multiple_of(head * HD, HD), HD)


def kernel(
    qs_ref, ks_ref, vs_ref, qc_ref, kd_ref, vd_ref, shard_ref, row_ref, out_ref,
    qs, ks, vs, qc, k0, v0, q2, q3, kd, vd, idx, idx_s, cross, scores, tops, totals, accs,
    part_out, stat_out, part_in, stat_in, mixed, cross_out,
    x_send, x_recv, qc_send, qc_recv, idx_send, idx_recv, back_send, back_recv, z_send, z_recv,
    y_send, core_send, db_recv, own_sem, db_own, number_sem, ready,
):
    dp = lax.axis_index("dp")
    me = lax.axis_index("ctx")
    row = me // XS
    x = lax.rem(me, XS)
    near = lax.rem(dp, HALF)
    side = dp - near
    away = HALF - side
    y = near // 2
    core = lax.rem(near, 2)
    other_core = dp + 1 - 2 * core
    far_ctx = (3 - row) * XS + x
    edge = (row == 0) | (row == 3)
    first_side = dp < HALF
    inner = (row == 1) | (row == 2)
    pair = row + 1 - 2 * lax.rem(row, 2)
    cross_row = jnp.where(inner, pair, row)
    cross_part = jnp.where(inner, 1, 0)

    def x_at(k):
        return lax.rem(x + k, XS)

    def y_at(home, k):
        return home + lax.rem(near + 2 * k, HALF)

    def loop(first, last, body):
        def step(k, carry):
            body(k)
            return carry

        lax.fori_loop(first, last, step, 0)

    barrier = pltpu.get_barrier_semaphore()

    def greet(dp_of, ctx_of):
        pl.semaphore_signal(barrier, inc=1, device_id={"dp": dp_of, "ctx": ctx_of}, device_id_type=MESH)

    def plane(k):
        return lax.rem(y + k // XS, 4), x_at(lax.rem(k, XS))

    def greet_plane(of_row):
        def step(k):
            to_y, to_x = plane(k)
            greet(side + 2 * to_y + core, of_row * XS + to_x)

        return step

    loop(1, jnp.where(edge, 4 * XS, XS), greet_plane(row))
    loop(1, 4 * XS, greet_plane(pair))
    for k in range(1, 4):
        greet(dp, lax.rem(row + k, 4) * XS + x)

    @pl.when(edge)
    def _():
        greet(other_core, me)

    @pl.when(edge & first_side)
    def _():
        for k in range(4):
            greet(y_at(away, k), far_ctx)

    lane = lax.broadcasted_iota(jnp.int32, (8, 128), 1)
    tile = jnp.zeros((8, 128), jnp.int32)
    for g in range(TOK // GROUP):
        for n in range(NEIGH):
            block = shard_ref[0, g, n] * DB_DEV + row_ref[0, g, n]
            tile = jnp.where(lane == g * NEIGH + n, block, tile)
    idx[cross_part, y, x] = tile

    arrays = {KS: (ks_ref, ks), VS: (vs_ref, vs), QS: (qs_ref, qs)}
    blocks = ((kd_ref, kd), (vd_ref, vd))
    head = x * LOCAL + y

    def own_copy(kind):
        arg, buf = arrays[kind]
        return pltpu.make_async_copy(arg.at[:, pl.ds(pl.multiple_of(x * WIDE, WIDE), WIDE)], buf.at[x], own_sem.at[kind, 0])

    def own_qc():
        return pltpu.make_async_copy(qc_ref.at[:, cols(head)], qc.at[0, y, x], own_sem.at[QC, 0])

    def own_db(kind):
        arg, buf = blocks[kind]
        return pltpu.make_async_copy(arg.at[:, :, cols(head)], buf.at[pl.ds(dp * DB_DEV, DB_DEV)], db_own.at[kind])

    for kind in (KS, VS, QS):
        own_copy(kind).start()

    @pl.when(edge)
    def _():
        own_qc().start()
        for kind in range(2):
            own_db(kind).start()

    pl.semaphore_wait(barrier, 21 + jnp.where(edge, 13, 0) + jnp.where(edge & (dp >= HALF), 4, 0))

    @pl.when(edge & (dp >= HALF))
    def _():
        for k in range(4):
            pl.semaphore_signal(ready, inc=1, device_id={"dp": y_at(away, k), "ctx": far_ctx}, device_id_type=MESH)

    def shard_copy(kind, shard, src, send, target, target_ctx):
        part = blocks[kind][1].at[pl.ds(shard * DB_DEV, DB_DEV)]
        return pltpu.make_async_remote_copy(
            part if src is None else src, part, send, db_recv.at[kind, shard],
            device_id={"dp": target, "ctx": target_ctx}, device_id_type=MESH,
        )

    def y_copy(kind, far, k):
        src = blocks[kind][0].at[:, :, cols(x * LOCAL + lax.rem(y + k, 4))]
        target = y_at(away if far else side, k)
        return shard_copy(kind, dp, src, y_send.at[kind, far, k], target, far_ctx if far else me)

    def core_pass(kind, far, k):
        src = blocks[kind][0].at[:, :, cols(head)] if (far, k) == (0, 0) else None
        return shard_copy(kind, y_at(away if far else side, k), src, core_send.at[kind, far, k], other_core, me)

    def wait_shard(kind, shard):
        shard_copy(kind, shard, None, y_send.at[kind, 0, 0], other_core, me).wait_recv()

    def qc_copy(k):
        to_y, to_x = plane(k)
        return pltpu.make_async_remote_copy(
            qc_ref.at[:, cols(to_x * LOCAL + to_y)], qc.at[cross_part, y, x], qc_send.at[k], qc_recv.at[cross_part, y, x],
            device_id={"dp": side + 2 * to_y + core, "ctx": cross_row * XS + to_x}, device_id_type=MESH,
        )

    def idx_copy(k):
        to_y, to_x = plane(k)
        return pltpu.make_async_remote_copy(
            idx.at[cross_part, y, x], idx.at[cross_part, y, x], idx_send.at[k], idx_recv.at[cross_part, y, x],
            device_id={"dp": side + 2 * to_y + core, "ctx": cross_row * XS + to_x}, device_id_type=MESH,
        )

    def wait_plane(part):
        def step(k):
            from_y, from_x = plane(k)
            for buf, sent, received in ((idx, idx_send, idx_recv), (qc, qc_send, qc_recv)):
                there = buf.at[part, from_y, from_x]
                pltpu.make_async_remote_copy(
                    there, there, sent.at[k], received.at[part, from_y, from_x],
                    device_id={"dp": side + 2 * from_y + core, "ctx": jnp.where(part == 1, pair, row) * XS + from_x},
                    device_id_type=MESH,
                ).wait_recv()

        return step

    def back_copy(part, k):
        to_y = lax.rem(y + k, 4)
        return pltpu.make_async_remote_copy(
            cross_out.at[part, to_y], cross.at[y], back_send.at[part, k], back_recv.at[y],
            device_id={"dp": y_at(side, k), "ctx": jnp.where(part == 1, pair, row) * XS + x}, device_id_type=MESH,
        )

    def own_back():
        return pltpu.make_async_copy(cross_out.at[0, y], cross.at[y], own_sem.at[QC, 1])

    def x_copy(kind, p, to):
        arg, buf = arrays[kind]
        part = pl.ds(pl.multiple_of(p * PART, PART), PART)
        return pltpu.make_async_remote_copy(
            arg.at[:, pl.ds(pl.multiple_of(to * WIDE + p * PART, PART), PART)], buf.at[x, :, part],
            x_send.at[kind, p, to], x_recv.at[kind, p, x],
            device_id={"dp": dp, "ctx": row * XS + to}, device_id_type=MESH,
        )

    def arrived(kind, h):
        @pl.when(h == 0)
        def _():
            own_copy(kind).wait()

        @pl.when(lax.rem(h, 2) == 0)
        def _():
            p = h // 2
            for k in range(1, XS):
                source = x_at(k)
                buf = arrays[kind][1].at[source, :, pl.ds(pl.multiple_of(p * PART, PART), PART)]
                pltpu.make_async_remote_copy(
                    buf, buf, x_send.at[kind, p, source], x_recv.at[kind, p, source],
                    device_id={"dp": dp, "ctx": row * XS + source}, device_id_type=MESH,
                ).wait_recv()

    def start_x(kinds):
        for p in range(2):
            for k in (1, 3, 2):
                for kind in kinds:
                    x_copy(kind, p, x_at(k)).start()

    first_plane = jnp.where(inner, 0, 1)

    def start_plane():
        def step(k):
            idx_copy(k).start()
            qc_copy(k).start()

        loop(first_plane, 4 * XS, step)

    def start_near():
        for kind in range(2):
            for k in (1, 3, 2):
                y_copy(kind, 0, k).start()
            core_pass(kind, 0, 0).start()

    def start_far_first():
        @pl.when(dp >= HALF)
        def _():
            for kind in range(2):
                for k in range(4):
                    y_copy(kind, 1, k).start()

    def start_far_second():
        @pl.when(first_side)
        def _():
            pl.semaphore_wait(ready, 4)
            for kind in range(2):
                for k in range(4):
                    y_copy(kind, 1, k).start()

    @pl.when(row == 0)
    def _():
        start_far_first()
        start_x((KS, VS))
        start_near()
        start_plane()
        start_far_second()
        start_x((QS,))

    @pl.when(row == 1)
    def _():
        start_plane()
        start_x((KS, VS))
        start_x((QS,))

    @pl.when(row == 2)
    def _():
        start_x((QS,))
        start_plane()
        start_x((KS, VS))

    @pl.when(row == 3)
    def _():
        start_far_first()
        start_x((QS,))
        start_near()
        start_plane()
        start_far_second()
        start_x((KS, VS))

    def z_copy(kind, h):
        src, dst, to = {
            ZK: (ks.at[:, :, cols(h)], k0.at[h], 1),
            ZV: (vs.at[:, :, cols(h)], v0.at[h], 1),
            ZQ2: (qs.at[:, :, cols(h)], q2.at[h], 1),
            ZQ3: (qs.at[:, :, cols(h)], q3.at[h], 1),
            ZQ3B: (qs.at[:, :, cols(h)], q3.at[h], 2),
            ZO2: (part_out.at[0, h], part_in.at[0, h], 2),
            ZS2: (stat_out.at[0, h], stat_in.at[0, h], 2),
            ZO3: (part_out.at[1, h], part_in.at[0, h], 3),
            ZS3: (stat_out.at[1, h], stat_in.at[0, h], 3),
            ZO3B: (part_out.at[1, h], part_in.at[1, h], 3),
            ZS3B: (stat_out.at[1, h], stat_in.at[1, h], 3),
        }[kind]
        return pltpu.make_async_remote_copy(
            src, dst, z_send.at[kind, h], z_recv.at[kind, h],
            device_id={"dp": dp, "ctx": to * XS + x}, device_id_type=MESH,
        )

    def relay(h):
        @pl.when(row == 0)
        def _():
            arrived(KS, h)
            z_copy(ZK, h).start()
            arrived(VS, h)
            z_copy(ZV, h).start()

        @pl.when(row == 2)
        def _():
            arrived(QS, h)
            z_copy(ZQ2, h).start()

        @pl.when(row == 3)
        def _():
            arrived(QS, h)
            z_copy(ZQ3, h).start()
            z_copy(ZQ3B, h).start()

    def core_stage():
        for far in range(2):
            for kind in range(2):
                for k in (0, 1, 3, 2)[1 - far :]:
                    wait_shard(kind, y_at(away if far else side, k))
                    core_pass(kind, far, k).start()

    diagonal = lax.broadcasted_iota(jnp.int32, (ROWS, ROWS), 0) >= lax.broadcasted_iota(jnp.int32, (ROWS, ROWS), 1)
    eye = lax.broadcasted_iota(jnp.int32, (TOK, TOK), 0) == lax.broadcasted_iota(jnp.int32, (TOK, TOK), 1)

    def by_head(buf):
        return lambda h, b: buf[h, pl.ds(b * PER, PER)]

    def by_source(buf):
        return lambda h, b: buf[pl.ds(b * PER, PER), :, cols(h)]

    own_q, own_k, own_v = by_source(qs), by_source(ks), by_source(vs)

    def score_block(queries, h, b, chunks, slot):
        q = queries(h, b).reshape(ROWS, HD)
        peak = None
        for j, (keys, values, c, masked) in enumerate(chunks):
            k = keys(h, c).reshape(ROWS, HD)
            s = lax.dot_general(q, k, NT, preferred_element_type=jnp.float32)
            if masked:
                s = jnp.where(diagonal, s, -1e30)
            scores[slot, j] = s
            folded = jnp.maximum(s[:, :HD], s[:, HD:])
            peak = folded if peak is None else jnp.maximum(peak, folded)
        return jnp.max(peak, axis=1, keepdims=True)

    def weigh_block(h, chunks, slot, top):
        total = jnp.zeros((ROWS, HD), jnp.float32)
        acc = jnp.zeros((ROWS, HD), jnp.float32)
        for j, (keys, values, c, masked) in enumerate(chunks):
            w = jnp.exp2((scores[slot, j] - top) * EXPO)
            total = total + (w[:, :HD] + w[:, HD:])
            v = values(h, c).reshape(ROWS, HD)
            acc = acc + lax.dot_general(w.astype(jnp.bfloat16), v, NN, preferred_element_type=jnp.float32)
        return jnp.sum(total, axis=1, keepdims=True), acc

    def attend(h, jobs):
        tops_of = []
        for n in range(len(jobs) + 1):
            if n < len(jobs):
                queries, b, chunks, done = jobs[n]
                tops_of.append(score_block(queries, h, b, chunks, n % 3))
            if n >= 1:
                queries, b, chunks, done = jobs[n - 1]
                done(b, tops_of[n - 1], *weigh_block(h, chunks, (n - 1) % 3, tops_of[n - 1]))

    def partial(queries, h, chunks, place):
        def done(b, top, total, acc):
            part_out[place, h, pl.ds(b * PER, PER)] = (acc / total).astype(jnp.bfloat16).reshape(PER, TOK, HD)
            for p in range(PER):
                rows = slice(p * TOK, (p + 1) * TOK)
                at = b * PER + p
                stat_out[place, h, at : at + 1] = jnp.sum(jnp.where(eye, top[rows], 0.0), axis=0, keepdims=True)
                stat_out[place, h, XS + at : XS + at + 1] = jnp.sum(jnp.where(eye, total[rows], 0.0), axis=0, keepdims=True)

        return [(queries, b, chunks, done) for b in range(QB)]

    def own_rows(h, extra, final):
        def done(b, top, total, acc):
            at = h * QB + b
            if final:
                accs[at] = acc / total
            else:
                accs[at] = acc
                tops[at] = jnp.broadcast_to(top, (ROWS, HD))
                totals[at] = jnp.broadcast_to(total, (ROWS, HD))

        return [(own_q, b, extra + [(own_k, own_v, c, c == b) for c in range(b + 1)], done) for b in range(QB)]

    whole_own = [(own_k, own_v, c, False) for c in range(QB)]
    whole_first = [(by_head(k0), by_head(v0), c, False) for c in range(QB)]

    def between(h):
        @pl.when(row == 1)
        def _():
            arrived(KS, h)
            arrived(VS, h)
            z_copy(ZK, h).wait_recv()
            z_copy(ZV, h).wait_recv()
            z_copy(ZQ2, h).wait_recv()
            z_copy(ZQ3, h).wait_recv()
            attend(h, partial(by_head(q2), h, whole_first + whole_own, 0) + partial(by_head(q3), h, whole_first + whole_own, 1))
            z_copy(ZO2, h).start()
            z_copy(ZS2, h).start()
            z_copy(ZO3, h).start()
            z_copy(ZS3, h).start()

        @pl.when(row == 2)
        def _():
            arrived(KS, h)
            arrived(VS, h)
            z_copy(ZQ3B, h).wait_recv()
            attend(h, partial(by_head(q3), h, whole_own, 1))
            z_copy(ZO3B, h).start()
            z_copy(ZS3B, h).start()

    def own_others(h):
        @pl.when(row == 0)
        def _():
            arrived(QS, h)
            attend(h, own_rows(h, [], True))

        @pl.when(row == 1)
        def _():
            arrived(QS, h)
            attend(h, own_rows(h, whole_first, True))

        @pl.when(row == 2)
        def _():
            attend(h, own_rows(h, [], False))

        @pl.when(row == 3)
        def _():
            arrived(KS, h)
            arrived(VS, h)
            attend(h, own_rows(h, [], False))

    def cross_document(part, k):
        doc = lax.rem(y + k, 4)
        groups = [(t, g) for t in range(XS) for g in range(TOK // GROUP)]
        picks = [[idx_s[part, doc, t, 0, g * NEIGH + n] for n in range(NEIGH)] for t, g in groups]
        s = []
        for (t, g), pick in zip(groups, picks):
            keys = jnp.concatenate([kd[block] for block in pick], axis=0)
            q = qc[part, doc, t, pl.ds(g * GROUP, GROUP), :]
            s.append(lax.dot_general(q, keys, NT, preferred_element_type=jnp.float32))
        top = [jnp.max(one, axis=1, keepdims=True) for one in s]
        w = [jnp.exp2((one - high) * EXPO) for one, high in zip(s, top)]
        total = [jnp.sum(one, axis=1, keepdims=True) for one in w]
        o = []
        for one, pick in zip(w, picks):
            values = jnp.concatenate([vd[block] for block in pick], axis=0)
            o.append(lax.dot_general(one.astype(jnp.bfloat16), values, NN, preferred_element_type=jnp.float32))
        for (t, g), one, whole in zip(groups, o, total):
            cross_out[part, doc, t, pl.ds(g * GROUP, GROUP), :] = (one / whole).astype(jnp.bfloat16)

        here = (part == 0) & (k == 0)

        @pl.when(jnp.logical_not(here))
        def _():
            back_copy(part, k).start()

        @pl.when(here)
        def _():
            own_back().start()

    def cross_stage():
        own_qc().wait()
        for kind in range(2):
            own_db(kind).wait()

        def wait_other_core(k):
            for kind in range(2):
                wait_shard(kind, 2 * k + 1 - core)

        loop(0, HALF, wait_other_core)

        def cross_row_of(n):
            part = 1 - n
            loop(n, 4 * XS, wait_plane(part))
            numbers = pltpu.make_async_copy(idx.at[part], idx_s.at[part], number_sem)
            numbers.start()
            numbers.wait()
            loop(0, 4, lambda k: cross_document(part, 3 - k))

        loop(0, 2, cross_row_of)

    @pl.when(row == 0)
    def _():
        loop(0, LOCAL, relay)

    @pl.when(row >= 2)
    def _():
        loop(0, LOCAL, relay)

    @pl.when(edge)
    def _():
        core_stage()
        cross_stage()

    loop(0, LOCAL, between)

    def merge(h, parts):
        for b in range(QB):
            at = h * QB + b
            for p in range(PER):
                rows = slice(p * TOK, (p + 1) * TOK)
                sub = b * PER + p
                top = tops[at, rows, :1]
                others = []
                for place in range(parts):
                    column = [
                        jnp.sum(jnp.where(eye, stat_in[place, h, n : n + 1], 0.0), axis=1, keepdims=True)
                        for n in (sub, XS + sub)
                    ]
                    others.append(column)
                peak = top
                for other_top, _ in others:
                    peak = jnp.maximum(peak, other_top)
                keep = jnp.exp2((top - peak) * EXPO)
                total = totals[at, rows, :1] * keep
                acc = accs[at, rows, :] * keep
                for place, (other_top, other_total) in enumerate(others):
                    w = jnp.exp2((other_top - peak) * EXPO) * other_total
                    total = total + w
                    acc = acc + part_in[place, h, sub].astype(jnp.float32) * w
                accs[at, rows, :] = acc / total

    def out_copy(h, t):
        return pltpu.make_async_remote_copy(
            mixed.at[h, t], out_ref.at[:, cols(x * LOCAL + h)], x_send.at[OUT, h, t], x_recv.at[OUT, h, x],
            device_id={"dp": dp, "ctx": row * XS + t}, device_id_type=MESH,
        )

    def own_out(h):
        return pltpu.make_async_copy(mixed.at[h, x], out_ref.at[:, cols(x * LOCAL + h)], own_sem.at[OUT, h])

    def emit(h):
        @pl.when(row == 2)
        def _():
            z_copy(ZO2, h).wait_recv()
            z_copy(ZS2, h).wait_recv()
            merge(h, 1)

        @pl.when(row == 3)
        def _():
            z_copy(ZO3, h).wait_recv()
            z_copy(ZS3, h).wait_recv()
            z_copy(ZO3B, h).wait_recv()
            z_copy(ZS3B, h).wait_recv()
            merge(h, 2)

        @pl.when((h != y) | inner)
        def _():
            there = cross.at[h]
            pltpu.make_async_remote_copy(
                there, there, back_send.at[0, 0], back_recv.at[h],
                device_id={"dp": side + 2 * h + core, "ctx": cross_row * XS + x}, device_id_type=MESH,
            ).wait_recv()

        @pl.when((h == y) & edge)
        def _():
            own_back().wait()

        self_out = accs[pl.ds(h * QB, QB)].astype(jnp.bfloat16).astype(jnp.float32).reshape(XS, TOK, HD)
        mixed[h] = (self_out + cross[h].astype(jnp.float32)).astype(jnp.bfloat16)
        for k in (1, 3, 2):
            out_copy(h, x_at(k)).start()
        own_out(h).start()

    def own_and_emit(h):
        own_others(h)
        emit(h)

    loop(0, LOCAL, own_and_emit)

    @pl.when(edge)
    def _():
        for kind in range(2):
            for far in range(2):
                for k in range(1 - far, 4):
                    y_copy(kind, far, k).wait_send()
                for k in range(4):
                    core_pass(kind, far, k).wait_send()
        for k in range(1, 4):
            back_copy(0, k).wait_send()
        for k in range(4):
            back_copy(1, k).wait_send()

    def finish_plane(k):
        idx_copy(k).wait_send()
        qc_copy(k).wait_send()

    loop(first_plane, 4 * XS, finish_plane)
    def finish(h):
        @pl.when(h < 2)
        def _():
            for k in range(1, XS):
                for kind in (KS, VS, QS):
                    x_copy(kind, h, x_at(k)).wait_send()

        for at, kinds in enumerate(((ZK, ZV), (ZO2, ZS2, ZO3, ZS3), (ZQ2, ZO3B, ZS3B), (ZQ3, ZQ3B))):

            @pl.when(row == at)
            def _():
                for kind in kinds:
                    z_copy(kind, h).wait_send()

    def finish_out(h):
        own_out(h).wait()
        for k in range(1, XS):
            peer = x_at(k)
            out_copy(h, peer).wait_send()
            pltpu.make_async_remote_copy(
                mixed.at[h, peer], out_ref.at[:, cols(peer * LOCAL + h)], x_send.at[OUT, h, peer], x_recv.at[OUT, h, peer],
                device_id={"dp": dp, "ctx": row * XS + peer}, device_id_type=MESH,
            ).wait_recv()

    loop(0, LOCAL, finish)
    loop(0, LOCAL, finish_out)


def shards(q_self, k_self, v_self, q_cross, db_keys, db_values, nb_shard, nb_row):
    anywhere = pl.BlockSpec(memory_space=pl.ANY)
    scalars = pl.BlockSpec(memory_space=pltpu.SMEM)
    heads = pltpu.VMEM((LOCAL, XS, TOK, HD), jnp.bfloat16)
    sources = pltpu.VMEM((XS, TOK, WIDE), jnp.bfloat16)
    database = pltpu.VMEM((N_DP * DB_DEV, NLEN, HD), jnp.bfloat16)
    state = pltpu.VMEM((LOCAL * QB, ROWS, HD), jnp.float32)
    parts = pltpu.VMEM((2, LOCAL, XS, TOK, HD), jnp.bfloat16)
    stats = pltpu.VMEM((2, LOCAL, 8, 128), jnp.float32)
    dma = pltpu.SemaphoreType.DMA
    out = pl.pallas_call(
        kernel,
        out_shape=jax.ShapeDtypeStruct((TOK, HEADS * HD), jnp.bfloat16),
        in_specs=[anywhere] * 6 + [scalars] * 2,
        out_specs=anywhere,
        scratch_shapes=[
            sources, sources, sources, parts, heads, heads, heads, heads, database, database,
            pltpu.VMEM((2, 4, XS, 8, 128), jnp.int32),
            pltpu.SMEM((2, 4, XS, 8, 128), jnp.int32),
            heads,
            pltpu.VMEM((3, 2 * QB, ROWS, ROWS), jnp.float32),
            state, state, state,
            parts, stats, parts, stats, heads, parts,
            dma((5, LOCAL, XS)), dma((5, LOCAL, XS)), dma((4 * XS,)), dma((2, 4, XS)), dma((4 * XS,)), dma((2, 4, XS)),
            dma((2, 4)), dma((4,)), dma((11, LOCAL)), dma((11, LOCAL)),
            dma((2, 2, 4)), dma((2, 2, 4)), dma((2, N_DP)), dma((5, LOCAL)), dma((2,)), dma,
            pltpu.SemaphoreType.REGULAR,
        ],
        compiler_params=pltpu.CompilerParams(
            collective_id=0, has_side_effects=True, vmem_limit_bytes=60 * 1024 * 1024
        ),
    )(q_self[0], k_self[0], v_self[0], q_cross[0], db_keys, db_values, nb_shard, nb_row)
    return out[None]


def solution(mesh):
    return jax.shard_map(
        shards,
        mesh=mesh,
        in_specs=(
            P("dp", "ctx", None),
            P("dp", "ctx", None),
            P("dp", "ctx", None),
            P("dp", "ctx", None),
            P("dp", None, None),
            P("dp", None, None),
            P("dp", "ctx", None),
            P("dp", "ctx", None),
        ),
        out_specs=P("dp", "ctx", None),
        check_vma=False,
    )
```

```python
import jax
import jax.numpy as jnp
from jax import lax
from jax.experimental import pallas as pl
from jax.experimental.pallas import tpu as pltpu
from jax.sharding import PartitionSpec as P

HEADS = 16
HD = 128
GROUP = 64
NEIGH = 2
NLEN = 128
TOK = 128
DB_DEV = 2
N_DP = 16
HALF = 8
XS = 4
LOCAL = HEADS // XS
ROWS = 256
PER = ROWS // TOK
QB = XS // PER
EXPO = HD**-0.5 * 1.4426950408889634
MESH = pl.DeviceIdType.MESH
NT = (((1,), (1,)), ((), ()))
NN = (((1,), (0,)), ((), ()))
QC, KS, VS, QS, OUT = range(5)
ZK, ZV, ZQ2, ZQ3, ZQ3B, ZO2, ZS2, ZO3, ZS3, ZO3B, ZS3B = range(11)


def cols(head):
    return pl.ds(pl.multiple_of(head * HD, HD), HD)


def kernel(
    qs_ref, ks_ref, vs_ref, qc_ref, kd_ref, vd_ref, shard_ref, row_ref, out_ref,
    qs, ks, vs, qc, k0, v0, q2, q3, kd, vd, idx, idx_s, cross, scores, tops, totals, accs,
    part_out, stat_out, part_in, stat_in, mixed, cross_out,
    x_send, x_recv, qc_send, qc_recv, idx_send, idx_recv, back_send, back_recv, z_send, z_recv,
    y_send, core_send, db_recv, own_sem, db_own, number_sem, ready,
):
    dp = lax.axis_index("dp")
    me = lax.axis_index("ctx")
    row = me // XS
    x = lax.rem(me, XS)
    near = lax.rem(dp, HALF)
    side = dp - near
    away = HALF - side
    y = near // 2
    core = lax.rem(near, 2)
    other_core = dp + 1 - 2 * core
    far_ctx = (3 - row) * XS + x
    edge = (row == 0) | (row == 3)
    first_side = dp < HALF
    inner = (row == 1) | (row == 2)
    pair = row + 1 - 2 * lax.rem(row, 2)
    cross_row = jnp.where(inner, pair, row)
    cross_part = jnp.where(inner, 1, 0)

    def x_at(k):
        return lax.rem(x + k, XS)

    def y_at(home, k):
        return home + lax.rem(near + 2 * k, HALF)

    def loop(first, last, body):
        def step(k, carry):
            body(k)
            return carry

        lax.fori_loop(first, last, step, 0)

    barrier = pltpu.get_barrier_semaphore()

    def greet(dp_of, ctx_of):
        pl.semaphore_signal(barrier, inc=1, device_id={"dp": dp_of, "ctx": ctx_of}, device_id_type=MESH)

    def plane(k):
        return lax.rem(y + k // XS, 4), x_at(lax.rem(k, XS))

    def greet_plane(of_row):
        def step(k):
            to_y, to_x = plane(k)
            greet(side + 2 * to_y + core, of_row * XS + to_x)

        return step

    loop(1, jnp.where(edge, 4 * XS, XS), greet_plane(row))
    loop(1, 4 * XS, greet_plane(pair))
    for k in range(1, 4):
        greet(dp, lax.rem(row + k, 4) * XS + x)

    @pl.when(edge)
    def _():
        greet(other_core, me)

    @pl.when(edge & first_side)
    def _():
        for k in range(4):
            greet(y_at(away, k), far_ctx)

    lane = lax.broadcasted_iota(jnp.int32, (8, 128), 1)
    tile = jnp.zeros((8, 128), jnp.int32)
    for g in range(TOK // GROUP):
        for n in range(NEIGH):
            block = shard_ref[0, g, n] * DB_DEV + row_ref[0, g, n]
            tile = jnp.where(lane == g * NEIGH + n, block, tile)
    idx[cross_part, y, x] = tile

    arrays = {KS: (ks_ref, ks), VS: (vs_ref, vs), QS: (qs_ref, qs)}
    blocks = ((kd_ref, kd), (vd_ref, vd))
    head = x * LOCAL + y

    def own_copy(kind, h):
        arg, buf = arrays[kind]
        return pltpu.make_async_copy(arg.at[:, cols(x * LOCAL + h)], buf.at[h, x], own_sem.at[kind, h])

    def own_qc():
        return pltpu.make_async_copy(qc_ref.at[:, cols(head)], qc.at[0, y, x], own_sem.at[QC, 0])

    def own_db(kind):
        arg, buf = blocks[kind]
        return pltpu.make_async_copy(arg.at[:, :, cols(head)], buf.at[pl.ds(dp * DB_DEV, DB_DEV)], db_own.at[kind])

    def start_own(h):
        for kind in (KS, VS, QS):
            own_copy(kind, h).start()

    loop(0, LOCAL, start_own)

    @pl.when(edge)
    def _():
        own_qc().start()
        for kind in range(2):
            own_db(kind).start()

    pl.semaphore_wait(barrier, 21 + jnp.where(edge, 13, 0) + jnp.where(edge & (dp >= HALF), 4, 0))

    @pl.when(edge & (dp >= HALF))
    def _():
        for k in range(4):
            pl.semaphore_signal(ready, inc=1, device_id={"dp": y_at(away, k), "ctx": far_ctx}, device_id_type=MESH)

    def shard_copy(kind, shard, src, send, target, target_ctx):
        part = blocks[kind][1].at[pl.ds(shard * DB_DEV, DB_DEV)]
        return pltpu.make_async_remote_copy(
            part if src is None else src, part, send, db_recv.at[kind, shard],
            device_id={"dp": target, "ctx": target_ctx}, device_id_type=MESH,
        )

    def y_copy(kind, far, k):
        src = blocks[kind][0].at[:, :, cols(x * LOCAL + lax.rem(y + k, 4))]
        target = y_at(away if far else side, k)
        return shard_copy(kind, dp, src, y_send.at[kind, far, k], target, far_ctx if far else me)

    def core_pass(kind, far, k):
        src = blocks[kind][0].at[:, :, cols(head)] if (far, k) == (0, 0) else None
        return shard_copy(kind, y_at(away if far else side, k), src, core_send.at[kind, far, k], other_core, me)

    def wait_shard(kind, shard):
        shard_copy(kind, shard, None, y_send.at[kind, 0, 0], other_core, me).wait_recv()

    def qc_copy(k):
        to_y, to_x = plane(k)
        return pltpu.make_async_remote_copy(
            qc_ref.at[:, cols(to_x * LOCAL + to_y)], qc.at[cross_part, y, x], qc_send.at[k], qc_recv.at[cross_part, y, x],
            device_id={"dp": side + 2 * to_y + core, "ctx": cross_row * XS + to_x}, device_id_type=MESH,
        )

    def idx_copy(k):
        to_y, to_x = plane(k)
        return pltpu.make_async_remote_copy(
            idx.at[cross_part, y, x], idx.at[cross_part, y, x], idx_send.at[k], idx_recv.at[cross_part, y, x],
            device_id={"dp": side + 2 * to_y + core, "ctx": cross_row * XS + to_x}, device_id_type=MESH,
        )

    def wait_plane(part):
        def step(k):
            from_y, from_x = plane(k)
            for buf, sent, received in ((idx, idx_send, idx_recv), (qc, qc_send, qc_recv)):
                there = buf.at[part, from_y, from_x]
                pltpu.make_async_remote_copy(
                    there, there, sent.at[k], received.at[part, from_y, from_x],
                    device_id={"dp": side + 2 * from_y + core, "ctx": jnp.where(part == 1, pair, row) * XS + from_x},
                    device_id_type=MESH,
                ).wait_recv()

        return step

    def back_copy(part, k):
        to_y = lax.rem(y + k, 4)
        return pltpu.make_async_remote_copy(
            cross_out.at[part, to_y], cross.at[y], back_send.at[part, k], back_recv.at[y],
            device_id={"dp": y_at(side, k), "ctx": jnp.where(part == 1, pair, row) * XS + x}, device_id_type=MESH,
        )

    def own_back():
        return pltpu.make_async_copy(cross_out.at[0, y], cross.at[y], own_sem.at[QC, 1])

    def x_copy(kind, h, to):
        arg, buf = arrays[kind]
        return pltpu.make_async_remote_copy(
            arg.at[:, cols(to * LOCAL + h)], buf.at[h, x], x_send.at[kind, h, to], x_recv.at[kind, h, x],
            device_id={"dp": dp, "ctx": row * XS + to}, device_id_type=MESH,
        )

    def arrived(kind, h):
        own_copy(kind, h).wait()
        for k in range(1, XS):
            source = x_at(k)
            buf = arrays[kind][1].at[h, source]
            pltpu.make_async_remote_copy(
                buf, buf, x_send.at[kind, h, source], x_recv.at[kind, h, source],
                device_id={"dp": dp, "ctx": row * XS + source}, device_id_type=MESH,
            ).wait_recv()

    def start_x(kinds):
        def step(h):
            for k in (1, 3, 2):
                for kind in kinds:
                    x_copy(kind, h, x_at(k)).start()

        loop(0, LOCAL, step)

    first_plane = jnp.where(inner, 0, 1)

    def start_plane():
        def step(k):
            idx_copy(k).start()
            qc_copy(k).start()

        loop(first_plane, 4 * XS, step)

    def start_near():
        for kind in range(2):
            for k in (1, 3, 2):
                y_copy(kind, 0, k).start()
            core_pass(kind, 0, 0).start()

    def start_far_first():
        @pl.when(dp >= HALF)
        def _():
            for kind in range(2):
                for k in range(4):
                    y_copy(kind, 1, k).start()

    def start_far_second():
        @pl.when(first_side)
        def _():
            pl.semaphore_wait(ready, 4)
            for kind in range(2):
                for k in range(4):
                    y_copy(kind, 1, k).start()

    @pl.when(row == 0)
    def _():
        start_far_first()
        start_x((KS, VS))
        start_near()
        start_plane()
        start_far_second()
        start_x((QS,))

    @pl.when(row == 1)
    def _():
        start_plane()
        start_x((KS, VS))
        start_x((QS,))

    @pl.when(row == 2)
    def _():
        start_x((QS,))
        start_plane()
        start_x((KS, VS))

    @pl.when(row == 3)
    def _():
        start_far_first()
        start_x((QS,))
        start_near()
        start_plane()
        start_far_second()
        start_x((KS, VS))

    def z_copy(kind, h):
        src, dst, to = {
            ZK: (ks.at[h], k0.at[h], 1),
            ZV: (vs.at[h], v0.at[h], 1),
            ZQ2: (qs.at[h], q2.at[h], 1),
            ZQ3: (qs.at[h], q3.at[h], 1),
            ZQ3B: (qs.at[h], q3.at[h], 2),
            ZO2: (part_out.at[0, h], part_in.at[0, h], 2),
            ZS2: (stat_out.at[0, h], stat_in.at[0, h], 2),
            ZO3: (part_out.at[1, h], part_in.at[0, h], 3),
            ZS3: (stat_out.at[1, h], stat_in.at[0, h], 3),
            ZO3B: (part_out.at[1, h], part_in.at[1, h], 3),
            ZS3B: (stat_out.at[1, h], stat_in.at[1, h], 3),
        }[kind]
        return pltpu.make_async_remote_copy(
            src, dst, z_send.at[kind, h], z_recv.at[kind, h],
            device_id={"dp": dp, "ctx": to * XS + x}, device_id_type=MESH,
        )

    def relay(h):
        @pl.when(row == 0)
        def _():
            arrived(KS, h)
            z_copy(ZK, h).start()
            arrived(VS, h)
            z_copy(ZV, h).start()

        @pl.when(row == 2)
        def _():
            arrived(QS, h)
            z_copy(ZQ2, h).start()

        @pl.when(row == 3)
        def _():
            arrived(QS, h)
            z_copy(ZQ3, h).start()
            z_copy(ZQ3B, h).start()

    def core_stage():
        for far in range(2):
            for kind in range(2):
                for k in (0, 1, 3, 2)[1 - far :]:
                    wait_shard(kind, y_at(away if far else side, k))
                    core_pass(kind, far, k).start()

    diagonal = lax.broadcasted_iota(jnp.int32, (ROWS, ROWS), 0) >= lax.broadcasted_iota(jnp.int32, (ROWS, ROWS), 1)
    eye = lax.broadcasted_iota(jnp.int32, (TOK, TOK), 0) == lax.broadcasted_iota(jnp.int32, (TOK, TOK), 1)

    def score_block(queries, h, b, chunks, slot):
        q = queries[h, pl.ds(b * PER, PER)].reshape(ROWS, HD)
        peak = None
        for j, (keys, values, c, masked) in enumerate(chunks):
            k = keys[h, pl.ds(c * PER, PER)].reshape(ROWS, HD)
            s = lax.dot_general(q, k, NT, preferred_element_type=jnp.float32)
            if masked:
                s = jnp.where(diagonal, s, -1e30)
            scores[slot, j] = s
            folded = jnp.maximum(s[:, :HD], s[:, HD:])
            peak = folded if peak is None else jnp.maximum(peak, folded)
        return jnp.max(peak, axis=1, keepdims=True)

    def weigh_block(h, chunks, slot, top):
        total = jnp.zeros((ROWS, HD), jnp.float32)
        acc = jnp.zeros((ROWS, HD), jnp.float32)
        for j, (keys, values, c, masked) in enumerate(chunks):
            w = jnp.exp2((scores[slot, j] - top) * EXPO)
            total = total + (w[:, :HD] + w[:, HD:])
            v = values[h, pl.ds(c * PER, PER)].reshape(ROWS, HD)
            acc = acc + lax.dot_general(w.astype(jnp.bfloat16), v, NN, preferred_element_type=jnp.float32)
        return jnp.sum(total, axis=1, keepdims=True), acc

    def attend(h, jobs):
        tops_of = []
        for n in range(len(jobs) + 1):
            if n < len(jobs):
                queries, b, chunks, done = jobs[n]
                tops_of.append(score_block(queries, h, b, chunks, n % 3))
            if n >= 1:
                queries, b, chunks, done = jobs[n - 1]
                done(b, tops_of[n - 1], *weigh_block(h, chunks, (n - 1) % 3, tops_of[n - 1]))

    def partial(queries, h, chunks, place):
        def done(b, top, total, acc):
            part_out[place, h, pl.ds(b * PER, PER)] = (acc / total).astype(jnp.bfloat16).reshape(PER, TOK, HD)
            for p in range(PER):
                rows = slice(p * TOK, (p + 1) * TOK)
                at = b * PER + p
                stat_out[place, h, at : at + 1] = jnp.sum(jnp.where(eye, top[rows], 0.0), axis=0, keepdims=True)
                stat_out[place, h, XS + at : XS + at + 1] = jnp.sum(jnp.where(eye, total[rows], 0.0), axis=0, keepdims=True)

        return [(queries, b, chunks, done) for b in range(QB)]

    def own_rows(h, extra, final):
        def done(b, top, total, acc):
            at = h * QB + b
            if final:
                accs[at] = acc / total
            else:
                accs[at] = acc
                tops[at] = jnp.broadcast_to(top, (ROWS, HD))
                totals[at] = jnp.broadcast_to(total, (ROWS, HD))

        return [(qs, b, extra + [(ks, vs, c, c == b) for c in range(b + 1)], done) for b in range(QB)]

    whole_own = [(ks, vs, c, False) for c in range(QB)]
    whole_first = [(k0, v0, c, False) for c in range(QB)]

    def between(h):
        @pl.when(row == 1)
        def _():
            arrived(KS, h)
            arrived(VS, h)
            z_copy(ZK, h).wait_recv()
            z_copy(ZV, h).wait_recv()
            z_copy(ZQ2, h).wait_recv()
            z_copy(ZQ3, h).wait_recv()
            attend(h, partial(q2, h, whole_first + whole_own, 0) + partial(q3, h, whole_first + whole_own, 1))
            z_copy(ZO2, h).start()
            z_copy(ZS2, h).start()
            z_copy(ZO3, h).start()
            z_copy(ZS3, h).start()

        @pl.when(row == 2)
        def _():
            arrived(KS, h)
            arrived(VS, h)
            z_copy(ZQ3B, h).wait_recv()
            attend(h, partial(q3, h, whole_own, 1))
            z_copy(ZO3B, h).start()
            z_copy(ZS3B, h).start()

    def own_others(h):
        @pl.when(row == 0)
        def _():
            arrived(QS, h)
            attend(h, own_rows(h, [], True))

        @pl.when(row == 1)
        def _():
            arrived(QS, h)
            attend(h, own_rows(h, whole_first, True))

        @pl.when(row == 2)
        def _():
            attend(h, own_rows(h, [], False))

        @pl.when(row == 3)
        def _():
            arrived(KS, h)
            arrived(VS, h)
            attend(h, own_rows(h, [], False))

    def cross_document(part, k):
        doc = lax.rem(y + k, 4)
        groups = [(t, g) for t in range(XS) for g in range(TOK // GROUP)]
        picks = [[idx_s[part, doc, t, 0, g * NEIGH + n] for n in range(NEIGH)] for t, g in groups]
        s = []
        for (t, g), pick in zip(groups, picks):
            keys = jnp.concatenate([kd[block] for block in pick], axis=0)
            q = qc[part, doc, t, pl.ds(g * GROUP, GROUP), :]
            s.append(lax.dot_general(q, keys, NT, preferred_element_type=jnp.float32))
        top = [jnp.max(one, axis=1, keepdims=True) for one in s]
        w = [jnp.exp2((one - high) * EXPO) for one, high in zip(s, top)]
        total = [jnp.sum(one, axis=1, keepdims=True) for one in w]
        o = []
        for one, pick in zip(w, picks):
            values = jnp.concatenate([vd[block] for block in pick], axis=0)
            o.append(lax.dot_general(one.astype(jnp.bfloat16), values, NN, preferred_element_type=jnp.float32))
        for (t, g), one, whole in zip(groups, o, total):
            cross_out[part, doc, t, pl.ds(g * GROUP, GROUP), :] = (one / whole).astype(jnp.bfloat16)

        here = (part == 0) & (k == 0)

        @pl.when(jnp.logical_not(here))
        def _():
            back_copy(part, k).start()

        @pl.when(here)
        def _():
            own_back().start()

    def cross_stage():
        own_qc().wait()
        for kind in range(2):
            own_db(kind).wait()

        def wait_other_core(k):
            for kind in range(2):
                wait_shard(kind, 2 * k + 1 - core)

        loop(0, HALF, wait_other_core)

        def cross_row_of(n):
            part = 1 - n
            loop(n, 4 * XS, wait_plane(part))
            numbers = pltpu.make_async_copy(idx.at[part], idx_s.at[part], number_sem)
            numbers.start()
            numbers.wait()
            loop(0, 4, lambda k: cross_document(part, 3 - k))

        loop(0, 2, cross_row_of)

    @pl.when(row == 0)
    def _():
        loop(0, LOCAL, relay)

    @pl.when(row >= 2)
    def _():
        loop(0, LOCAL, relay)

    @pl.when(edge)
    def _():
        core_stage()
        cross_stage()

    loop(0, LOCAL, between)

    def merge(h, parts):
        for b in range(QB):
            at = h * QB + b
            for p in range(PER):
                rows = slice(p * TOK, (p + 1) * TOK)
                sub = b * PER + p
                top = tops[at, rows, :1]
                others = []
                for place in range(parts):
                    column = [
                        jnp.sum(jnp.where(eye, stat_in[place, h, n : n + 1], 0.0), axis=1, keepdims=True)
                        for n in (sub, XS + sub)
                    ]
                    others.append(column)
                peak = top
                for other_top, _ in others:
                    peak = jnp.maximum(peak, other_top)
                keep = jnp.exp2((top - peak) * EXPO)
                total = totals[at, rows, :1] * keep
                acc = accs[at, rows, :] * keep
                for place, (other_top, other_total) in enumerate(others):
                    w = jnp.exp2((other_top - peak) * EXPO) * other_total
                    total = total + w
                    acc = acc + part_in[place, h, sub].astype(jnp.float32) * w
                accs[at, rows, :] = acc / total

    def out_copy(h, t):
        return pltpu.make_async_remote_copy(
            mixed.at[h, t], out_ref.at[:, cols(x * LOCAL + h)], x_send.at[OUT, h, t], x_recv.at[OUT, h, x],
            device_id={"dp": dp, "ctx": row * XS + t}, device_id_type=MESH,
        )

    def own_out(h):
        return pltpu.make_async_copy(mixed.at[h, x], out_ref.at[:, cols(x * LOCAL + h)], own_sem.at[OUT, h])

    def emit(h):
        @pl.when(row == 2)
        def _():
            z_copy(ZO2, h).wait_recv()
            z_copy(ZS2, h).wait_recv()
            merge(h, 1)

        @pl.when(row == 3)
        def _():
            z_copy(ZO3, h).wait_recv()
            z_copy(ZS3, h).wait_recv()
            z_copy(ZO3B, h).wait_recv()
            z_copy(ZS3B, h).wait_recv()
            merge(h, 2)

        @pl.when((h != y) | inner)
        def _():
            there = cross.at[h]
            pltpu.make_async_remote_copy(
                there, there, back_send.at[0, 0], back_recv.at[h],
                device_id={"dp": side + 2 * h + core, "ctx": cross_row * XS + x}, device_id_type=MESH,
            ).wait_recv()

        @pl.when((h == y) & edge)
        def _():
            own_back().wait()

        self_out = accs[pl.ds(h * QB, QB)].astype(jnp.bfloat16).astype(jnp.float32).reshape(XS, TOK, HD)
        mixed[h] = (self_out + cross[h].astype(jnp.float32)).astype(jnp.bfloat16)
        for k in (1, 3, 2):
            out_copy(h, x_at(k)).start()
        own_out(h).start()

    def own_and_emit(h):
        own_others(h)
        emit(h)

    loop(0, LOCAL, own_and_emit)

    @pl.when(edge)
    def _():
        for kind in range(2):
            for far in range(2):
                for k in range(1 - far, 4):
                    y_copy(kind, far, k).wait_send()
                for k in range(4):
                    core_pass(kind, far, k).wait_send()
        for k in range(1, 4):
            back_copy(0, k).wait_send()
        for k in range(4):
            back_copy(1, k).wait_send()

    def finish_plane(k):
        idx_copy(k).wait_send()
        qc_copy(k).wait_send()

    loop(first_plane, 4 * XS, finish_plane)
    def finish(h):
        for k in range(1, XS):
            peer = x_at(k)
            for kind in (KS, VS, QS):
                x_copy(kind, h, peer).wait_send()
        for at, kinds in enumerate(((ZK, ZV), (ZO2, ZS2, ZO3, ZS3), (ZQ2, ZO3B, ZS3B), (ZQ3, ZQ3B))):

            @pl.when(row == at)
            def _():
                for kind in kinds:
                    z_copy(kind, h).wait_send()

    def finish_out(h):
        own_out(h).wait()
        for k in range(1, XS):
            peer = x_at(k)
            out_copy(h, peer).wait_send()
            pltpu.make_async_remote_copy(
                mixed.at[h, peer], out_ref.at[:, cols(peer * LOCAL + h)], x_send.at[OUT, h, peer], x_recv.at[OUT, h, peer],
                device_id={"dp": dp, "ctx": row * XS + peer}, device_id_type=MESH,
            ).wait_recv()

    loop(0, LOCAL, finish)
    loop(0, LOCAL, finish_out)


def shards(q_self, k_self, v_self, q_cross, db_keys, db_values, nb_shard, nb_row):
    anywhere = pl.BlockSpec(memory_space=pl.ANY)
    scalars = pl.BlockSpec(memory_space=pltpu.SMEM)
    heads = pltpu.VMEM((LOCAL, XS, TOK, HD), jnp.bfloat16)
    database = pltpu.VMEM((N_DP * DB_DEV, NLEN, HD), jnp.bfloat16)
    state = pltpu.VMEM((LOCAL * QB, ROWS, HD), jnp.float32)
    parts = pltpu.VMEM((2, LOCAL, XS, TOK, HD), jnp.bfloat16)
    stats = pltpu.VMEM((2, LOCAL, 8, 128), jnp.float32)
    dma = pltpu.SemaphoreType.DMA
    out = pl.pallas_call(
        kernel,
        out_shape=jax.ShapeDtypeStruct((TOK, HEADS * HD), jnp.bfloat16),
        in_specs=[anywhere] * 6 + [scalars] * 2,
        out_specs=anywhere,
        scratch_shapes=[
            heads, heads, heads, parts, heads, heads, heads, heads, database, database,
            pltpu.VMEM((2, 4, XS, 8, 128), jnp.int32),
            pltpu.SMEM((2, 4, XS, 8, 128), jnp.int32),
            heads,
            pltpu.VMEM((3, 2 * QB, ROWS, ROWS), jnp.float32),
            state, state, state,
            parts, stats, parts, stats, heads, parts,
            dma((5, LOCAL, XS)), dma((5, LOCAL, XS)), dma((4 * XS,)), dma((2, 4, XS)), dma((4 * XS,)), dma((2, 4, XS)),
            dma((2, 4)), dma((4,)), dma((11, LOCAL)), dma((11, LOCAL)),
            dma((2, 2, 4)), dma((2, 2, 4)), dma((2, N_DP)), dma((5, LOCAL)), dma((2,)), dma,
            pltpu.SemaphoreType.REGULAR,
        ],
        compiler_params=pltpu.CompilerParams(
            collective_id=0, has_side_effects=True, vmem_limit_bytes=53 * 1024 * 1024
        ),
    )(q_self[0], k_self[0], v_self[0], q_cross[0], db_keys, db_values, nb_shard, nb_row)
    return out[None]


def solution(mesh):
    return jax.shard_map(
        shards,
        mesh=mesh,
        in_specs=(
            P("dp", "ctx", None),
            P("dp", "ctx", None),
            P("dp", "ctx", None),
            P("dp", "ctx", None),
            P("dp", None, None),
            P("dp", None, None),
            P("dp", "ctx", None),
            P("dp", "ctx", None),
        ),
        out_specs=P("dp", "ctx", None),
        check_vma=False,
    )
```
